32 devices in a mesh: clip: 2 (over y), row: 16 (over z, x, core).
Axes of the slice: x: 2, y: 2, z: 4, core: 2. Of those that a mesh axis runs over, the one named last changes fastest.
Arguments:
- frames: bfloat16 [3, 48, 512], P(None, None, ('clip', 'row')), parts along dimension 2, may hold values from -1 to 1
- frame_owner: int32 [32], P('clip'), parts along dimension 0, may hold values from 0 to 15, each once
- picks: int32 [16], P('clip'), parts along dimension 0, may hold values from 0 to 15
- patch_weight: bfloat16 [768, 1024], replicated, may hold values from -0.21875 to 0.21875
- patch_bias: float32 [1024], replicated, may hold values from -6 to 6
- norm_gain: float32 [1024], replicated, may hold values from 0.1 to 1.9
- head_weight: bfloat16 [1024, 1024], replicated, may hold values from -0.1875 to 0.1875
- head_bias: float32 [1024], replicated, may hold values from -6 to 6
- head_out: float32 [1024], replicated, may hold values from -6 to 6
- hidden_state: bfloat16 [96, 16, 16, 128], P(('clip', 'row')), parts along dimension 0
- group_gain: float32 [128], replicated, may hold values from 0.1 to 1.9
- group_shift: float32 [128], replicated, may hold values from -6 to 6
- out_weight: bfloat16 [3, 3, 3, 3, 128], replicated, may hold values from -0.625 to 0.625
- inner_weight: bfloat16 [3, 3, 3, 128, 128], replicated, may hold values from -0.109375 to 0.109375
Outputs:
- inner_grad: bfloat16 [96, 16, 16, 128], P(('clip', 'row')), parts along dimension 0
The draws below stay inside these ranges and needn't reach their ends.
There are 2 independent parts, one for each index of `clip`. The reference program is written for one: setup_inputs(seed, part) draws one part's arguments, and reference() takes and returns one part's arrays. A program takes and returns all parts, laid end to end along the dimension named above; an argument that names none is the same for every part. Nothing has to cross between parts.
Inputs may be any that keep to these rules, and one draw needn't show every extreme that they name: `frame_owner`: each of the 16 frames appears once.
All inputs are finite; a program needn't handle non-finite values.
Results may differ from the reference program's by a relative error of at most 0.0051.
The reference program's roundings to bfloat16 on the way (of `tokens`, `token_grad`, `pixel_grad`, `ordered` and `state_grad`) count: a program that leaves them out, or rounds other values in their place, can miss the bound.
Values may be sent and summed in bfloat16 or wider, within the bound.
No kernel may reach another device: no remote copies, remote signals or barrier semaphores. Data moves between devices by JAX's collectives and lax.ppermute only.
A program may use at most 192 MiB of HBM per device.

```python
import jax
import jax.numpy as jnp
from jax import lax

D = 1024
PATCH = 16
PIX = 768
C = 128
GROUPS = 32
FRAMES = 16
NPICK = 8
H = 48
W = 16


def draw_hidden_state(key, part):
    key_a, key_b, key_c = jax.random.split(jax.random.fold_in(key, 11), 3)
    row_pos = jnp.arange(H, dtype=jnp.float32) / (H - 1)
    random_part = jax.random.normal(key_a, (H, FRAMES, W, C), jnp.float32)
    row_scale = jnp.exp(jnp.log(3.0) * row_pos)
    trend = 2.0 * (2.0 * row_pos - 1.0)
    chan_scale = jnp.exp(jax.random.uniform(key_b, (C,), jnp.float32, jnp.log(0.5), jnp.log(2.0)))
    offset = 0.5 * jax.random.normal(key_c, (C,), jnp.float32)
    shaped = random_part * row_scale[:, None, None, None] + trend[:, None, None, None]
    result_values = shaped * chan_scale + offset
    return result_values.astype(jnp.bfloat16)


def touch_ends(result, stream_key, least, largest):
    shape = result.shape
    spot = [jax.random.randint(jax.random.fold_in(stream_key, axis), (), 0, shape[axis]) for axis in range(len(shape))]
    result = result.at[tuple(spot)].set(least)
    longest = shape.index(max(shape))
    spot[longest] = (spot[longest] + 1) % shape[longest]
    return result.at[tuple(spot)].set(largest)


def levels(own_key, extent, cuts, smallest, top_value):
    factor_of = 1.0
    for dim, blocks in cuts:
        draws = jax.random.uniform(jax.random.fold_in(jax.random.fold_in(own_key, 6), dim), (blocks,), jnp.float32, smallest / len(cuts), top_value / len(cuts))
        factor_of = factor_of * jnp.repeat(jnp.exp(draws), extent[dim] // blocks).reshape((-1,) + (1,) * (len(extent) - 1 - dim))
    return factor_of


def scatter_about(key, shape, width, reach, kind=jnp.bfloat16):
    drawn = width * jax.random.normal(key, shape, jnp.float32)
    return jnp.clip(drawn, min=-reach, max=reach).astype(kind)


def setup_inputs(seed: int = 0, part: int = 0) -> dict:
    seeds = jax.random.split(jax.random.key(seed), 15)
    own_keys = jax.random.split(jax.random.fold_in(seeds[14], part), 15)
    frames = jnp.clip(jax.random.uniform(own_keys[0], (3, H, FRAMES * W), jnp.float32, -1.0, 1.0) * levels(own_keys[0], (3, H, FRAMES * W), ((2, 16),), -0.4, 0.0), -1.0, 1.0).astype(jnp.bfloat16)
    frame_owner = jax.random.permutation(own_keys[1], FRAMES).astype(jnp.int32)
    picks = touch_ends(jax.random.randint(own_keys[2], (NPICK,), 0, FRAMES), jax.random.fold_in(own_keys[2], 1), 0, FRAMES - 1).astype(jnp.int32)
    patch_weight = scatter_about(seeds[3], (PIX, D), PIX ** -0.5, 0.21875)
    patch_bias = scatter_about(seeds[4], (D,), 1.0, 6.0, jnp.float32)
    norm_gain = jnp.clip(1.0 + 0.18 * jax.random.normal(seeds[5], (D,), jnp.float32), 0.1, 1.9)
    head_weight = scatter_about(seeds[6], (D, D), D ** -0.5, 0.1875)
    head_bias = scatter_about(seeds[7], (D,), 1.0, 6.0, jnp.float32)
    head_out = scatter_about(seeds[8], (D,), 1.0, 6.0, jnp.float32)
    hidden_state = draw_hidden_state(jax.random.fold_in(jax.random.fold_in(seeds[14], part), 71), part)
    group_gain = jnp.clip(1.0 + 0.18 * jax.random.normal(seeds[10], (C,), jnp.float32), 0.1, 1.9)
    group_shift = scatter_about(seeds[11], (C,), 1.0, 6.0, jnp.float32)
    out_weight = scatter_about(seeds[12], (3, 3, 3, 3, C), (27 * 3) ** -0.5, 0.625)
    inner_weight = scatter_about(seeds[13], (3, 3, 3, C, C), (27 * C) ** -0.5, 0.109375)
    return dict(frames=frames, frame_owner=frame_owner, picks=picks, patch_weight=patch_weight, patch_bias=patch_bias, norm_gain=norm_gain, head_weight=head_weight, head_bias=head_bias, head_out=head_out, hidden_state=hidden_state, group_gain=group_gain, group_shift=group_shift, out_weight=out_weight, inner_weight=inner_weight)


eps_norm = 1e-06

def silu_slope(values):
    sigmoid = jax.nn.sigmoid(values)
    return sigmoid * (1.0 + values * (1.0 - sigmoid))

def pixel_rows(padded, out_weight, amount):
    frame_count = padded.shape[2]
    columns = padded.shape[3]
    widened = jnp.pad(padded, ((0, 0), (0, 0), (0, 2), (1, 1)))
    summed = jnp.zeros((amount * frame_count * columns, out_weight.shape[4]), jnp.float32)
    for time_tap in range(3):
        for row_tap in range(3):
            for col_tap in range(3):
                window = widened[:, 2 - row_tap:2 - row_tap + amount, 2 - time_tap:2 - time_tap + frame_count, 2 - col_tap:2 - col_tap + columns]
                flat_window = window.reshape(3, amount * frame_count * columns).T
                summed = summed + jnp.dot(flat_window, out_weight[time_tap, row_tap, col_tap], preferred_element_type=jnp.float32)
    return summed.reshape(amount, frame_count, columns, out_weight.shape[4])

def inner_rows(padded, inner_weight, amount):
    frame_count = padded.shape[1]
    columns = padded.shape[2]
    channel_count = padded.shape[3]
    widened = jnp.pad(padded, ((0, 0), (0, 2), (1, 1), (0, 0)))
    summed = jnp.zeros((amount * frame_count * columns, inner_weight.shape[3]), jnp.float32)
    for time_tap in range(3):
        for row_tap in range(3):
            for col_tap in range(3):
                window = widened[2 - row_tap:2 - row_tap + amount, 2 - time_tap:2 - time_tap + frame_count, 2 - col_tap:2 - col_tap + columns, :]
                summed = summed + jnp.dot(window.reshape(amount * frame_count * columns, channel_count), inner_weight[time_tap, row_tap, col_tap].T, preferred_element_type=jnp.float32)
    return summed.reshape(amount, frame_count, columns, inner_weight.shape[3])

def by_blocks(padded, row_axis, height, function):
    row_block = 8

    def one_block(start):
        piece = lax.dynamic_slice_in_dim(padded, start, row_block + 2, row_axis)
        return function(piece, row_block)
    starts = jnp.arange(height // row_block, dtype=jnp.int32) * row_block
    blocks = lax.map(one_block, starts)
    return blocks.reshape((height,) + blocks.shape[2:])

def reference(frames, frame_owner, picks, patch_weight, patch_bias, norm_gain, head_weight, head_bias, head_out, hidden_state, group_gain, group_shift, out_weight, inner_weight):
    height = frames.shape[1]
    frame_width = hidden_state.shape[2]
    total_columns = frames.shape[2]
    tokens = frames.reshape(3, height // PATCH, PATCH, total_columns // PATCH, PATCH).transpose(1, 3, 0, 2, 4).reshape(-1, PIX)
    embedded = jnp.dot(tokens, patch_weight, preferred_element_type=jnp.float32) + patch_bias
    centred = embedded - lax.optimization_barrier(jnp.mean(embedded, axis=1, keepdims=True))
    inv_spread = lax.rsqrt(lax.optimization_barrier(jnp.mean(centred * centred, axis=1, keepdims=True)) + eps_norm)
    normed = centred * inv_spread
    per_slot = (normed * norm_gain).reshape(height // PATCH, FRAMES, frame_width // PATCH, D)
    pooled = lax.optimization_barrier(jnp.mean(per_slot, axis=(0, 2)))
    head_full = head_weight.astype(jnp.float32)
    before = jnp.dot(pooled, head_full, precision=lax.Precision.HIGHEST) + head_bias
    pulled = jnp.dot(head_out * silu_slope(before), head_full.T, precision=lax.Precision.HIGHEST)
    picked = lax.optimization_barrier(jnp.sum((picks[:, None] == frame_owner[None, :]).astype(jnp.float32), axis=0))
    slot_grad = picked[:, None] * pulled
    spread_grad = jnp.broadcast_to(slot_grad[None, :, None, :], per_slot.shape).reshape(-1, D)
    scaled = norm_gain * spread_grad
    token_grad = inv_spread * (scaled - lax.optimization_barrier(jnp.mean(scaled, axis=1, keepdims=True)) - normed * lax.optimization_barrier(jnp.mean(scaled * normed, axis=1, keepdims=True)))
    token_grad = token_grad.astype(jnp.bfloat16)
    patch_grad = jnp.dot(token_grad, patch_weight.T, preferred_element_type=jnp.float32)
    pixel_grad = patch_grad.reshape(height // PATCH, total_columns // PATCH, 3, PATCH, PATCH).transpose(2, 0, 3, 1, 4).reshape(3, height, total_columns).astype(jnp.bfloat16)
    by_slot = pixel_grad.reshape(3, height, FRAMES, frame_width)
    owner_table = (frame_owner[:, None] == jnp.arange(FRAMES, dtype=jnp.int32)[None, :]).astype(jnp.float32)
    ordered = jnp.einsum('krbw,bf->krfw', by_slot.astype(jnp.float32), owner_table).astype(jnp.bfloat16)
    grouped = hidden_state.astype(jnp.float32).reshape(hidden_state.shape[:3] + (GROUPS, C // GROUPS))
    cell_total = grouped.size // GROUPS
    group_mean = lax.optimization_barrier(jnp.sum(grouped, axis=(0, 1, 2, 4))) / cell_total
    second_mean = lax.optimization_barrier(jnp.sum(grouped * grouped, axis=(0, 1, 2, 4))) / cell_total
    inverse = lax.rsqrt(second_mean - group_mean * group_mean + eps_norm)
    normed_state = (grouped - group_mean[:, None]) * inverse[:, None]
    gain_table = group_gain.reshape(GROUPS, C // GROUPS)
    affine = normed_state * gain_table + group_shift.reshape(GROUPS, C // GROUPS)
    padded_pixels = jnp.pad(ordered, ((0, 0), (1, 1), (0, 0), (0, 0)))
    slope_in = by_blocks(padded_pixels, 1, height, lambda piece, amount: pixel_rows(piece, out_weight, amount))
    upstream = slope_in.reshape(grouped.shape) * silu_slope(affine) * gain_table
    first_part = lax.optimization_barrier(jnp.sum(upstream, axis=(0, 1, 2, 4))) / cell_total
    second_part = lax.optimization_barrier(jnp.sum(upstream * normed_state, axis=(0, 1, 2, 4))) / cell_total
    state_grad = ((upstream - first_part[:, None] - normed_state * second_part[:, None]) * inverse[:, None]).reshape(hidden_state.shape).astype(jnp.bfloat16)
    padded_state = jnp.pad(state_grad, ((1, 1), (0, 0), (0, 0), (0, 0)))
    inner_grad = by_blocks(padded_state, 0, height, lambda piece, amount: inner_rows(piece, inner_weight, amount))
    return inner_grad.astype(jnp.bfloat16)
```

```python
import functools

import jax
import jax.numpy as jnp
from jax import lax
from jax.experimental import pallas as pl
from jax.experimental.pallas import tpu as pltpu
from jax.sharding import PartitionSpec as P

PATCH = 16
GROUPS = 32
FRAMES = 16
LANES = 128
eps_norm = 1e-06
BF16 = jnp.bfloat16
F32 = jnp.float32
BIG = 56 * 1024 * 1024


def iota(shape, dim):
    return lax.broadcasted_iota(jnp.int32, shape, dim)


def ones_where(condition):
    return jnp.where(condition, 1.0, 0.0).astype(BF16)


def matmul(left, right):
    return jnp.dot(left, right, preferred_element_type=F32)


def matmul_t(left, right):
    return lax.dot_general(left, right, (((1,), (1,)), ((), ())), preferred_element_type=F32)


def pieces(row):
    high = row.astype(BF16).astype(F32)
    rest = row - high
    middle = rest.astype(BF16).astype(F32)
    low = rest - middle
    place = iota((16, row.shape[1]), 0)
    stacked = jnp.where(place == 0, high, jnp.where(place == 1, middle, jnp.where(place == 2, low, 0.0)))
    return stacked.astype(BF16)


def silu_slope(values):
    sigmoid = jax.nn.sigmoid(values)
    return sigmoid * (1.0 + values * (1.0 - sigmoid))


def to_tokens(pixels, token_rows):
    channels, height, columns = pixels.shape
    flat = pixels.reshape(channels * height, columns)
    width = channels * PATCH * columns
    spread = ones_where((iota((columns, width), 1) % columns) == iota((columns, width), 0))
    tiled = matmul(flat, spread)
    place = iota((channels * height, 1), 0)
    code = place // height * PATCH + place % PATCH
    kept = jnp.where(code == iota((channels * height, width), 1) // columns, tiled, 0.0).astype(BF16)
    column = iota((token_rows, channels * height), 1)
    chosen = ones_where(column % height // PATCH == iota((token_rows, channels * height), 0))
    return matmul(chosen, kept).astype(BF16)


def forward_part(frames, bias, gain, load_patch):
    height = frames.shape[1]
    count = height // PATCH
    token_rows = -(-count // 16) * 16
    tokens = to_tokens(frames[...], token_rows)
    embedded = bias[...]
    for low, high, weight in load_patch():
        embedded = embedded + matmul(tokens[:, low:high], weight)
    centred = embedded - jnp.mean(embedded, axis=1, keepdims=True)
    inv_spread = lax.rsqrt(jnp.mean(centred * centred, axis=1, keepdims=True) + eps_norm)
    normed = centred * inv_spread
    real = iota((token_rows, 1), 0) < count
    pooled = jnp.sum(jnp.where(real, normed * gain[...], 0.0), axis=0, keepdims=True)
    return normed, inv_spread, pooled


def send_plan(devices, height, own_rows):
    message = iota((4 * devices, 1), 0)
    target, colour = message // 4, message % 4
    plans = []
    for j in range(own_rows + 4):
        row = target * own_rows - 2 + j
        wanted = jnp.where((row >= 0) & (row < height) & (colour < 3), colour * height + row, -1)
        plans.append(ones_where(iota((4 * devices, 3 * height), 1) == wanted))
    return plans


def group_sums(hidden):
    channels = hidden.shape[-1]
    values = hidden.reshape(-1, channels).astype(F32)
    first = jnp.sum(values, axis=0, keepdims=True)
    second = jnp.sum(values * values, axis=0, keepdims=True)
    lane = iota((channels, LANES), 1)
    group = iota((channels, LANES), 0) // (channels // GROUPS)
    low = matmul(pieces(first), ones_where(lane == group))
    high = matmul(pieces(second), ones_where(lane == group + GROUPS))
    return jnp.sum(low + high, axis=0, keepdims=True)


def backward_part(
    owner, picks, hidden, gain, head_bias, head_out, normed, inv_spread, pooled, weight, head, slot, plans, send
):
    count = weight.shape[0]
    height = plans[0].shape[1] // 3
    before = jnp.sum(matmul(pieces(pooled), head()), axis=0, keepdims=True) + head_bias[...]
    wanted = owner[slot]
    picked = jnp.int32(0)
    for k in range(picks.shape[0]):
        picked = picked + jnp.where(picks[k] == wanted, 1, 0)
    pulled = jnp.sum(matmul_t(pieces(head_out[...] * silu_slope(before)), head()), axis=0, keepdims=True)
    scaled = gain[...] * (picked.astype(F32) * pulled)
    token_grad = inv_spread * (
        scaled
        - jnp.mean(scaled, axis=1, keepdims=True)
        - normed * jnp.mean(scaled * normed, axis=1, keepdims=True)
    )
    patch_grad = matmul_t(token_grad.astype(BF16), weight[...]).astype(BF16)
    rows = 3 * height
    place = iota((rows, 1), 0)
    copied = matmul(
        ones_where(place % height // PATCH == iota((rows, normed.shape[0]), 1)), patch_grad
    )
    code = place // height * PATCH + place % PATCH
    kept = jnp.where(code == iota((rows, count), 1) // PATCH, copied, 0.0).astype(BF16)
    fold = ones_where(iota((count, LANES), 0) % PATCH == iota((count, LANES), 1) % PATCH)
    pixels = matmul(kept, fold).astype(BF16)
    messages = plans[0].shape[0]
    lane = iota((messages, LANES), 1) // PATCH
    result = jnp.where(iota((messages, LANES), 0) % 4 == 3, group_sums(hidden[...]), 0.0)
    for j, plan in enumerate(plans):
        result = result + jnp.where(lane == j, matmul(plan, pixels), 0.0)
    send[...] = result.reshape(send.shape)


def reward_kernel(
    owner, picks, place, frames, hidden, bias, gain, head_bias, head_out, patch_far, head_far, send, patch, head, sems
):
    steps = 3
    depth = patch.shape[0] // steps
    copies = [
        pltpu.make_async_copy(
            patch_far.at[pl.ds(i * depth, depth)], patch.at[pl.ds(i * depth, depth)], sems.at[i]
        )
        for i in range(steps)
    ]
    copies.append(pltpu.make_async_copy(head_far, head, sems.at[steps]))
    for copy in copies:
        copy.start()

    def load_patch():
        for i in range(steps):
            copies[i].wait()
            yield i * depth, (i + 1) * depth, patch[i * depth : (i + 1) * depth, :]

    devices = send.shape[0]
    plans = send_plan(devices, frames.shape[1], hidden.shape[0])
    normed, inv_spread, pooled = forward_part(frames, bias, gain, load_patch)
    pooled = pooled / (frames.shape[1] // PATCH)
    copies[steps].wait()
    backward_part(
        owner,
        picks,
        hidden,
        gain,
        head_bias,
        head_out,
        normed,
        inv_spread,
        pooled,
        patch,
        lambda: head[...],
        place[0],
        plans,
        send,
    )


def forward_kernel(frames, bias, gain, patch, normed, inv_spread, pooled):
    width = patch.shape[0]
    normed[...], spread, pooled[...] = forward_part(frames, bias, gain, lambda: [(0, width, patch[...])])
    inv_spread[...] = jnp.broadcast_to(spread, inv_spread.shape)


def backward_kernel(
    owner, picks, place, hidden, gain, head_bias, head_out, normed, inv_spread, pooled, patch, head, send, height
):
    backward_part(
        owner,
        picks,
        hidden,
        gain,
        head_bias,
        head_out,
        normed[...],
        inv_spread[...][:, :1],
        pooled[...],
        patch,
        lambda: head[...],
        place[0],
        send_plan(send.shape[0], height, hidden.shape[0]),
        send,
    )


SMEM = pl.BlockSpec(memory_space=pltpu.SMEM)
VMEM = pl.BlockSpec(memory_space=pltpu.VMEM)
FAR = pl.BlockSpec(memory_space=pl.ANY)


def params():
    return pltpu.CompilerParams(vmem_limit_bytes=BIG)


def prepare_kernel(out_weight, inner_weight, wide, turned, scratch):
    window = scratch.shape[0] // 9
    amount = scratch.shape[1] // LANES
    scratch[...] = jnp.zeros_like(scratch)
    for a in range(3):
        for e in range(3):
            base = (a * 3 + e) * window
            for b in range(3):
                piece = out_weight[a, b, e].astype(F32)
                for i in range(amount):
                    start = base + 3 * (i - b + 2)
                    scratch[start : start + 3, i * LANES : (i + 1) * LANES] = piece
    wide[...] = scratch[...].astype(BF16)
    size = inner_weight.shape[3]
    for b in range(3):
        for a in range(3):
            for e in range(3):
                at = ((b * 3 + a) * 3 + e) * size
                turned[at : at + size, :] = inner_weight[a, b, e].T


def slope_kernel(owner, arrived, hidden, low_edge, high_edge, gain, shift, wide, upstream, stats, sums):
    devices = arrived.shape[0]
    own_rows, frame_count, width, channels = hidden.shape
    cells = frame_count * width
    per_frame = devices // frame_count
    window = wide.shape[0] // 9
    got = arrived[...].reshape(4 * devices, LANES)
    row = iota((4 * devices, 1), 0)

    totals = jnp.sum(jnp.where(row % 4 == 3, got, 0.0), axis=0, keepdims=True)
    lane = iota((LANES, 2 * channels), 0)
    column = iota((LANES, 2 * channels), 1)
    wanted = column % channels // (channels // GROUPS) + jnp.where(column >= channels, GROUPS, 0)
    spread = jnp.sum(matmul(pieces(totals), ones_where(lane == wanted)), axis=0, keepdims=True)
    cell_total = own_rows * devices * cells * (channels // GROUPS)
    mean = spread[:, :channels] / cell_total
    inverse = lax.rsqrt(spread[:, channels:] / cell_total - mean * mean + eps_norm)
    stats[0:1, :] = mean
    stats[1:2, :] = inverse

    source = row // 4
    block = source // per_frame
    frame = jnp.zeros_like(block)
    for b in range(frame_count):
        frame = jnp.where(block == b, owner[b], frame)
    home = (frame * per_frame + source % per_frame) == iota((4 * devices, cells), 1) // PATCH
    fold = ones_where(iota((LANES, cells), 0) % PATCH == iota((LANES, cells), 1) % PATCH)
    place = iota((window, 1), 0)
    message = iota((window, 4 * devices), 1)
    held = iota((4 * devices, LANES), 1) // PATCH
    pixels = jnp.zeros((window, cells), F32)
    for j in range(own_rows + 4):
        placed = matmul(jnp.where(held == j, got, 0.0).astype(BF16), fold)
        kept = jnp.where(home, placed, 0.0).astype(BF16)
        chosen = ones_where((place // 3 == j) & (place % 3 == message % 4))
        pixels = pixels + matmul(chosen, kept)

    lane = iota((window, cells), 1)
    in_frame = lane % width
    shifted = []
    for a in range(3):
        for e in range(3):
            step = (2 - a) * width + 1 - e
            moved = pltpu.roll(pixels, (-step) % cells, 1) if step else pixels
            inside = (lane < cells - (2 - a) * width) & (in_frame >= e - 1) & (in_frame < width + e - 1)
            shifted.append(jnp.where(inside, moved, 0.0))
    stacked = jnp.concatenate(shifted, axis=0).astype(BF16)
    slopes = lax.dot_general(stacked, wide[...], (((0,), (0,)), ((), ())), preferred_element_type=F32)

    first = jnp.zeros((1, channels), F32)
    second = jnp.zeros((1, channels), F32)
    for i in range(own_rows + 2):
        if i == 0:
            state = low_edge[0]
        elif i == own_rows + 1:
            state = high_edge[0]
        else:
            state = hidden[i - 1]
        normed = (state.reshape(cells, channels).astype(F32) - mean) * inverse
        affine = normed * gain[...] + shift[...]
        up = slopes[:, i * channels : (i + 1) * channels] * silu_slope(affine) * gain[...]
        upstream[i] = up
        if 0 < i < own_rows + 1:
            first = first + jnp.sum(up, axis=0, keepdims=True)
            second = second + jnp.sum(up * normed, axis=0, keepdims=True)
    both = jnp.where(iota((2, channels), 0) == 0, first, second)
    sums[...] = jnp.broadcast_to(both[None], sums.shape)


def inner_kernel(place, arrived, hidden, low_edge, high_edge, stats, upstream, turned, out, padded):
    devices = arrived.shape[0]
    own_rows, frame_count, width, channels = hidden.shape
    cells = frame_count * width
    totals = jnp.sum(arrived[...], axis=0)
    same = ones_where(
        iota((channels, channels), 0) // (channels // GROUPS)
        == iota((channels, channels), 1) // (channels // GROUPS)
    )
    cell_total = own_rows * devices * cells * (channels // GROUPS)
    first = jnp.sum(matmul(pieces(totals[0:1]), same), axis=0, keepdims=True) / cell_total
    second = jnp.sum(matmul(pieces(totals[1:2]), same), axis=0, keepdims=True) / cell_total
    mean = stats[0:1, :]
    inverse = stats[1:2, :]
    position = place[0]
    in_frame = iota((cells, 1), 0) % width
    for i in range(own_rows + 2):
        if i == 0:
            state = low_edge[0]
        elif i == own_rows + 1:
            state = high_edge[0]
        else:
            state = hidden[i - 1]
        normed = (state.reshape(cells, channels).astype(F32) - mean) * inverse
        grad = (upstream[i] - first - normed * second) * inverse
        if i == 0:
            grad = jnp.where(position > 0, grad, 0.0)
        if i == own_rows + 1:
            grad = jnp.where(position < devices - 1, grad, 0.0)
        after = jnp.where(in_frame < width - 1, pltpu.roll(grad, cells - 1, 0), 0.0)
        prior = jnp.where(in_frame > 0, pltpu.roll(grad, 1, 0), 0.0)
        padded[i, :cells, 0:channels] = after.astype(BF16)
        padded[i, :cells, channels : 2 * channels] = grad.astype(BF16)
        padded[i, :cells, 2 * channels :] = prior.astype(BF16)
        padded[i, cells:, :] = jnp.zeros((2 * width, 3 * channels), BF16)
    depth = 3 * channels
    for r in range(own_rows):
        total = jnp.zeros((cells, channels), F32)
        for b in range(3):
            joined = jnp.concatenate(
                [padded[r - b + 2, (2 - a) * width : (2 - a) * width + cells, :] for a in range(3)], axis=1
            )
            total = total + matmul(joined, turned[b * 3 * depth : (b + 1) * 3 * depth, :])
        out[r] = total.reshape(frame_count, width, channels).astype(BF16)


def per_device(
    frames,
    frame_owner,
    picks,
    patch_weight,
    patch_bias,
    norm_gain,
    head_weight,
    head_bias,
    head_out,
    hidden_state,
    group_gain,
    group_shift,
    out_weight,
    inner_weight,
):
    devices = lax.axis_size("row")
    position = lax.axis_index("row")
    per_frame = devices // FRAMES
    height = frames.shape[1]
    own_rows, _, frame_width, channels = hidden_state.shape
    cells = FRAMES * frame_width
    width = patch_weight.shape[1]
    forward = [(i, i + 1) for i in range(devices - 1)]
    backward = [(target, source) for source, target in forward]
    low_edge = lax.ppermute(hidden_state[own_rows - 1 :], "row", forward)
    high_edge = lax.ppermute(hidden_state[:1], "row", backward)
    slot = (position // per_frame).astype(jnp.int32).reshape(1)
    bias = patch_bias.reshape(1, width)
    gain = norm_gain.reshape(1, width)
    head_bias_row = head_bias.reshape(1, width)
    head_out_row = head_out.reshape(1, width)
    message = jax.ShapeDtypeStruct((devices, 4, LANES), F32)
    if per_frame == 1:
        send = pl.pallas_call(
            reward_kernel,
            out_shape=message,
            in_specs=[SMEM] * 3 + [VMEM] * 6 + [FAR] * 2,
            out_specs=VMEM,
            scratch_shapes=[
                pltpu.VMEM(patch_weight.shape, BF16),
                pltpu.VMEM(head_weight.shape, BF16),
                pltpu.SemaphoreType.DMA((4,)),
            ],
            compiler_params=params(),
            name="reward",
        )(
            frame_owner,
            picks,
            slot,
            frames,
            hidden_state,
            bias,
            gain,
            head_bias_row,
            head_out_row,
            patch_weight,
            head_weight,
        )
    else:
        count = height // PATCH
        token_rows = -(-count // 16) * 16
        normed, inv_spread, partial = pl.pallas_call(
            forward_kernel,
            out_shape=(
                jax.ShapeDtypeStruct((token_rows, width), F32),
                jax.ShapeDtypeStruct((token_rows, LANES), F32),
                jax.ShapeDtypeStruct((1, width), F32),
            ),
            compiler_params=params(),
            name="reward_forward",
        )(frames, bias, gain, patch_weight)
        members = [[b * per_frame + i for i in range(per_frame)] for b in range(FRAMES)]
        pooled = lax.psum(partial, "row", axis_index_groups=members) / (count * per_frame)
        send = pl.pallas_call(
            functools.partial(backward_kernel, height=height),
            out_shape=message,
            in_specs=[SMEM] * 3 + [VMEM] * 9,
            out_specs=VMEM,
            compiler_params=params(),
            name="reward_backward",
        )(
            frame_owner,
            picks,
            slot,
            hidden_state,
            gain,
            head_bias_row,
            head_out_row,
            normed,
            inv_spread,
            pooled,
            patch_weight,
            head_weight,
        )
    window = -(-3 * (own_rows + 4) // 8) * 8
    wide, turned = pl.pallas_call(
        prepare_kernel,
        out_shape=(
            jax.ShapeDtypeStruct((9 * window, (own_rows + 2) * channels), BF16),
            jax.ShapeDtypeStruct((27 * channels, channels), BF16),
        ),
        scratch_shapes=[pltpu.VMEM((9 * window, (own_rows + 2) * channels), F32)],
        compiler_params=params(),
        name="prepare",
    )(out_weight, inner_weight)
    arrived = lax.all_to_all(send, "row", split_axis=0, concat_axis=0, tiled=True)
    gain_row = group_gain.reshape(1, channels)
    shift_row = group_shift.reshape(1, channels)
    upstream, stats, sums = pl.pallas_call(
        slope_kernel,
        out_shape=(
            jax.ShapeDtypeStruct((own_rows + 2, cells, channels), F32),
            jax.ShapeDtypeStruct((8, channels), F32),
            jax.ShapeDtypeStruct((devices, 2, channels), F32),
        ),
        in_specs=[SMEM] + [VMEM] * 7,
        compiler_params=params(),
        name="slope",
    )(frame_owner, arrived, hidden_state, low_edge, high_edge, gain_row, shift_row, wide)
    summed = lax.all_to_all(sums, "row", split_axis=0, concat_axis=0, tiled=True)
    return pl.pallas_call(
        inner_kernel,
        out_shape=jax.ShapeDtypeStruct(hidden_state.shape, BF16),
        in_specs=[SMEM] + [VMEM] * 7,
        scratch_shapes=[pltpu.VMEM((own_rows + 2, cells + 2 * frame_width, 3 * channels), BF16)],
        compiler_params=params(),
        name="inner",
    )(position.astype(jnp.int32).reshape(1), summed, hidden_state, low_edge, high_edge, stats, upstream, turned)


def solution(mesh):
    return jax.shard_map(
        per_device,
        mesh=mesh,
        in_specs=(
            P(None, None, ("clip", "row")),
            P("clip"),
            P("clip"),
            P(),
            P(),
            P(),
            P(),
            P(),
            P(),
            P(("clip", "row"), None, None, None),
            P(),
            P(),
            P(),
            P(),
        ),
        out_specs=P(("clip", "row"), None, None, None),
        check_vma=False,
    )
```

```python
import functools

import jax
import jax.numpy as jnp
from jax import lax
from jax.experimental import pallas as pl
from jax.experimental.pallas import tpu as pltpu
from jax.sharding import PartitionSpec as P

PATCH = 16
GROUPS = 32
FRAMES = 16
LANES = 128
eps_norm = 1e-06
BF16 = jnp.bfloat16
F32 = jnp.float32


def iota(shape, dim):
    return lax.broadcasted_iota(jnp.int32, shape, dim)


def ones_where(condition):
    return jnp.where(condition, 1.0, 0.0).astype(BF16)


def matmul(left, right):
    return jnp.dot(left, right, preferred_element_type=F32)


def matmul_t(left, right):
    return lax.dot_general(left, right, (((1,), (1,)), ((), ())), preferred_element_type=F32)


def pieces(row):
    high = row.astype(BF16).astype(F32)
    rest = row - high
    middle = rest.astype(BF16).astype(F32)
    low = rest - middle
    place = iota((16, row.shape[1]), 0)
    stacked = jnp.where(place == 0, high, jnp.where(place == 1, middle, jnp.where(place == 2, low, 0.0)))
    return stacked.astype(BF16)


def silu_slope(values):
    sigmoid = jax.nn.sigmoid(values)
    return sigmoid * (1.0 + values * (1.0 - sigmoid))


def to_tokens(pixels, token_rows):
    channels, columns, height = pixels.shape
    flat = pixels.reshape(channels * columns, height)
    width = channels * PATCH * columns
    lane = iota((channels * columns, width), 1)
    place = iota((channels * columns, 1), 0)
    code = place // columns * (PATCH * columns) + place % columns
    mine = (lane // (PATCH * columns) * (PATCH * columns) + lane % columns) == code
    pixel_row = iota((height, 1), 0)
    in_patch = iota((height, width), 1) // columns % PATCH
    tokens = jnp.zeros((token_rows, width), F32)
    for t in range(height // PATCH):
        tiled = matmul(flat, ones_where(pixel_row == in_patch + t * PATCH))
        kept = jnp.where(mine, tiled, 0.0).astype(BF16)
        tokens = tokens + matmul(ones_where(iota((token_rows, channels * columns), 0) == t), kept)
    return tokens.astype(BF16)


def forward_part(tokens, count, bias, gain, load_patch):
    embedded = bias[...]
    for low, high, weight in load_patch():
        embedded = embedded + matmul(tokens[:, low:high], weight)
    centred = embedded - jnp.mean(embedded, axis=1, keepdims=True)
    inv_spread = lax.rsqrt(jnp.mean(centred * centred, axis=1, keepdims=True) + eps_norm)
    normed = centred * inv_spread
    real = iota((tokens.shape[0], 1), 0) < count
    pooled = jnp.sum(jnp.where(real, normed * gain[...], 0.0), axis=0, keepdims=True)
    return normed, inv_spread, pooled


def send_plan(devices, height, own_rows):
    message = iota((4 * devices, 1), 0)
    target, colour = message // 4, message % 4
    plans = []
    for j in range(own_rows + 4):
        row = target * own_rows - 2 + j
        wanted = jnp.where((row >= 0) & (row < height) & (colour < 3), colour * height + row, -1)
        plans.append(ones_where(iota((4 * devices, 3 * height), 1) == wanted))
    return plans


def group_sums(hidden):
    channels = hidden.shape[-1]
    values = hidden.reshape(-1, channels).astype(F32)
    first = jnp.sum(values, axis=0, keepdims=True)
    second = jnp.sum(values * values, axis=0, keepdims=True)
    lane = iota((channels, LANES), 1)
    group = iota((channels, LANES), 0) // (channels // GROUPS)
    low = matmul(pieces(first), ones_where(lane == group))
    high = matmul(pieces(second), ones_where(lane == group + GROUPS))
    return jnp.sum(low + high, axis=0, keepdims=True)


def backward_part(
    owner, picks, hidden, gain, head_bias, head_out, normed, inv_spread, pooled, weight, head, slot, plans, send
):
    count = weight.shape[0]
    height = plans[0].shape[1] // 3
    before = jnp.sum(matmul(pieces(pooled), head()), axis=0, keepdims=True) + head_bias[...]
    wanted = owner[slot]
    picked = jnp.int32(0)
    for k in range(picks.shape[0]):
        picked = picked + jnp.where(picks[k] == wanted, 1, 0)
    pulled = jnp.sum(matmul_t(pieces(head_out[...] * silu_slope(before)), head()), axis=0, keepdims=True)
    scaled = gain[...] * (picked.astype(F32) * pulled)
    token_grad = inv_spread * (
        scaled
        - jnp.mean(scaled, axis=1, keepdims=True)
        - normed * jnp.mean(scaled * normed, axis=1, keepdims=True)
    )
    patch_grad = matmul_t(token_grad.astype(BF16), weight[...]).astype(BF16)
    rows = 3 * height
    place = iota((rows, 1), 0)
    copied = matmul(
        ones_where(place % height // PATCH == iota((rows, normed.shape[0]), 1)), patch_grad
    )
    code = place // height * PATCH + place % PATCH
    kept = jnp.where(code == iota((rows, count), 1) // PATCH, copied, 0.0).astype(BF16)
    fold = ones_where(iota((count, LANES), 0) % PATCH == iota((count, LANES), 1) % PATCH)
    pixels = matmul(kept, fold).astype(BF16)
    messages = plans[0].shape[0]
    lane = iota((messages, LANES), 1) // PATCH
    result = jnp.where(iota((messages, LANES), 0) % 4 == 3, group_sums(hidden[...]), 0.0)
    for j, plan in enumerate(plans):
        result = result + jnp.where(lane == j, matmul(plan, pixels), 0.0)
    send[...] = result.reshape(send.shape)


def reward_kernel(owner, picks, place, *refs):
    count = 8
    far, send, near, sems = refs[:count], refs[count], refs[count + 1 : 2 * count + 1], refs[-1]
    steps = 3
    depth = near[6].shape[0] // steps
    copies = [pltpu.make_async_copy(far[i], near[i], sems.at[i]) for i in range(2)]
    patch_copies = [
        pltpu.make_async_copy(
            far[6].at[pl.ds(i * depth, depth)], near[6].at[pl.ds(i * depth, depth)], sems.at[count + i]
        )
        for i in range(steps)
    ]
    more_copies = [pltpu.make_async_copy(far[i], near[i], sems.at[i]) for i in (2, 3, 4, 5, 7)]
    for copy in copies + patch_copies + more_copies:
        copy.start()
    frames, bias, gain, head_bias, head_out, hidden, patch, head = near

    def load_patch():
        for i in range(steps):
            patch_copies[i].wait()
            yield i * depth, (i + 1) * depth, patch[i * depth : (i + 1) * depth, :]

    devices = send.shape[0]
    height = frames.shape[2]
    patches = height // PATCH
    plans = send_plan(devices, height, hidden.shape[0])
    for copy in copies:
        copy.wait()
    tokens = to_tokens(frames[...], -(-patches // 16) * 16)
    more_copies[0].wait()
    normed, inv_spread, pooled = forward_part(tokens, patches, bias, gain, load_patch)
    pooled = pooled / patches
    for copy in more_copies[1:]:
        copy.wait()
    backward_part(
        owner,
        picks,
        hidden,
        gain,
        head_bias,
        head_out,
        normed,
        inv_spread,
        pooled,
        patch,
        lambda: head[...],
        place[0],
        plans,
        send,
    )


def forward_kernel(frames, bias, gain, patch, normed, inv_spread, pooled):
    width = patch.shape[0]
    patches = frames.shape[2] // PATCH
    tokens = to_tokens(frames[...], normed.shape[0])
    normed[...], spread, pooled[...] = forward_part(
        tokens, patches, bias, gain, lambda: [(0, width, patch[...])]
    )
    inv_spread[...] = jnp.broadcast_to(spread, inv_spread.shape)


def backward_kernel(
    owner, picks, place, hidden, gain, head_bias, head_out, normed, inv_spread, pooled, patch, head, send, height
):
    backward_part(
        owner,
        picks,
        hidden,
        gain,
        head_bias,
        head_out,
        normed[...],
        inv_spread[...][:, :1],
        pooled[...],
        patch,
        lambda: head[...],
        place[0],
        send_plan(send.shape[0], height, hidden.shape[0]),
        send,
    )


SMEM = pl.BlockSpec(memory_space=pltpu.SMEM)
VMEM = pl.BlockSpec(memory_space=pltpu.VMEM)
FAR = pl.BlockSpec(memory_space=pl.ANY)


def params(cells):
    return pltpu.CompilerParams(vmem_limit_bytes=min(16 + cells // 64, 48) * 1024 * 1024)


def near(array):
    return pltpu.with_memory_space_constraint(array, pltpu.VMEM)


def prepare_kernel(out_weight, inner_weight, wide, turned, scratch):
    window = scratch.shape[0] // 9
    amount = scratch.shape[1] // LANES
    scratch[...] = jnp.zeros_like(scratch)
    for a in range(3):
        for e in range(3):
            base = (a * 3 + e) * window
            for b in range(3):
                piece = out_weight[a, b, e].astype(F32)
                for i in range(amount):
                    start = base + 3 * (i - b + 2)
                    scratch[start : start + 3, i * LANES : (i + 1) * LANES] = piece
    wide[...] = scratch[...].astype(BF16)
    size = inner_weight.shape[3]
    for b in range(3):
        for a in range(3):
            for e in range(3):
                at = ((b * 3 + a) * 3 + e) * size
                turned[at : at + size, :] = inner_weight[a, b, e].T


def slope_kernel(
    owner, place, arrived, hidden, even_pair, odd_pair, gain, shift, wide, direct, scaled, stats, sums, edges, sems
):
    own_rows = hidden.shape[0]

    def edge_copies(low_pair, high_pair):
        return [
            pltpu.make_async_copy(low_pair.at[0, own_rows - 1], edges.at[0], sems.at[0]),
            pltpu.make_async_copy(high_pair.at[1, 0], edges.at[1], sems.at[1]),
        ]

    @pl.when(place[0] % 2 == 0)
    def _():
        for copy in edge_copies(odd_pair, even_pair):
            copy.start()

    @pl.when(place[0] % 2 == 1)
    def _():
        for copy in edge_copies(even_pair, odd_pair):
            copy.start()

    devices = arrived.shape[0]
    own_rows, frame_count, width, channels = hidden.shape
    cells = frame_count * width
    per_frame = devices // frame_count
    window = wide.shape[0] // 9
    got = arrived[...].reshape(4 * devices, LANES)
    row = iota((4 * devices, 1), 0)

    totals = jnp.sum(jnp.where(row % 4 == 3, got, 0.0), axis=0, keepdims=True)
    lane = iota((LANES, 2 * channels), 0)
    column = iota((LANES, 2 * channels), 1)
    wanted = column % channels // (channels // GROUPS) + jnp.where(column >= channels, GROUPS, 0)
    spread = jnp.sum(matmul(pieces(totals), ones_where(lane == wanted)), axis=0, keepdims=True)
    cell_total = own_rows * devices * cells * (channels // GROUPS)
    mean = spread[:, :channels] / cell_total
    inverse = lax.rsqrt(spread[:, channels:] / cell_total - mean * mean + eps_norm)
    stats[...] = jnp.broadcast_to(inverse, stats.shape)

    source = row // 4
    block = source // per_frame
    frame = jnp.zeros_like(block)
    for b in range(frame_count):
        frame = jnp.where(block == b, owner[b], frame)
    home = (frame * per_frame + source % per_frame) == iota((4 * devices, cells), 1) // PATCH
    fold = ones_where(iota((LANES, cells), 0) % PATCH == iota((LANES, cells), 1) % PATCH)
    place = iota((window, 1), 0)
    message = iota((window, 4 * devices), 1)
    held = iota((4 * devices, LANES), 1) // PATCH
    pixels = jnp.zeros((window, cells), F32)
    for j in range(own_rows + 4):
        placed = matmul(jnp.where(held == j, got, 0.0).astype(BF16), fold)
        kept = jnp.where(home, placed, 0.0).astype(BF16)
        chosen = ones_where((place // 3 == j) & (place % 3 == message % 4))
        pixels = pixels + matmul(chosen, kept)

    lane = iota((window, cells), 1)
    in_frame = lane % width
    shifted = []
    for a in range(3):
        for e in range(3):
            step = (2 - a) * width + 1 - e
            moved = pltpu.roll(pixels, (-step) % cells, 1) if step else pixels
            inside = (lane < cells - (2 - a) * width) & (in_frame >= e - 1) & (in_frame < width + e - 1)
            shifted.append(jnp.where(inside, moved, 0.0))
    stacked = jnp.concatenate(shifted, axis=0).astype(BF16)
    slopes = lax.dot_general(stacked, wide[...], (((0,), (0,)), ((), ())), preferred_element_type=F32)

    first = jnp.zeros((1, channels), F32)
    second = jnp.zeros((1, channels), F32)
    for i in list(range(1, own_rows + 1)) + [0, own_rows + 1]:
        if i == 0:
            for copy in edge_copies(even_pair, odd_pair):
                copy.wait()
        if i == 0 or i == own_rows + 1:
            state = edges[min(i, 1)]
        else:
            state = hidden[i - 1]
        normed = (state.reshape(cells, channels).astype(F32) - mean) * inverse
        affine = normed * gain[...] + shift[...]
        up = slopes[:, i * channels : (i + 1) * channels] * silu_slope(affine) * gain[...]
        direct[i] = up * inverse
        scaled[i] = normed * inverse
        if 0 < i < own_rows + 1:
            first = first + jnp.sum(up, axis=0, keepdims=True)
            second = second + jnp.sum(up * normed, axis=0, keepdims=True)
    sums[...] = jnp.where(iota((2, channels), 0) == 0, first, second)


def inner_kernel(place, arrived, stats, direct, scaled, turned, out, padded, *, devices):
    own_rows, frame_count, width, channels = out.shape
    cells = frame_count * width
    totals = jnp.sum(arrived[...], axis=0)
    same = ones_where(
        iota((channels, channels), 0) // (channels // GROUPS)
        == iota((channels, channels), 1) // (channels // GROUPS)
    )
    cell_total = own_rows * devices * cells * (channels // GROUPS)
    first = jnp.sum(matmul(pieces(totals[0:1]), same), axis=0, keepdims=True) / cell_total
    second = jnp.sum(matmul(pieces(totals[1:2]), same), axis=0, keepdims=True) / cell_total
    constant = first * stats[0:1, :]
    position = place[0]
    in_frame = iota((cells, 1), 0) % width
    for i in range(own_rows + 2):
        grad = direct[i] - constant - scaled[i] * second
        if i == 0:
            grad = jnp.where(position > 0, grad, 0.0)
        if i == own_rows + 1:
            grad = jnp.where(position < devices - 1, grad, 0.0)
        after = jnp.where(in_frame < width - 1, pltpu.roll(grad, cells - 1, 0), 0.0)
        prior = jnp.where(in_frame > 0, pltpu.roll(grad, 1, 0), 0.0)
        padded[i, :cells, 0:channels] = after.astype(BF16)
        padded[i, :cells, channels : 2 * channels] = grad.astype(BF16)
        padded[i, :cells, 2 * channels :] = prior.astype(BF16)
        padded[i, cells:, :] = jnp.zeros((2 * width, 3 * channels), BF16)
    depth = 3 * channels
    for r in range(own_rows):
        total = jnp.zeros((cells, channels), F32)
        for b in range(3):
            joined = jnp.concatenate(
                [padded[r - b + 2, (2 - a) * width : (2 - a) * width + cells, :] for a in range(3)], axis=1
            )
            total = total + matmul(joined, turned[b * 3 * depth : (b + 1) * 3 * depth, :])
        out[r] = total.reshape(frame_count, width, channels).astype(BF16)


def summed_over_row(values, devices):
    inner = 1
    while inner * inner * 4 <= devices and devices % (inner * 2) == 0:
        inner *= 2
    outer = devices // inner
    near_groups = [[o * inner + i for i in range(inner)] for o in range(outer)]
    far_groups = [[o * inner + i for o in range(outer)] for i in range(inner)]
    part = jnp.broadcast_to(values[None], (inner,) + values.shape)
    part = lax.all_to_all(part, "row", 0, 0, axis_index_groups=near_groups, tiled=True)
    part = jnp.broadcast_to(jnp.sum(part, axis=0, keepdims=True), (outer,) + values.shape)
    return lax.all_to_all(part, "row", 0, 0, axis_index_groups=far_groups, tiled=True)


def per_device(
    frames,
    frame_owner,
    picks,
    patch_weight,
    patch_bias,
    norm_gain,
    head_weight,
    head_bias,
    head_out,
    hidden_state,
    group_gain,
    group_shift,
    out_weight,
    inner_weight,
):
    devices = lax.axis_size("row")
    position = lax.axis_index("row")
    per_frame = devices // FRAMES
    height = frames.shape[1]
    own_rows, _, frame_width, channels = hidden_state.shape
    cells = FRAMES * frame_width
    width = patch_weight.shape[1]
    even_pairs = [[2 * i, 2 * i + 1] for i in range(devices // 2)]
    odd_pairs = [[2 * i + 1, (2 * i + 2) % devices] for i in range(devices // 2)]
    even_pair = lax.all_gather(hidden_state, "row", axis_index_groups=even_pairs)
    odd_pair = lax.all_gather(hidden_state, "row", axis_index_groups=odd_pairs)
    turned_frames = jnp.transpose(frames, (0, 2, 1))
    position = position.astype(jnp.int32).reshape(1)
    slot = position // per_frame
    bias = patch_bias.reshape(1, width)
    gain = norm_gain.reshape(1, width)
    head_bias_row = head_bias.reshape(1, width)
    head_out_row = head_out.reshape(1, width)
    message = jax.ShapeDtypeStruct((devices, 4, LANES), F32)
    arrays = (
        turned_frames,
        bias,
        gain,
        head_bias_row,
        head_out_row,
        hidden_state,
        patch_weight,
        head_weight,
    )
    if per_frame == 1:
        send = pl.pallas_call(
            reward_kernel,
            out_shape=message,
            in_specs=[SMEM] * 3 + [FAR] * 8,
            out_specs=VMEM,
            scratch_shapes=[pltpu.VMEM(x.shape, x.dtype) for x in arrays] + [pltpu.SemaphoreType.DMA((11,))],
            compiler_params=params(0),
            name="reward",
        )(
            frame_owner,
            picks,
            slot,
            *arrays,
        )
    else:
        count = height // PATCH
        token_rows = -(-count // 16) * 16
        normed, inv_spread, partial = pl.pallas_call(
            forward_kernel,
            out_shape=(
                jax.ShapeDtypeStruct((token_rows, width), F32),
                jax.ShapeDtypeStruct((token_rows, LANES), F32),
                jax.ShapeDtypeStruct((1, width), F32),
            ),
            compiler_params=params(cells),
            name="reward_forward",
        )(turned_frames, bias, gain, patch_weight)
        members = [[b * per_frame + i for i in range(per_frame)] for b in range(FRAMES)]
        pooled = lax.psum(partial, "row", axis_index_groups=members) / (count * per_frame)
        send = pl.pallas_call(
            functools.partial(backward_kernel, height=height),
            out_shape=message,
            in_specs=[SMEM] * 3 + [VMEM] * 9,
            out_specs=VMEM,
            compiler_params=params(cells),
            name="reward_backward",
        )(
            frame_owner,
            picks,
            slot,
            hidden_state,
            gain,
            head_bias_row,
            head_out_row,
            normed,
            inv_spread,
            pooled,
            patch_weight,
            head_weight,
        )
    window = -(-3 * (own_rows + 4) // 8) * 8
    wide, turned = pl.pallas_call(
        prepare_kernel,
        out_shape=(
            pltpu.VMEM((9 * window, (own_rows + 2) * channels), BF16),
            pltpu.VMEM((27 * channels, channels), BF16),
        ),
        scratch_shapes=[pltpu.VMEM((9 * window, (own_rows + 2) * channels), F32)],
        compiler_params=params(cells),
        name="prepare",
    )(out_weight, inner_weight)
    arrived = lax.all_to_all(send, "row", split_axis=0, concat_axis=0, tiled=True)
    gain_row = group_gain.reshape(1, channels)
    shift_row = group_shift.reshape(1, channels)
    direct, scaled, stats, sums = pl.pallas_call(
        slope_kernel,
        out_shape=(
            pltpu.VMEM((own_rows + 2, cells, channels), F32),
            pltpu.VMEM((own_rows + 2, cells, channels), F32),
            pltpu.VMEM((8, channels), F32),
            pltpu.VMEM((2, channels), F32),
        ),
        in_specs=[SMEM] * 2 + [VMEM] * 2 + [FAR] * 2 + [VMEM] * 3,
        scratch_shapes=[
            pltpu.VMEM((2,) + hidden_state.shape[1:], BF16),
            pltpu.SemaphoreType.DMA((2,)),
        ],
        compiler_params=params(cells),
        name="slope",
    )(
        frame_owner,
        position,
        near(arrived),
        near(hidden_state),
        even_pair,
        odd_pair,
        gain_row,
        shift_row,
        near(wide),
    )
    summed = summed_over_row(sums, devices)
    return pl.pallas_call(
        functools.partial(inner_kernel, devices=devices),
        out_shape=jax.ShapeDtypeStruct(hidden_state.shape, BF16),
        in_specs=[SMEM] + [VMEM] * 5,
        scratch_shapes=[pltpu.VMEM((own_rows + 2, cells + 2 * frame_width, 3 * channels), BF16)],
        compiler_params=params(cells),
        name="inner",
    )(position, near(summed), near(stats), near(direct), near(scaled), near(turned))


def solution(mesh):
    return jax.shard_map(
        per_device,
        mesh=mesh,
        in_specs=(
            P(None, None, ("clip", "row")),
            P("clip"),
            P("clip"),
            P(),
            P(),
            P(),
            P(),
            P(),
            P(),
            P(("clip", "row"), None, None, None),
            P(),
            P(),
            P(),
            P(),
        ),
        out_specs=P(("clip", "row"), None, None, None),
        check_vma=False,
    )
```

```python
import functools

import jax
import jax.numpy as jnp
from jax import lax
from jax.experimental import pallas as pl
from jax.experimental.pallas import tpu as pltpu
from jax.sharding import PartitionSpec as P

PATCH = 16
GROUPS = 32
FRAMES = 16
LANES = 128
SLOTS = LANES // PATCH
PAIR = 2
eps_norm = 1e-06
BF16 = jnp.bfloat16
F32 = jnp.float32

SMEM = pl.BlockSpec(memory_space=pltpu.SMEM)
VMEM = pl.BlockSpec(memory_space=pltpu.VMEM)
FAR = pl.BlockSpec(memory_space=pl.ANY)


def iota(shape, dim):
    return lax.broadcasted_iota(jnp.int32, shape, dim)


def div(values, count):
    if count & (count - 1):
        return values // count
    return values >> (count.bit_length() - 1)


def mod(values, count):
    if count & (count - 1):
        return values % count
    return values & (count - 1)


def ones_where(condition):
    return jnp.where(condition, 1.0, 0.0).astype(BF16)


def matmul(left, right):
    return jnp.dot(left, right, preferred_element_type=F32)


def matmul_t(left, right):
    return lax.dot_general(left, right, (((1,), (1,)), ((), ())), preferred_element_type=F32)


def exact_rows(rows, product):
    place = iota((16, rows[0].shape[1]), 0)
    stacked = jnp.zeros(place.shape, F32)
    for index, row in enumerate(rows):
        high = row.astype(BF16).astype(F32)
        rest = row - high
        middle = rest.astype(BF16).astype(F32)
        for step, piece in enumerate((high, middle, rest - middle)):
            stacked = jnp.where(place == 3 * index + step, piece, stacked)
    result = product(stacked.astype(BF16))
    return [
        result[3 * i : 3 * i + 1] + result[3 * i + 1 : 3 * i + 2] + result[3 * i + 2 : 3 * i + 3]
        for i in range(len(rows))
    ]


def silu_slope(values):
    sigmoid = jax.nn.sigmoid(values)
    return sigmoid * (1.0 + values * (1.0 - sigmoid))


def token_rows_of(height):
    return -(-PAIR * (height // PATCH) // 16) * 16


def to_tokens(pixels):
    strips, channels, columns, height = pixels.shape
    count = height // PATCH
    rows = strips * channels * columns
    token_rows = token_rows_of(height)
    flat = pixels.reshape(rows, height)
    width = channels * PATCH * columns
    lane = iota((1, width), 1)
    place = iota((rows, 1), 0)
    mine = mod(div(place, columns), channels) * columns + mod(place, columns) == (
        div(lane, PATCH * columns) * columns + mod(lane, columns)
    )
    in_patch = mod(div(lane, columns), PATCH)
    strip = div(iota((1, rows), 1), channels * columns)
    pixel_row = iota((height, 1), 0)
    token = iota((token_rows, 1), 0)
    tokens = jnp.zeros((token_rows, width), F32)
    for t in range(count):
        tiled = matmul(flat, ones_where(pixel_row == in_patch + t * PATCH))
        kept = jnp.where(mine, tiled, 0.0).astype(BF16)
        tokens = tokens + matmul(ones_where(token == strip * count + t), kept)
    return tokens.astype(BF16)


def forward_part(tokens, count, bias, gain, load_patch):
    embedded = bias[...]
    for low, high, weight in load_patch():
        embedded = embedded + matmul(tokens[:, low:high], weight)
    centred = embedded - jnp.mean(embedded, axis=1, keepdims=True)
    inv_spread = lax.rsqrt(jnp.mean(centred * centred, axis=1, keepdims=True) + eps_norm)
    normed = centred * inv_spread
    weighted = normed * gain[...]
    token = iota((tokens.shape[0], 1), 0)
    pooled = []
    for s in range(PAIR):
        inside = (token >= s * count) & (token < (s + 1) * count)
        pooled.append(jnp.sum(jnp.where(inside, weighted, 0.0), axis=0, keepdims=True))
    return normed, inv_spread, pooled


def layout(own_rows):
    window = PAIR * own_rows + 3
    per_row = PAIR * 3
    data_rows = -(-per_row * window // SLOTS)
    message_rows = -(-(data_rows + 1) // 8) * 8
    entries = {}
    for q in range(SLOTS):
        for m in range(data_rows):
            entry = q * data_rows + m
            if entry < per_row * window:
                entries[q, m] = (entry // per_row, entry % per_row // 3, entry % 3)
    return window, data_rows, message_rows, entries


def send_plan(targets, height, own_rows, core):
    _, data_rows, message_rows, entries = layout(own_rows)
    rows = targets * message_rows
    message = iota((rows, 1), 0)
    kind = mod(message, message_rows)
    first = div(message, message_rows) * (PAIR * own_rows) + core - 2
    source = iota((1, PAIR * 3 * height), 1)
    spacing = 4 * height
    source = div(source, height) * spacing + mod(source, height) + height
    plans = []
    for q in range(SLOTS):
        wanted = jnp.full((rows, 1), -spacing, jnp.int32)
        for m in range(data_rows):
            if (q, m) in entries:
                j, s, k = entries[q, m]
                wanted = jnp.where(kind == m, (s * 3 + k) * spacing + j + height, wanted)
        plans.append(ones_where(source == wanted + first))
    return plans


def group_sums(hidden):
    channels = hidden.shape[-1]
    values = hidden.reshape(-1, channels).astype(F32)
    first = jnp.sum(values, axis=0, keepdims=True)
    second = jnp.sum(values * values, axis=0, keepdims=True)
    lane = iota((1, LANES), 1)
    group = div(iota((channels, 1), 0), channels // GROUPS)
    low = exact_rows([first], lambda rows: matmul(rows, ones_where(lane == group)))[0]
    high = exact_rows([second], lambda rows: matmul(rows, ones_where(lane == group + GROUPS)))[0]
    return low + high


def backward_part(owner, picks, gain, head_bias, head_out, normed, inv_spread, pooled, weight, head, slots, plans, sums, send):
    width = weight.shape[0]
    message_rows = send.shape[1]
    height = plans[0].shape[1] // (PAIR * 3)
    count = height // PATCH
    before = exact_rows(pooled, lambda rows: matmul(rows, head[...]))
    slopes = [head_out[...] * silu_slope(row + head_bias[...]) for row in before]
    pulled = exact_rows(slopes, lambda rows: matmul_t(rows, head[...]))
    token = iota((normed.shape[0], 1), 0)
    scaled = jnp.zeros(normed.shape, F32)
    for s in range(PAIR):
        wanted = owner[slots[s]]
        picked = jnp.int32(0)
        for k in range(picks.shape[0]):
            picked = picked + jnp.where(picks[k] == wanted, 1, 0)
        inside = (token >= s * count) & (token < (s + 1) * count)
        scaled = jnp.where(inside, gain[...] * (picked.astype(F32) * pulled[s]), scaled)
    token_grad = inv_spread * (
        scaled
        - jnp.mean(scaled, axis=1, keepdims=True)
        - normed * jnp.mean(scaled * normed, axis=1, keepdims=True)
    )
    patch_grad = matmul_t(token_grad.astype(BF16), weight[...]).astype(BF16)
    rows = PAIR * 3 * height
    place = iota((rows, 1), 0)
    strip = div(place, 3 * height)
    pixel_row = mod(place, height)
    colour = mod(div(place, height), 3)
    copied = matmul(
        ones_where(strip * count + div(pixel_row, PATCH) == iota((1, normed.shape[0]), 1)), patch_grad
    )
    kept = jnp.where(
        colour * PATCH + mod(pixel_row, PATCH) == div(iota((1, width), 1), PATCH), copied, 0.0
    ).astype(BF16)
    fold = ones_where(mod(iota((width, 1), 0), PATCH) == mod(iota((1, LANES), 1), PATCH))
    pixels = matmul(kept, fold).astype(BF16)
    messages = plans[0].shape[0]
    lane = div(iota((1, LANES), 1), PATCH)
    result = jnp.where(mod(iota((messages, 1), 0), message_rows) == message_rows - 1, sums, 0.0)
    for q, plan in enumerate(plans):
        result = result + jnp.where(lane == q, matmul(plan, pixels), 0.0)
    send[...] = result.reshape(send.shape)


def reward_kernel(place, *refs):
    count = 10
    far, send, near, sems = refs[:count], refs[count], refs[count + 1 : 2 * count + 1], refs[-1]
    frames, hidden, bias, owner, picks, gain, head_bias, head_out, patch, head = near
    steps = 3
    depth = patch.shape[0] // steps
    copies = {i: pltpu.make_async_copy(far[i], near[i], sems.at[i]) for i in range(count) if i != 8}
    patch_copies = [
        pltpu.make_async_copy(
            far[8].at[pl.ds(i * depth, depth)], patch.at[pl.ds(i * depth, depth)], sems.at[count + i]
        )
        for i in range(steps)
    ]
    for copy in [copies[i] for i in range(3)] + patch_copies + [copies[i] for i in (3, 4, 5, 6, 7, 9)]:
        copy.start()

    def load_patch():
        for i in range(steps):
            patch_copies[i].wait()
            yield i * depth, (i + 1) * depth, patch[i * depth : (i + 1) * depth, :]

    height = frames.shape[3]
    patches = height // PATCH
    plans = send_plan(send.shape[0], height, hidden.shape[1], place[0] % PAIR)
    copies[0].wait()
    tokens = to_tokens(frames[...])
    copies[1].wait()
    sums = group_sums(hidden[...])
    copies[2].wait()
    for i in range(3, 8):
        copies[i].wait()
    normed, inv_spread, pooled = forward_part(tokens, patches, bias, gain, load_patch)
    pooled = [row / patches for row in pooled]
    copies[9].wait()
    start = place[0] - place[0] % PAIR
    slots = [start + s for s in range(PAIR)]
    backward_part(
        owner, picks, gain, head_bias, head_out, normed, inv_spread, pooled, patch, head, slots, plans, sums, send
    )


def forward_kernel(place, frames, bias, gain, patch, normed, inv_spread, pooled):
    width = patch.shape[0]
    tokens = to_tokens(frames[...])
    patches = frames.shape[3] // PATCH
    normed[...], spread, strips = forward_part(tokens, patches, bias, gain, lambda: [(0, width, patch[...])])
    inv_spread[...] = jnp.broadcast_to(spread, inv_spread.shape)
    pooled[...] = jnp.where(place[0] % PAIR == 0, strips[0], strips[1])


def backward_kernel(
    owner, picks, place, hidden, gain, head_bias, head_out, normed, inv_spread, pooled, patch, head, send, *, height, per_frame
):
    plans = send_plan(send.shape[0], height, hidden.shape[1], place[0] % PAIR)
    sums = group_sums(hidden[...])
    slots = [place[0] // per_frame] * PAIR
    backward_part(
        owner,
        picks,
        gain,
        head_bias,
        head_out,
        normed[...],
        inv_spread[...][:, :1],
        [pooled[...]] * PAIR,
        patch,
        head,
        slots,
        plans,
        sums,
        send,
    )


def params(cells):
    return pltpu.CompilerParams(vmem_limit_bytes=min(16 + cells // 64, 48) * 1024 * 1024)


def near(array):
    return pltpu.with_memory_space_constraint(array, pltpu.VMEM)


def far(array):
    return pltpu.with_memory_space_constraint(array, pltpu.HBM)


def prepare_kernel(place, sent, hidden, out_weight, inner_weight, wide, turned, edge, scratch, sem):
    own_rows = hidden.shape[0]
    row = jnp.where(place[0] % PAIR == 0, 0, own_rows - 1)
    copy = pltpu.make_async_copy(hidden.at[pl.ds(row, 1)], edge, sem.at[0])
    copy.start()
    window = scratch.shape[0] // 9
    amount = scratch.shape[1] // LANES
    scratch[...] = jnp.zeros_like(scratch)
    for a in range(3):
        for e in range(3):
            base = (a * 3 + e) * window
            for b in range(3):
                piece = out_weight[a, b, e].astype(F32)
                for i in range(amount):
                    start = base + 3 * (i - b + 2)
                    scratch[start : start + 3, i * LANES : (i + 1) * LANES] = piece
    wide[...] = scratch[...].astype(BF16)
    size = inner_weight.shape[3]
    for b in range(3):
        for a in range(3):
            for e in range(3):
                at = ((b * 3 + a) * 3 + e) * size
                turned[at : at + size, :] = inner_weight[a, b, e].T
    copy.wait()


def slope_kernel(
    owner, place, arrived, pair, edge, gain, shift, wide, direct, states, stats, sums, sems
):
    sources, message_rows, _ = arrived.shape
    _, own_rows, frame_count, width, channels = pair.shape
    rows = PAIR * own_rows + 1
    core = place[0] % PAIR
    copies = [
        pltpu.make_async_copy(
            pair.at[s], states.at[pl.ds(1 - core + s * own_rows, own_rows)], sems.at[s]
        )
        for s in range(PAIR)
    ]
    copies.append(pltpu.make_async_copy(edge.at[0], states.at[core * (rows - 1)], sems.at[PAIR]))
    for copy in copies:
        copy.start()
    cells = frame_count * width
    devices = sources * PAIR
    per_frame = devices // frame_count
    window = wide.shape[0] // 9
    _, data_rows, _, entries = layout(own_rows)
    total_rows = sources * message_rows
    got = arrived[...].reshape(total_rows, LANES)
    row = iota((total_rows, 1), 0)
    kind = mod(row, message_rows)

    totals = jnp.sum(jnp.where(kind == message_rows - 1, got, 0.0), axis=0, keepdims=True)
    column = iota((1, PAIR * channels), 1)
    wanted = div(mod(column, channels), channels // GROUPS) + jnp.where(column >= channels, GROUPS, 0)
    spread = exact_rows([totals], lambda r: matmul(r, ones_where(iota((LANES, 1), 0) == wanted)))[0]
    cell_total = own_rows * devices * cells * (channels // GROUPS)
    mean = spread[:, :channels] / cell_total
    inverse = lax.rsqrt(spread[:, channels:] / cell_total - mean * mean + eps_norm)
    stats[0:1, :] = mean
    stats[1:2, :] = inverse

    homes = []
    for s in range(PAIR):
        strip = div(row, message_rows) * PAIR + s
        block = div(strip, per_frame)
        frame = jnp.zeros_like(block)
        for b in range(frame_count):
            frame = jnp.where(block == b, owner[b], frame)
        homes.append(frame * per_frame + mod(strip, per_frame))
    fold = ones_where(mod(iota((LANES, 1), 0), PATCH) == mod(iota((1, cells), 1), PATCH))
    lane_home = div(iota((1, cells), 1), PATCH)
    lane_kind = mod(iota((1, total_rows), 1), message_rows)
    held = div(iota((1, LANES), 1), PATCH)
    place_row = iota((window, 1), 0)
    pixels = jnp.zeros((window, cells), F32)
    for q in range(SLOTS):
        home = jnp.full_like(row, -1)
        chosen = jnp.full_like(lane_kind, -1)
        for m in range(data_rows):
            if (q, m) in entries:
                j, s, k = entries[q, m]
                home = jnp.where(kind == m, homes[s], home)
                chosen = jnp.where(lane_kind == m, j * 3 + k, chosen)
        placed = matmul(jnp.where(held == q, got, 0.0).astype(BF16), fold)
        kept = jnp.where(home == lane_home, placed, 0.0).astype(BF16)
        pixels = pixels + matmul(ones_where(place_row == chosen), kept)

    lane = iota((1, cells), 1)
    in_frame = mod(lane, width)
    shifted = []
    for a in range(3):
        for e in range(3):
            step = (2 - a) * width + 1 - e
            moved = pltpu.roll(pixels, (-step) % cells, 1) if step else pixels
            inside = (lane < cells - (2 - a) * width) & (in_frame >= e - 1) & (in_frame < width + e - 1)
            shifted.append(jnp.where(inside, moved, 0.0))
    stacked = jnp.concatenate(shifted, axis=0).astype(BF16)
    slopes = lax.dot_general(stacked, wide[...], (((0,), (0,)), ((), ())), preferred_element_type=F32)

    for copy in copies:
        copy.wait()
    first = jnp.zeros((1, channels), F32)
    second = jnp.zeros((1, channels), F32)
    for i in range(rows):
        normed = (states[i].reshape(cells, channels).astype(F32) - mean) * inverse
        affine = normed * gain[...] + shift[...]
        up = slopes[:, i * channels : (i + 1) * channels] * silu_slope(affine) * gain[...]
        direct[i] = up * inverse
        row_first = jnp.sum(up, axis=0, keepdims=True)
        row_second = jnp.sum(up * normed, axis=0, keepdims=True)
        if i == 0 or i == rows - 1:
            counted = core == (1 if i == 0 else 0)
            row_first = jnp.where(counted, row_first, 0.0)
            row_second = jnp.where(counted, row_second, 0.0)
        first = first + row_first
        second = second + row_second
    both = jnp.where(iota((2, channels), 0) == 0, first, second)
    sums[...] = jnp.broadcast_to(both[None], sums.shape)


def inner_kernel(place, arrived, stats, direct, states, turned_far, out, padded, turned, sem, *, devices):
    copy = pltpu.make_async_copy(turned_far, turned, sem.at[0])
    copy.start()
    own_rows, frame_count, width, channels = out.shape
    cells = frame_count * width
    totals = jnp.sum(arrived[...], axis=0)
    same = ones_where(
        div(iota((channels, 1), 0), channels // GROUPS) == div(iota((1, channels), 1), channels // GROUPS)
    )
    cell_total = own_rows * devices * cells * (channels // GROUPS)
    first, second = exact_rows([totals[0:1], totals[1:2]], lambda rows: matmul(rows, same))
    mean = stats[0:1, :]
    inverse = stats[1:2, :]
    constant = first / cell_total * inverse
    factor = second / cell_total * inverse * inverse
    position = place[0]
    base = position % PAIR * (own_rows - 1)
    in_frame = mod(iota((cells, 1), 0), width)
    for i in range(own_rows + 2):
        state = states[base + i].reshape(cells, channels).astype(F32)
        grad = direct[base + i] - constant - (state - mean) * factor
        if i == 0:
            grad = jnp.where(position > 0, grad, 0.0)
        if i == own_rows + 1:
            grad = jnp.where(position < devices - 1, grad, 0.0)
        after = jnp.where(in_frame < width - 1, pltpu.roll(grad, cells - 1, 0), 0.0)
        prior = jnp.where(in_frame > 0, pltpu.roll(grad, 1, 0), 0.0)
        padded[i, :cells, 0:channels] = after.astype(BF16)
        padded[i, :cells, channels : 2 * channels] = grad.astype(BF16)
        padded[i, :cells, 2 * channels :] = prior.astype(BF16)
        padded[i, cells:, :] = jnp.zeros((2 * width, 3 * channels), BF16)
    copy.wait()
    depth = 3 * channels
    for r in range(own_rows):
        total = jnp.zeros((cells, channels), F32)
        for b in range(3):
            joined = jnp.concatenate(
                [padded[r - b + 2, (2 - a) * width : (2 - a) * width + cells, :] for a in range(3)], axis=1
            )
            total = total + matmul(joined, turned[b * 3 * depth : (b + 1) * 3 * depth, :])
        out[r] = total.reshape(frame_count, width, channels).astype(BF16)


def per_device(
    frames,
    frame_owner,
    picks,
    patch_weight,
    patch_bias,
    norm_gain,
    head_weight,
    head_bias,
    head_out,
    hidden_state,
    group_gain,
    group_shift,
    out_weight,
    inner_weight,
):
    devices = lax.axis_size("row")
    position = lax.axis_index("row").astype(jnp.int32).reshape(1)
    per_frame = devices // FRAMES
    height = frames.shape[1]
    own_rows, _, frame_width, channels = hidden_state.shape
    cells = FRAMES * frame_width
    width = patch_weight.shape[1]
    chips = devices // PAIR
    pairs = [[PAIR * i + s for s in range(PAIR)] for i in range(chips)]
    alike = [[PAIR * i + s for i in range(chips)] for s in range(PAIR)]
    pair_frames = lax.all_gather(jnp.transpose(frames, (0, 2, 1)), "row", axis_index_groups=pairs)
    pair_state = lax.all_gather(hidden_state, "row", axis_index_groups=pairs)
    bias = patch_bias.reshape(1, width)
    gain = norm_gain.reshape(1, width)
    head_bias_row = head_bias.reshape(1, width)
    head_out_row = head_out.reshape(1, width)
    window, _, message_rows, _ = layout(own_rows)
    message = jax.ShapeDtypeStruct((chips, message_rows, LANES), F32)
    if per_frame == 1:
        arrays = [
            pair_frames,
            pair_state,
            bias,
            frame_owner,
            picks,
            gain,
            head_bias_row,
            head_out_row,
            patch_weight,
            head_weight,
        ]
        send = pl.pallas_call(
            reward_kernel,
            out_shape=message,
            in_specs=[SMEM] + [FAR] * len(arrays),
            out_specs=VMEM,
            scratch_shapes=[
                (pltpu.SMEM if x.dtype == jnp.int32 else pltpu.VMEM)(x.shape, x.dtype) for x in arrays
            ]
            + [pltpu.SemaphoreType.DMA((len(arrays) + 3,))],
            compiler_params=params(0),
            name="reward",
        )(position, *[far(x) for x in arrays])
    else:
        count = height // PATCH
        normed, inv_spread, partial = pl.pallas_call(
            forward_kernel,
            out_shape=(
                jax.ShapeDtypeStruct((token_rows_of(height), width), F32),
                jax.ShapeDtypeStruct((token_rows_of(height), LANES), F32),
                jax.ShapeDtypeStruct((1, width), F32),
            ),
            in_specs=[SMEM] + [VMEM] * 4,
            compiler_params=params(cells),
            name="reward_forward",
        )(position, pair_frames, bias, gain, patch_weight)
        members = [[b * per_frame + i for i in range(per_frame)] for b in range(FRAMES)]
        pooled = lax.psum(partial, "row", axis_index_groups=members) / (count * per_frame)
        send = pl.pallas_call(
            functools.partial(backward_kernel, height=height, per_frame=per_frame),
            out_shape=message,
            in_specs=[SMEM] * 3 + [VMEM] * 9,
            out_specs=VMEM,
            compiler_params=params(cells),
            name="reward_backward",
        )(
            frame_owner,
            picks,
            position,
            pair_state,
            gain,
            head_bias_row,
            head_out_row,
            normed,
            inv_spread,
            pooled,
            patch_weight,
            head_weight,
        )
    window_rows = -(-3 * window // 16) * 16
    state_rows = PAIR * own_rows + 1
    wide, turned, edge = pl.pallas_call(
        prepare_kernel,
        out_shape=(
            pltpu.VMEM((9 * window_rows, state_rows * channels), BF16),
            jax.ShapeDtypeStruct((27 * channels, channels), BF16),
            jax.ShapeDtypeStruct((1,) + hidden_state.shape[1:], BF16),
        ),
        in_specs=[SMEM] + [FAR] * 2 + [VMEM] * 2,
        out_specs=[VMEM, VMEM, FAR],
        scratch_shapes=[
            pltpu.VMEM((9 * window_rows, state_rows * channels), F32),
            pltpu.SemaphoreType.DMA((1,)),
        ],
        compiler_params=params(cells),
        name="prepare",
    )(position, far(send), far(hidden_state), out_weight, inner_weight)
    arrived = lax.all_to_all(send, "row", 0, 0, axis_index_groups=alike, tiled=True)
    swaps = [(PAIR * i - 1, PAIR * i) for i in range(1, chips)]
    edge = lax.ppermute(edge, "row", swaps + [(b, a) for a, b in swaps])
    direct, states, stats, sums = pl.pallas_call(
        slope_kernel,
        out_shape=(
            pltpu.VMEM((state_rows, cells, channels), F32),
            pltpu.VMEM((state_rows,) + hidden_state.shape[1:], BF16),
            pltpu.VMEM((8, channels), F32),
            jax.ShapeDtypeStruct((chips, 2, channels), F32),
        ),
        in_specs=[SMEM] * 2 + [VMEM] + [FAR] * 2 + [VMEM] * 3,
        scratch_shapes=[pltpu.SemaphoreType.DMA((PAIR + 1,))],
        compiler_params=params(cells),
        name="slope",
    )(
        frame_owner,
        position,
        near(arrived),
        far(pair_state),
        edge,
        group_gain.reshape(1, channels),
        group_shift.reshape(1, channels),
        near(wide),
    )
    summed = lax.all_to_all(sums, "row", 0, 0, axis_index_groups=alike, tiled=True)
    return pl.pallas_call(
        functools.partial(inner_kernel, devices=devices),
        out_shape=jax.ShapeDtypeStruct(hidden_state.shape, BF16),
        in_specs=[SMEM] + [VMEM] * 4 + [FAR],
        scratch_shapes=[
            pltpu.VMEM((own_rows + 2, cells + 2 * frame_width, 3 * channels), BF16),
            pltpu.VMEM((27 * channels, channels), BF16),
            pltpu.SemaphoreType.DMA((1,)),
        ],
        compiler_params=params(cells),
        name="inner",
    )(position, near(summed), near(stats), near(direct), near(states), far(turned))


def solution(mesh):
    return jax.shard_map(
        per_device,
        mesh=mesh,
        in_specs=(
            P(None, None, ("clip", "row")),
            P("clip"),
            P("clip"),
            P(),
            P(),
            P(),
            P(),
            P(),
            P(),
            P(("clip", "row"), None, None, None),
            P(),
            P(),
            P(),
            P(),
        ),
        out_specs=P(("clip", "row"), None, None, None),
        check_vma=False,
    )
```

```python
import functools

import jax
import jax.numpy as jnp
from jax import lax
from jax.experimental import pallas as pl
from jax.experimental.pallas import tpu as pltpu
from jax.sharding import PartitionSpec as P

PATCH = 16
GROUPS = 32
FRAMES = 16
LANES = 128
SLOTS = LANES // PATCH
eps_norm = 1e-06
BF16 = jnp.bfloat16
F32 = jnp.float32

SMEM = pl.BlockSpec(memory_space=pltpu.SMEM)
VMEM = pl.BlockSpec(memory_space=pltpu.VMEM)
FAR = pl.BlockSpec(memory_space=pl.ANY)


def iota(shape, dim):
    return lax.broadcasted_iota(jnp.int32, shape, dim)


def div(values, count):
    if count & (count - 1):
        return values // count
    return values >> (count.bit_length() - 1)


def mod(values, count):
    if count & (count - 1):
        return values % count
    return values & (count - 1)


def ones_where(condition):
    return jnp.where(condition, 1.0, 0.0).astype(BF16)


def matmul(left, right):
    return jnp.dot(left, right, preferred_element_type=F32)


def matmul_t(left, right):
    return lax.dot_general(left, right, (((1,), (1,)), ((), ())), preferred_element_type=F32)


def exact_rows(rows, product):
    place = iota((16, rows[0].shape[1]), 0)
    stacked = jnp.zeros(place.shape, F32)
    for index, row in enumerate(rows):
        high = row.astype(BF16).astype(F32)
        rest = row - high
        middle = rest.astype(BF16).astype(F32)
        for step, piece in enumerate((high, middle, rest - middle)):
            stacked = jnp.where(place == 3 * index + step, piece, stacked)
    result = product(stacked.astype(BF16))
    return [
        result[3 * i : 3 * i + 1] + result[3 * i + 1 : 3 * i + 2] + result[3 * i + 2 : 3 * i + 3]
        for i in range(len(rows))
    ]


def silu_slope(values):
    sigmoid = jax.nn.sigmoid(values)
    return sigmoid * (1.0 + values * (1.0 - sigmoid))


def token_rows_of(height):
    return -(-(height // PATCH) // 16) * 16


def to_tokens(pixels):
    channels, columns, height = pixels.shape
    rows = channels * columns
    token_rows = token_rows_of(height)
    flat = pixels.reshape(rows, height)
    width = channels * PATCH * columns
    lane = iota((1, width), 1)
    place = iota((rows, 1), 0)
    mine = place == div(lane, PATCH * columns) * columns + mod(lane, columns)
    in_patch = mod(div(lane, columns), PATCH)
    pixel_row = iota((height, 1), 0)
    token = iota((token_rows, rows), 0)
    tokens = jnp.zeros((token_rows, width), F32)
    for t in range(height // PATCH):
        tiled = matmul(flat, ones_where(pixel_row == in_patch + t * PATCH))
        kept = jnp.where(mine, tiled, 0.0).astype(BF16)
        tokens = tokens + matmul(ones_where(token == t), kept)
    return tokens.astype(BF16)


def forward_part(tokens, count, bias, gain, load_patch):
    embedded = bias[...]
    for low, high, weight in load_patch():
        embedded = embedded + matmul(tokens[:, low:high], weight)
    centred = embedded - jnp.mean(embedded, axis=1, keepdims=True)
    inv_spread = lax.rsqrt(jnp.mean(centred * centred, axis=1, keepdims=True) + eps_norm)
    normed = centred * inv_spread
    weighted = normed * gain[...]
    inside = iota((tokens.shape[0], 1), 0) < count
    pooled = jnp.sum(jnp.where(inside, weighted, 0.0), axis=0, keepdims=True)
    return normed, inv_spread, pooled


def layout(own_rows):
    return own_rows + 4, 4


def send_plan(targets, height, own_rows):
    window, message_rows = layout(own_rows)
    rows = targets * message_rows
    message = iota((rows, 1), 0)
    colour = mod(message, message_rows)
    first = div(message, message_rows) * own_rows - 2
    source = iota((1, 3 * height), 1)
    spacing = 4 * height
    source = div(source, height) * spacing + mod(source, height) + height
    wanted = colour * spacing + height + first
    return [ones_where(source == wanted + j) for j in range(window)]


def group_sums(hidden):
    channels = hidden.shape[-1]
    values = hidden.reshape(-1, channels).astype(F32)
    first = jnp.sum(values, axis=0, keepdims=True)
    second = jnp.sum(values * values, axis=0, keepdims=True)
    lane = iota((1, LANES), 1)
    group = div(iota((channels, 1), 0), channels // GROUPS)
    low = exact_rows([first], lambda rows: matmul(rows, ones_where(lane == group)))[0]
    high = exact_rows([second], lambda rows: matmul(rows, ones_where(lane == group + GROUPS)))[0]
    return low + high


def backward_part(
    owner, picks, gain, head_bias, head_out, normed, inv_spread, pooled, weight, head, slot, plans, sums, send
):
    width = weight.shape[0]
    message_rows = send.shape[1]
    height = plans[0].shape[1] // 3
    (before,) = exact_rows([pooled], lambda rows: matmul(rows, head[...]))
    slope = head_out[...] * silu_slope(before + head_bias[...])
    (pulled,) = exact_rows([slope], lambda rows: matmul_t(rows, head[...]))
    wanted = owner[slot]
    picked = jnp.int32(0)
    for k in range(picks.shape[0]):
        picked = picked + jnp.where(picks[k] == wanted, 1, 0)
    scaled = gain[...] * (picked.astype(F32) * pulled)
    token_grad = inv_spread * (
        scaled
        - jnp.mean(scaled, axis=1, keepdims=True)
        - normed * jnp.mean(scaled * normed, axis=1, keepdims=True)
    )
    patch_grad = matmul_t(token_grad.astype(BF16), weight[...]).astype(BF16)
    rows = 3 * height
    place = iota((rows, 1), 0)
    pixel_row = mod(place, height)
    colour = div(place, height)
    copied = matmul(ones_where(div(pixel_row, PATCH) == iota((1, normed.shape[0]), 1)), patch_grad)
    kept = jnp.where(
        colour * PATCH + mod(pixel_row, PATCH) == div(iota((1, width), 1), PATCH), copied, 0.0
    ).astype(BF16)
    fold = ones_where(mod(iota((width, 1), 0), PATCH) == mod(iota((1, LANES), 1), PATCH))
    pixels = matmul(kept, fold).astype(BF16)
    messages = plans[0].shape[0]
    lane = div(iota((1, LANES), 1), PATCH)
    result = jnp.where(mod(iota((messages, 1), 0), message_rows) == message_rows - 1, sums, 0.0)
    for j, plan in enumerate(plans):
        result = result + jnp.where(lane == j, matmul(plan, pixels), 0.0)
    send[...] = result.reshape(send.shape)


def write_edges(place, hidden, across, along):
    last = hidden.shape[0] - 1
    even = place[0] % 2 == 0
    across[0] = hidden[jnp.where(even, last, 0)]
    along[0] = hidden[jnp.where(even, 0, last)]


def reward_kernel(place, *refs):
    count = 10
    far, send, across, along = refs[:count], refs[count], refs[count + 1], refs[count + 2]
    near, sems = refs[count + 3 : 2 * count + 3], refs[-1]
    frames, hidden, bias, owner, picks, gain, head_bias, head_out, patch, head = near
    steps = 3
    depth = patch.shape[0] // steps
    copies = {i: pltpu.make_async_copy(far[i], near[i], sems.at[i]) for i in range(count) if i != 8}
    patch_copies = [
        pltpu.make_async_copy(
            far[8].at[pl.ds(i * depth, depth)], patch.at[pl.ds(i * depth, depth)], sems.at[count + i]
        )
        for i in range(steps)
    ]
    for copy in [copies[i] for i in range(3)] + patch_copies + [copies[i] for i in (3, 4, 5, 6, 7, 9)]:
        copy.start()

    def load_patch():
        for i in range(steps):
            patch_copies[i].wait()
            yield i * depth, (i + 1) * depth, patch[i * depth : (i + 1) * depth, :]

    height = frames.shape[2]
    patches = height // PATCH
    plans = send_plan(send.shape[0], height, hidden.shape[0])
    copies[0].wait()
    tokens = to_tokens(frames[...])
    copies[1].wait()
    sums = group_sums(hidden[...])
    write_edges(place, hidden, across, along)
    for i in range(2, 8):
        copies[i].wait()
    normed, inv_spread, pooled = forward_part(tokens, patches, bias, gain, load_patch)
    copies[9].wait()
    backward_part(
        owner,
        picks,
        gain,
        head_bias,
        head_out,
        normed,
        inv_spread,
        pooled / patches,
        patch,
        head,
        place[0],
        plans,
        sums,
        send,
    )


def forward_kernel(frames, bias, gain, patch, normed, inv_spread, pooled):
    width = patch.shape[0]
    tokens = to_tokens(frames[...])
    normed[...], spread, pooled[...] = forward_part(
        tokens, frames.shape[2] // PATCH, bias, gain, lambda: [(0, width, patch[...])]
    )
    inv_spread[...] = jnp.broadcast_to(spread, inv_spread.shape)


def backward_kernel(
    owner,
    picks,
    place,
    hidden,
    gain,
    head_bias,
    head_out,
    normed,
    inv_spread,
    pooled,
    patch,
    head,
    send,
    across,
    along,
    *,
    height,
    per_frame,
):
    write_edges(place, hidden, across, along)
    backward_part(
        owner,
        picks,
        gain,
        head_bias,
        head_out,
        normed[...],
        inv_spread[...][:, :1],
        pooled[...],
        patch,
        head,
        place[0] // per_frame,
        send_plan(send.shape[0], height, hidden.shape[0]),
        group_sums(hidden[...]),
        send,
    )


def params(cells):
    return pltpu.CompilerParams(vmem_limit_bytes=min(16 + cells // 64, 48) * 1024 * 1024)


def near(array):
    return pltpu.with_memory_space_constraint(array, pltpu.VMEM)


def far(array):
    return pltpu.with_memory_space_constraint(array, pltpu.HBM)


def prepare_kernel(across, along, out_weight, wide, scratch):
    window = scratch.shape[0] // 9
    amount = scratch.shape[1] // LANES
    scratch[...] = jnp.zeros_like(scratch)
    for a in range(3):
        for e in range(3):
            base = (a * 3 + e) * window
            for b in range(3):
                piece = out_weight[a, b, e].astype(F32)
                for i in range(amount):
                    start = base + 3 * (i - b + 2)
                    scratch[start : start + 3, i * LANES : (i + 1) * LANES] = piece
    wide[...] = scratch[...].astype(BF16)


def turn_kernel(stats, inner_weight, turned):
    size = inner_weight.shape[3]
    for b in range(3):
        for a in range(3):
            for e in range(3):
                at = ((b * 3 + a) * 3 + e) * size
                turned[at : at + size, :] = inner_weight[a, b, e].T


def slope_kernel(
    owner, place, arrived, hidden, across, along, gain, shift, wide, direct, states, stats, sums, sems
):
    devices, message_rows, _ = arrived.shape
    own_rows, frame_count, width, channels = hidden.shape
    rows = own_rows + 2
    odd = place[0] % 2
    copies = [
        pltpu.make_async_copy(hidden, states.at[pl.ds(1, own_rows)], sems.at[0]),
        pltpu.make_async_copy(across.at[0], states.at[(1 - odd) * (rows - 1)], sems.at[1]),
        pltpu.make_async_copy(along.at[0], states.at[odd * (rows - 1)], sems.at[2]),
    ]
    for copy in copies:
        copy.start()
    cells = frame_count * width
    per_frame = devices // frame_count
    window = wide.shape[0] // 9
    total_rows = devices * message_rows
    got = arrived[...].reshape(total_rows, LANES)
    row = iota((total_rows, 1), 0)
    kind = mod(row, message_rows)

    totals = jnp.sum(jnp.where(kind == message_rows - 1, got, 0.0), axis=0, keepdims=True)
    column = iota((1, 2 * channels), 1)
    wanted = div(mod(column, channels), channels // GROUPS) + jnp.where(column >= channels, GROUPS, 0)
    spread = exact_rows([totals], lambda r: matmul(r, ones_where(iota((LANES, 1), 0) == wanted)))[0]
    cell_total = own_rows * devices * cells * (channels // GROUPS)
    mean = spread[:, :channels] / cell_total
    inverse = lax.rsqrt(spread[:, channels:] / cell_total - mean * mean + eps_norm)
    stats[0:1, :] = mean
    stats[1:2, :] = inverse

    source = div(row, message_rows)
    block = div(source, per_frame)
    frame = jnp.zeros_like(block)
    for b in range(frame_count):
        frame = jnp.where(block == b, owner[b], frame)
    home = frame * per_frame + mod(source, per_frame)
    fold = ones_where(mod(iota((LANES, 1), 0), PATCH) == mod(iota((1, cells), 1), PATCH))
    home = home == div(iota((1, cells), 1), PATCH)
    lane_kind = mod(iota((1, total_rows), 1), message_rows)
    lane_kind = jnp.where(lane_kind == message_rows - 1, -4 * window, lane_kind)
    held = div(iota((1, LANES), 1), PATCH)
    place_row = iota((window, 1), 0)
    pixels = jnp.zeros((window, cells), F32)
    for j in range(own_rows + 4):
        placed = matmul(jnp.where(held == j, got, 0.0).astype(BF16), fold)
        kept = jnp.where(home, placed, 0.0).astype(BF16)
        pixels = pixels + matmul(ones_where(place_row == lane_kind + 3 * j), kept)

    lane = iota((1, cells), 1)
    in_frame = mod(lane, width)
    shifted = []
    for a in range(3):
        for e in range(3):
            step = (2 - a) * width + 1 - e
            moved = pltpu.roll(pixels, (-step) % cells, 1) if step else pixels
            inside = (lane < cells - (2 - a) * width) & (in_frame >= e - 1) & (in_frame < width + e - 1)
            shifted.append(jnp.where(inside, moved, 0.0))
    stacked = jnp.concatenate(shifted, axis=0).astype(BF16)
    slopes = lax.dot_general(stacked, wide[...], (((0,), (0,)), ((), ())), preferred_element_type=F32)

    for copy in copies:
        copy.wait()
    first = jnp.zeros((1, channels), F32)
    second = jnp.zeros((1, channels), F32)
    for i in range(rows):
        normed = (states[i].reshape(cells, channels).astype(F32) - mean) * inverse
        affine = normed * gain[...] + shift[...]
        up = slopes[:, i * channels : (i + 1) * channels] * silu_slope(affine) * gain[...]
        direct[i] = up * inverse
        row_first = jnp.sum(up, axis=0, keepdims=True)
        row_second = jnp.sum(up * normed, axis=0, keepdims=True)
        if 0 < i < rows - 1:
            first = first + row_first
            second = second + row_second
    both = jnp.where(iota((2, channels), 0) == 0, first, second)
    sums[...] = jnp.broadcast_to(both[None], sums.shape)


def inner_kernel(place, arrived, stats, direct, states, turned, out, padded, *, devices):
    own_rows, frame_count, width, channels = out.shape
    cells = frame_count * width
    totals = jnp.sum(arrived[...], axis=0)
    same = ones_where(
        div(iota((channels, 1), 0), channels // GROUPS) == div(iota((1, channels), 1), channels // GROUPS)
    )
    cell_total = own_rows * devices * cells * (channels // GROUPS)
    first, second = exact_rows([totals[0:1], totals[1:2]], lambda rows: matmul(rows, same))
    mean = stats[0:1, :]
    inverse = stats[1:2, :]
    constant = first / cell_total * inverse
    factor = second / cell_total * inverse * inverse
    position = place[0]
    in_frame = mod(iota((cells, 1), 0), width)
    for i in range(own_rows + 2):
        state = states[i].reshape(cells, channels).astype(F32)
        grad = direct[i] - constant - (state - mean) * factor
        if i == 0:
            grad = jnp.where(position > 0, grad, 0.0)
        if i == own_rows + 1:
            grad = jnp.where(position < devices - 1, grad, 0.0)
        after = jnp.where(in_frame < width - 1, pltpu.roll(grad, cells - 1, 0), 0.0)
        prior = jnp.where(in_frame > 0, pltpu.roll(grad, 1, 0), 0.0)
        padded[i, :cells, 0:channels] = after.astype(BF16)
        padded[i, :cells, channels : 2 * channels] = grad.astype(BF16)
        padded[i, :cells, 2 * channels :] = prior.astype(BF16)
        padded[i, cells:, :] = jnp.zeros((2 * width, 3 * channels), BF16)
    depth = 3 * channels
    for r in range(own_rows):
        total = jnp.zeros((cells, channels), F32)
        for b in range(3):
            joined = jnp.concatenate(
                [padded[r - b + 2, (2 - a) * width : (2 - a) * width + cells, :] for a in range(3)], axis=1
            )
            total = total + matmul(joined, turned[b * 3 * depth : (b + 1) * 3 * depth, :])
        out[r] = total.reshape(frame_count, width, channels).astype(BF16)


def per_device(
    frames,
    frame_owner,
    picks,
    patch_weight,
    patch_bias,
    norm_gain,
    head_weight,
    head_bias,
    head_out,
    hidden_state,
    group_gain,
    group_shift,
    out_weight,
    inner_weight,
):
    devices = lax.axis_size("row")
    position = lax.axis_index("row").astype(jnp.int32).reshape(1)
    per_frame = devices // FRAMES
    height = frames.shape[1]
    own_rows, _, frame_width, channels = hidden_state.shape
    cells = FRAMES * frame_width
    width = patch_weight.shape[1]
    turned_frames = jnp.transpose(frames, (0, 2, 1))
    bias = patch_bias.reshape(1, width)
    gain = norm_gain.reshape(1, width)
    head_bias_row = head_bias.reshape(1, width)
    head_out_row = head_out.reshape(1, width)
    window, message_rows = layout(own_rows)
    edge = jax.ShapeDtypeStruct((1,) + hidden_state.shape[1:], BF16)
    message = (jax.ShapeDtypeStruct((devices, message_rows, LANES), F32), edge, edge)
    if per_frame == 1:
        arrays = [
            turned_frames,
            hidden_state,
            bias,
            frame_owner,
            picks,
            gain,
            head_bias_row,
            head_out_row,
            patch_weight,
            head_weight,
        ]
        send, across, along = pl.pallas_call(
            reward_kernel,
            out_shape=message,
            in_specs=[SMEM] + [FAR] * len(arrays),
            out_specs=[VMEM] * 3,
            scratch_shapes=[
                (pltpu.SMEM if x.dtype == jnp.int32 else pltpu.VMEM)(x.shape, x.dtype) for x in arrays
            ]
            + [pltpu.SemaphoreType.DMA((len(arrays) + 3,))],
            compiler_params=params(0),
            name="reward",
        )(position, *[far(x) for x in arrays])
    else:
        count = height // PATCH
        normed, inv_spread, partial = pl.pallas_call(
            forward_kernel,
            out_shape=(
                jax.ShapeDtypeStruct((token_rows_of(height), width), F32),
                jax.ShapeDtypeStruct((token_rows_of(height), LANES), F32),
                jax.ShapeDtypeStruct((1, width), F32),
            ),
            compiler_params=params(cells),
            name="reward_forward",
        )(turned_frames, bias, gain, patch_weight)
        members = [[b * per_frame + i for i in range(per_frame)] for b in range(FRAMES)]
        pooled = lax.psum(partial, "row", axis_index_groups=members) / (count * per_frame)
        send, across, along = pl.pallas_call(
            functools.partial(backward_kernel, height=height, per_frame=per_frame),
            out_shape=message,
            in_specs=[SMEM] * 3 + [VMEM] * 9,
            out_specs=[VMEM] * 3,
            compiler_params=params(cells),
            name="reward_backward",
        )(
            frame_owner,
            picks,
            position,
            hidden_state,
            gain,
            head_bias_row,
            head_out_row,
            normed,
            inv_spread,
            pooled,
            patch_weight,
            head_weight,
        )
    window_rows = -(-3 * window // 8) * 8
    state_rows = own_rows + 2
    arrived = lax.all_to_all(send, "row", 0, 0, tiled=True)
    swaps = [(2 * i, 2 * i + 1) for i in range(devices // 2)]
    across = lax.ppermute(across, "row", swaps + [(b, a) for a, b in swaps])
    swaps = [(2 * i - 1, 2 * i) for i in range(1, devices // 2)]
    along = lax.ppermute(along, "row", swaps + [(b, a) for a, b in swaps])
    wide = pl.pallas_call(
        prepare_kernel,
        out_shape=pltpu.VMEM((9 * window_rows, state_rows * channels), BF16),
        in_specs=[FAR] * 2 + [VMEM],
        scratch_shapes=[pltpu.VMEM((9 * window_rows, state_rows * channels), F32)],
        compiler_params=params(cells),
        name="prepare",
    )(across, along, out_weight)
    direct, states, stats, sums = pl.pallas_call(
        slope_kernel,
        out_shape=(
            pltpu.VMEM((state_rows, cells, channels), F32),
            pltpu.VMEM((state_rows,) + hidden_state.shape[1:], BF16),
            pltpu.VMEM((8, channels), F32),
            jax.ShapeDtypeStruct((devices, 2, channels), F32),
        ),
        in_specs=[SMEM] * 2 + [VMEM] + [FAR] * 3 + [VMEM] * 3,
        scratch_shapes=[pltpu.SemaphoreType.DMA((3,))],
        compiler_params=params(cells),
        name="slope",
    )(
        frame_owner,
        position,
        near(arrived),
        far(hidden_state),
        across,
        along,
        group_gain.reshape(1, channels),
        group_shift.reshape(1, channels),
        near(wide),
    )
    summed = lax.all_to_all(sums, "row", 0, 0, tiled=True)
    turned = pl.pallas_call(
        turn_kernel,
        out_shape=pltpu.VMEM((27 * channels, channels), BF16),
        in_specs=[FAR, VMEM],
        compiler_params=params(cells),
        name="turn",
    )(stats, inner_weight)
    return pl.pallas_call(
        functools.partial(inner_kernel, devices=devices),
        out_shape=jax.ShapeDtypeStruct(hidden_state.shape, BF16),
        in_specs=[SMEM] + [VMEM] * 5,
        scratch_shapes=[pltpu.VMEM((own_rows + 2, cells + 2 * frame_width, 3 * channels), BF16)],
        compiler_params=params(cells),
        name="inner",
    )(position, near(summed), near(stats), near(direct), near(states), near(turned))


def solution(mesh):
    return jax.shard_map(
        per_device,
        mesh=mesh,
        in_specs=(
            P(None, None, ("clip", "row")),
            P("clip"),
            P("clip"),
            P(),
            P(),
            P(),
            P(),
            P(),
            P(),
            P(("clip", "row"), None, None, None),
            P(),
            P(),
            P(),
            P(),
        ),
        out_specs=P(("clip", "row"), None, None, None),
        check_vma=False,
    )
```

```python
import functools

import jax
import jax.numpy as jnp
from jax import lax
from jax.experimental import pallas as pl
from jax.experimental.pallas import tpu as pltpu
from jax.sharding import PartitionSpec as P

PATCH = 16
GROUPS = 32
FRAMES = 16
LANES = 128
SLOTS = LANES // PATCH
PAIR = 2
SLOTS = LANES // PATCH
eps_norm = 1e-06
BF16 = jnp.bfloat16
F32 = jnp.float32

SMEM = pl.BlockSpec(memory_space=pltpu.SMEM)
VMEM = pl.BlockSpec(memory_space=pltpu.VMEM)
FAR = pl.BlockSpec(memory_space=pl.ANY)


def iota(shape, dim):
    return lax.broadcasted_iota(jnp.int32, shape, dim)


def div(values, count):
    if count & (count - 1):
        return values // count
    return values >> (count.bit_length() - 1)


def mod(values, count):
    if count & (count - 1):
        return values % count
    return values & (count - 1)


def ones_where(condition):
    return jnp.where(condition, 1.0, 0.0).astype(BF16)


def matmul(left, right):
    return jnp.dot(left, right, preferred_element_type=F32)


def matmul_t(left, right):
    return lax.dot_general(left, right, (((1,), (1,)), ((), ())), preferred_element_type=F32)


def exact_rows(rows, product):
    place = iota((16, rows[0].shape[1]), 0)
    stacked = jnp.zeros(place.shape, F32)
    for index, row in enumerate(rows):
        high = row.astype(BF16).astype(F32)
        rest = row - high
        middle = rest.astype(BF16).astype(F32)
        for step, piece in enumerate((high, middle, rest - middle)):
            stacked = jnp.where(place == 3 * index + step, piece, stacked)
    result = product(stacked.astype(BF16))
    return [
        result[3 * i : 3 * i + 1] + result[3 * i + 1 : 3 * i + 2] + result[3 * i + 2 : 3 * i + 3]
        for i in range(len(rows))
    ]


def silu_slope(values):
    sigmoid = jax.nn.sigmoid(values)
    return sigmoid * (1.0 + values * (1.0 - sigmoid))


def token_rows_of(height):
    return -(-PAIR * (height // PATCH) // 16) * 16


def to_tokens(strips):
    channels, columns, height = strips[0].shape
    count = height // PATCH
    rows = channels * columns
    token_rows = token_rows_of(height)
    width = channels * PATCH * columns
    lane = iota((1, width), 1)
    place = iota((rows, 1), 0)
    mine = place == div(lane, PATCH * columns) * columns + mod(lane, columns)
    in_patch = mod(div(lane, columns), PATCH)
    pixel_row = iota((height, 1), 0)
    token = iota((token_rows, rows), 0)
    tokens = jnp.zeros((token_rows, width), F32)
    for t in range(count):
        picked = ones_where(pixel_row == in_patch + t * PATCH)
        for s, strip in enumerate(strips):
            tiled = matmul(strip.reshape(rows, height), picked)
            kept = jnp.where(mine, tiled, 0.0).astype(BF16)
            tokens = tokens + matmul(ones_where(token == s * count + t), kept)
    return tokens.astype(BF16)


def forward_part(tokens, count, bias, gain, load_patch):
    embedded = bias[...]
    for low, high, weight in load_patch():
        embedded = embedded + matmul(tokens[:, low:high], weight)
    centred = embedded - jnp.mean(embedded, axis=1, keepdims=True)
    inv_spread = lax.rsqrt(jnp.mean(centred * centred, axis=1, keepdims=True) + eps_norm)
    normed = centred * inv_spread
    weighted = normed * gain[...]
    token = iota((tokens.shape[0], 1), 0)
    pooled = []
    for s in range(PAIR):
        inside = (token >= s * count) & (token < (s + 1) * count)
        pooled.append(jnp.sum(jnp.where(inside, weighted, 0.0), axis=0, keepdims=True))
    return normed, inv_spread, pooled


def layout(own_rows):
    window = PAIR * own_rows + 3
    per_row = PAIR * 3
    data_rows = -(-per_row * window // SLOTS)
    message_rows = -(-(data_rows + 1) // 8) * 8
    entries = {}
    for q in range(SLOTS):
        for m in range(data_rows):
            entry = q * data_rows + m
            if entry < per_row * window:
                entries[q, m] = (entry // per_row, entry % per_row // 3, entry % 3)
    return window, data_rows, message_rows, entries


def send_plan(targets, height, own_rows, core):
    _, data_rows, message_rows, entries = layout(own_rows)
    rows = targets * message_rows
    message = iota((rows, 1), 0)
    kind = mod(message, message_rows)
    first = div(message, message_rows) * (PAIR * own_rows) + core - 2
    source = iota((1, PAIR * 3 * height), 1)
    spacing = 4 * height
    source = div(source, height) * spacing + mod(source, height) + height
    plans = []
    for q in range(SLOTS):
        wanted = jnp.full((rows, 1), -spacing, jnp.int32)
        for m in range(data_rows):
            if (q, m) in entries:
                j, s, k = entries[q, m]
                wanted = jnp.where(kind == m, (s * 3 + k) * spacing + j + height, wanted)
        plans.append(ones_where(source == wanted + first))
    return plans


def group_sums(states):
    channels = states[0].shape[-1]
    first = jnp.zeros((1, channels), F32)
    second = jnp.zeros((1, channels), F32)
    for state in states:
        values = state.reshape(-1, channels).astype(F32)
        first = first + jnp.sum(values, axis=0, keepdims=True)
        second = second + jnp.sum(values * values, axis=0, keepdims=True)
    lane = iota((1, LANES), 1)
    group = div(iota((channels, 1), 0), channels // GROUPS)
    low = exact_rows([first], lambda rows: matmul(rows, ones_where(lane == group)))[0]
    high = exact_rows([second], lambda rows: matmul(rows, ones_where(lane == group + GROUPS)))[0]
    return low + high


def backward_part(
    owner, picks, gain, head_bias, head_out, normed, inv_spread, pooled, weight, head, slots, plans, sums, send
):
    width = weight.shape[0]
    message_rows = send.shape[1]
    height = plans[0].shape[1] // (PAIR * 3)
    count = height // PATCH
    before = exact_rows(pooled, lambda rows: matmul(rows, head[...]))
    slopes = [head_out[...] * silu_slope(row + head_bias[...]) for row in before]
    pulled = exact_rows(slopes, lambda rows: matmul_t(rows, head[...]))
    token = iota((normed.shape[0], 1), 0)
    scaled = jnp.zeros(normed.shape, F32)
    for s in range(PAIR):
        wanted = owner[slots[s]]
        picked = jnp.int32(0)
        for k in range(picks.shape[0]):
            picked = picked + jnp.where(picks[k] == wanted, 1, 0)
        inside = (token >= s * count) & (token < (s + 1) * count)
        scaled = jnp.where(inside, gain[...] * (picked.astype(F32) * pulled[s]), scaled)
    token_grad = inv_spread * (
        scaled
        - jnp.mean(scaled, axis=1, keepdims=True)
        - normed * jnp.mean(scaled * normed, axis=1, keepdims=True)
    )
    patch_grad = matmul_t(token_grad.astype(BF16), weight[...]).astype(BF16)
    rows = PAIR * 3 * height
    place = iota((rows, 1), 0)
    strip = div(place, 3 * height)
    pixel_row = mod(place, height)
    colour = mod(div(place, height), 3)
    copied = matmul(
        ones_where(strip * count + div(pixel_row, PATCH) == iota((1, normed.shape[0]), 1)), patch_grad
    )
    kept = jnp.where(
        colour * PATCH + mod(pixel_row, PATCH) == div(iota((1, width), 1), PATCH), copied, 0.0
    ).astype(BF16)
    fold = ones_where(mod(iota((width, 1), 0), PATCH) == mod(iota((1, LANES), 1), PATCH))
    pixels = matmul(kept, fold).astype(BF16)
    messages = plans[0].shape[0]
    lane = div(iota((1, LANES), 1), PATCH)
    result = jnp.where(mod(iota((messages, 1), 0), message_rows) == message_rows - 1, sums, 0.0)
    for q, plan in enumerate(plans):
        result = result + jnp.where(lane == q, matmul(plan, pixels), 0.0)
    send[...] = result.reshape(send.shape)


def write_edge(place, hidden, edge):
    edge[0] = hidden[jnp.where(place[0] % PAIR == 0, 0, hidden.shape[0] - 1)]


def reward_kernel(place, *refs):
    count = 12
    far, send, edge = refs[:count], refs[count], refs[count + 1]
    near, sems = refs[count + 2 : 2 * count + 2], refs[-1]
    frames, other_frames, hidden, other_hidden, bias, owner, picks, gain, head_bias, head_out, patch, head = near
    steps = 3
    depth = patch.shape[0] // steps
    copies = {i: pltpu.make_async_copy(far[i], near[i], sems.at[i]) for i in range(count) if i != 10}
    patch_copies = [
        pltpu.make_async_copy(
            far[10].at[pl.ds(i * depth, depth)], patch.at[pl.ds(i * depth, depth)], sems.at[count + i]
        )
        for i in range(steps)
    ]
    for copy in [copies[i] for i in range(5)] + patch_copies + [copies[i] for i in (5, 6, 7, 8, 9, 11)]:
        copy.start()

    def load_patch():
        for i in range(steps):
            patch_copies[i].wait()
            yield i * depth, (i + 1) * depth, patch[i * depth : (i + 1) * depth, :]

    height = frames.shape[2]
    patches = height // PATCH
    position = place[0]
    core = position % PAIR
    plans = send_plan(send.shape[0], height, hidden.shape[0], core)
    copies[0].wait()
    copies[1].wait()
    tokens = to_tokens([frames[...], other_frames[...]])
    copies[2].wait()
    copies[3].wait()
    sums = group_sums([hidden[...], other_hidden[...]])
    write_edge(place, hidden, edge)
    for i in range(4, 10):
        copies[i].wait()
    normed, inv_spread, pooled = forward_part(tokens, patches, bias, gain, load_patch)
    pooled = [row / patches for row in pooled]
    copies[11].wait()
    slots = [position, position + 1 - 2 * core]
    backward_part(
        owner, picks, gain, head_bias, head_out, normed, inv_spread, pooled, patch, head, slots, plans, sums, send
    )


def forward_kernel(frames, other_frames, bias, gain, patch, normed, inv_spread, pooled):
    width = patch.shape[0]
    tokens = to_tokens([frames[...], other_frames[...]])
    normed[...], spread, strips = forward_part(
        tokens, frames.shape[2] // PATCH, bias, gain, lambda: [(0, width, patch[...])]
    )
    inv_spread[...] = jnp.broadcast_to(spread, inv_spread.shape)
    pooled[...] = strips[0]


def backward_kernel(
    owner,
    picks,
    place,
    hidden,
    other_hidden,
    gain,
    head_bias,
    head_out,
    normed,
    inv_spread,
    pooled,
    patch,
    head,
    send,
    edge,
    *,
    height,
    per_frame,
):
    write_edge(place, hidden, edge)
    backward_part(
        owner,
        picks,
        gain,
        head_bias,
        head_out,
        normed[...],
        inv_spread[...][:, :1],
        [pooled[...]] * PAIR,
        patch,
        head,
        [place[0] // per_frame] * PAIR,
        send_plan(send.shape[0], height, hidden.shape[0], place[0] % PAIR),
        group_sums([hidden[...], other_hidden[...]]),
        send,
    )


def params(cells):
    return pltpu.CompilerParams(vmem_limit_bytes=min(16 + cells // 64, 48) * 1024 * 1024)


def near(array):
    return pltpu.with_memory_space_constraint(array, pltpu.VMEM)


def far(array):
    return pltpu.with_memory_space_constraint(array, pltpu.HBM)


def prepare_kernel(place, hidden, other_hidden, edge, out_weight, states, wide, scratch, sems):
    own_rows = hidden.shape[0]
    core = place[0] % PAIR
    copies = [
        pltpu.make_async_copy(hidden, states.at[pl.ds(1 + core * (own_rows - 1), own_rows)], sems.at[0]),
        pltpu.make_async_copy(
            other_hidden, states.at[pl.ds((1 - core) * (own_rows + 1), own_rows)], sems.at[1]
        ),
        pltpu.make_async_copy(edge.at[0], states.at[core * PAIR * own_rows], sems.at[2]),
    ]
    for copy in copies:
        copy.start()
    window = scratch.shape[0] // 9
    amount = scratch.shape[1] // LANES
    scratch[...] = jnp.zeros_like(scratch)
    for a in range(3):
        for e in range(3):
            base = (a * 3 + e) * window
            for b in range(3):
                piece = out_weight[a, b, e].astype(F32)
                for i in range(amount):
                    start = base + 3 * (i - b + 2)
                    scratch[start : start + 3, i * LANES : (i + 1) * LANES] = piece
    wide[...] = scratch[...].astype(BF16)
    for copy in copies:
        copy.wait()


def turn_kernel(stats, inner_weight, turned):
    size = inner_weight.shape[3]
    for b in range(3):
        for a in range(3):
            for e in range(3):
                at = ((b * 3 + a) * 3 + e) * size
                turned[at : at + size, :] = inner_weight[a, b, e].T


def slope_kernel(owner, place, arrived, states, gain, shift, wide, direct, stats, sums, slopes):
    chips, message_rows, _ = arrived.shape
    rows, frame_count, width, channels = states.shape
    own_rows = (rows - 1) // PAIR
    devices = chips * PAIR
    core = place[0] % PAIR
    cells = frame_count * width
    per_frame = devices // frame_count
    window = wide.shape[0] // 9
    _, data_rows, _, entries = layout(own_rows)
    total_rows = chips * message_rows
    got = arrived[...].reshape(total_rows, LANES)
    row = iota((total_rows, 1), 0)
    kind = mod(row, message_rows)

    totals = jnp.sum(jnp.where(kind == message_rows - 1, got, 0.0), axis=0, keepdims=True)
    column = iota((1, 2 * channels), 1)
    wanted = div(mod(column, channels), channels // GROUPS) + jnp.where(column >= channels, GROUPS, 0)
    spread = exact_rows([totals], lambda r: matmul(r, ones_where(iota((LANES, 1), 0) == wanted)))[0]
    cell_total = own_rows * devices * cells * (channels // GROUPS)
    mean = spread[:, :channels] / cell_total
    inverse = lax.rsqrt(spread[:, channels:] / cell_total - mean * mean + eps_norm)
    stats[0:1, :] = mean
    stats[1:2, :] = inverse

    homes = []
    for s in range(PAIR):
        strip = div(row, message_rows) * PAIR + (core if s == 0 else 1 - core)
        block = div(strip, per_frame)
        frame = jnp.zeros_like(block)
        for b in range(frame_count):
            frame = jnp.where(block == b, owner[b], frame)
        homes.append(frame * per_frame + mod(strip, per_frame))
    fold = ones_where(mod(iota((LANES, 1), 0), PATCH) == mod(iota((1, cells), 1), PATCH))
    lane_home = div(iota((1, cells), 1), PATCH)
    lane_kind = mod(iota((1, total_rows), 1), message_rows)
    held = div(iota((1, LANES), 1), PATCH)
    place_row = iota((window, 1), 0)
    pixels = jnp.zeros((window, cells), F32)
    for q in range(SLOTS):
        home = jnp.full_like(row, -1)
        chosen = jnp.full_like(lane_kind, -1)
        for m in range(data_rows):
            if (q, m) in entries:
                j, s, k = entries[q, m]
                home = jnp.where(kind == m, homes[s], home)
                chosen = jnp.where(lane_kind == m, j * 3 + k, chosen)
        placed = matmul(jnp.where(held == q, got, 0.0).astype(BF16), fold)
        kept = jnp.where(home == lane_home, placed, 0.0).astype(BF16)
        pixels = pixels + matmul(ones_where(place_row == chosen), kept)

    lane = iota((1, cells), 1)
    in_frame = mod(lane, width)
    shifted = []
    for a in range(3):
        for e in range(3):
            step = (2 - a) * width + 1 - e
            moved = pltpu.roll(pixels, (-step) % cells, 1) if step else pixels
            inside = (lane < cells - (2 - a) * width) & (in_frame >= e - 1) & (in_frame < width + e - 1)
            shifted.append(jnp.where(inside, moved, 0.0))
    stacked = jnp.concatenate(shifted, axis=0).astype(BF16)
    result = lax.dot_general(stacked, wide[...], (((0,), (0,)), ((), ())), preferred_element_type=F32)
    for i in range(rows):
        slopes[i] = result[:, i * channels : (i + 1) * channels]

    first = jnp.zeros((1, channels), F32)
    second = jnp.zeros((1, channels), F32)
    needed = own_rows + 2
    for i in range(rows):
        if i < needed:
            at = core * (own_rows - 1) + i
        else:
            at = i - core * needed
        normed = (states[at].reshape(cells, channels).astype(F32) - mean) * inverse
        affine = normed * gain[...] + shift[...]
        up = slopes[at] * silu_slope(affine) * gain[...]
        if i < needed:
            direct[i] = up * inverse
        row_first = jnp.sum(up, axis=0, keepdims=True)
        row_second = jnp.sum(up * normed, axis=0, keepdims=True)
        if i == 0 or i == needed - 1:
            counted = core == (1 if i == 0 else 0)
            row_first = jnp.where(counted, row_first, 0.0)
            row_second = jnp.where(counted, row_second, 0.0)
        first = first + row_first
        second = second + row_second
    both = jnp.where(iota((2, channels), 0) == 0, first, second)
    sums[...] = jnp.broadcast_to(both[None], sums.shape)


def inner_kernel(place, arrived, stats, direct, states, turned, out, padded, *, devices):
    own_rows, frame_count, width, channels = out.shape
    cells = frame_count * width
    totals = jnp.sum(arrived[...], axis=0)
    same = ones_where(
        div(iota((channels, 1), 0), channels // GROUPS) == div(iota((1, channels), 1), channels // GROUPS)
    )
    cell_total = own_rows * devices * cells * (channels // GROUPS)
    first, second = exact_rows([totals[0:1], totals[1:2]], lambda rows: matmul(rows, same))
    mean = stats[0:1, :]
    inverse = stats[1:2, :]
    constant = first / cell_total * inverse
    factor = second / cell_total * inverse * inverse
    position = place[0]
    base = position % PAIR * (own_rows - 1)
    in_frame = mod(iota((cells, 1), 0), width)
    for i in range(own_rows + 2):
        state = states[base + i].reshape(cells, channels).astype(F32)
        grad = direct[i] - constant - (state - mean) * factor
        if i == 0:
            grad = jnp.where(position > 0, grad, 0.0)
        if i == own_rows + 1:
            grad = jnp.where(position < devices - 1, grad, 0.0)
        after = jnp.where(in_frame < width - 1, pltpu.roll(grad, cells - 1, 0), 0.0)
        prior = jnp.where(in_frame > 0, pltpu.roll(grad, 1, 0), 0.0)
        padded[i, :cells, 0:channels] = after.astype(BF16)
        padded[i, :cells, channels : 2 * channels] = grad.astype(BF16)
        padded[i, :cells, 2 * channels :] = prior.astype(BF16)
        padded[i, cells:, :] = jnp.zeros((2 * width, 3 * channels), BF16)
    depth = 3 * channels
    for r in range(own_rows):
        total = jnp.zeros((cells, channels), F32)
        for b in range(3):
            joined = jnp.concatenate(
                [padded[r - b + 2, (2 - a) * width : (2 - a) * width + cells, :] for a in range(3)], axis=1
            )
            total = total + matmul(joined, turned[b * 3 * depth : (b + 1) * 3 * depth, :])
        out[r] = total.reshape(frame_count, width, channels).astype(BF16)


def per_device(
    frames,
    frame_owner,
    picks,
    patch_weight,
    patch_bias,
    norm_gain,
    head_weight,
    head_bias,
    head_out,
    hidden_state,
    group_gain,
    group_shift,
    out_weight,
    inner_weight,
):
    devices = lax.axis_size("row")
    position = lax.axis_index("row").astype(jnp.int32).reshape(1)
    per_frame = devices // FRAMES
    height = frames.shape[1]
    own_rows, _, frame_width, channels = hidden_state.shape
    cells = FRAMES * frame_width
    width = patch_weight.shape[1]
    chips = devices // PAIR
    swaps = [(PAIR * i, PAIR * i + 1) for i in range(chips)]
    swaps = swaps + [(b, a) for a, b in swaps]
    alike = [[PAIR * i + s for i in range(chips)] for s in range(PAIR)]
    turned_frames = jnp.transpose(frames, (0, 2, 1))
    other_frames = lax.ppermute(turned_frames, "row", swaps)
    other_state = lax.ppermute(hidden_state, "row", swaps)
    bias = patch_bias.reshape(1, width)
    gain = norm_gain.reshape(1, width)
    head_bias_row = head_bias.reshape(1, width)
    head_out_row = head_out.reshape(1, width)
    window, _, message_rows, _ = layout(own_rows)
    message = (
        jax.ShapeDtypeStruct((chips, message_rows, LANES), F32),
        jax.ShapeDtypeStruct((1,) + hidden_state.shape[1:], BF16),
    )
    if per_frame == 1:
        arrays = [
            turned_frames,
            other_frames,
            hidden_state,
            other_state,
            bias,
            frame_owner,
            picks,
            gain,
            head_bias_row,
            head_out_row,
            patch_weight,
            head_weight,
        ]
        send, edge = pl.pallas_call(
            reward_kernel,
            out_shape=message,
            in_specs=[SMEM] + [FAR] * len(arrays),
            out_specs=[VMEM] * 2,
            scratch_shapes=[
                (pltpu.SMEM if x.dtype == jnp.int32 else pltpu.VMEM)(x.shape, x.dtype) for x in arrays
            ]
            + [pltpu.SemaphoreType.DMA((len(arrays) + 3,))],
            compiler_params=params(0),
            name="reward",
        )(position, *[x if x is other_frames or x is other_state else far(x) for x in arrays])
    else:
        count = height // PATCH
        normed, inv_spread, partial = pl.pallas_call(
            forward_kernel,
            out_shape=(
                jax.ShapeDtypeStruct((token_rows_of(height), width), F32),
                jax.ShapeDtypeStruct((token_rows_of(height), LANES), F32),
                jax.ShapeDtypeStruct((1, width), F32),
            ),
            compiler_params=params(cells),
            name="reward_forward",
        )(turned_frames, other_frames, bias, gain, patch_weight)
        members = [[b * per_frame + i for i in range(per_frame)] for b in range(FRAMES)]
        pooled = lax.psum(partial, "row", axis_index_groups=members) / (count * per_frame)
        send, edge = pl.pallas_call(
            functools.partial(backward_kernel, height=height, per_frame=per_frame),
            out_shape=message,
            in_specs=[SMEM] * 3 + [VMEM] * 10,
            out_specs=[VMEM] * 2,
            compiler_params=params(cells),
            name="reward_backward",
        )(
            frame_owner,
            picks,
            position,
            hidden_state,
            other_state,
            gain,
            head_bias_row,
            head_out_row,
            normed,
            inv_spread,
            pooled,
            patch_weight,
            head_weight,
        )
    window_rows = -(-3 * window // 16) * 16
    state_rows = PAIR * own_rows + 1
    arrived = lax.all_to_all(send, "row", 0, 0, axis_index_groups=alike, tiled=True)
    swaps = [(PAIR * i - 1, PAIR * i) for i in range(1, chips)]
    edge = lax.ppermute(edge, "row", swaps + [(b, a) for a, b in swaps])
    states, wide = pl.pallas_call(
        prepare_kernel,
        out_shape=(
            pltpu.VMEM((state_rows,) + hidden_state.shape[1:], BF16),
            pltpu.VMEM((9 * window_rows, state_rows * channels), BF16),
        ),
        in_specs=[SMEM] + [FAR] * 3 + [VMEM],
        scratch_shapes=[
            pltpu.VMEM((9 * window_rows, state_rows * channels), F32),
            pltpu.SemaphoreType.DMA((3,)),
        ],
        compiler_params=params(cells),
        name="prepare",
    )(position, far(hidden_state), other_state, edge, out_weight)
    direct, stats, sums = pl.pallas_call(
        slope_kernel,
        out_shape=(
            pltpu.VMEM((own_rows + 2, cells, channels), F32),
            pltpu.VMEM((8, channels), F32),
            jax.ShapeDtypeStruct((chips, 2, channels), F32),
        ),
        in_specs=[SMEM] * 2 + [VMEM] * 5,
        scratch_shapes=[pltpu.VMEM((state_rows, cells, channels), F32)],
        compiler_params=params(cells),
        name="slope",
    )(
        frame_owner,
        position,
        near(arrived),
        near(states),
        group_gain.reshape(1, channels),
        group_shift.reshape(1, channels),
        near(wide),
    )
    summed = lax.all_to_all(sums, "row", 0, 0, axis_index_groups=alike, tiled=True)
    turned = pl.pallas_call(
        turn_kernel,
        out_shape=pltpu.VMEM((27 * channels, channels), BF16),
        in_specs=[FAR, VMEM],
        compiler_params=params(cells),
        name="turn",
    )(stats, inner_weight)
    return pl.pallas_call(
        functools.partial(inner_kernel, devices=devices),
        out_shape=jax.ShapeDtypeStruct(hidden_state.shape, BF16),
        in_specs=[SMEM] + [VMEM] * 5,
        scratch_shapes=[pltpu.VMEM((own_rows + 2, cells + 2 * frame_width, 3 * channels), BF16)],
        compiler_params=params(cells),
        name="inner",
    )(position, near(summed), near(stats), near(direct), near(states), near(turned))


def solution(mesh):
    return jax.shard_map(
        per_device,
        mesh=mesh,
        in_specs=(
            P(None, None, ("clip", "row")),
            P("clip"),
            P("clip"),
            P(),
            P(),
            P(),
            P(),
            P(),
            P(),
            P(("clip", "row"), None, None, None),
            P(),
            P(),
            P(),
            P(),
        ),
        out_specs=P(("clip", "row"), None, None, None),
        check_vma=False,
    )
```

```python
import functools

import jax
import jax.numpy as jnp
from jax import lax
from jax.experimental import pallas as pl
from jax.experimental.pallas import tpu as pltpu
from jax.sharding import PartitionSpec as P

PATCH = 16
GROUPS = 32
FRAMES = 16
LANES = 128
SLOTS = LANES // PATCH
eps_norm = 1e-06
BF16 = jnp.bfloat16
F32 = jnp.float32

SMEM = pl.BlockSpec(memory_space=pltpu.SMEM)
VMEM = pl.BlockSpec(memory_space=pltpu.VMEM)
FAR = pl.BlockSpec(memory_space=pl.ANY)


def iota(shape, dim):
    return lax.broadcasted_iota(jnp.int32, shape, dim)


def div(values, count):
    if count & (count - 1):
        return values // count
    return values >> (count.bit_length() - 1)


def mod(values, count):
    if count & (count - 1):
        return values % count
    return values & (count - 1)


def ones_where(condition):
    return jnp.where(condition, 1.0, 0.0).astype(BF16)


def matmul(left, right):
    return jnp.dot(left, right, preferred_element_type=F32)


def matmul_t(left, right):
    return lax.dot_general(left, right, (((1,), (1,)), ((), ())), preferred_element_type=F32)


def cut_in_three(values):
    high = values.astype(BF16)
    rest = values - high.astype(F32)
    middle = rest.astype(BF16)
    low = (rest - middle.astype(F32)).astype(BF16)
    return high, middle, low


def spread_exactly(ones, values):
    high, middle, low = cut_in_three(values)
    return matmul(ones, high) + matmul(ones, middle) + matmul(ones, low)


def exact_rows(rows, product):
    place = iota((16, rows[0].shape[1]), 0)
    stacked = jnp.zeros(place.shape, F32)
    for index, row in enumerate(rows):
        for step, piece in enumerate(cut_in_three(row)):
            stacked = jnp.where(place == 3 * index + step, piece.astype(F32), stacked)
    result = product(stacked.astype(BF16))
    return [
        result[3 * i : 3 * i + 1] + result[3 * i + 1 : 3 * i + 2] + result[3 * i + 2 : 3 * i + 3]
        for i in range(len(rows))
    ]


def exact_block(values, product):
    count = values.shape[0]
    result = product(jnp.concatenate(cut_in_three(values), axis=0))
    return result[:count] + result[count : 2 * count] + result[2 * count :]


def silu_slope(values):
    sigmoid = jax.nn.sigmoid(values)
    return sigmoid * (1.0 + values * (1.0 - sigmoid))


def token_rows_of(height):
    return -(-(height // PATCH) // 16) * 16


def to_tokens(pixels):
    channels, columns, height = pixels.shape
    rows = channels * columns
    token_rows = token_rows_of(height)
    flat = pixels.reshape(rows, height)
    width = channels * PATCH * columns
    lane = iota((1, width), 1)
    place = iota((rows, 1), 0)
    mine = place == div(lane, PATCH * columns) * columns + mod(lane, columns)
    in_patch = mod(div(lane, columns), PATCH)
    pixel_row = iota((height, 1), 0)
    token = iota((token_rows, rows), 0)
    tokens = jnp.zeros((token_rows, width), F32)
    for t in range(height // PATCH):
        tiled = matmul(flat, ones_where(pixel_row == in_patch + t * PATCH))
        kept = jnp.where(mine, tiled, 0.0).astype(BF16)
        tokens = tokens + matmul(ones_where(token == t), kept)
    return tokens.astype(BF16)


def forward_part(tokens, count, bias, gain, load_patch):
    embedded = bias[...]
    for low, high, weight in load_patch():
        embedded = embedded + matmul(tokens[:, low:high], weight)
    centred = embedded - jnp.mean(embedded, axis=1, keepdims=True)
    inv_spread = lax.rsqrt(jnp.mean(centred * centred, axis=1, keepdims=True) + eps_norm)
    normed = centred * inv_spread
    weighted = normed * gain[...]
    inside = iota((tokens.shape[0], 1), 0) < count
    pooled = jnp.sum(jnp.where(inside, weighted, 0.0), axis=0, keepdims=True)
    return normed, inv_spread, pooled


def layout(own_rows):
    return own_rows + 4, 4


def send_plan(targets, height, own_rows):
    window, message_rows = layout(own_rows)
    rows = targets * message_rows
    message = iota((rows, 1), 0)
    colour = mod(message, message_rows)
    first = div(message, message_rows) * own_rows - 2
    source = iota((1, 3 * height), 1)
    spacing = 4 * height
    source = div(source, height) * spacing + mod(source, height) + height
    wanted = colour * spacing + height + first
    return [ones_where(source == wanted + j) for j in range(window)]


def group_sums(hidden):
    channels = hidden.shape[-1]
    values = hidden.reshape(-1, channels).astype(F32)
    first = jnp.sum(values, axis=0, keepdims=True)
    second = jnp.sum(values * values, axis=0, keepdims=True)
    lane = iota((1, LANES), 1)
    group = div(iota((channels, 1), 0), channels // GROUPS)
    low = exact_rows([first], lambda rows: matmul(rows, ones_where(lane == group)))[0]
    high = exact_rows([second], lambda rows: matmul(rows, ones_where(lane == group + GROUPS)))[0]
    return low + high


def backward_part(
    owner, picks, gain, head_bias, head_out, normed, inv_spread, pooled, weight, head, slot, plans, sums, send
):
    width = weight.shape[0]
    message_rows = send.shape[1]
    height = plans[0].shape[1] // 3
    (before,) = exact_rows([pooled], lambda rows: matmul(rows, head[...]))
    slope = head_out[...] * silu_slope(before + head_bias[...])
    (pulled,) = exact_rows([slope], lambda rows: matmul_t(rows, head[...]))
    wanted = owner[slot]
    picked = jnp.int32(0)
    for k in range(picks.shape[0]):
        picked = picked + jnp.where(picks[k] == wanted, 1, 0)
    scaled = gain[...] * (picked.astype(F32) * pulled)
    token_grad = inv_spread * (
        scaled
        - jnp.mean(scaled, axis=1, keepdims=True)
        - normed * jnp.mean(scaled * normed, axis=1, keepdims=True)
    )
    patch_grad = matmul_t(token_grad.astype(BF16), weight[...]).astype(BF16)
    rows = 3 * height
    place = iota((rows, 1), 0)
    pixel_row = mod(place, height)
    colour = div(place, height)
    copied = matmul(ones_where(div(pixel_row, PATCH) == iota((1, normed.shape[0]), 1)), patch_grad)
    kept = jnp.where(
        colour * PATCH + mod(pixel_row, PATCH) == div(iota((1, width), 1), PATCH), copied, 0.0
    ).astype(BF16)
    fold = ones_where(mod(iota((width, 1), 0), PATCH) == mod(iota((1, LANES), 1), PATCH))
    pixels = matmul(kept, fold).astype(BF16)
    messages = plans[0].shape[0]
    lane = div(iota((1, LANES), 1), PATCH)
    result = jnp.where(mod(iota((messages, 1), 0), message_rows) == message_rows - 1, sums, 0.0)
    for j, plan in enumerate(plans):
        result = result + jnp.where(lane == j, matmul(plan, pixels), 0.0)
    send[...] = result.reshape(send.shape)


def write_edges(place, hidden, across, along):
    last = hidden.shape[0] - 1
    even = place[0] % 2 == 0
    across[0] = hidden[jnp.where(even, last, 0)]
    along[0] = hidden[jnp.where(even, 0, last)]


def packed_rows(height):
    return -(-(height // PATCH + 1) // 4) * 4


def pack_kernel(place, far_frames, far_hidden, message, across, along, frames, hidden, sems):
    copies = [
        pltpu.make_async_copy(far_frames, frames, sems.at[0]),
        pltpu.make_async_copy(far_hidden, hidden, sems.at[1]),
    ]
    for copy in copies:
        copy.start()
    copies[0].wait()
    height = frames.shape[2]
    tokens = to_tokens(frames[...]).astype(F32)
    rows = packed_rows(height)
    runs = message.shape[1] // rows
    whole = jnp.concatenate([tokens[:rows, c * LANES : (c + 1) * LANES] for c in range(runs)], axis=0)
    copies[1].wait()
    write_edges(place, hidden, across, along)
    row = iota((message.shape[1], 1), 0)
    for step, piece in enumerate(cut_in_three(group_sums(hidden[...]))):
        whole = jnp.where(row == (step + 1) * rows - 1, piece.astype(F32), whole)
    message[...] = jnp.broadcast_to(whole.astype(BF16)[None], message.shape)


def forward_kernel(frames, bias, gain, patch, normed, inv_spread, pooled):
    width = patch.shape[0]
    tokens = to_tokens(frames[...])
    normed[...], spread, pooled[...] = forward_part(
        tokens, frames.shape[2] // PATCH, bias, gain, lambda: [(0, width, patch[...])]
    )
    inv_spread[...] = jnp.broadcast_to(spread, inv_spread.shape)


def backward_kernel(
    owner,
    picks,
    place,
    hidden,
    gain,
    head_bias,
    head_out,
    normed,
    inv_spread,
    pooled,
    patch,
    head,
    send,
    across,
    along,
    *,
    height,
    per_frame,
):
    write_edges(place, hidden, across, along)
    backward_part(
        owner,
        picks,
        gain,
        head_bias,
        head_out,
        normed[...],
        inv_spread[...][:, :1],
        pooled[...],
        patch,
        head,
        place[0] // per_frame,
        send_plan(send.shape[0], height, hidden.shape[0]),
        group_sums(hidden[...]),
        send,
    )


def params(cells):
    return pltpu.CompilerParams(vmem_limit_bytes=min(16 + cells // 64, 48) * 1024 * 1024)


def near(array):
    return pltpu.with_memory_space_constraint(array, pltpu.VMEM)


def far(array):
    return pltpu.with_memory_space_constraint(array, pltpu.HBM)


def prepare_kernel(out_weight, wide, scratch):
    window = scratch.shape[0] // 9
    amount = scratch.shape[1] // LANES
    scratch[...] = jnp.zeros_like(scratch)
    for a in range(3):
        for e in range(3):
            base = (a * 3 + e) * window
            for b in range(3):
                piece = out_weight[a, b, e].astype(F32)
                for i in range(amount):
                    start = base + 3 * (i - b + 2)
                    scratch[start : start + 3, i * LANES : (i + 1) * LANES] = piece
    wide[...] = scratch[...].astype(BF16)


def norm_constants(totals, channels, cell_total):
    column = iota((1, 2 * channels), 1)
    wanted = div(mod(column, channels), channels // GROUPS) + jnp.where(column >= channels, GROUPS, 0)
    (spread,) = exact_rows([totals], lambda r: matmul(r, ones_where(iota((LANES, 1), 0) == wanted)))
    mean = spread[:, :channels] / cell_total
    inverse = lax.rsqrt(spread[:, channels:] / cell_total - mean * mean + eps_norm)
    return mean, inverse


def norm_slopes(state, mean, inverse, gain, shift):
    normed = (state - mean) * inverse
    return normed, silu_slope(normed * gain + shift) * gain


def slope_part(pixels, width, wide, hidden, slopes_own, mean, inverse, direct, edge_slopes, stats, sums):
    own_rows, frame_count, _, channels = hidden.shape
    window, cells = pixels.shape
    lane = iota((1, cells), 1)
    in_frame = mod(lane, width)
    shifted = []
    for a in range(3):
        for e in range(3):
            step = (2 - a) * width + 1 - e
            moved = pltpu.roll(pixels, (-step) % cells, 1) if step else pixels
            inside = (lane < cells - (2 - a) * width) & (in_frame >= e - 1) & (in_frame < width + e - 1)
            shifted.append(jnp.where(inside, moved, 0.0))
    stacked = jnp.concatenate(shifted, axis=0).astype(BF16)
    result = lax.dot_general(stacked, wide[...], (((0,), (0,)), ((), ())), preferred_element_type=F32)
    first = jnp.zeros((1, channels), F32)
    second = jnp.zeros((1, channels), F32)
    for i in range(own_rows):
        state = hidden[i].reshape(cells, channels).astype(F32)
        up = result[:, (i + 1) * channels : (i + 2) * channels] * slopes_own[i]
        direct[i] = up * inverse
        first = first + jnp.sum(up, axis=0, keepdims=True)
        second = second + jnp.sum(up * ((state - mean) * inverse), axis=0, keepdims=True)
    edge_slopes[0] = result[:, :channels]
    edge_slopes[1] = result[:, (own_rows + 1) * channels :]
    stats[0:1, :] = mean
    stats[1:2, :] = inverse
    both = jnp.where(iota((2, channels), 0) == 0, first, second)
    sums[...] = jnp.broadcast_to(both[None], sums.shape)


def own_slopes(hidden, mean, inverse, gain, shift, slopes_own):
    own_rows, frame_count, width, channels = hidden.shape
    for i in range(own_rows):
        state = hidden[i].reshape(frame_count * width, channels).astype(F32)
        slopes_own[i] = norm_slopes(state, mean, inverse, gain[...], shift[...])[1]


def gathered_kernel(place, arrived, hidden, gain, shift, wide, *refs):
    count = 8
    far, outs, near = refs[:count], refs[count : count + 4], refs[count + 4 : 2 * count + 4]
    slopes_own, sems = refs[-2:]
    owner, picks, bias, norm_gain, head_bias, head_out, patch, head = near
    steps = 3
    depth = patch.shape[0] // steps
    copies = {i: pltpu.make_async_copy(far[i], near[i], sems.at[i]) for i in range(count) if i != 6}
    patch_copies = [
        pltpu.make_async_copy(
            far[6].at[pl.ds(i * depth, depth)], patch.at[pl.ds(i * depth, depth)], sems.at[count + i]
        )
        for i in range(steps)
    ]
    for copy in patch_copies + list(copies.values()):
        copy.start()

    devices = arrived.shape[0]
    own_rows, frame_count, width, channels = hidden.shape
    cells = frame_count * width
    pixel_rows = own_rows * devices
    patches = pixel_rows // PATCH
    rows = packed_rows(pixel_rows)
    token_rows = devices * rows
    got = arrived[...].astype(F32)
    message_row = iota((1, got.shape[1], 1), 1)
    is_sum = mod(message_row, rows) == rows - 1
    is_sum = is_sum & (message_row < 3 * rows)
    totals = jnp.sum(jnp.where(is_sum, got, 0.0), axis=0)
    totals = jnp.sum(totals, axis=0, keepdims=True)
    mean, inverse = norm_constants(totals, channels, pixel_rows * cells * (channels // GROUPS))
    got = jnp.where(is_sum, 0.0, got)
    tokens = jnp.concatenate(
        [
            got[:, c * rows : (c + 1) * rows, :].reshape(token_rows, LANES)
            for c in range(got.shape[1] // rows)
        ],
        axis=1,
    ).astype(BF16)

    own_slopes(hidden, mean, inverse, gain, shift, slopes_own)

    copies[2].wait()
    embedded = bias[...]
    for i in range(steps):
        patch_copies[i].wait()
        embedded = embedded + matmul(
            tokens[:, i * depth : (i + 1) * depth], patch[i * depth : (i + 1) * depth, :]
        )
    for i in (0, 1, 3, 4, 5, 7):
        copies[i].wait()
    centred = embedded - jnp.mean(embedded, axis=1, keepdims=True)
    inv_spread = lax.rsqrt(jnp.mean(centred * centred, axis=1, keepdims=True) + eps_norm)
    normed = centred * inv_spread
    token = iota((1, token_rows), 1)
    members = ones_where((iota((devices, 1), 0) == div(token, rows)) & (mod(token, rows) < patches))
    pooled = spread_exactly(members, normed * norm_gain[...]) / patches
    before = exact_block(pooled, lambda block: matmul(block, head[...])) + head_bias[...]
    pulled = exact_block(head_out[...] * silu_slope(before), lambda block: matmul_t(block, head[...]))
    block = iota((devices, 1), 0)
    owners = jnp.zeros((devices, 1), jnp.int32)
    for b in range(devices):
        owners = jnp.where(block == b, owner[b], owners)
    picked = jnp.zeros((devices, 1), F32)
    for k in range(picks.shape[0]):
        picked = picked + jnp.where(owners == picks[k], 1.0, 0.0)
    scaled = norm_gain[...] * (picked * pulled)
    back = iota((token_rows, 1), 0)
    scaled = spread_exactly(ones_where(div(back, rows) == iota((1, devices), 1)), scaled)
    token_grad = inv_spread * (
        scaled
        - jnp.mean(scaled, axis=1, keepdims=True)
        - normed * jnp.mean(scaled * normed, axis=1, keepdims=True)
    )

    window = own_rows + 4
    slabs = []
    entry = iota((window * 3 * PATCH, 1), 0)
    wanted = jnp.full(entry.shape, -1, jnp.int32)
    for j in range(window):
        y = place[0] * own_rows - 2 + j
        inside = (y >= 0) & (y < pixel_rows)
        in_patch = y & (PATCH - 1)
        row = jnp.where(inside, y >> (PATCH.bit_length() - 1), -1)
        span = (entry >= j * 3 * PATCH) & (entry < (j + 1) * 3 * PATCH)
        wanted = jnp.where(span, row, wanted)
        for k in range(3):
            start = pl.multiple_of(k * PATCH * PATCH + in_patch * PATCH, PATCH)
            slabs.append(patch[pl.ds(start, PATCH), :])
    pixel_grad = matmul_t(jnp.concatenate(slabs, axis=0), token_grad.astype(BF16)).astype(BF16).astype(F32)
    pixel_grad = jnp.where(mod(token, rows) == wanted, pixel_grad, 0.0).astype(BF16)
    owners = jnp.zeros((token_rows, 1), jnp.int32)
    for b in range(devices):
        owners = jnp.where(div(back, rows) == b, owner[b], owners)
    lane = iota((1, cells), 1)
    home = matmul(pixel_grad, ones_where(owners == div(lane, PATCH)))
    home = jnp.where(mod(entry, PATCH) == mod(lane, PATCH), home, 0.0).astype(BF16)
    pixel_rows_out = wide.shape[0] // 9
    column = iota((1, entry.shape[0]), 1)
    pixels = matmul(ones_where(iota((pixel_rows_out, 1), 0) == div(column, PATCH)), home)
    slope_part(pixels, width, wide, hidden, slopes_own, mean, inverse, *outs)


def exchanged_kernel(owner, arrived, hidden, gain, shift, wide, direct, edge_slopes, stats, sums, slopes_own):
    devices, message_rows, _ = arrived.shape
    own_rows, frame_count, width, channels = hidden.shape
    cells = frame_count * width
    per_frame = devices // frame_count
    window = wide.shape[0] // 9
    total_rows = devices * message_rows
    got = arrived[...].reshape(total_rows, LANES)
    row = iota((total_rows, 1), 0)
    kind = mod(row, message_rows)
    totals = jnp.sum(jnp.where(kind == message_rows - 1, got, 0.0), axis=0, keepdims=True)
    mean, inverse = norm_constants(totals, channels, own_rows * devices * cells * (channels // GROUPS))
    own_slopes(hidden, mean, inverse, gain, shift, slopes_own)
    source = div(row, message_rows)
    block = div(source, per_frame)
    frame = jnp.zeros_like(block)
    for b in range(frame_count):
        frame = jnp.where(block == b, owner[b], frame)
    home = frame * per_frame + mod(source, per_frame)
    fold = ones_where(mod(iota((LANES, 1), 0), PATCH) == mod(iota((1, cells), 1), PATCH))
    home = home == div(iota((1, cells), 1), PATCH)
    lane_kind = mod(iota((1, total_rows), 1), message_rows)
    lane_kind = jnp.where(lane_kind == message_rows - 1, -4 * window, lane_kind)
    held = div(iota((1, LANES), 1), PATCH)
    place_row = iota((window, 1), 0)
    pixels = jnp.zeros((window, cells), F32)
    for j in range(own_rows + 4):
        placed = matmul(jnp.where(held == j, got, 0.0).astype(BF16), fold)
        kept = jnp.where(home, placed, 0.0).astype(BF16)
        pixels = pixels + matmul(ones_where(place_row == lane_kind + 3 * j), kept)
    slope_part(pixels, width, wide, hidden, slopes_own, mean, inverse, direct, edge_slopes, stats, sums)


def late_kernel(place, across, along, slopes, stats, gain, shift, inner_weight, direct, states, turned):
    cells, channels = slopes.shape[1:]
    odd = place[0] % 2 == 1
    mean = stats[0:1, :]
    inverse = stats[1:2, :]
    for i in range(2):
        state = jnp.where(odd == (i == 0), across[0], along[0])
        states[i] = state
        values = state.reshape(cells, channels).astype(F32)
        direct[i] = slopes[i] * norm_slopes(values, mean, inverse, gain[...], shift[...])[1] * inverse
    size = inner_weight.shape[3]
    for b in range(3):
        for a in range(3):
            for e in range(3):
                at = ((b * 3 + a) * 3 + e) * size
                turned[at : at + size, :] = inner_weight[a, b, e].T


def inner_kernel(
    place, arrived, stats, direct, hidden, edge_direct, edge_states, turned, out, padded, *, devices
):
    own_rows, frame_count, width, channels = out.shape
    cells = frame_count * width
    totals = jnp.sum(arrived[...], axis=0)
    same = ones_where(
        div(iota((channels, 1), 0), channels // GROUPS) == div(iota((1, channels), 1), channels // GROUPS)
    )
    cell_total = own_rows * devices * cells * (channels // GROUPS)
    first, second = exact_rows([totals[0:1], totals[1:2]], lambda rows: matmul(rows, same))
    mean = stats[0:1, :]
    inverse = stats[1:2, :]
    constant = first / cell_total * inverse
    factor = second / cell_total * inverse * inverse
    position = place[0]
    in_frame = mod(iota((cells, 1), 0), width)
    for i in range(own_rows + 2):
        if 0 < i < own_rows + 1:
            state, part = hidden[i - 1], direct[i - 1]
        else:
            state, part = edge_states[min(i, 1)], edge_direct[min(i, 1)]
        grad = part - constant - (state.reshape(cells, channels).astype(F32) - mean) * factor
        if i == 0:
            grad = jnp.where(position > 0, grad, 0.0)
        if i == own_rows + 1:
            grad = jnp.where(position < devices - 1, grad, 0.0)
        after = jnp.where(in_frame < width - 1, pltpu.roll(grad, cells - 1, 0), 0.0)
        prior = jnp.where(in_frame > 0, pltpu.roll(grad, 1, 0), 0.0)
        padded[i, :cells, 0:channels] = after.astype(BF16)
        padded[i, :cells, channels : 2 * channels] = grad.astype(BF16)
        padded[i, :cells, 2 * channels :] = prior.astype(BF16)
        padded[i, cells:, :] = jnp.zeros((2 * width, 3 * channels), BF16)
    depth = 3 * channels
    for r in range(own_rows):
        total = jnp.zeros((cells, channels), F32)
        for b in range(3):
            joined = jnp.concatenate(
                [padded[r - b + 2, (2 - a) * width : (2 - a) * width + cells, :] for a in range(3)], axis=1
            )
            total = total + matmul(joined, turned[b * 3 * depth : (b + 1) * 3 * depth, :])
        out[r] = total.reshape(frame_count, width, channels).astype(BF16)


def per_device(
    frames,
    frame_owner,
    picks,
    patch_weight,
    patch_bias,
    norm_gain,
    head_weight,
    head_bias,
    head_out,
    hidden_state,
    group_gain,
    group_shift,
    out_weight,
    inner_weight,
):
    devices = lax.axis_size("row")
    position = lax.axis_index("row").astype(jnp.int32).reshape(1)
    per_frame = devices // FRAMES
    height = frames.shape[1]
    own_rows, _, frame_width, channels = hidden_state.shape
    cells = FRAMES * frame_width
    width = patch_weight.shape[1]
    turned_frames = jnp.transpose(frames, (0, 2, 1))
    bias = patch_bias.reshape(1, width)
    gain = norm_gain.reshape(1, width)
    head_bias_row = head_bias.reshape(1, width)
    head_out_row = head_out.reshape(1, width)
    window, message_rows = layout(own_rows)
    window_rows = -(-3 * window // 8) * 8
    state_rows = own_rows + 2
    edge = jax.ShapeDtypeStruct((1,) + hidden_state.shape[1:], BF16)
    message = (jax.ShapeDtypeStruct((devices, message_rows, LANES), F32), edge, edge)
    gain_row = group_gain.reshape(1, channels)
    shift_row = group_shift.reshape(1, channels)
    wide = pl.pallas_call(
        prepare_kernel,
        out_shape=pltpu.VMEM((9 * window_rows, state_rows * channels), BF16),
        scratch_shapes=[pltpu.VMEM((9 * window_rows, state_rows * channels), F32)],
        compiler_params=params(cells),
        name="prepare",
    )(out_weight)
    slope_outs = (
        pltpu.VMEM((own_rows, cells, channels), F32),
        pltpu.VMEM((2, cells, channels), F32),
        pltpu.VMEM((8, channels), F32),
        jax.ShapeDtypeStruct((devices, 2, channels), F32),
    )
    slopes_own = pltpu.VMEM((own_rows, cells, channels), F32)
    if per_frame == 1:
        runs = patch_weight.shape[0] // LANES
        message_rows = packed_rows(height) * runs
        send, across, along = pl.pallas_call(
            pack_kernel,
            out_shape=(jax.ShapeDtypeStruct((devices, message_rows, LANES), BF16), edge, edge),
            in_specs=[SMEM] + [FAR] * 2,
            scratch_shapes=[
                pltpu.VMEM(turned_frames.shape, BF16),
                pltpu.VMEM(hidden_state.shape, BF16),
                pltpu.SemaphoreType.DMA((2,)),
            ],
            compiler_params=params(0),
            name="pack",
        )(position, far(turned_frames), far(hidden_state))
        arrived = lax.all_to_all(send, "row", 0, 0, tiled=True)
        arrays = [
            frame_owner,
            picks,
            bias,
            gain,
            head_bias_row,
            head_out_row,
            patch_weight,
            head_weight,
        ]
        direct, edge_slopes, stats, sums = pl.pallas_call(
            gathered_kernel,
            out_shape=slope_outs,
            in_specs=[SMEM] + [VMEM] * 5 + [FAR] * len(arrays),
            scratch_shapes=[
                (pltpu.SMEM if x.dtype == jnp.int32 else pltpu.VMEM)(x.shape, x.dtype) for x in arrays
            ]
            + [slopes_own, pltpu.SemaphoreType.DMA((len(arrays) + 3,))],
            compiler_params=params(0),
            name="gathered",
        )(
            position,
            near(arrived),
            near(hidden_state),
            gain_row,
            shift_row,
            near(wide),
            *[far(x) for x in arrays],
        )
    else:
        count = height // PATCH
        normed, inv_spread, partial = pl.pallas_call(
            forward_kernel,
            out_shape=(
                jax.ShapeDtypeStruct((token_rows_of(height), width), F32),
                jax.ShapeDtypeStruct((token_rows_of(height), LANES), F32),
                jax.ShapeDtypeStruct((1, width), F32),
            ),
            compiler_params=params(cells),
            name="reward_forward",
        )(turned_frames, bias, gain, patch_weight)
        members = [[b * per_frame + i for i in range(per_frame)] for b in range(FRAMES)]
        pooled = lax.psum(partial, "row", axis_index_groups=members) / (count * per_frame)
        send, across, along = pl.pallas_call(
            functools.partial(backward_kernel, height=height, per_frame=per_frame),
            out_shape=message,
            in_specs=[SMEM] * 3 + [VMEM] * 9,
            out_specs=[VMEM] * 3,
            compiler_params=params(cells),
            name="reward_backward",
        )(
            frame_owner,
            picks,
            position,
            hidden_state,
            gain,
            head_bias_row,
            head_out_row,
            normed,
            inv_spread,
            pooled,
            patch_weight,
            head_weight,
        )
        arrived = lax.all_to_all(send, "row", 0, 0, tiled=True)
        direct, edge_slopes, stats, sums = pl.pallas_call(
            exchanged_kernel,
            out_shape=slope_outs,
            in_specs=[SMEM] + [VMEM] * 5,
            scratch_shapes=[slopes_own],
            compiler_params=params(cells),
            name="exchanged",
        )(frame_owner, near(arrived), near(hidden_state), gain_row, shift_row, near(wide))
    swaps = [(2 * i, 2 * i + 1) for i in range(devices // 2)]
    across = lax.ppermute(across, "row", swaps + [(b, a) for a, b in swaps])
    swaps = [(2 * i - 1, 2 * i) for i in range(1, devices // 2)]
    along = lax.ppermute(along, "row", swaps + [(b, a) for a, b in swaps])
    summed = lax.all_to_all(sums, "row", 0, 0, tiled=True)
    edge_direct, edge_states, turned = pl.pallas_call(
        late_kernel,
        out_shape=(
            pltpu.VMEM((2, cells, channels), F32),
            pltpu.VMEM((2,) + hidden_state.shape[1:], BF16),
            pltpu.VMEM((27 * channels, channels), BF16),
        ),
        in_specs=[SMEM] + [VMEM] * 7,
        input_output_aliases={3: 0},
        compiler_params=params(cells),
        name="late",
    )(position, near(across), near(along), near(edge_slopes), near(stats), gain_row, shift_row, inner_weight)
    return pl.pallas_call(
        functools.partial(inner_kernel, devices=devices),
        out_shape=jax.ShapeDtypeStruct(hidden_state.shape, BF16),
        in_specs=[SMEM] + [VMEM] * 7,
        scratch_shapes=[pltpu.VMEM((own_rows + 2, cells + 2 * frame_width, 3 * channels), BF16)],
        compiler_params=params(cells),
        name="inner",
    )(
        position,
        near(summed),
        near(stats),
        near(direct),
        near(hidden_state),
        near(edge_direct),
        near(edge_states),
        near(turned),
    )


def solution(mesh):
    return jax.shard_map(
        per_device,
        mesh=mesh,
        in_specs=(
            P(None, None, ("clip", "row")),
            P("clip"),
            P("clip"),
            P(),
            P(),
            P(),
            P(),
            P(),
            P(),
            P(("clip", "row"), None, None, None),
            P(),
            P(),
            P(),
            P(),
        ),
        out_specs=P(("clip", "row"), None, None, None),
        check_vma=False,
    )
```

```python
import functools

import jax
import jax.numpy as jnp
from jax import lax
from jax.experimental import pallas as pl
from jax.experimental.pallas import tpu as pltpu
from jax.sharding import PartitionSpec as P

PATCH = 16
GROUPS = 32
FRAMES = 16
LANES = 128
SLOTS = LANES // PATCH
eps_norm = 1e-06
BF16 = jnp.bfloat16
F32 = jnp.float32

SMEM = pl.BlockSpec(memory_space=pltpu.SMEM)
VMEM = pl.BlockSpec(memory_space=pltpu.VMEM)
FAR = pl.BlockSpec(memory_space=pl.ANY)


def iota(shape, dim):
    return lax.broadcasted_iota(jnp.int32, shape, dim)


def div(values, count):
    if count & (count - 1):
        return values // count
    return values >> (count.bit_length() - 1)


def mod(values, count):
    if count & (count - 1):
        return values % count
    return values & (count - 1)


def ones_where(condition):
    return jnp.where(condition, 1.0, 0.0).astype(BF16)


def matmul(left, right):
    return jnp.dot(left, right, preferred_element_type=F32)


def matmul_t(left, right):
    return lax.dot_general(left, right, (((1,), (1,)), ((), ())), preferred_element_type=F32)


def cut_in_three(values):
    high = values.astype(BF16)
    rest = values - high.astype(F32)
    middle = rest.astype(BF16)
    low = (rest - middle.astype(F32)).astype(BF16)
    return high, middle, low


def spread_exactly(ones, values):
    high, middle, low = cut_in_three(values)
    return matmul(ones, high) + matmul(ones, middle) + matmul(ones, low)


def exact_rows(rows, product):
    place = iota((16, rows[0].shape[1]), 0)
    stacked = jnp.zeros(place.shape, F32)
    for index, row in enumerate(rows):
        for step, piece in enumerate(cut_in_three(row)):
            stacked = jnp.where(place == 3 * index + step, piece.astype(F32), stacked)
    result = product(stacked.astype(BF16))
    return [
        result[3 * i : 3 * i + 1] + result[3 * i + 1 : 3 * i + 2] + result[3 * i + 2 : 3 * i + 3]
        for i in range(len(rows))
    ]


def exact_block(values, product):
    count = values.shape[0]
    result = product(jnp.concatenate(cut_in_three(values), axis=0))
    return result[:count] + result[count : 2 * count] + result[2 * count :]


def silu_slope(values):
    sigmoid = jax.nn.sigmoid(values)
    return sigmoid * (1.0 + values * (1.0 - sigmoid))


def token_rows_of(height):
    return -(-(height // PATCH) // 16) * 16


def to_tokens(pixels):
    channels, columns, height = pixels.shape
    rows = channels * columns
    token_rows = token_rows_of(height)
    flat = pixels.reshape(rows, height)
    width = channels * PATCH * columns
    lane = iota((1, width), 1)
    place = iota((rows, 1), 0)
    mine = place == div(lane, PATCH * columns) * columns + mod(lane, columns)
    in_patch = mod(div(lane, columns), PATCH)
    pixel_row = iota((height, 1), 0)
    token = iota((token_rows, rows), 0)
    tokens = jnp.zeros((token_rows, width), F32)
    for t in range(height // PATCH):
        tiled = matmul(flat, ones_where(pixel_row == in_patch + t * PATCH))
        kept = jnp.where(mine, tiled, 0.0).astype(BF16)
        tokens = tokens + matmul(ones_where(token == t), kept)
    return tokens.astype(BF16)


def forward_part(tokens, count, bias, gain, load_patch):
    embedded = bias[...]
    for low, high, weight in load_patch():
        embedded = embedded + matmul(tokens[:, low:high], weight)
    centred = embedded - jnp.mean(embedded, axis=1, keepdims=True)
    inv_spread = lax.rsqrt(jnp.mean(centred * centred, axis=1, keepdims=True) + eps_norm)
    normed = centred * inv_spread
    weighted = normed * gain[...]
    inside = iota((tokens.shape[0], 1), 0) < count
    pooled = jnp.sum(jnp.where(inside, weighted, 0.0), axis=0, keepdims=True)
    return normed, inv_spread, pooled


def layout(own_rows):
    return own_rows + 4, 8


def send_plan(targets, height, own_rows):
    window, message_rows = layout(own_rows)
    rows = targets * message_rows
    message = iota((rows, 1), 0)
    colour = mod(message, message_rows)
    colour = jnp.where(colour < 3, colour, -8)
    first = div(message, message_rows) * own_rows - 2
    source = iota((1, 3 * height), 1)
    spacing = 4 * height
    source = div(source, height) * spacing + mod(source, height) + height
    wanted = colour * spacing + height + first
    return [ones_where(source == wanted + j) for j in range(window)]


def channel_sums(hidden):
    values = hidden.reshape(-1, hidden.shape[-1]).astype(F32)
    return jnp.sum(values, axis=0, keepdims=True), jnp.sum(values * values, axis=0, keepdims=True)


def same_group(channels):
    size = channels // GROUPS
    return ones_where(div(iota((channels, 1), 0), size) == div(iota((1, channels), 1), size))


def backward_part(
    owner, picks, gain, head_bias, head_out, normed, inv_spread, pooled, weight, head, slot, plans, sums, send
):
    width = weight.shape[0]
    message_rows = send.shape[1]
    height = plans[0].shape[1] // 3
    (before,) = exact_rows([pooled], lambda rows: matmul(rows, head[...]))
    slope = head_out[...] * silu_slope(before + head_bias[...])
    (pulled,) = exact_rows([slope], lambda rows: matmul_t(rows, head[...]))
    wanted = owner[slot]
    picked = jnp.int32(0)
    for k in range(picks.shape[0]):
        picked = picked + jnp.where(picks[k] == wanted, 1, 0)
    scaled = gain[...] * (picked.astype(F32) * pulled)
    token_grad = inv_spread * (
        scaled
        - jnp.mean(scaled, axis=1, keepdims=True)
        - normed * jnp.mean(scaled * normed, axis=1, keepdims=True)
    )
    patch_grad = matmul_t(token_grad.astype(BF16), weight[...]).astype(BF16)
    rows = 3 * height
    place = iota((rows, 1), 0)
    pixel_row = mod(place, height)
    colour = div(place, height)
    copied = matmul(ones_where(div(pixel_row, PATCH) == iota((1, normed.shape[0]), 1)), patch_grad)
    kept = jnp.where(
        colour * PATCH + mod(pixel_row, PATCH) == div(iota((1, width), 1), PATCH), copied, 0.0
    ).astype(BF16)
    fold = ones_where(mod(iota((width, 1), 0), PATCH) == mod(iota((1, LANES), 1), PATCH))
    pixels = matmul(kept, fold).astype(BF16)
    messages = plans[0].shape[0]
    lane = div(iota((1, LANES), 1), PATCH)
    kind = mod(iota((messages, 1), 0), message_rows)
    result = jnp.where(kind == 3, sums[0], jnp.where(kind == 4, sums[1], 0.0))
    for j, plan in enumerate(plans):
        result = result + jnp.where(lane == j, matmul(plan, pixels), 0.0)
    send[...] = result.reshape(send.shape)


def write_edges(place, hidden, across, along):
    last = hidden.shape[0] - 1
    even = place[0] % 2 == 0
    across[0] = hidden[jnp.where(even, last, 0)]
    along[0] = hidden[jnp.where(even, 0, last)]


def packed_rows(height):
    return -(-(height // PATCH + 1) // 4) * 4


def pack_kernel(place, far_frames, far_hidden, message, across, along, frames, hidden, sems):
    copies = [
        pltpu.make_async_copy(far_frames, frames, sems.at[0]),
        pltpu.make_async_copy(far_hidden, hidden, sems.at[1]),
    ]
    for copy in copies:
        copy.start()
    copies[0].wait()
    height = frames.shape[2]
    tokens = to_tokens(frames[...]).astype(F32)
    rows = packed_rows(height)
    runs = message.shape[1] // rows
    whole = jnp.concatenate([tokens[:rows, c * LANES : (c + 1) * LANES] for c in range(runs)], axis=0)
    copies[1].wait()
    write_edges(place, hidden, across, along)
    row = iota((message.shape[1], 1), 0)
    first, second = channel_sums(hidden[...])
    for step, piece in enumerate(cut_in_three(first) + cut_in_three(second)):
        whole = jnp.where(row == (step + 1) * rows - 1, piece.astype(F32), whole)
    message[...] = jnp.broadcast_to(whole.astype(BF16)[None], message.shape)


def forward_kernel(frames, bias, gain, patch, normed, inv_spread, pooled):
    width = patch.shape[0]
    tokens = to_tokens(frames[...])
    normed[...], spread, pooled[...] = forward_part(
        tokens, frames.shape[2] // PATCH, bias, gain, lambda: [(0, width, patch[...])]
    )
    inv_spread[...] = jnp.broadcast_to(spread, inv_spread.shape)


def backward_kernel(
    owner,
    picks,
    place,
    hidden,
    gain,
    head_bias,
    head_out,
    normed,
    inv_spread,
    pooled,
    patch,
    head,
    send,
    across,
    along,
    *,
    height,
    per_frame,
):
    write_edges(place, hidden, across, along)
    backward_part(
        owner,
        picks,
        gain,
        head_bias,
        head_out,
        normed[...],
        inv_spread[...][:, :1],
        pooled[...],
        patch,
        head,
        place[0] // per_frame,
        send_plan(send.shape[0], height, hidden.shape[0]),
        channel_sums(hidden[...]),
        send,
    )


def params(cells):
    return pltpu.CompilerParams(vmem_limit_bytes=min(16 + cells // 64, 48) * 1024 * 1024)


def near(array):
    return pltpu.with_memory_space_constraint(array, pltpu.VMEM)


def far(array):
    return pltpu.with_memory_space_constraint(array, pltpu.HBM)


def prepare_kernel(far_weight, *refs):
    count = (len(refs) - 4) // 2
    fars, wide, nears = refs[:count], refs[count], refs[count + 1 : 2 * count + 1]
    out_weight, scratch, sems = refs[2 * count + 1 :]
    copies = [pltpu.make_async_copy(far_weight, out_weight, sems.at[count])]
    copies += [pltpu.make_async_copy(fars[i], nears[i], sems.at[i]) for i in range(count)]
    for copy in copies:
        copy.start()
    window = scratch.shape[0] // 9
    amount = scratch.shape[1] // LANES
    scratch[...] = jnp.zeros_like(scratch)
    copies[0].wait()
    for a in range(3):
        for e in range(3):
            base = (a * 3 + e) * window
            for b in range(3):
                piece = out_weight[a, b, e].astype(F32)
                for i in range(amount):
                    start = base + 3 * (i - b + 2)
                    scratch[start : start + 3, i * LANES : (i + 1) * LANES] = piece
    wide[...] = scratch[...].astype(BF16)
    for copy in copies[1:]:
        copy.wait()


def norm_constants(first, second, cell_total):
    same = same_group(first.shape[1])
    first, second = exact_rows([first, second], lambda rows: matmul(rows, same))
    mean = first / cell_total
    return mean, lax.rsqrt(second / cell_total - mean * mean + eps_norm)


def norm_slopes(state, mean, inverse, gain, shift):
    normed = (state - mean) * inverse
    return normed, silu_slope(normed * gain + shift) * gain


def slope_part(pixels, width, wide, hidden, slopes_own, mean, inverse, direct, edge_slopes, stats, sums):
    own_rows, frame_count, _, channels = hidden.shape
    window, cells = pixels.shape
    lane = iota((1, cells), 1)
    in_frame = mod(lane, width)
    shifted = []
    for a in range(3):
        for e in range(3):
            step = (2 - a) * width + 1 - e
            moved = pltpu.roll(pixels, (-step) % cells, 1) if step else pixels
            inside = (lane < cells - (2 - a) * width) & (in_frame >= e - 1) & (in_frame < width + e - 1)
            shifted.append(jnp.where(inside, moved, 0.0))
    stacked = jnp.concatenate(shifted, axis=0).astype(BF16)
    result = lax.dot_general(stacked, wide[...], (((0,), (0,)), ((), ())), preferred_element_type=F32)
    first = jnp.zeros((1, channels), F32)
    second = jnp.zeros((1, channels), F32)
    for i in range(own_rows):
        state = hidden[i].reshape(cells, channels).astype(F32)
        up = result[:, (i + 1) * channels : (i + 2) * channels] * slopes_own[i]
        direct[i] = up * inverse
        first = first + jnp.sum(up, axis=0, keepdims=True)
        second = second + jnp.sum(up * ((state - mean) * inverse), axis=0, keepdims=True)
    edge_slopes[0] = result[:, :channels]
    edge_slopes[1] = result[:, (own_rows + 1) * channels :]
    stats[0:1, :] = mean
    stats[1:2, :] = inverse
    both = jnp.where(iota((2, channels), 0) == 0, first, second)
    sums[...] = jnp.broadcast_to(both[None], sums.shape)


def own_slopes(hidden, mean, inverse, gain, shift, slopes_own):
    own_rows, frame_count, width, channels = hidden.shape
    for i in range(own_rows):
        state = hidden[i].reshape(frame_count * width, channels).astype(F32)
        slopes_own[i] = norm_slopes(state, mean, inverse, gain[...], shift[...])[1]


def gathered_kernel(
    place, arrived, hidden, gain, shift, bias, norm_gain, head_bias, head_out, wide, *refs
):
    count = 4
    far, outs, near = refs[:count], refs[count : count + 4], refs[count + 4 : 2 * count + 4]
    slopes_own, received, sems = refs[-3:]
    owner, picks, patch, head = near
    steps = 3
    depth = patch.shape[0] // steps
    patch_copies = [
        pltpu.make_async_copy(
            far[2].at[pl.ds(i * depth, depth)], patch.at[pl.ds(i * depth, depth)], sems.at[count + i]
        )
        for i in range(steps)
    ]
    copies = [pltpu.make_async_copy(far[i], near[i], sems.at[i]) for i in (0, 1, 3)]
    for copy in patch_copies + copies:
        copy.start()

    devices = arrived.shape[0]
    own_rows, frame_count, width, channels = hidden.shape
    cells = frame_count * width
    pixel_rows = own_rows * devices
    patches = pixel_rows // PATCH
    message_rows = arrived.shape[1]
    rows = packed_rows(pixel_rows)
    runs = message_rows // rows
    token_rows = patches * devices
    received[...] = arrived[...].astype(F32).reshape(received.shape)

    def from_all(row):
        return received[pl.ds(row, devices, stride=message_rows), :]

    partial = [jnp.sum(from_all((c + 1) * rows - 1), axis=0, keepdims=True) for c in range(6)]
    mean, inverse = norm_constants(
        partial[0] + partial[1] + partial[2],
        partial[3] + partial[4] + partial[5],
        pixel_rows * cells * (channels // GROUPS),
    )
    tokens = jnp.concatenate(
        [
            jnp.concatenate([from_all(c * rows + t) for c in range(runs)], axis=1)
            for t in range(patches)
        ],
        axis=0,
    ).astype(BF16)

    own_slopes(hidden, mean, inverse, gain, shift, slopes_own)

    embedded = bias[...]
    for i in range(steps):
        patch_copies[i].wait()
        embedded = embedded + matmul(
            tokens[:, i * depth : (i + 1) * depth], patch[i * depth : (i + 1) * depth, :]
        )
    for copy in copies:
        copy.wait()
    centred = embedded - jnp.mean(embedded, axis=1, keepdims=True)
    inv_spread = lax.rsqrt(jnp.mean(centred * centred, axis=1, keepdims=True) + eps_norm)
    normed = centred * inv_spread
    weighted = normed * norm_gain[...]
    pooled = weighted[:devices]
    for t in range(1, patches):
        pooled = pooled + weighted[t * devices : (t + 1) * devices]
    pooled = pooled / patches
    before = exact_block(pooled, lambda block: matmul(block, head[...])) + head_bias[...]
    pulled = exact_block(head_out[...] * silu_slope(before), lambda block: matmul_t(block, head[...]))
    block = iota((devices, 1), 0)
    owners = jnp.zeros((devices, 1), jnp.int32)
    for b in range(devices):
        owners = jnp.where(block == b, owner[b], owners)
    picked = jnp.zeros((devices, 1), F32)
    for k in range(picks.shape[0]):
        picked = picked + jnp.where(owners == picks[k], 1.0, 0.0)
    scaled = norm_gain[...] * (picked * pulled)
    scaled = scaled - jnp.mean(scaled, axis=1, keepdims=True), scaled
    centred_scale, scaled = [jnp.concatenate([x] * patches, axis=0) for x in scaled]
    token_grad = inv_spread * (centred_scale - normed * jnp.mean(scaled * normed, axis=1, keepdims=True))

    window = own_rows + 4
    slabs = []
    entry = iota((window * 3 * PATCH, 1), 0)
    wanted = jnp.full(entry.shape, -1, jnp.int32)
    for j in range(window):
        y = place[0] * own_rows - 2 + j
        inside = (y >= 0) & (y < pixel_rows)
        in_patch = y & (PATCH - 1)
        row = jnp.where(inside, y >> (PATCH.bit_length() - 1), -1)
        span = (entry >= j * 3 * PATCH) & (entry < (j + 1) * 3 * PATCH)
        wanted = jnp.where(span, row, wanted)
        for k in range(3):
            start = pl.multiple_of(k * PATCH * PATCH + in_patch * PATCH, PATCH)
            slabs.append(patch[pl.ds(start, PATCH), :])
    pixel_grad = matmul_t(jnp.concatenate(slabs, axis=0), token_grad.astype(BF16)).astype(BF16).astype(F32)
    token = iota((1, token_rows), 1)
    pixel_grad = jnp.where(div(token, devices) == wanted, pixel_grad, 0.0).astype(BF16)
    owners = jnp.concatenate([owners] * patches, axis=0)
    lane = iota((1, cells), 1)
    home = matmul(pixel_grad, ones_where(owners == div(lane, PATCH)))
    home = jnp.where(mod(entry, PATCH) == mod(lane, PATCH), home, 0.0).astype(BF16)
    pixel_rows_out = wide.shape[0] // 9
    column = iota((1, entry.shape[0]), 1)
    pixels = matmul(ones_where(iota((pixel_rows_out, 1), 0) == div(column, PATCH)), home)
    slope_part(pixels, width, wide, hidden, slopes_own, mean, inverse, *outs)


def exchanged_kernel(owner, arrived, hidden, gain, shift, wide, direct, edge_slopes, stats, sums, slopes_own):
    devices, message_rows, _ = arrived.shape
    own_rows, frame_count, width, channels = hidden.shape
    cells = frame_count * width
    per_frame = devices // frame_count
    window = wide.shape[0] // 9
    total_rows = devices * message_rows
    got = arrived[...].reshape(total_rows, LANES)
    row = iota((total_rows, 1), 0)
    kind = mod(row, message_rows)
    first = jnp.sum(jnp.where(kind == 3, got, 0.0), axis=0, keepdims=True)
    second = jnp.sum(jnp.where(kind == 4, got, 0.0), axis=0, keepdims=True)
    mean, inverse = norm_constants(first, second, own_rows * devices * cells * (channels // GROUPS))
    own_slopes(hidden, mean, inverse, gain, shift, slopes_own)
    source = div(row, message_rows)
    block = div(source, per_frame)
    frame = jnp.zeros_like(block)
    for b in range(frame_count):
        frame = jnp.where(block == b, owner[b], frame)
    home = frame * per_frame + mod(source, per_frame)
    fold = ones_where(mod(iota((LANES, 1), 0), PATCH) == mod(iota((1, cells), 1), PATCH))
    home = home == div(iota((1, cells), 1), PATCH)
    lane_kind = mod(iota((1, total_rows), 1), message_rows)
    lane_kind = jnp.where(lane_kind < 3, lane_kind, -4 * window)
    held = div(iota((1, LANES), 1), PATCH)
    place_row = iota((window, 1), 0)
    pixels = jnp.zeros((window, cells), F32)
    for j in range(own_rows + 4):
        placed = matmul(jnp.where(held == j, got, 0.0).astype(BF16), fold)
        kept = jnp.where(home, placed, 0.0).astype(BF16)
        pixels = pixels + matmul(ones_where(place_row == lane_kind + 3 * j), kept)
    slope_part(pixels, width, wide, hidden, slopes_own, mean, inverse, direct, edge_slopes, stats, sums)


def late_kernel(place, across, along, slopes, stats, gain, shift, inner_weight, direct, states, turned):
    cells, channels = slopes.shape[1:]
    odd = place[0] % 2 == 1
    mean = stats[0:1, :]
    inverse = stats[1:2, :]
    for i in range(2):
        state = jnp.where(odd == (i == 0), across[0], along[0])
        states[i] = state
        values = state.reshape(cells, channels).astype(F32)
        direct[i] = slopes[i] * norm_slopes(values, mean, inverse, gain[...], shift[...])[1] * inverse
    size = inner_weight.shape[3]
    for b in range(3):
        for a in range(3):
            for e in range(3):
                at = (a * 3 + e) * size
                turned[at : at + size, b * size : (b + 1) * size] = inner_weight[a, b, e].T


def inner_kernel(
    place, arrived, stats, direct, hidden, edge_direct, edge_states, turned, out, padded, *, devices
):
    own_rows, frame_count, width, channels = out.shape
    cells = frame_count * width
    totals = jnp.sum(arrived[...], axis=0)
    same = same_group(channels)
    cell_total = own_rows * devices * cells * (channels // GROUPS)
    first, second = exact_rows([totals[0:1], totals[1:2]], lambda rows: matmul(rows, same))
    mean = stats[0:1, :]
    inverse = stats[1:2, :]
    constant = first / cell_total * inverse
    factor = second / cell_total * inverse * inverse
    position = place[0]
    in_frame = mod(iota((cells, 1), 0), width)
    for i in range(own_rows + 2):
        if 0 < i < own_rows + 1:
            state, part = hidden[i - 1], direct[i - 1]
        else:
            state, part = edge_states[min(i, 1)], edge_direct[min(i, 1)]
        grad = part - constant - (state.reshape(cells, channels).astype(F32) - mean) * factor
        if i == 0:
            grad = jnp.where(position > 0, grad, 0.0)
        if i == own_rows + 1:
            grad = jnp.where(position < devices - 1, grad, 0.0)
        after = jnp.where(in_frame < width - 1, pltpu.roll(grad, cells - 1, 0), 0.0)
        prior = jnp.where(in_frame > 0, pltpu.roll(grad, 1, 0), 0.0)
        padded[i, :cells, 0:channels] = after.astype(BF16)
        padded[i, :cells, channels : 2 * channels] = grad.astype(BF16)
        padded[i, :cells, 2 * channels :] = prior.astype(BF16)
        padded[i, cells:, :] = jnp.zeros((2 * width, 3 * channels), BF16)
    results = [jnp.zeros((cells, channels), F32) for _ in range(own_rows)]
    for i in range(own_rows + 2):
        joined = jnp.concatenate(
            [padded[i, (2 - a) * width : (2 - a) * width + cells, :] for a in range(3)], axis=1
        )
        taps = [b for b in range(3) if 0 <= i + b - 2 < own_rows]
        for low in range(0, len(taps), 2):
            some = taps[low : low + 2]
            product = matmul(joined, turned[:, some[0] * channels : (some[-1] + 1) * channels])
            for step, b in enumerate(some):
                results[i + b - 2] = results[i + b - 2] + product[:, step * channels : (step + 1) * channels]
    for r in range(own_rows):
        out[r] = results[r].reshape(frame_count, width, channels).astype(BF16)


def per_device(
    frames,
    frame_owner,
    picks,
    patch_weight,
    patch_bias,
    norm_gain,
    head_weight,
    head_bias,
    head_out,
    hidden_state,
    group_gain,
    group_shift,
    out_weight,
    inner_weight,
):
    devices = lax.axis_size("row")
    position = lax.axis_index("row").astype(jnp.int32).reshape(1)
    per_frame = devices // FRAMES
    height = frames.shape[1]
    own_rows, _, frame_width, channels = hidden_state.shape
    cells = FRAMES * frame_width
    width = patch_weight.shape[1]
    turned_frames = jnp.transpose(frames, (0, 2, 1))
    bias = patch_bias.reshape(1, width)
    gain = norm_gain.reshape(1, width)
    head_bias_row = head_bias.reshape(1, width)
    head_out_row = head_out.reshape(1, width)
    window, message_rows = layout(own_rows)
    window_rows = -(-3 * window // 8) * 8
    state_rows = own_rows + 2
    edge = jax.ShapeDtypeStruct((1,) + hidden_state.shape[1:], BF16)
    message = (jax.ShapeDtypeStruct((devices, message_rows, LANES), F32), edge, edge)
    gain_row = group_gain.reshape(1, channels)
    shift_row = group_shift.reshape(1, channels)
    early = [hidden_state, gain_row, shift_row, bias, gain, head_bias_row, head_out_row]
    wide, *early = pl.pallas_call(
        prepare_kernel,
        out_shape=(
            pltpu.VMEM((9 * window_rows, state_rows * channels), BF16),
            *[pltpu.VMEM(x.shape, x.dtype) for x in early],
        ),
        in_specs=[FAR] * (1 + len(early)),
        scratch_shapes=[
            pltpu.VMEM(out_weight.shape, BF16),
            pltpu.VMEM((9 * window_rows, state_rows * channels), F32),
            pltpu.SemaphoreType.DMA((1 + len(early),)),
        ],
        compiler_params=params(cells),
        name="prepare",
    )(far(out_weight), *[far(x) for x in early])
    early = [near(x) for x in early]
    slope_outs = (
        pltpu.VMEM((own_rows, cells, channels), F32),
        pltpu.VMEM((2, cells, channels), F32),
        pltpu.VMEM((8, channels), F32),
        jax.ShapeDtypeStruct((devices, 2, channels), F32),
    )
    slopes_own = pltpu.VMEM((own_rows, cells, channels), F32)
    if per_frame == 1:
        runs = patch_weight.shape[0] // LANES
        message_rows = packed_rows(height) * runs
        send, across, along = pl.pallas_call(
            pack_kernel,
            out_shape=(jax.ShapeDtypeStruct((devices, message_rows, LANES), BF16), edge, edge),
            in_specs=[SMEM] + [FAR] * 2,
            scratch_shapes=[
                pltpu.VMEM(turned_frames.shape, BF16),
                pltpu.VMEM(hidden_state.shape, BF16),
                pltpu.SemaphoreType.DMA((2,)),
            ],
            compiler_params=params(0),
            name="pack",
        )(position, far(turned_frames), far(hidden_state))
        arrived = lax.all_to_all(send, "row", 0, 0, tiled=True)
        arrays = [frame_owner, picks, patch_weight, head_weight]
        direct, edge_slopes, stats, sums = pl.pallas_call(
            gathered_kernel,
            out_shape=slope_outs,
            in_specs=[SMEM] + [VMEM] * 9 + [FAR] * len(arrays),
            scratch_shapes=[
                (pltpu.SMEM if x.dtype == jnp.int32 else pltpu.VMEM)(x.shape, x.dtype) for x in arrays
            ]
            + [
                slopes_own,
                pltpu.VMEM((devices * message_rows, LANES), F32),
                pltpu.SemaphoreType.DMA((len(arrays) + 3,)),
            ],
            compiler_params=params(0),
            name="gathered",
        )(
            position,
            near(arrived),
            *early,
            near(wide),
            *[far(x) for x in arrays],
        )
    else:
        count = height // PATCH
        normed, inv_spread, partial = pl.pallas_call(
            forward_kernel,
            out_shape=(
                jax.ShapeDtypeStruct((token_rows_of(height), width), F32),
                jax.ShapeDtypeStruct((token_rows_of(height), LANES), F32),
                jax.ShapeDtypeStruct((1, width), F32),
            ),
            compiler_params=params(cells),
            name="reward_forward",
        )(turned_frames, bias, gain, patch_weight)
        members = [[b * per_frame + i for i in range(per_frame)] for b in range(FRAMES)]
        pooled = lax.psum(partial, "row", axis_index_groups=members) / (count * per_frame)
        send, across, along = pl.pallas_call(
            functools.partial(backward_kernel, height=height, per_frame=per_frame),
            out_shape=message,
            in_specs=[SMEM] * 3 + [VMEM] * 9,
            out_specs=[VMEM] * 3,
            compiler_params=params(cells),
            name="reward_backward",
        )(
            frame_owner,
            picks,
            position,
            hidden_state,
            gain,
            head_bias_row,
            head_out_row,
            normed,
            inv_spread,
            pooled,
            patch_weight,
            head_weight,
        )
        arrived = lax.all_to_all(send, "row", 0, 0, tiled=True)
        direct, edge_slopes, stats, sums = pl.pallas_call(
            exchanged_kernel,
            out_shape=slope_outs,
            in_specs=[SMEM] + [VMEM] * 5,
            scratch_shapes=[slopes_own],
            compiler_params=params(cells),
            name="exchanged",
        )(frame_owner, near(arrived), *early[:3], near(wide))
    swaps = [(2 * i, 2 * i + 1) for i in range(devices // 2)]
    across = lax.ppermute(across, "row", swaps + [(b, a) for a, b in swaps])
    swaps = [(2 * i - 1, 2 * i) for i in range(1, devices // 2)]
    along = lax.ppermute(along, "row", swaps + [(b, a) for a, b in swaps])
    summed = lax.all_to_all(sums, "row", 0, 0, tiled=True)
    edge_direct, edge_states, turned = pl.pallas_call(
        late_kernel,
        out_shape=(
            pltpu.VMEM((2, cells, channels), F32),
            pltpu.VMEM((2,) + hidden_state.shape[1:], BF16),
            pltpu.VMEM((9 * channels, 3 * channels), BF16),
        ),
        in_specs=[SMEM] + [VMEM] * 7,
        input_output_aliases={3: 0},
        compiler_params=params(cells),
        name="late",
    )(position, near(across), near(along), near(edge_slopes), near(stats), *early[1:3], inner_weight)
    return pl.pallas_call(
        functools.partial(inner_kernel, devices=devices),
        out_shape=jax.ShapeDtypeStruct(hidden_state.shape, BF16),
        in_specs=[SMEM] + [VMEM] * 7,
        scratch_shapes=[pltpu.VMEM((own_rows + 2, cells + 2 * frame_width, 3 * channels), BF16)],
        compiler_params=params(cells),
        name="inner",
    )(
        position,
        near(summed),
        near(stats),
        near(direct),
        early[0],
        near(edge_direct),
        near(edge_states),
        near(turned),
    )


def solution(mesh):
    return jax.shard_map(
        per_device,
        mesh=mesh,
        in_specs=(
            P(None, None, ("clip", "row")),
            P("clip"),
            P("clip"),
            P(),
            P(),
            P(),
            P(),
            P(),
            P(),
            P(("clip", "row"), None, None, None),
            P(),
            P(),
            P(),
            P(),
        ),
        out_specs=P(("clip", "row"), None, None, None),
        check_vma=False,
    )
```

```python
import functools

import jax
import jax.numpy as jnp
from jax import lax
from jax.experimental import pallas as pl
from jax.experimental.pallas import tpu as pltpu
from jax.sharding import PartitionSpec as P

PATCH = 16
GROUPS = 32
FRAMES = 16
LANES = 128
SLOTS = LANES // PATCH
eps_norm = 1e-06
BF16 = jnp.bfloat16
F32 = jnp.float32

SMEM = pl.BlockSpec(memory_space=pltpu.SMEM)
VMEM = pl.BlockSpec(memory_space=pltpu.VMEM)
FAR = pl.BlockSpec(memory_space=pl.ANY)


def iota(shape, dim):
    return lax.broadcasted_iota(jnp.int32, shape, dim)


def div(values, count):
    if count & (count - 1):
        return values // count
    return values >> (count.bit_length() - 1)


def mod(values, count):
    if count & (count - 1):
        return values % count
    return values & (count - 1)


def ones_where(condition):
    return jnp.where(condition, 1.0, 0.0).astype(BF16)


def matmul(left, right):
    return jnp.dot(left, right, preferred_element_type=F32)


def matmul_t(left, right):
    return lax.dot_general(left, right, (((1,), (1,)), ((), ())), preferred_element_type=F32)


def cut_in_three(values):
    high = values.astype(BF16)
    rest = values - high.astype(F32)
    middle = rest.astype(BF16)
    low = (rest - middle.astype(F32)).astype(BF16)
    return high, middle, low


def exact_rows(rows, product):
    place = iota((16, rows[0].shape[1]), 0)
    stacked = jnp.zeros(place.shape, F32)
    for index, row in enumerate(rows):
        for step, piece in enumerate(cut_in_three(row)):
            stacked = jnp.where(place == 3 * index + step, piece.astype(F32), stacked)
    result = product(stacked.astype(BF16))
    return [
        result[3 * i : 3 * i + 1] + result[3 * i + 1 : 3 * i + 2] + result[3 * i + 2 : 3 * i + 3]
        for i in range(len(rows))
    ]


def silu_slope(values):
    sigmoid = jax.nn.sigmoid(values)
    return sigmoid * (1.0 + values * (1.0 - sigmoid))


def token_rows_of(height):
    return -(-(height // PATCH) // 16) * 16


def to_tokens(pixels):
    channels, columns, height = pixels.shape
    rows = channels * columns
    token_rows = token_rows_of(height)
    flat = pixels.reshape(rows, height)
    width = channels * PATCH * columns
    lane = iota((1, width), 1)
    place = iota((rows, 1), 0)
    mine = place == div(lane, PATCH * columns) * columns + mod(lane, columns)
    in_patch = mod(div(lane, columns), PATCH)
    pixel_row = iota((height, 1), 0)
    token = iota((token_rows, 1), 0)
    tokens = jnp.zeros((token_rows, width), F32)
    for t in range(height // PATCH):
        tiled = matmul(flat, ones_where(pixel_row == in_patch + t * PATCH))
        row = jnp.sum(jnp.where(mine, tiled, 0.0), axis=0, keepdims=True)
        tokens = jnp.where(token == t, row, tokens)
    return tokens.astype(BF16)


def forward_part(tokens, count, bias, gain, load_patch):
    embedded = bias[...]
    for low, high, weight in load_patch():
        embedded = embedded + matmul(tokens[:, low:high], weight)
    centred = embedded - jnp.mean(embedded, axis=1, keepdims=True)
    inv_spread = lax.rsqrt(jnp.mean(centred * centred, axis=1, keepdims=True) + eps_norm)
    normed = centred * inv_spread
    weighted = normed * gain[...]
    inside = iota((tokens.shape[0], 1), 0) < count
    pooled = jnp.sum(jnp.where(inside, weighted, 0.0), axis=0, keepdims=True)
    return normed, inv_spread, pooled


def message_shape(devices):
    return jax.ShapeDtypeStruct((devices, 4, LANES), F32)


def write_windows(patch_grad, sums, own_rows, height, send):
    span = PATCH * PATCH
    line = jnp.concatenate(
        [
            jnp.concatenate([patch_grad[t : t + 1, k * span : (k + 1) * span] for t in range(height // PATCH)], axis=1)
            for k in range(3)
        ]
        + [jnp.zeros((1, height * PATCH), F32)],
        axis=0,
    )
    line = jnp.concatenate([jnp.zeros((4, LANES), F32), line, jnp.zeros((4, LANES), F32)], axis=1)
    used = iota((4, LANES), 1) < (own_rows + 4) * PATCH
    colour = iota((4, LANES), 0)
    for d in range(send.shape[0]):
        start = LANES + (d * own_rows - 2) * PATCH
        window = jnp.where(used, line[:, start : start + LANES], 0.0)
        send[d] = jnp.where(colour < 3, window, sums)


def group_sums(hidden):
    channels = hidden.shape[-1]
    first, second = channel_sums(hidden)
    lane = iota((1, LANES), 1)
    group = div(iota((channels, 1), 0), channels // GROUPS)
    (low,) = exact_rows([first], lambda rows: matmul(rows, ones_where(lane == group)))
    (high,) = exact_rows([second], lambda rows: matmul(rows, ones_where(lane == group + GROUPS)))
    return low + high


def channel_sums(hidden):
    values = hidden.reshape(-1, hidden.shape[-1]).astype(F32)
    return jnp.sum(values, axis=0, keepdims=True), jnp.sum(values * values, axis=0, keepdims=True)


def same_group(channels):
    size = channels // GROUPS
    return ones_where(div(iota((channels, 1), 0), size) == div(iota((1, channels), 1), size))


def backward_part(
    owner, picks, gain, head_bias, head_out, normed, inv_spread, pooled, weight, head, slot, own_rows, height, sums, send
):
    (before,) = exact_rows([pooled], lambda rows: matmul(rows, head[...]))
    slope = head_out[...] * silu_slope(before + head_bias[...])
    (pulled,) = exact_rows([slope], lambda rows: matmul_t(rows, head[...]))
    wanted = owner[slot]
    picked = jnp.int32(0)
    for k in range(picks.shape[0]):
        picked = picked + jnp.where(picks[k] == wanted, 1, 0)
    scaled = gain[...] * (picked.astype(F32) * pulled)
    token_grad = inv_spread * (
        scaled
        - jnp.mean(scaled, axis=1, keepdims=True)
        - normed * jnp.mean(scaled * normed, axis=1, keepdims=True)
    )
    patch_grad = matmul_t(token_grad.astype(BF16), weight[...]).astype(BF16).astype(F32)
    write_windows(patch_grad, sums, own_rows, height, send)


def write_edges(place, hidden, across, along):
    last = hidden.shape[0] - 1
    even = place[0] % 2 == 0
    across[0] = hidden[jnp.where(even, last, 0)]
    along[0] = hidden[jnp.where(even, 0, last)]


def reward_kernel(place, *refs):
    count = 10
    far, send, across, along = refs[:count], refs[count], refs[count + 1], refs[count + 2]
    near, sems = refs[count + 3 : 2 * count + 3], refs[-1]
    frames, hidden, bias, owner, picks, gain, head_bias, head_out, patch, head = near
    steps = 3
    depth = patch.shape[0] // steps
    copies = {i: pltpu.make_async_copy(far[i], near[i], sems.at[i]) for i in range(count) if i != 8}
    patch_copies = [
        pltpu.make_async_copy(
            far[8].at[pl.ds(i * depth, depth)], patch.at[pl.ds(i * depth, depth)], sems.at[count + i]
        )
        for i in range(steps)
    ]
    for copy in [copies[i] for i in range(3)] + patch_copies + [copies[i] for i in (3, 4, 5, 6, 7, 9)]:
        copy.start()

    def load_patch():
        for i in range(steps):
            patch_copies[i].wait()
            yield i * depth, (i + 1) * depth, patch[i * depth : (i + 1) * depth, :]

    height = frames.shape[2]
    patches = height // PATCH
    copies[0].wait()
    tokens = to_tokens(frames[...])
    copies[1].wait()
    sums = group_sums(hidden[...])
    write_edges(place, hidden, across, along)
    for i in range(2, 8):
        copies[i].wait()
    normed, inv_spread, pooled = forward_part(tokens, patches, bias, gain, load_patch)
    copies[9].wait()
    backward_part(
        owner,
        picks,
        gain,
        head_bias,
        head_out,
        normed,
        inv_spread,
        pooled / patches,
        patch,
        head,
        place[0],
        hidden.shape[0],
        height,
        sums,
        send,
    )


def forward_kernel(frames, bias, gain, patch, normed, inv_spread, pooled):
    width = patch.shape[0]
    tokens = to_tokens(frames[...])
    normed[...], spread, pooled[...] = forward_part(
        tokens, frames.shape[2] // PATCH, bias, gain, lambda: [(0, width, patch[...])]
    )
    inv_spread[...] = jnp.broadcast_to(spread, inv_spread.shape)


def backward_kernel(
    owner,
    picks,
    place,
    hidden,
    gain,
    head_bias,
    head_out,
    normed,
    inv_spread,
    pooled,
    patch,
    head,
    send,
    across,
    along,
    *,
    height,
    per_frame,
):
    write_edges(place, hidden, across, along)
    backward_part(
        owner,
        picks,
        gain,
        head_bias,
        head_out,
        normed[...],
        inv_spread[...][:, :1],
        pooled[...],
        patch,
        head,
        place[0] // per_frame,
        hidden.shape[0],
        height,
        group_sums(hidden[...]),
        send,
    )


def params(cells):
    return pltpu.CompilerParams(vmem_limit_bytes=min(16 + cells // 64, 48) * 1024 * 1024)


def near(array):
    return pltpu.with_memory_space_constraint(array, pltpu.VMEM)


def far(array):
    return pltpu.with_memory_space_constraint(array, pltpu.HBM)


def prepare_kernel(far_weight, *refs):
    count = (len(refs) - 4) // 2
    fars, wide, nears = refs[:count], refs[count], refs[count + 1 : 2 * count + 1]
    out_weight, scratch, sems = refs[2 * count + 1 :]
    copies = [pltpu.make_async_copy(far_weight, out_weight, sems.at[count])]
    copies += [pltpu.make_async_copy(fars[i], nears[i], sems.at[i]) for i in range(count)]
    for copy in copies:
        copy.start()
    block = scratch.shape[0] // 3
    amount = scratch.shape[1] // LANES
    span = 3 * (amount + 2)
    scratch[...] = jnp.zeros_like(scratch)
    copies[0].wait()
    for a in range(3):
        for e in range(3):
            for b in range(3):
                piece = out_weight[a, b, e].astype(F32)
                for i in range(amount):
                    start = a * block + e * span + 3 * (i - b + 2)
                    scratch[start : start + 3, i * LANES : (i + 1) * LANES] = piece
    wide[...] = scratch[...].astype(BF16)
    for copy in copies[1:]:
        copy.wait()


def norm_constants(totals, channels, cell_total):
    column = iota((1, 2 * channels), 1)
    wanted = div(mod(column, channels), channels // GROUPS) + jnp.where(column >= channels, GROUPS, 0)
    (spread,) = exact_rows([totals], lambda r: matmul(r, ones_where(iota((LANES, 1), 0) == wanted)))
    mean = spread[:, :channels] / cell_total
    return mean, lax.rsqrt(spread[:, channels:] / cell_total - mean * mean + eps_norm)


def norm_slopes(state, mean, inverse, gain, shift):
    normed = (state - mean) * inverse
    return normed, silu_slope(normed * gain + shift) * gain


def slope_kernel(
    owner, arrived, hidden, gain, shift, wide, direct, edge_slopes, stats, sums, slopes_own, received
):
    devices, message_rows, _ = arrived.shape
    own_rows, frame_count, width, channels = hidden.shape
    cells = frame_count * width
    per_frame = devices // frame_count
    received[...] = arrived[...].reshape(received.shape)

    def from_all(row):
        return received[pl.ds(row, devices, stride=message_rows), :]

    totals = jnp.sum(from_all(3), axis=0, keepdims=True)
    mean, inverse = norm_constants(totals, channels, own_rows * devices * cells * (channels // GROUPS))
    for i in range(own_rows):
        state = hidden[i].reshape(cells, channels).astype(F32)
        slopes_own[i] = norm_slopes(state, mean, inverse, gain[...], shift[...])[1]

    lines = jnp.concatenate([from_all(k) for k in range(3)], axis=1).astype(BF16)
    source = iota((1, devices), 1)
    home = jnp.zeros((1, devices), jnp.int32)
    for b in range(frame_count):
        home = jnp.where(div(source, per_frame) == b, owner[b] * per_frame, home)
    home = home + mod(source, per_frame)
    cell = iota((cells, 1), 0)
    column = mod(cell, width)
    frame_strip = div(cell, width) * per_frame
    lane = mod(iota((1, 3 * LANES), 1), PATCH)
    kept = []
    placed = None
    for e in range(3):
        wanted = column - e + 1
        if per_frame > 1 or placed is None:
            strip = frame_strip + div(wanted, PATCH) if per_frame > 1 else frame_strip
            placed = matmul(ones_where(home == strip), lines)
        inside = jnp.where((wanted >= 0) & (wanted < width), mod(wanted, PATCH), -1)
        kept.append(jnp.where(lane == inside, placed, 0.0).astype(BF16))
    block = wide.shape[0] // 3
    span = 3 * (own_rows + 4)
    entry = iota((3 * LANES, 1), 0)
    entry = div(mod(entry, LANES), PATCH) * 3 + div(entry, LANES)
    entry = jnp.where(entry < span, entry, -3 * span)
    tap = iota((1, block), 1)
    folds = jnp.concatenate([ones_where(tap == entry + e * span) for e in range(3)], axis=0)
    taps = matmul(jnp.concatenate(kept, axis=1), folds).astype(BF16)
    later = []
    for a in range(3):
        skip = (2 - a) * width
        later.append(
            jnp.concatenate([taps[skip:], jnp.zeros((skip, block), BF16)], axis=0) if skip else taps
        )
    result = matmul(jnp.concatenate(later, axis=1), wide[...])

    first = jnp.zeros((1, channels), F32)
    second = jnp.zeros((1, channels), F32)
    for i in range(own_rows):
        state = hidden[i].reshape(cells, channels).astype(F32)
        up = result[:, (i + 1) * channels : (i + 2) * channels] * slopes_own[i]
        direct[i] = up * inverse
        first = first + jnp.sum(up, axis=0, keepdims=True)
        second = second + jnp.sum(up * ((state - mean) * inverse), axis=0, keepdims=True)
    edge_slopes[0] = result[:, :channels]
    edge_slopes[1] = result[:, (own_rows + 1) * channels :]
    stats[0:1, :] = mean
    stats[1:2, :] = inverse
    both = jnp.where(iota((2, channels), 0) == 0, first, second)
    sums[...] = jnp.broadcast_to(both[None], sums.shape)


def late_kernel(place, across, along, slopes, stats, gain, shift, inner_weight, direct, states, turned):
    cells, channels = slopes.shape[1:]
    odd = place[0] % 2 == 1
    mean = stats[0:1, :]
    inverse = stats[1:2, :]
    for i in range(2):
        state = jnp.where(odd == (i == 0), across[0], along[0])
        states[i] = state
        values = state.reshape(cells, channels).astype(F32)
        direct[i] = slopes[i] * norm_slopes(values, mean, inverse, gain[...], shift[...])[1] * inverse
    size = inner_weight.shape[3]
    for b in range(3):
        for a in range(3):
            for e in range(3):
                at = (a * 3 + e) * size
                turned[at : at + size, b * size : (b + 1) * size] = inner_weight[a, b, e].T


def inner_kernel(
    place, arrived, stats, direct, hidden, edge_direct, edge_states, turned, far_out, padded, out, sems, *, devices
):
    own_rows, frame_count, width, channels = out.shape
    cells = frame_count * width
    totals = jnp.sum(arrived[...], axis=0)
    same = same_group(channels)
    cell_total = own_rows * devices * cells * (channels // GROUPS)
    first, second = exact_rows([totals[0:1], totals[1:2]], lambda rows: matmul(rows, same))
    mean = stats[0:1, :]
    inverse = stats[1:2, :]
    constant = first / cell_total * inverse
    factor = second / cell_total * inverse * inverse
    position = place[0]
    in_frame = mod(iota((cells, 1), 0), width)
    for i in range(own_rows + 2):
        if 0 < i < own_rows + 1:
            state, part = hidden[i - 1], direct[i - 1]
        else:
            state, part = edge_states[min(i, 1)], edge_direct[min(i, 1)]
        grad = part - constant - (state.reshape(cells, channels).astype(F32) - mean) * factor
        if i == 0:
            grad = jnp.where(position > 0, grad, 0.0)
        if i == own_rows + 1:
            grad = jnp.where(position < devices - 1, grad, 0.0)
        after = jnp.where(in_frame < width - 1, pltpu.roll(grad, cells - 1, 0), 0.0)
        prior = jnp.where(in_frame > 0, pltpu.roll(grad, 1, 0), 0.0)
        padded[i, :cells, 0:channels] = after.astype(BF16)
        padded[i, :cells, channels : 2 * channels] = grad.astype(BF16)
        padded[i, :cells, 2 * channels :] = prior.astype(BF16)
        padded[i, cells:, :] = jnp.zeros((2 * width, 3 * channels), BF16)
    results = [jnp.zeros((cells, channels), F32) for _ in range(own_rows)]
    copies = []
    for i in range(own_rows + 2):
        joined = jnp.concatenate(
            [padded[i, (2 - a) * width : (2 - a) * width + cells, :] for a in range(3)], axis=1
        )
        taps = [b for b in range(3) if 0 <= i + b - 2 < own_rows]
        for low in range(0, len(taps), 2):
            some = taps[low : low + 2]
            product = matmul(joined, turned[:, some[0] * channels : (some[-1] + 1) * channels])
            for step, b in enumerate(some):
                results[i + b - 2] = results[i + b - 2] + product[:, step * channels : (step + 1) * channels]
        if i >= 2:
            out[i - 2] = results[i - 2].reshape(frame_count, width, channels).astype(BF16)
            copies.append(pltpu.make_async_copy(out.at[i - 2], far_out.at[i - 2], sems.at[i - 2]))
            copies[-1].start()
    for copy in copies:
        copy.wait()


def per_device(
    frames,
    frame_owner,
    picks,
    patch_weight,
    patch_bias,
    norm_gain,
    head_weight,
    head_bias,
    head_out,
    hidden_state,
    group_gain,
    group_shift,
    out_weight,
    inner_weight,
):
    devices = lax.axis_size("row")
    position = lax.axis_index("row").astype(jnp.int32).reshape(1)
    per_frame = devices // FRAMES
    height = frames.shape[1]
    own_rows, _, frame_width, channels = hidden_state.shape
    cells = FRAMES * frame_width
    width = patch_weight.shape[1]
    turned_frames = jnp.transpose(frames, (0, 2, 1))
    bias = patch_bias.reshape(1, width)
    gain = norm_gain.reshape(1, width)
    head_bias_row = head_bias.reshape(1, width)
    head_out_row = head_out.reshape(1, width)
    state_rows = own_rows + 2
    tap_rows = -(-9 * (own_rows + 4) // LANES) * LANES
    edge = jax.ShapeDtypeStruct((1,) + hidden_state.shape[1:], BF16)
    message = (message_shape(devices), edge, edge)
    gain_row = group_gain.reshape(1, channels)
    shift_row = group_shift.reshape(1, channels)
    early = [hidden_state, gain_row, shift_row]
    wide, *early = pl.pallas_call(
        prepare_kernel,
        out_shape=(
            pltpu.VMEM((3 * tap_rows, state_rows * channels), BF16),
            *[pltpu.VMEM(x.shape, x.dtype) for x in early],
        ),
        in_specs=[FAR] * (1 + len(early)),
        scratch_shapes=[
            pltpu.VMEM(out_weight.shape, BF16),
            pltpu.VMEM((3 * tap_rows, state_rows * channels), F32),
            pltpu.SemaphoreType.DMA((1 + len(early),)),
        ],
        compiler_params=params(cells),
        name="prepare",
    )(far(out_weight), *[far(x) for x in early])
    early = [near(x) for x in early]
    slope_outs = (
        pltpu.VMEM((own_rows, cells, channels), F32),
        pltpu.VMEM((2, cells, channels), F32),
        pltpu.VMEM((8, channels), F32),
        jax.ShapeDtypeStruct((devices, 2, channels), F32),
    )
    if per_frame == 1:
        arrays = [
            turned_frames,
            hidden_state,
            bias,
            frame_owner,
            picks,
            gain,
            head_bias_row,
            head_out_row,
            patch_weight,
            head_weight,
        ]
        send, across, along = pl.pallas_call(
            reward_kernel,
            out_shape=message,
            in_specs=[SMEM] + [FAR] * len(arrays),
            out_specs=[VMEM] * 3,
            scratch_shapes=[
                (pltpu.SMEM if x.dtype == jnp.int32 else pltpu.VMEM)(x.shape, x.dtype) for x in arrays
            ]
            + [pltpu.SemaphoreType.DMA((len(arrays) + 3,))],
            compiler_params=params(0),
            name="reward",
        )(position, *[far(x) for x in arrays])
    else:
        count = height // PATCH
        normed, inv_spread, partial = pl.pallas_call(
            forward_kernel,
            out_shape=(
                jax.ShapeDtypeStruct((token_rows_of(height), width), F32),
                jax.ShapeDtypeStruct((token_rows_of(height), LANES), F32),
                jax.ShapeDtypeStruct((1, width), F32),
            ),
            compiler_params=params(cells),
            name="reward_forward",
        )(turned_frames, bias, gain, patch_weight)
        members = [[b * per_frame + i for i in range(per_frame)] for b in range(FRAMES)]
        pooled = lax.psum(partial, "row", axis_index_groups=members) / (count * per_frame)
        send, across, along = pl.pallas_call(
            functools.partial(backward_kernel, height=height, per_frame=per_frame),
            out_shape=message,
            in_specs=[SMEM] * 3 + [VMEM] * 9,
            out_specs=[VMEM] * 3,
            compiler_params=params(cells),
            name="reward_backward",
        )(
            frame_owner,
            picks,
            position,
            hidden_state,
            gain,
            head_bias_row,
            head_out_row,
            normed,
            inv_spread,
            pooled,
            patch_weight,
            head_weight,
        )
    arrived = lax.all_to_all(send, "row", 0, 0, tiled=True)
    direct, edge_slopes, stats, sums = pl.pallas_call(
        slope_kernel,
        out_shape=slope_outs,
        in_specs=[SMEM] + [VMEM] * 5,
        scratch_shapes=[
            pltpu.VMEM((own_rows, cells, channels), F32),
            pltpu.VMEM((4 * devices, LANES), F32),
        ],
        compiler_params=params(cells),
        name="slope",
    )(frame_owner, near(arrived), *early, near(wide))
    swaps = [(2 * i, 2 * i + 1) for i in range(devices // 2)]
    across = lax.ppermute(across, "row", swaps + [(b, a) for a, b in swaps])
    swaps = [(2 * i - 1, 2 * i) for i in range(1, devices // 2)]
    along = lax.ppermute(along, "row", swaps + [(b, a) for a, b in swaps])
    summed = lax.all_to_all(sums, "row", 0, 0, tiled=True)
    edge_direct, edge_states, turned = pl.pallas_call(
        late_kernel,
        out_shape=(
            pltpu.VMEM((2, cells, channels), F32),
            pltpu.VMEM((2,) + hidden_state.shape[1:], BF16),
            pltpu.VMEM((9 * channels, 3 * channels), BF16),
        ),
        in_specs=[SMEM] + [VMEM] * 7,
        input_output_aliases={3: 0},
        compiler_params=params(cells),
        name="late",
    )(position, near(across), near(along), near(edge_slopes), near(stats), *early[1:3], inner_weight)
    return pl.pallas_call(
        functools.partial(inner_kernel, devices=devices),
        out_shape=jax.ShapeDtypeStruct(hidden_state.shape, BF16),
        in_specs=[SMEM] + [VMEM] * 7,
        out_specs=FAR,
        scratch_shapes=[
            pltpu.VMEM((own_rows + 2, cells + 2 * frame_width, 3 * channels), BF16),
            pltpu.VMEM(hidden_state.shape, BF16),
            pltpu.SemaphoreType.DMA((own_rows,)),
        ],
        compiler_params=params(cells),
        name="inner",
    )(
        position,
        near(summed),
        near(stats),
        near(direct),
        early[0],
        near(edge_direct),
        near(edge_states),
        near(turned),
    )


def solution(mesh):
    return jax.shard_map(
        per_device,
        mesh=mesh,
        in_specs=(
            P(None, None, ("clip", "row")),
            P("clip"),
            P("clip"),
            P(),
            P(),
            P(),
            P(),
            P(),
            P(),
            P(("clip", "row"), None, None, None),
            P(),
            P(),
            P(),
            P(),
        ),
        out_specs=P(("clip", "row"), None, None, None),
        check_vma=False,
    )
```

```python
import functools

import jax
import jax.numpy as jnp
from jax import lax
from jax.experimental import pallas as pl
from jax.experimental.pallas import tpu as pltpu
from jax.sharding import PartitionSpec as P

PATCH = 16
GROUPS = 32
FRAMES = 16
LANES = 128
SLOTS = LANES // PATCH
eps_norm = 1e-06
BF16 = jnp.bfloat16
F32 = jnp.float32

SMEM = pl.BlockSpec(memory_space=pltpu.SMEM)
VMEM = pl.BlockSpec(memory_space=pltpu.VMEM)
FAR = pl.BlockSpec(memory_space=pl.ANY)


def iota(shape, dim):
    return lax.broadcasted_iota(jnp.int32, shape, dim)


def div(values, count):
    if count & (count - 1):
        return values // count
    return values >> (count.bit_length() - 1)


def mod(values, count):
    if count & (count - 1):
        return values % count
    return values & (count - 1)


def ones_where(condition):
    return jnp.where(condition, 1.0, 0.0).astype(BF16)


def matmul(left, right):
    return jnp.dot(left, right, preferred_element_type=F32)


def matmul_t(rows, weight):
    count = rows.shape[0]
    padded = -(-count // LANES) * LANES
    rows = jnp.concatenate([rows, jnp.zeros((padded - count, rows.shape[1]), rows.dtype)], axis=0)
    product = lax.dot_general(weight, rows, (((1,), (1,)), ((), ())), preferred_element_type=F32)
    return product.T[:count]


def cut_in_three(values):
    high = values.astype(BF16)
    rest = values - high.astype(F32)
    middle = rest.astype(BF16)
    low = (rest - middle.astype(F32)).astype(BF16)
    return high, middle, low


def exact_rows(rows, product):
    place = iota((16, rows[0].shape[1]), 0)
    stacked = jnp.zeros(place.shape, F32)
    for index, row in enumerate(rows):
        for step, piece in enumerate(cut_in_three(row)):
            stacked = jnp.where(place == 3 * index + step, piece.astype(F32), stacked)
    result = product(stacked.astype(BF16))
    return [
        result[3 * i : 3 * i + 1] + result[3 * i + 1 : 3 * i + 2] + result[3 * i + 2 : 3 * i + 3]
        for i in range(len(rows))
    ]


def silu_slope(values):
    sigmoid = jax.nn.sigmoid(values)
    return sigmoid * (1.0 + values * (1.0 - sigmoid))


def token_rows_of(height):
    return -(-(height // PATCH) // 16) * 16


def to_tokens(pixels):
    channels, columns, height = pixels.shape
    rows = channels * columns
    token_rows = token_rows_of(height)
    flat = pixels.reshape(rows, height)
    width = channels * PATCH * columns
    lane = iota((1, width), 1)
    place = iota((rows, 1), 0)
    mine = place == div(lane, PATCH * columns) * columns + mod(lane, columns)
    in_patch = mod(div(lane, columns), PATCH)
    pixel_row = iota((height, 1), 0)
    token = iota((token_rows, 1), 0)
    tokens = jnp.zeros((token_rows, width), F32)
    for t in range(height // PATCH):
        tiled = matmul(flat, ones_where(pixel_row == in_patch + t * PATCH))
        row = jnp.sum(jnp.where(mine, tiled, 0.0), axis=0, keepdims=True)
        tokens = jnp.where(token == t, row, tokens)
    return tokens.astype(BF16)


def forward_part(tokens, count, bias, gain, load_patch):
    embedded = bias[...]
    for low, high, weight in load_patch():
        embedded = embedded + matmul(tokens[:, low:high], weight)
    centred = embedded - jnp.mean(embedded, axis=1, keepdims=True)
    inv_spread = lax.rsqrt(jnp.mean(centred * centred, axis=1, keepdims=True) + eps_norm)
    normed = centred * inv_spread
    weighted = normed * gain[...]
    inside = iota((tokens.shape[0], 1), 0) < count
    pooled = jnp.sum(jnp.where(inside, weighted, 0.0), axis=0, keepdims=True)
    return normed, inv_spread, pooled


def message_shape(devices):
    return jax.ShapeDtypeStruct((devices, 4, LANES), F32)


def write_windows(patch_grad, sums, own_rows, height, send):
    span = PATCH * PATCH
    line = jnp.concatenate(
        [
            jnp.concatenate([patch_grad[t : t + 1, k * span : (k + 1) * span] for t in range(height // PATCH)], axis=1)
            for k in range(3)
        ]
        + [jnp.zeros((1, height * PATCH), F32)],
        axis=0,
    )
    line = jnp.concatenate([jnp.zeros((4, LANES), F32), line, jnp.zeros((4, LANES), F32)], axis=1)
    used = iota((4, LANES), 1) < (own_rows + 4) * PATCH
    colour = iota((4, LANES), 0)
    for d in range(send.shape[0]):
        start = LANES + (d * own_rows - 2) * PATCH
        window = jnp.where(used, line[:, start : start + LANES], 0.0)
        send[d] = jnp.where(colour < 3, window, sums)


def group_sums(hidden):
    channels = hidden.shape[-1]
    first, second = channel_sums(hidden)
    lane = iota((1, LANES), 1)
    group = div(iota((channels, 1), 0), channels // GROUPS)
    (low,) = exact_rows([first], lambda rows: matmul(rows, ones_where(lane == group)))
    (high,) = exact_rows([second], lambda rows: matmul(rows, ones_where(lane == group + GROUPS)))
    return low + high


def channel_sums(hidden):
    values = hidden.reshape(-1, hidden.shape[-1]).astype(F32)
    return jnp.sum(values, axis=0, keepdims=True), jnp.sum(values * values, axis=0, keepdims=True)


def same_group(channels):
    size = channels // GROUPS
    return ones_where(div(iota((channels, 1), 0), size) == div(iota((1, channels), 1), size))


def backward_part(
    owner, picks, gain, head_bias, head_out, normed, inv_spread, pooled, weight, head, slot, own_rows, height, sums, send
):
    (before,) = exact_rows([pooled], lambda rows: matmul(rows, head[...]))
    slope = head_out[...] * silu_slope(before + head_bias[...])
    (pulled,) = exact_rows([slope], lambda rows: matmul_t(rows, head[...]))
    wanted = owner[slot]
    picked = jnp.int32(0)
    for k in range(picks.shape[0]):
        picked = picked + jnp.where(picks[k] == wanted, 1, 0)
    scaled = gain[...] * (picked.astype(F32) * pulled)
    token_grad = inv_spread * (
        scaled
        - jnp.mean(scaled, axis=1, keepdims=True)
        - normed * jnp.mean(scaled * normed, axis=1, keepdims=True)
    )
    patch_grad = matmul_t(token_grad.astype(BF16), weight[...]).astype(BF16).astype(F32)
    write_windows(patch_grad, sums, own_rows, height, send)


def write_edges(place, hidden, across, along):
    last = hidden.shape[0] - 1
    even = place[0] % 2 == 0
    across[0] = hidden[jnp.where(even, last, 0)]
    along[0] = hidden[jnp.where(even, 0, last)]


def reward_kernel(place, *refs):
    count = 10
    far, send, across, along = refs[:count], refs[count], refs[count + 1], refs[count + 2]
    near, sems = refs[count + 3 : 2 * count + 3], refs[-1]
    frames, hidden, bias, owner, picks, gain, head_bias, head_out, patch, head = near
    steps = 3
    depth = patch.shape[0] // steps
    copies = {i: pltpu.make_async_copy(far[i], near[i], sems.at[i]) for i in range(count) if i != 8}
    patch_copies = [
        pltpu.make_async_copy(
            far[8].at[pl.ds(i * depth, depth)], patch.at[pl.ds(i * depth, depth)], sems.at[count + i]
        )
        for i in range(steps)
    ]
    for copy in [copies[i] for i in range(3)] + patch_copies + [copies[i] for i in (3, 4, 5, 6, 7, 9)]:
        copy.start()

    def load_patch():
        for i in range(steps):
            patch_copies[i].wait()
            yield i * depth, (i + 1) * depth, patch[i * depth : (i + 1) * depth, :]

    height = frames.shape[2]
    patches = height // PATCH
    copies[0].wait()
    tokens = to_tokens(frames[...])
    copies[1].wait()
    sums = group_sums(hidden[...])
    write_edges(place, hidden, across, along)
    for i in range(2, 8):
        copies[i].wait()
    normed, inv_spread, pooled = forward_part(tokens, patches, bias, gain, load_patch)
    copies[9].wait()
    backward_part(
        owner,
        picks,
        gain,
        head_bias,
        head_out,
        normed,
        inv_spread,
        pooled / patches,
        patch,
        head,
        place[0],
        hidden.shape[0],
        height,
        sums,
        send,
    )


def forward_kernel(frames, bias, gain, patch, normed, inv_spread, pooled):
    width = patch.shape[0]
    tokens = to_tokens(frames[...])
    normed[...], spread, pooled[...] = forward_part(
        tokens, frames.shape[2] // PATCH, bias, gain, lambda: [(0, width, patch[...])]
    )
    inv_spread[...] = jnp.broadcast_to(spread, inv_spread.shape)


def backward_kernel(
    owner,
    picks,
    place,
    hidden,
    gain,
    head_bias,
    head_out,
    normed,
    inv_spread,
    pooled,
    patch,
    head,
    send,
    across,
    along,
    *,
    height,
    per_frame,
):
    write_edges(place, hidden, across, along)
    backward_part(
        owner,
        picks,
        gain,
        head_bias,
        head_out,
        normed[...],
        inv_spread[...][:, :1],
        pooled[...],
        patch,
        head,
        place[0] // per_frame,
        hidden.shape[0],
        height,
        group_sums(hidden[...]),
        send,
    )


def params(cells):
    return pltpu.CompilerParams(vmem_limit_bytes=min(16 + cells // 64, 48) * 1024 * 1024)


def near(array):
    return pltpu.with_memory_space_constraint(array, pltpu.VMEM)


def far(array):
    return pltpu.with_memory_space_constraint(array, pltpu.HBM)


def prepare_kernel(far_weight, *refs):
    count = (len(refs) - 4) // 2
    fars, wide, nears = refs[:count], refs[count], refs[count + 1 : 2 * count + 1]
    out_weight, scratch, sems = refs[2 * count + 1 :]
    copies = [pltpu.make_async_copy(far_weight, out_weight, sems.at[count])]
    copies += [pltpu.make_async_copy(fars[i], nears[i], sems.at[i]) for i in range(count)]
    for copy in copies:
        copy.start()
    block = scratch.shape[0] // 3
    amount = scratch.shape[1] // LANES
    span = 3 * (amount + 2)
    scratch[...] = jnp.zeros_like(scratch)
    copies[0].wait()
    for a in range(3):
        for e in range(3):
            for b in range(3):
                piece = out_weight[a, b, e].astype(F32)
                for i in range(amount):
                    start = a * block + e * span + 3 * (i - b + 2)
                    scratch[start : start + 3, i * LANES : (i + 1) * LANES] = piece
    wide[...] = scratch[...].astype(BF16)
    for copy in copies[1:]:
        copy.wait()


def norm_constants(totals, channels, cell_total):
    column = iota((1, 2 * channels), 1)
    wanted = div(mod(column, channels), channels // GROUPS) + jnp.where(column >= channels, GROUPS, 0)
    (spread,) = exact_rows([totals], lambda r: matmul(r, ones_where(iota((LANES, 1), 0) == wanted)))
    mean = spread[:, :channels] / cell_total
    return mean, lax.rsqrt(spread[:, channels:] / cell_total - mean * mean + eps_norm)


def norm_slopes(state, mean, inverse, gain, shift):
    normed = (state - mean) * inverse
    return normed, silu_slope(normed * gain + shift) * gain


def slope_kernel(
    owner, arrived, hidden, gain, shift, wide, direct, edge_slopes, stats, sums, slopes_own, received
):
    devices, message_rows, _ = arrived.shape
    own_rows, frame_count, width, channels = hidden.shape
    cells = frame_count * width
    per_frame = devices // frame_count
    received[...] = arrived[...].reshape(received.shape)

    def from_all(row):
        return received[pl.ds(row, devices, stride=message_rows), :]

    totals = jnp.sum(from_all(3), axis=0, keepdims=True)
    mean, inverse = norm_constants(totals, channels, own_rows * devices * cells * (channels // GROUPS))
    for i in range(own_rows):
        state = hidden[i].reshape(cells, channels).astype(F32)
        slopes_own[i] = norm_slopes(state, mean, inverse, gain[...], shift[...])[1]

    lines = jnp.concatenate([from_all(k) for k in range(3)], axis=1).astype(BF16)
    source = iota((1, devices), 1)
    home = jnp.zeros((1, devices), jnp.int32)
    for b in range(frame_count):
        home = jnp.where(div(source, per_frame) == b, owner[b] * per_frame, home)
    home = home + mod(source, per_frame)
    cell = iota((cells, 1), 0)
    column = mod(cell, width)
    frame_strip = div(cell, width) * per_frame
    lane = mod(iota((1, 3 * LANES), 1), PATCH)
    kept = []
    placed = None
    for e in range(3):
        wanted = column - e + 1
        if per_frame > 1 or placed is None:
            strip = frame_strip + div(wanted, PATCH) if per_frame > 1 else frame_strip
            placed = matmul(ones_where(home == strip), lines)
        inside = jnp.where((wanted >= 0) & (wanted < width), mod(wanted, PATCH), -1)
        kept.append(jnp.where(lane == inside, placed, 0.0).astype(BF16))
    block = wide.shape[0] // 3
    span = 3 * (own_rows + 4)
    entry = iota((3 * LANES, 1), 0)
    entry = div(mod(entry, LANES), PATCH) * 3 + div(entry, LANES)
    entry = jnp.where(entry < span, entry, -3 * span)
    tap = iota((1, block), 1)
    folds = jnp.concatenate([ones_where(tap == entry + e * span) for e in range(3)], axis=0)
    taps = matmul(jnp.concatenate(kept, axis=1), folds).astype(BF16)
    later = []
    for a in range(3):
        skip = (2 - a) * width
        later.append(
            jnp.concatenate([taps[skip:], jnp.zeros((skip, block), BF16)], axis=0) if skip else taps
        )
    result = matmul(jnp.concatenate(later, axis=1), wide[...])

    first = jnp.zeros((1, channels), F32)
    second = jnp.zeros((1, channels), F32)
    for i in range(own_rows):
        state = hidden[i].reshape(cells, channels).astype(F32)
        up = result[:, (i + 1) * channels : (i + 2) * channels] * slopes_own[i]
        direct[i] = up * inverse
        first = first + jnp.sum(up, axis=0, keepdims=True)
        second = second + jnp.sum(up * ((state - mean) * inverse), axis=0, keepdims=True)
    edge_slopes[0] = result[:, :channels]
    edge_slopes[1] = result[:, (own_rows + 1) * channels :]
    stats[0:1, :] = mean
    stats[1:2, :] = inverse
    both = jnp.where(iota((2, channels), 0) == 0, first, second)
    sums[...] = jnp.broadcast_to(both[None], sums.shape)


def late_kernel(place, across, along, slopes, stats, gain, shift, inner_weight, direct, states, turned):
    cells, channels = slopes.shape[1:]
    odd = place[0] % 2 == 1
    mean = stats[0:1, :]
    inverse = stats[1:2, :]
    for i in range(2):
        state = jnp.where(odd == (i == 0), across[0], along[0])
        states[i] = state
        values = state.reshape(cells, channels).astype(F32)
        direct[i] = slopes[i] * norm_slopes(values, mean, inverse, gain[...], shift[...])[1] * inverse
    size = inner_weight.shape[3]
    for b in range(3):
        for a in range(3):
            for e in range(3):
                at = (a * 3 + e) * size
                turned[at : at + size, b * size : (b + 1) * size] = inner_weight[a, b, e].T


def inner_kernel(
    place, arrived, stats, direct, hidden, edge_direct, edge_states, turned, far_out, padded, out, sems, *, devices
):
    own_rows, frame_count, width, channels = out.shape
    cells = frame_count * width
    totals = jnp.sum(arrived[...], axis=0)
    same = same_group(channels)
    cell_total = own_rows * devices * cells * (channels // GROUPS)
    first, second = exact_rows([totals[0:1], totals[1:2]], lambda rows: matmul(rows, same))
    mean = stats[0:1, :]
    inverse = stats[1:2, :]
    constant = first / cell_total * inverse
    factor = second / cell_total * inverse * inverse
    position = place[0]
    in_frame = mod(iota((cells, 1), 0), width)
    for i in range(own_rows + 2):
        if 0 < i < own_rows + 1:
            state, part = hidden[i - 1], direct[i - 1]
        else:
            state, part = edge_states[min(i, 1)], edge_direct[min(i, 1)]
        grad = part - constant - (state.reshape(cells, channels).astype(F32) - mean) * factor
        if i == 0:
            grad = jnp.where(position > 0, grad, 0.0)
        if i == own_rows + 1:
            grad = jnp.where(position < devices - 1, grad, 0.0)
        after = jnp.where(in_frame < width - 1, pltpu.roll(grad, cells - 1, 0), 0.0)
        prior = jnp.where(in_frame > 0, pltpu.roll(grad, 1, 0), 0.0)
        padded[i, :cells, 0:channels] = after.astype(BF16)
        padded[i, :cells, channels : 2 * channels] = grad.astype(BF16)
        padded[i, :cells, 2 * channels :] = prior.astype(BF16)
        padded[i, cells:, :] = jnp.zeros((2 * width, 3 * channels), BF16)
    results = [jnp.zeros((cells, channels), F32) for _ in range(own_rows)]
    copies = []
    for i in range(own_rows + 2):
        joined = jnp.concatenate(
            [padded[i, (2 - a) * width : (2 - a) * width + cells, :] for a in range(3)], axis=1
        )
        taps = [b for b in range(3) if 0 <= i + b - 2 < own_rows]
        for low in range(0, len(taps), 2):
            some = taps[low : low + 2]
            product = matmul(joined, turned[:, some[0] * channels : (some[-1] + 1) * channels])
            for step, b in enumerate(some):
                results[i + b - 2] = results[i + b - 2] + product[:, step * channels : (step + 1) * channels]
        if i >= 2:
            out[i - 2] = results[i - 2].reshape(frame_count, width, channels).astype(BF16)
            copies.append(pltpu.make_async_copy(out.at[i - 2], far_out.at[i - 2], sems.at[i - 2]))
            copies[-1].start()
    for copy in copies:
        copy.wait()


def per_device(
    frames,
    frame_owner,
    picks,
    patch_weight,
    patch_bias,
    norm_gain,
    head_weight,
    head_bias,
    head_out,
    hidden_state,
    group_gain,
    group_shift,
    out_weight,
    inner_weight,
):
    devices = lax.axis_size("row")
    position = lax.axis_index("row").astype(jnp.int32).reshape(1)
    per_frame = devices // FRAMES
    height = frames.shape[1]
    own_rows, _, frame_width, channels = hidden_state.shape
    cells = FRAMES * frame_width
    width = patch_weight.shape[1]
    turned_frames = jnp.transpose(frames, (0, 2, 1))
    bias = patch_bias.reshape(1, width)
    gain = norm_gain.reshape(1, width)
    head_bias_row = head_bias.reshape(1, width)
    head_out_row = head_out.reshape(1, width)
    state_rows = own_rows + 2
    tap_rows = -(-9 * (own_rows + 4) // LANES) * LANES
    edge = jax.ShapeDtypeStruct((1,) + hidden_state.shape[1:], BF16)
    message = (message_shape(devices), edge, edge)
    gain_row = group_gain.reshape(1, channels)
    shift_row = group_shift.reshape(1, channels)
    early = [hidden_state, gain_row, shift_row]
    wide, *early = pl.pallas_call(
        prepare_kernel,
        out_shape=(
            pltpu.VMEM((3 * tap_rows, state_rows * channels), BF16),
            *[pltpu.VMEM(x.shape, x.dtype) for x in early],
        ),
        in_specs=[FAR] * (1 + len(early)),
        scratch_shapes=[
            pltpu.VMEM(out_weight.shape, BF16),
            pltpu.VMEM((3 * tap_rows, state_rows * channels), F32),
            pltpu.SemaphoreType.DMA((1 + len(early),)),
        ],
        compiler_params=params(cells),
        name="prepare",
    )(far(out_weight), *[far(x) for x in early])
    early = [near(x) for x in early]
    slope_outs = (
        pltpu.VMEM((own_rows, cells, channels), F32),
        pltpu.VMEM((2, cells, channels), F32),
        pltpu.VMEM((8, channels), F32),
        jax.ShapeDtypeStruct((devices, 2, channels), F32),
    )
    if per_frame == 1:
        arrays = [
            turned_frames,
            hidden_state,
            bias,
            frame_owner,
            picks,
            gain,
            head_bias_row,
            head_out_row,
            patch_weight,
            head_weight,
        ]
        send, across, along = pl.pallas_call(
            reward_kernel,
            out_shape=message,
            in_specs=[SMEM] + [FAR] * len(arrays),
            out_specs=[VMEM] * 3,
            scratch_shapes=[
                (pltpu.SMEM if x.dtype == jnp.int32 else pltpu.VMEM)(x.shape, x.dtype) for x in arrays
            ]
            + [pltpu.SemaphoreType.DMA((len(arrays) + 3,))],
            compiler_params=params(0),
            name="reward",
        )(position, *[far(x) for x in arrays])
    else:
        count = height // PATCH
        normed, inv_spread, partial = pl.pallas_call(
            forward_kernel,
            out_shape=(
                jax.ShapeDtypeStruct((token_rows_of(height), width), F32),
                jax.ShapeDtypeStruct((token_rows_of(height), LANES), F32),
                jax.ShapeDtypeStruct((1, width), F32),
            ),
            compiler_params=params(cells),
            name="reward_forward",
        )(turned_frames, bias, gain, patch_weight)
        members = [[b * per_frame + i for i in range(per_frame)] for b in range(FRAMES)]
        pooled = lax.psum(partial, "row", axis_index_groups=members) / (count * per_frame)
        send, across, along = pl.pallas_call(
            functools.partial(backward_kernel, height=height, per_frame=per_frame),
            out_shape=message,
            in_specs=[SMEM] * 3 + [VMEM] * 9,
            out_specs=[VMEM] * 3,
            compiler_params=params(cells),
            name="reward_backward",
        )(
            frame_owner,
            picks,
            position,
            hidden_state,
            gain,
            head_bias_row,
            head_out_row,
            normed,
            inv_spread,
            pooled,
            patch_weight,
            head_weight,
        )
    arrived = lax.all_to_all(send, "row", 0, 0, tiled=True)
    direct, edge_slopes, stats, sums = pl.pallas_call(
        slope_kernel,
        out_shape=slope_outs,
        in_specs=[SMEM] + [VMEM] * 5,
        scratch_shapes=[
            pltpu.VMEM((own_rows, cells, channels), F32),
            pltpu.VMEM((4 * devices, LANES), F32),
        ],
        compiler_params=params(cells),
        name="slope",
    )(frame_owner, near(arrived), *early, near(wide))
    swaps = [(2 * i, 2 * i + 1) for i in range(devices // 2)]
    across = lax.ppermute(across, "row", swaps + [(b, a) for a, b in swaps])
    swaps = [(2 * i - 1, 2 * i) for i in range(1, devices // 2)]
    along = lax.ppermute(along, "row", swaps + [(b, a) for a, b in swaps])
    summed = lax.all_to_all(sums, "row", 0, 0, tiled=True)
    edge_direct, edge_states, turned = pl.pallas_call(
        late_kernel,
        out_shape=(
            pltpu.VMEM((2, cells, channels), F32),
            pltpu.VMEM((2,) + hidden_state.shape[1:], BF16),
            pltpu.VMEM((9 * channels, 3 * channels), BF16),
        ),
        in_specs=[SMEM] + [VMEM] * 7,
        input_output_aliases={3: 0},
        compiler_params=params(cells),
        name="late",
    )(position, near(across), near(along), near(edge_slopes), near(stats), *early[1:3], inner_weight)
    return pl.pallas_call(
        functools.partial(inner_kernel, devices=devices),
        out_shape=jax.ShapeDtypeStruct(hidden_state.shape, BF16),
        in_specs=[SMEM] + [VMEM] * 7,
        out_specs=FAR,
        scratch_shapes=[
            pltpu.VMEM((own_rows + 2, cells + 2 * frame_width, 3 * channels), BF16),
            pltpu.VMEM(hidden_state.shape, BF16),
            pltpu.SemaphoreType.DMA((own_rows,)),
        ],
        compiler_params=params(cells),
        name="inner",
    )(
        position,
        near(summed),
        near(stats),
        near(direct),
        early[0],
        near(edge_direct),
        near(edge_states),
        near(turned),
    )


def solution(mesh):
    return jax.shard_map(
        per_device,
        mesh=mesh,
        in_specs=(
            P(None, None, ("clip", "row")),
            P("clip"),
            P("clip"),
            P(),
            P(),
            P(),
            P(),
            P(),
            P(),
            P(("clip", "row"), None, None, None),
            P(),
            P(),
            P(),
            P(),
        ),
        out_specs=P(("clip", "row"), None, None, None),
        check_vma=False,
    )
```

```python
import functools

import jax
import jax.numpy as jnp
from jax import lax
from jax.experimental import pallas as pl
from jax.experimental.pallas import tpu as pltpu
from jax.sharding import PartitionSpec as P

PATCH = 16
GROUPS = 32
FRAMES = 16
LANES = 128
SLOTS = LANES // PATCH
eps_norm = 1e-06
BF16 = jnp.bfloat16
F32 = jnp.float32

SMEM = pl.BlockSpec(memory_space=pltpu.SMEM)
VMEM = pl.BlockSpec(memory_space=pltpu.VMEM)
FAR = pl.BlockSpec(memory_space=pl.ANY)


def iota(shape, dim):
    return lax.broadcasted_iota(jnp.int32, shape, dim)


def div(values, count):
    if count & (count - 1):
        return values // count
    return values >> (count.bit_length() - 1)


def mod(values, count):
    if count & (count - 1):
        return values % count
    return values & (count - 1)


def ones_where(condition):
    return jnp.where(condition, 1.0, 0.0).astype(BF16)


def matmul(left, right):
    return jnp.dot(left, right, preferred_element_type=F32)


def matmul_t(left, right):
    return lax.dot_general(left, right, (((1,), (1,)), ((), ())), preferred_element_type=F32)


def cut_in_three(values):
    high = values.astype(BF16)
    rest = values - high.astype(F32)
    middle = rest.astype(BF16)
    low = (rest - middle.astype(F32)).astype(BF16)
    return high, middle, low


def exact_rows(rows, product):
    place = iota((16, rows[0].shape[1]), 0)
    stacked = jnp.zeros(place.shape, F32)
    for index, row in enumerate(rows):
        for step, piece in enumerate(cut_in_three(row)):
            stacked = jnp.where(place == 3 * index + step, piece.astype(F32), stacked)
    result = product(stacked.astype(BF16))
    return [
        result[3 * i : 3 * i + 1] + result[3 * i + 1 : 3 * i + 2] + result[3 * i + 2 : 3 * i + 3]
        for i in range(len(rows))
    ]


def silu_slope(values):
    sigmoid = jax.nn.sigmoid(values)
    return sigmoid * (1.0 + values * (1.0 - sigmoid))


def token_rows_of(height):
    return -(-(height // PATCH) // 16) * 16


def to_tokens(pixels):
    channels, columns, height = pixels.shape
    rows = channels * columns
    token_rows = token_rows_of(height)
    flat = pixels.reshape(rows, height)
    width = channels * PATCH * columns
    lane = iota((1, width), 1)
    place = iota((rows, 1), 0)
    mine = place == div(lane, PATCH * columns) * columns + mod(lane, columns)
    in_patch = mod(div(lane, columns), PATCH)
    pixel_row = iota((height, 1), 0)
    token = iota((token_rows, 1), 0)
    tokens = jnp.zeros((token_rows, width), F32)
    for t in range(height // PATCH):
        tiled = matmul(flat, ones_where(pixel_row == in_patch + t * PATCH))
        row = jnp.sum(jnp.where(mine, tiled, 0.0), axis=0, keepdims=True)
        tokens = jnp.where(token == t, row, tokens)
    return tokens.astype(BF16)


def forward_part(tokens, count, bias, gain, load_patch):
    embedded = bias[...]
    for low, high, weight in load_patch():
        embedded = embedded + matmul(tokens[:, low:high], weight)
    centred = embedded - jnp.mean(embedded, axis=1, keepdims=True)
    inv_spread = lax.rsqrt(jnp.mean(centred * centred, axis=1, keepdims=True) + eps_norm)
    normed = centred * inv_spread
    weighted = normed * gain[...]
    inside = iota((tokens.shape[0], 1), 0) < count
    pooled = jnp.sum(jnp.where(inside, weighted, 0.0), axis=0, keepdims=True)
    return normed, inv_spread, pooled


def message_shape(devices):
    return jax.ShapeDtypeStruct((devices, 4, LANES), F32)


def write_windows(patch_grad, sums, own_rows, height, send):
    span = PATCH * PATCH
    line = jnp.concatenate(
        [
            jnp.concatenate([patch_grad[t : t + 1, k * span : (k + 1) * span] for t in range(height // PATCH)], axis=1)
            for k in range(3)
        ]
        + [jnp.zeros((1, height * PATCH), F32)],
        axis=0,
    )
    line = jnp.concatenate([jnp.zeros((4, LANES), F32), line, jnp.zeros((4, LANES), F32)], axis=1)
    used = iota((4, LANES), 1) < (own_rows + 4) * PATCH
    colour = iota((4, LANES), 0)
    for d in range(send.shape[0]):
        start = LANES + (d * own_rows - 2) * PATCH
        window = jnp.where(used, line[:, start : start + LANES], 0.0)
        send[d] = jnp.where(colour < 3, window, sums[:4])


def channel_sums(hidden):
    values = hidden.reshape(-1, hidden.shape[-1]).astype(F32)
    return jnp.sum(values, axis=0, keepdims=True), jnp.sum(values * values, axis=0, keepdims=True)


def over_group(values, size):
    lane = iota(values.shape, 1)
    lanes = values.shape[1]
    step = 1
    while step < size:
        later = pltpu.roll(values, lanes - step, 1)
        earlier = pltpu.roll(values, step, 1)
        values = values + jnp.where((lane & step) == 0, later, earlier)
        step *= 2
    return values


def group_sums(hidden):
    channels = hidden.shape[-1]
    size = channels // GROUPS
    first, second = [
        over_group(jnp.broadcast_to(x, (8, channels)), size) for x in channel_sums(hidden)
    ]
    lane = mod(iota((8, channels), 1), size)
    return jnp.where(lane == 0, first, jnp.where(lane == 1, second, 0.0))


def backward_part(
    owner, picks, gain, head_bias, head_out, normed, inv_spread, pooled, weight, head, slot, own_rows, height, sums, send
):
    (before,) = exact_rows([pooled], lambda rows: matmul(rows, head[...]))
    slope = head_out[...] * silu_slope(before + head_bias[...])
    (pulled,) = exact_rows([slope], lambda rows: matmul_t(rows, head[...]))
    wanted = owner[slot]
    picked = jnp.int32(0)
    for k in range(picks.shape[0]):
        picked = picked + jnp.where(picks[k] == wanted, 1, 0)
    scaled = gain[...] * (picked.astype(F32) * pulled)
    token_grad = inv_spread * (
        scaled
        - jnp.mean(scaled, axis=1, keepdims=True)
        - normed * jnp.mean(scaled * normed, axis=1, keepdims=True)
    )
    patch_grad = matmul_t(token_grad.astype(BF16), weight[...]).astype(BF16).astype(F32)
    write_windows(patch_grad, sums, own_rows, height, send)


def write_edges(place, hidden, across, along):
    last = hidden.shape[0] - 1
    even = place[0] % 2 == 0
    across[0] = hidden[jnp.where(even, last, 0)]
    along[0] = hidden[jnp.where(even, 0, last)]


def reward_kernel(place, *refs):
    count = 8
    far, send, across, along = refs[: count + 2], refs[count + 2], refs[count + 3], refs[count + 4]
    near, sems = refs[count + 5 : 2 * count + 7], refs[-1]
    frames, bias, gain, owner, picks, head_bias, head_out, hidden, patch, head = near
    depth, depths = 256, (128, 256)
    small = [pltpu.make_async_copy(far[i], near[i], sems.at[i]) for i in range(count)]
    pieces = []
    used = count
    for index, rows in enumerate(depths):
        source, target = far[count + index], near[count + index]
        parts = []
        for low in range(0, target.shape[0], rows):
            part = pl.ds(low, rows)
            parts.append(pltpu.make_async_copy(source.at[part], target.at[part], sems.at[used]))
            used += 1
        pieces.append(parts)
    for copy in small[:2] + pieces[0] + small[2:7] + pieces[1] + small[7:]:
        copy.start()

    def load_patch():
        for low in range(0, patch.shape[0], depth):
            for copy in pieces[0][low // depths[0] : (low + depth) // depths[0]]:
                copy.wait()
            yield low, low + depth, patch[low : low + depth, :]

    height = frames.shape[2]
    patches = height // PATCH
    small[0].wait()
    tokens = to_tokens(frames[...])
    small[1].wait()
    small[2].wait()
    normed, inv_spread, pooled = forward_part(tokens, patches, bias, gain, load_patch)
    for copy in small[3:] + pieces[1]:
        copy.wait()
    write_edges(place, hidden, across, along)
    backward_part(
        owner,
        picks,
        gain,
        head_bias,
        head_out,
        normed,
        inv_spread,
        pooled / patches,
        patch,
        head,
        place[0],
        hidden.shape[0],
        height,
        group_sums(hidden[...]),
        send,
    )


def forward_kernel(frames, bias, gain, patch, normed, inv_spread, pooled):
    width = patch.shape[0]
    tokens = to_tokens(frames[...])
    normed[...], spread, pooled[...] = forward_part(
        tokens, frames.shape[2] // PATCH, bias, gain, lambda: [(0, width, patch[...])]
    )
    inv_spread[...] = jnp.broadcast_to(spread, inv_spread.shape)


def backward_kernel(
    owner,
    picks,
    place,
    hidden,
    gain,
    head_bias,
    head_out,
    normed,
    inv_spread,
    pooled,
    patch,
    head,
    send,
    across,
    along,
    *,
    height,
    per_frame,
):
    write_edges(place, hidden, across, along)
    backward_part(
        owner,
        picks,
        gain,
        head_bias,
        head_out,
        normed[...],
        inv_spread[...][:, :1],
        pooled[...],
        patch,
        head,
        place[0] // per_frame,
        hidden.shape[0],
        height,
        group_sums(hidden[...]),
        send,
    )


def params(cells):
    return pltpu.CompilerParams(vmem_limit_bytes=min(16 + cells // 64, 48) * 1024 * 1024)


def near(array):
    return pltpu.with_memory_space_constraint(array, pltpu.VMEM)


def far(array):
    return pltpu.with_memory_space_constraint(array, pltpu.HBM)


def prepare_kernel(far_weight, *refs):
    count = (len(refs) - 4) // 2
    fars, wide, nears = refs[:count], refs[count], refs[count + 1 : 2 * count + 1]
    out_weight, scratch, sems = refs[2 * count + 1 :]
    copies = [pltpu.make_async_copy(far_weight, out_weight, sems.at[count])]
    copies += [pltpu.make_async_copy(fars[i], nears[i], sems.at[i]) for i in range(count)]
    for copy in copies:
        copy.start()
    block = scratch.shape[0] // 3
    amount = scratch.shape[1] // LANES
    span = 3 * (amount + 2)
    scratch[...] = jnp.zeros_like(scratch)
    copies[0].wait()
    for a in range(3):
        for e in range(3):
            for b in range(3):
                piece = out_weight[a, b, e].astype(F32)
                for i in range(amount):
                    start = a * block + e * span + 3 * (i - b + 2)
                    scratch[start : start + 3, i * LANES : (i + 1) * LANES] = piece
    wide[...] = scratch[...].astype(BF16)
    for copy in copies[1:]:
        copy.wait()


def norm_constants(totals, cell_total):
    channels = totals.shape[1]
    size = channels // GROUPS
    totals = jnp.broadcast_to(totals, (8, channels))
    lane = mod(iota((8, channels), 1), size)
    first, second = [over_group(jnp.where(lane == i, totals, 0.0), size)[:1] for i in range(2)]
    mean = first / cell_total
    return mean, lax.rsqrt(second / cell_total - mean * mean + eps_norm)


def norm_slopes(state, mean, inverse, gain, shift):
    normed = (state - mean) * inverse
    return normed, silu_slope(normed * gain + shift) * gain


def slope_kernel(
    owner, arrived, hidden, gain, shift, wide, direct, edge_slopes, stats, sums, slopes_own, received
):
    devices, message_rows, _ = arrived.shape
    own_rows, frame_count, width, channels = hidden.shape
    cells = frame_count * width
    per_frame = devices // frame_count
    received[...] = arrived[...].reshape(received.shape)

    def from_all(row):
        return received[pl.ds(row, devices, stride=message_rows), :]

    totals = jnp.sum(from_all(3), axis=0, keepdims=True)
    mean, inverse = norm_constants(totals, own_rows * devices * cells * (channels // GROUPS))
    for i in range(own_rows):
        state = hidden[i].reshape(cells, channels).astype(F32)
        slopes_own[i] = norm_slopes(state, mean, inverse, gain[...], shift[...])[1]

    lines = jnp.concatenate([from_all(k) for k in range(3)], axis=1).astype(BF16)
    source = iota((1, devices), 1)
    home = jnp.zeros((1, devices), jnp.int32)
    for b in range(frame_count):
        home = jnp.where(div(source, per_frame) == b, owner[b] * per_frame, home)
    home = home + mod(source, per_frame)
    cell = iota((cells, 1), 0)
    column = mod(cell, width)
    frame_strip = div(cell, width) * per_frame
    lane = mod(iota((1, 3 * LANES), 1), PATCH)
    kept = []
    placed = None
    for e in range(3):
        wanted = column - e + 1
        if per_frame > 1 or placed is None:
            strip = frame_strip + div(wanted, PATCH) if per_frame > 1 else frame_strip
            placed = matmul(ones_where(home == strip), lines)
        inside = jnp.where((wanted >= 0) & (wanted < width), mod(wanted, PATCH), -1)
        kept.append(jnp.where(lane == inside, placed, 0.0).astype(BF16))
    block = wide.shape[0] // 3
    span = 3 * (own_rows + 4)
    entry = iota((3 * LANES, 1), 0)
    entry = div(mod(entry, LANES), PATCH) * 3 + div(entry, LANES)
    entry = jnp.where(entry < span, entry, -3 * span)
    tap = iota((1, block), 1)
    folds = jnp.concatenate([ones_where(tap == entry + e * span) for e in range(3)], axis=0)
    taps = matmul(jnp.concatenate(kept, axis=1), folds).astype(BF16)
    later = []
    for a in range(3):
        skip = (2 - a) * width
        later.append(
            jnp.concatenate([taps[skip:], jnp.zeros((skip, block), BF16)], axis=0) if skip else taps
        )
    result = matmul(jnp.concatenate(later, axis=1), wide[...])

    first = jnp.zeros((1, channels), F32)
    second = jnp.zeros((1, channels), F32)
    for i in range(own_rows):
        state = hidden[i].reshape(cells, channels).astype(F32)
        up = result[:, (i + 1) * channels : (i + 2) * channels] * slopes_own[i]
        direct[i] = up * inverse
        first = first + jnp.sum(up, axis=0, keepdims=True)
        second = second + jnp.sum(up * ((state - mean) * inverse), axis=0, keepdims=True)
    edge_slopes[0] = result[:, :channels]
    edge_slopes[1] = result[:, (own_rows + 1) * channels :]
    stats[0:1, :] = mean
    stats[1:2, :] = inverse
    both = jnp.where(iota((2, channels), 0) == 0, first, second)
    sums[...] = jnp.broadcast_to(both[None], sums.shape)


def late_kernel(
    place, across, along, slopes, stats, gain, shift, far_weight, direct, states, turned, inner_weight, sem
):
    copy = pltpu.make_async_copy(far_weight, inner_weight, sem.at[0])
    copy.start()
    cells, channels = slopes.shape[1:]
    odd = place[0] % 2 == 1
    mean = stats[0:1, :]
    inverse = stats[1:2, :]
    for i in range(2):
        state = jnp.where(odd == (i == 0), across[0], along[0])
        states[i] = state
        values = state.reshape(cells, channels).astype(F32)
        direct[i] = slopes[i] * norm_slopes(values, mean, inverse, gain[...], shift[...])[1] * inverse
    copy.wait()
    size = inner_weight.shape[3]
    for b in range(3):
        for a in range(3):
            for e in range(3):
                at = (a * 3 + e) * size
                turned[at : at + size, b * size : (b + 1) * size] = inner_weight[a, b, e].T


def inner_kernel(
    place, arrived, stats, direct, hidden, edge_direct, edge_states, turned, far_out, padded, out, sems, *, devices
):
    own_rows, frame_count, width, channels = out.shape
    cells = frame_count * width
    totals = jnp.sum(arrived[...], axis=0)
    cell_total = own_rows * devices * cells * (channels // GROUPS)
    place_row = iota((8, channels), 0)
    both = jnp.where(place_row == 0, totals[0:1], totals[1:2])
    both = over_group(both, channels // GROUPS)
    first, second = both[0:1], both[1:2]
    mean = stats[0:1, :]
    inverse = stats[1:2, :]
    constant = first / cell_total * inverse
    factor = second / cell_total * inverse * inverse
    position = place[0]
    in_frame = mod(iota((cells, 1), 0), width)
    for i in range(own_rows + 2):
        if 0 < i < own_rows + 1:
            state, part = hidden[i - 1], direct[i - 1]
        else:
            state, part = edge_states[min(i, 1)], edge_direct[min(i, 1)]
        grad = part - constant - (state.reshape(cells, channels).astype(F32) - mean) * factor
        if i == 0:
            grad = jnp.where(position > 0, grad, 0.0)
        if i == own_rows + 1:
            grad = jnp.where(position < devices - 1, grad, 0.0)
        after = jnp.where(in_frame < width - 1, pltpu.roll(grad, cells - 1, 0), 0.0)
        prior = jnp.where(in_frame > 0, pltpu.roll(grad, 1, 0), 0.0)
        padded[i, :cells, 0:channels] = after.astype(BF16)
        padded[i, :cells, channels : 2 * channels] = grad.astype(BF16)
        padded[i, :cells, 2 * channels :] = prior.astype(BF16)
        padded[i, cells:, :] = jnp.zeros((2 * width, 3 * channels), BF16)
    results = [jnp.zeros((cells, channels), F32) for _ in range(own_rows)]
    copies = []
    for i in range(own_rows + 2):
        joined = jnp.concatenate(
            [padded[i, (2 - a) * width : (2 - a) * width + cells, :] for a in range(3)], axis=1
        )
        taps = [b for b in range(3) if 0 <= i + b - 2 < own_rows]
        for low in range(0, len(taps), 2):
            some = taps[low : low + 2]
            product = matmul(joined, turned[:, some[0] * channels : (some[-1] + 1) * channels])
            for step, b in enumerate(some):
                results[i + b - 2] = results[i + b - 2] + product[:, step * channels : (step + 1) * channels]
        if i >= 2:
            out[i - 2] = results[i - 2].reshape(frame_count, width, channels).astype(BF16)
            copies.append(pltpu.make_async_copy(out.at[i - 2], far_out.at[i - 2], sems.at[i - 2]))
            copies[-1].start()
    for copy in copies:
        copy.wait()


def per_device(
    frames,
    frame_owner,
    picks,
    patch_weight,
    patch_bias,
    norm_gain,
    head_weight,
    head_bias,
    head_out,
    hidden_state,
    group_gain,
    group_shift,
    out_weight,
    inner_weight,
):
    devices = lax.axis_size("row")
    position = lax.axis_index("row").astype(jnp.int32).reshape(1)
    per_frame = devices // FRAMES
    height = frames.shape[1]
    own_rows, _, frame_width, channels = hidden_state.shape
    cells = FRAMES * frame_width
    width = patch_weight.shape[1]
    turned_frames = jnp.transpose(frames, (0, 2, 1))
    bias = patch_bias.reshape(1, width)
    gain = norm_gain.reshape(1, width)
    head_bias_row = head_bias.reshape(1, width)
    head_out_row = head_out.reshape(1, width)
    state_rows = own_rows + 2
    tap_rows = -(-9 * (own_rows + 4) // LANES) * LANES
    edge = jax.ShapeDtypeStruct((1,) + hidden_state.shape[1:], BF16)
    message = (message_shape(devices), edge, edge)
    gain_row = group_gain.reshape(1, channels)
    shift_row = group_shift.reshape(1, channels)
    early = [hidden_state, gain_row, shift_row]
    wide, *early = pl.pallas_call(
        prepare_kernel,
        out_shape=(
            pltpu.VMEM((3 * tap_rows, state_rows * channels), BF16),
            *[pltpu.VMEM(x.shape, x.dtype) for x in early],
        ),
        in_specs=[FAR] * (1 + len(early)),
        scratch_shapes=[
            pltpu.VMEM(out_weight.shape, BF16),
            pltpu.VMEM((3 * tap_rows, state_rows * channels), F32),
            pltpu.SemaphoreType.DMA((1 + len(early),)),
        ],
        compiler_params=params(cells),
        name="prepare",
    )(far(out_weight), *[far(x) for x in early])
    early = [near(x) for x in early]
    slope_outs = (
        pltpu.VMEM((own_rows, cells, channels), F32),
        pltpu.VMEM((2, cells, channels), F32),
        pltpu.VMEM((8, channels), F32),
        jax.ShapeDtypeStruct((devices, 2, channels), F32),
    )
    if per_frame == 1:
        arrays = [
            turned_frames,
            bias,
            gain,
            frame_owner,
            picks,
            head_bias_row,
            head_out_row,
            hidden_state,
            patch_weight,
            head_weight,
        ]
        send, across, along = pl.pallas_call(
            reward_kernel,
            out_shape=message,
            in_specs=[SMEM] + [FAR] * len(arrays),
            out_specs=[VMEM] * 3,
            scratch_shapes=[
                (pltpu.SMEM if x.dtype == jnp.int32 else pltpu.VMEM)(x.shape, x.dtype) for x in arrays
            ]
            + [pltpu.SemaphoreType.DMA((len(arrays) + 16,))],
            compiler_params=params(0),
            name="reward",
        )(position, *[far(x) for x in arrays])
    else:
        count = height // PATCH
        normed, inv_spread, partial = pl.pallas_call(
            forward_kernel,
            out_shape=(
                jax.ShapeDtypeStruct((token_rows_of(height), width), F32),
                jax.ShapeDtypeStruct((token_rows_of(height), LANES), F32),
                jax.ShapeDtypeStruct((1, width), F32),
            ),
            compiler_params=params(cells),
            name="reward_forward",
        )(turned_frames, bias, gain, patch_weight)
        members = [[b * per_frame + i for i in range(per_frame)] for b in range(FRAMES)]
        pooled = lax.psum(partial, "row", axis_index_groups=members) / (count * per_frame)
        send, across, along = pl.pallas_call(
            functools.partial(backward_kernel, height=height, per_frame=per_frame),
            out_shape=message,
            in_specs=[SMEM] * 3 + [VMEM] * 9,
            out_specs=[VMEM] * 3,
            compiler_params=params(cells),
            name="reward_backward",
        )(
            frame_owner,
            picks,
            position,
            hidden_state,
            gain,
            head_bias_row,
            head_out_row,
            normed,
            inv_spread,
            pooled,
            patch_weight,
            head_weight,
        )
    arrived = lax.all_to_all(send, "row", 0, 0, tiled=True)
    direct, edge_slopes, stats, sums = pl.pallas_call(
        slope_kernel,
        out_shape=slope_outs,
        in_specs=[SMEM] + [VMEM] * 5,
        scratch_shapes=[
            pltpu.VMEM((own_rows, cells, channels), F32),
            pltpu.VMEM((4 * devices, LANES), F32),
        ],
        compiler_params=params(cells),
        name="slope",
    )(frame_owner, near(arrived), *early, near(wide))
    swaps = [(2 * i, 2 * i + 1) for i in range(devices // 2)]
    across = lax.ppermute(across, "row", swaps + [(b, a) for a, b in swaps])
    swaps = [(2 * i - 1, 2 * i) for i in range(1, devices // 2)]
    along = lax.ppermute(along, "row", swaps + [(b, a) for a, b in swaps])
    summed = lax.all_to_all(sums, "row", 0, 0, tiled=True)
    edge_direct, edge_states, turned = pl.pallas_call(
        late_kernel,
        out_shape=(
            pltpu.VMEM((2, cells, channels), F32),
            pltpu.VMEM((2,) + hidden_state.shape[1:], BF16),
            pltpu.VMEM((9 * channels, 3 * channels), BF16),
        ),
        in_specs=[SMEM] + [VMEM] * 6 + [FAR],
        scratch_shapes=[pltpu.VMEM(inner_weight.shape, BF16), pltpu.SemaphoreType.DMA((1,))],
        input_output_aliases={3: 0},
        compiler_params=params(cells),
        name="late",
    )(position, near(across), near(along), near(edge_slopes), near(stats), *early[1:3], far(inner_weight))
    return pl.pallas_call(
        functools.partial(inner_kernel, devices=devices),
        out_shape=jax.ShapeDtypeStruct(hidden_state.shape, BF16),
        in_specs=[SMEM] + [VMEM] * 7,
        out_specs=FAR,
        scratch_shapes=[
            pltpu.VMEM((own_rows + 2, cells + 2 * frame_width, 3 * channels), BF16),
            pltpu.VMEM(hidden_state.shape, BF16),
            pltpu.SemaphoreType.DMA((own_rows,)),
        ],
        compiler_params=params(cells),
        name="inner",
    )(
        position,
        near(summed),
        near(stats),
        near(direct),
        early[0],
        near(edge_direct),
        near(edge_states),
        near(turned),
    )


def solution(mesh):
    return jax.shard_map(
        per_device,
        mesh=mesh,
        in_specs=(
            P(None, None, ("clip", "row")),
            P("clip"),
            P("clip"),
            P(),
            P(),
            P(),
            P(),
            P(),
            P(),
            P(("clip", "row"), None, None, None),
            P(),
            P(),
            P(),
            P(),
        ),
        out_specs=P(("clip", "row"), None, None, None),
        check_vma=False,
    )
```

```python
import functools

import jax
import jax.numpy as jnp
from jax import lax
from jax.experimental import pallas as pl
from jax.experimental.pallas import tpu as pltpu
from jax.sharding import PartitionSpec as P

PATCH = 16
GROUPS = 32
FRAMES = 16
LANES = 128
SLOTS = LANES // PATCH
eps_norm = 1e-06
BF16 = jnp.bfloat16
F32 = jnp.float32

SMEM = pl.BlockSpec(memory_space=pltpu.SMEM)
VMEM = pl.BlockSpec(memory_space=pltpu.VMEM)
FAR = pl.BlockSpec(memory_space=pl.ANY)


def iota(shape, dim):
    return lax.broadcasted_iota(jnp.int32, shape, dim)


def div(values, count):
    if count & (count - 1):
        return values // count
    return values >> (count.bit_length() - 1)


def mod(values, count):
    if count & (count - 1):
        return values % count
    return values & (count - 1)


def ones_where(condition):
    return jnp.where(condition, 1.0, 0.0).astype(BF16)


def matmul(left, right):
    return jnp.dot(left, right, preferred_element_type=F32)


def matmul_t(left, right):
    return lax.dot_general(left, right, (((1,), (1,)), ((), ())), preferred_element_type=F32)


def cut_in_three(values):
    high = values.astype(BF16)
    rest = values - high.astype(F32)
    middle = rest.astype(BF16)
    low = (rest - middle.astype(F32)).astype(BF16)
    return high, middle, low


def exact_rows(rows, product):
    place = iota((16, rows[0].shape[1]), 0)
    stacked = jnp.zeros(place.shape, F32)
    for index, row in enumerate(rows):
        for step, piece in enumerate(cut_in_three(row)):
            stacked = jnp.where(place == 3 * index + step, piece.astype(F32), stacked)
    result = product(stacked.astype(BF16))
    return [
        result[3 * i : 3 * i + 1] + result[3 * i + 1 : 3 * i + 2] + result[3 * i + 2 : 3 * i + 3]
        for i in range(len(rows))
    ]


def silu_slope(values):
    sigmoid = jax.nn.sigmoid(values)
    return sigmoid * (1.0 + values * (1.0 - sigmoid))


def token_rows_of(height):
    return -(-(height // PATCH) // 16) * 16


def to_tokens(pixels):
    channels, columns, height = pixels.shape
    rows = channels * columns
    token_rows = token_rows_of(height)
    flat = pixels.reshape(rows, height)
    width = channels * PATCH * columns
    lane = iota((1, width), 1)
    place = iota((rows, 1), 0)
    mine = place == div(lane, PATCH * columns) * columns + mod(lane, columns)
    in_patch = mod(div(lane, columns), PATCH)
    pixel_row = iota((height, 1), 0)
    token = iota((token_rows, 1), 0)
    tokens = jnp.zeros((token_rows, width), F32)
    for t in range(height // PATCH):
        tiled = matmul(flat, ones_where(pixel_row == in_patch + t * PATCH))
        row = jnp.sum(jnp.where(mine, tiled, 0.0), axis=0, keepdims=True)
        tokens = jnp.where(token == t, row, tokens)
    return tokens.astype(BF16)


def forward_part(tokens, count, bias, gain, load_patch):
    embedded = bias[...]
    for low, high, weight in load_patch():
        embedded = embedded + matmul(tokens[:, low:high], weight)
    centred = embedded - jnp.mean(embedded, axis=1, keepdims=True)
    inv_spread = lax.rsqrt(jnp.mean(centred * centred, axis=1, keepdims=True) + eps_norm)
    normed = centred * inv_spread
    weighted = normed * gain[...]
    inside = iota((tokens.shape[0], 1), 0) < count
    pooled = jnp.sum(jnp.where(inside, weighted, 0.0), axis=0, keepdims=True)
    return normed, inv_spread, pooled


def message_shape(devices):
    return jax.ShapeDtypeStruct((devices, 4, LANES), F32)


def write_windows(patch_grad, sums, own_rows, height, send):
    span = PATCH * PATCH
    line = jnp.concatenate(
        [
            jnp.concatenate([patch_grad[t : t + 1, k * span : (k + 1) * span] for t in range(height // PATCH)], axis=1)
            for k in range(3)
        ]
        + [jnp.zeros((1, height * PATCH), F32)],
        axis=0,
    )
    line = jnp.concatenate([jnp.zeros((4, LANES), F32), line, jnp.zeros((4, LANES), F32)], axis=1)
    used = iota((4, LANES), 1) < (own_rows + 4) * PATCH
    colour = iota((4, LANES), 0)
    for d in range(send.shape[0]):
        start = LANES + (d * own_rows - 2) * PATCH
        window = jnp.where(used, line[:, start : start + LANES], 0.0)
        send[d] = jnp.where(colour < 3, window, sums[:4])


def channel_sums(hidden):
    values = hidden.reshape(-1, hidden.shape[-1]).astype(F32)
    return jnp.sum(values, axis=0, keepdims=True), jnp.sum(values * values, axis=0, keepdims=True)


def over_group(values, size):
    lane = iota(values.shape, 1)
    lanes = values.shape[1]
    step = 1
    while step < size:
        later = pltpu.roll(values, lanes - step, 1)
        earlier = pltpu.roll(values, step, 1)
        values = values + jnp.where((lane & step) == 0, later, earlier)
        step *= 2
    return values


def group_sums(hidden):
    channels = hidden.shape[-1]
    size = channels // GROUPS
    first, second = [
        over_group(jnp.broadcast_to(x, (8, channels)), size) for x in channel_sums(hidden)
    ]
    lane = mod(iota((8, channels), 1), size)
    return jnp.where(lane == 0, first, jnp.where(lane == 1, second, 0.0))


def pull_back(row, weight):
    parts = []
    for low in range(0, weight.shape[0], LANES):
        product = weight[low : low + LANES, :].astype(F32) * row
        folded = product[:, :LANES]
        for start in range(LANES, weight.shape[1], LANES):
            folded = folded + product[:, start : start + LANES]
        parts.append(jnp.sum(folded.T, axis=0, keepdims=True))
    return jnp.concatenate(parts, axis=1)


def backward_part(
    owner, picks, gain, head_bias, head_out, normed, inv_spread, pooled, weight, head, slot, own_rows, height, sums, send
):
    (before,) = exact_rows([pooled], lambda rows: matmul(rows, head[...]))
    slope = head_out[...] * silu_slope(before + head_bias[...])
    pulled = pull_back(slope, head)
    wanted = owner[slot]
    picked = jnp.int32(0)
    for k in range(picks.shape[0]):
        picked = picked + jnp.where(picks[k] == wanted, 1, 0)
    scaled = gain[...] * (picked.astype(F32) * pulled)
    token_grad = inv_spread * (
        scaled
        - jnp.mean(scaled, axis=1, keepdims=True)
        - normed * jnp.mean(scaled * normed, axis=1, keepdims=True)
    )
    patch_grad = matmul_t(token_grad.astype(BF16), weight[...]).astype(BF16).astype(F32)
    write_windows(patch_grad, sums, own_rows, height, send)


def write_edges(place, hidden, across, along):
    last = hidden.shape[0] - 1
    even = place[0] % 2 == 0
    across[0] = hidden[jnp.where(even, last, 0)]
    along[0] = hidden[jnp.where(even, 0, last)]


def reward_kernel(place, *refs):
    count = 8
    far, send, across, along = refs[: count + 2], refs[count + 2], refs[count + 3], refs[count + 4]
    near, sems = refs[count + 5 : 2 * count + 7], refs[-1]
    frames, bias, gain, owner, picks, head_bias, head_out, hidden, patch, head = near
    depth, depths = 256, (128, 256)
    small = [pltpu.make_async_copy(far[i], near[i], sems.at[i]) for i in range(count)]
    pieces = []
    used = count
    for index, rows in enumerate(depths):
        source, target = far[count + index], near[count + index]
        parts = []
        for low in range(0, target.shape[0], rows):
            part = pl.ds(low, rows)
            parts.append(pltpu.make_async_copy(source.at[part], target.at[part], sems.at[used]))
            used += 1
        pieces.append(parts)
    for copy in small[:2] + pieces[0] + small[2:7] + pieces[1] + small[7:]:
        copy.start()

    def load_patch():
        for low in range(0, patch.shape[0], depth):
            for copy in pieces[0][low // depths[0] : (low + depth) // depths[0]]:
                copy.wait()
            yield low, low + depth, patch[low : low + depth, :]

    height = frames.shape[2]
    patches = height // PATCH
    small[0].wait()
    tokens = to_tokens(frames[...])
    small[1].wait()
    small[2].wait()
    normed, inv_spread, pooled = forward_part(tokens, patches, bias, gain, load_patch)
    for copy in small[3:] + pieces[1]:
        copy.wait()
    write_edges(place, hidden, across, along)
    backward_part(
        owner,
        picks,
        gain,
        head_bias,
        head_out,
        normed,
        inv_spread,
        pooled / patches,
        patch,
        head,
        place[0],
        hidden.shape[0],
        height,
        group_sums(hidden[...]),
        send,
    )


def forward_kernel(frames, bias, gain, patch, normed, inv_spread, pooled):
    width = patch.shape[0]
    tokens = to_tokens(frames[...])
    normed[...], spread, pooled[...] = forward_part(
        tokens, frames.shape[2] // PATCH, bias, gain, lambda: [(0, width, patch[...])]
    )
    inv_spread[...] = jnp.broadcast_to(spread, inv_spread.shape)


def backward_kernel(
    owner,
    picks,
    place,
    hidden,
    gain,
    head_bias,
    head_out,
    normed,
    inv_spread,
    pooled,
    patch,
    head,
    send,
    across,
    along,
    *,
    height,
    per_frame,
):
    write_edges(place, hidden, across, along)
    backward_part(
        owner,
        picks,
        gain,
        head_bias,
        head_out,
        normed[...],
        inv_spread[...][:, :1],
        pooled[...],
        patch,
        head,
        place[0] // per_frame,
        hidden.shape[0],
        height,
        group_sums(hidden[...]),
        send,
    )


def params(cells):
    return pltpu.CompilerParams(vmem_limit_bytes=min(16 + cells // 64, 48) * 1024 * 1024)


def near(array):
    return pltpu.with_memory_space_constraint(array, pltpu.VMEM)


def far(array):
    return pltpu.with_memory_space_constraint(array, pltpu.HBM)


def prepare_kernel(far_weight, *refs):
    count = (len(refs) - 4) // 2
    fars, wide, nears = refs[:count], refs[count], refs[count + 1 : 2 * count + 1]
    out_weight, scratch, sems = refs[2 * count + 1 :]
    copies = [pltpu.make_async_copy(far_weight, out_weight, sems.at[count])]
    copies += [pltpu.make_async_copy(fars[i], nears[i], sems.at[i]) for i in range(count)]
    for copy in copies:
        copy.start()
    block = scratch.shape[0] // 3
    amount = scratch.shape[1] // LANES
    span = 3 * (amount + 2)
    scratch[...] = jnp.zeros_like(scratch)
    copies[0].wait()
    for a in range(3):
        for e in range(3):
            for b in range(3):
                piece = out_weight[a, b, e].astype(F32)
                for i in range(amount):
                    start = a * block + e * span + 3 * (i - b + 2)
                    scratch[start : start + 3, i * LANES : (i + 1) * LANES] = piece
    wide[...] = scratch[...].astype(BF16)
    for copy in copies[1:]:
        copy.wait()


def norm_constants(totals, cell_total):
    channels = totals.shape[1]
    size = channels // GROUPS
    totals = jnp.broadcast_to(totals, (8, channels))
    lane = mod(iota((8, channels), 1), size)
    first, second = [over_group(jnp.where(lane == i, totals, 0.0), size)[:1] for i in range(2)]
    mean = first / cell_total
    return mean, lax.rsqrt(second / cell_total - mean * mean + eps_norm)


def norm_slopes(state, mean, inverse, gain, shift):
    normed = (state - mean) * inverse
    return normed, silu_slope(normed * gain + shift) * gain


def slope_kernel(
    owner, arrived, hidden, gain, shift, wide, direct, edge_slopes, stats, sums, slopes_own, received
):
    devices, message_rows, _ = arrived.shape
    own_rows, frame_count, width, channels = hidden.shape
    cells = frame_count * width
    per_frame = devices // frame_count
    received[...] = arrived[...].reshape(received.shape)

    def from_all(row):
        return received[pl.ds(row, devices, stride=message_rows), :]

    totals = jnp.sum(from_all(3), axis=0, keepdims=True)
    mean, inverse = norm_constants(totals, own_rows * devices * cells * (channels // GROUPS))
    for i in range(own_rows):
        state = hidden[i].reshape(cells, channels).astype(F32)
        slopes_own[i] = norm_slopes(state, mean, inverse, gain[...], shift[...])[1]

    lines = jnp.concatenate([from_all(k) for k in range(3)], axis=1).astype(BF16)
    source = iota((1, devices), 1)
    home = jnp.zeros((1, devices), jnp.int32)
    for b in range(frame_count):
        home = jnp.where(div(source, per_frame) == b, owner[b] * per_frame, home)
    home = home + mod(source, per_frame)
    cell = iota((cells, 1), 0)
    column = mod(cell, width)
    frame_strip = div(cell, width) * per_frame
    lane = mod(iota((1, 3 * LANES), 1), PATCH)
    kept = []
    placed = None
    for e in range(3):
        wanted = column - e + 1
        if per_frame > 1 or placed is None:
            strip = frame_strip + div(wanted, PATCH) if per_frame > 1 else frame_strip
            placed = matmul(ones_where(home == strip), lines)
        inside = jnp.where((wanted >= 0) & (wanted < width), mod(wanted, PATCH), -1)
        kept.append(jnp.where(lane == inside, placed, 0.0).astype(BF16))
    block = wide.shape[0] // 3
    span = 3 * (own_rows + 4)
    entry = iota((3 * LANES, 1), 0)
    entry = div(mod(entry, LANES), PATCH) * 3 + div(entry, LANES)
    entry = jnp.where(entry < span, entry, -3 * span)
    tap = iota((1, block), 1)
    folds = jnp.concatenate([ones_where(tap == entry + e * span) for e in range(3)], axis=0)
    taps = matmul(jnp.concatenate(kept, axis=1), folds).astype(BF16)
    later = []
    for a in range(3):
        skip = (2 - a) * width
        later.append(
            jnp.concatenate([taps[skip:], jnp.zeros((skip, block), BF16)], axis=0) if skip else taps
        )
    result = matmul(jnp.concatenate(later, axis=1), wide[...])

    first = jnp.zeros((1, channels), F32)
    second = jnp.zeros((1, channels), F32)
    for i in range(own_rows):
        state = hidden[i].reshape(cells, channels).astype(F32)
        up = result[:, (i + 1) * channels : (i + 2) * channels] * slopes_own[i]
        direct[i] = up * inverse
        first = first + jnp.sum(up, axis=0, keepdims=True)
        second = second + jnp.sum(up * ((state - mean) * inverse), axis=0, keepdims=True)
    edge_slopes[0] = result[:, :channels]
    edge_slopes[1] = result[:, (own_rows + 1) * channels :]
    stats[0:1, :] = mean
    stats[1:2, :] = inverse
    both = jnp.where(iota((2, channels), 0) == 0, first, second)
    sums[...] = jnp.broadcast_to(both[None], sums.shape)


def late_kernel(
    place, across, along, slopes, stats, gain, shift, far_weight, direct, states, turned, inner_weight, sem
):
    copy = pltpu.make_async_copy(far_weight, inner_weight, sem.at[0])
    copy.start()
    cells, channels = slopes.shape[1:]
    odd = place[0] % 2 == 1
    mean = stats[0:1, :]
    inverse = stats[1:2, :]
    for i in range(2):
        state = jnp.where(odd == (i == 0), across[0], along[0])
        states[i] = state
        values = state.reshape(cells, channels).astype(F32)
        direct[i] = slopes[i] * norm_slopes(values, mean, inverse, gain[...], shift[...])[1] * inverse
    copy.wait()
    size = inner_weight.shape[3]
    for b in range(3):
        for a in range(3):
            for e in range(3):
                at = (a * 3 + e) * size
                turned[at : at + size, b * size : (b + 1) * size] = inner_weight[a, b, e].T


def inner_kernel(
    place, arrived, stats, direct, hidden, edge_direct, edge_states, turned, far_out, padded, out, sems, *, devices
):
    own_rows, frame_count, width, channels = out.shape
    cells = frame_count * width
    totals = jnp.sum(arrived[...], axis=0)
    cell_total = own_rows * devices * cells * (channels // GROUPS)
    place_row = iota((8, channels), 0)
    both = jnp.where(place_row == 0, totals[0:1], totals[1:2])
    both = over_group(both, channels // GROUPS)
    first, second = both[0:1], both[1:2]
    mean = stats[0:1, :]
    inverse = stats[1:2, :]
    constant = first / cell_total * inverse
    factor = second / cell_total * inverse * inverse
    position = place[0]
    in_frame = mod(iota((cells, 1), 0), width)
    for i in range(own_rows + 2):
        if 0 < i < own_rows + 1:
            state, part = hidden[i - 1], direct[i - 1]
        else:
            state, part = edge_states[min(i, 1)], edge_direct[min(i, 1)]
        grad = part - constant - (state.reshape(cells, channels).astype(F32) - mean) * factor
        if i == 0:
            grad = jnp.where(position > 0, grad, 0.0)
        if i == own_rows + 1:
            grad = jnp.where(position < devices - 1, grad, 0.0)
        after = jnp.where(in_frame < width - 1, pltpu.roll(grad, cells - 1, 0), 0.0)
        prior = jnp.where(in_frame > 0, pltpu.roll(grad, 1, 0), 0.0)
        padded[i, :cells, 0:channels] = after.astype(BF16)
        padded[i, :cells, channels : 2 * channels] = grad.astype(BF16)
        padded[i, :cells, 2 * channels :] = prior.astype(BF16)
        padded[i, cells:, :] = jnp.zeros((2 * width, 3 * channels), BF16)
    results = [jnp.zeros((cells, channels), F32) for _ in range(own_rows)]
    copies = []
    for i in range(own_rows + 2):
        joined = jnp.concatenate(
            [padded[i, (2 - a) * width : (2 - a) * width + cells, :] for a in range(3)], axis=1
        )
        taps = [b for b in range(3) if 0 <= i + b - 2 < own_rows]
        for low in range(0, len(taps), 2):
            some = taps[low : low + 2]
            product = matmul(joined, turned[:, some[0] * channels : (some[-1] + 1) * channels])
            for step, b in enumerate(some):
                results[i + b - 2] = results[i + b - 2] + product[:, step * channels : (step + 1) * channels]
        if i >= 2:
            out[i - 2] = results[i - 2].reshape(frame_count, width, channels).astype(BF16)
            copies.append(pltpu.make_async_copy(out.at[i - 2], far_out.at[i - 2], sems.at[i - 2]))
            copies[-1].start()
    for copy in copies:
        copy.wait()


def per_device(
    frames,
    frame_owner,
    picks,
    patch_weight,
    patch_bias,
    norm_gain,
    head_weight,
    head_bias,
    head_out,
    hidden_state,
    group_gain,
    group_shift,
    out_weight,
    inner_weight,
):
    devices = lax.axis_size("row")
    position = lax.axis_index("row").astype(jnp.int32).reshape(1)
    per_frame = devices // FRAMES
    height = frames.shape[1]
    own_rows, _, frame_width, channels = hidden_state.shape
    cells = FRAMES * frame_width
    width = patch_weight.shape[1]
    turned_frames = jnp.transpose(frames, (0, 2, 1))
    bias = patch_bias.reshape(1, width)
    gain = norm_gain.reshape(1, width)
    head_bias_row = head_bias.reshape(1, width)
    head_out_row = head_out.reshape(1, width)
    state_rows = own_rows + 2
    tap_rows = -(-9 * (own_rows + 4) // LANES) * LANES
    edge = jax.ShapeDtypeStruct((1,) + hidden_state.shape[1:], BF16)
    message = (message_shape(devices), edge, edge)
    gain_row = group_gain.reshape(1, channels)
    shift_row = group_shift.reshape(1, channels)
    early = [hidden_state, gain_row, shift_row]
    wide, *early = pl.pallas_call(
        prepare_kernel,
        out_shape=(
            pltpu.VMEM((3 * tap_rows, state_rows * channels), BF16),
            *[pltpu.VMEM(x.shape, x.dtype) for x in early],
        ),
        in_specs=[FAR] * (1 + len(early)),
        scratch_shapes=[
            pltpu.VMEM(out_weight.shape, BF16),
            pltpu.VMEM((3 * tap_rows, state_rows * channels), F32),
            pltpu.SemaphoreType.DMA((1 + len(early),)),
        ],
        compiler_params=params(cells),
        name="prepare",
    )(far(out_weight), *[far(x) for x in early])
    early = [near(x) for x in early]
    slope_outs = (
        pltpu.VMEM((own_rows, cells, channels), F32),
        pltpu.VMEM((2, cells, channels), F32),
        pltpu.VMEM((8, channels), F32),
        jax.ShapeDtypeStruct((devices, 2, channels), F32),
    )
    if per_frame == 1:
        arrays = [
            turned_frames,
            bias,
            gain,
            frame_owner,
            picks,
            head_bias_row,
            head_out_row,
            hidden_state,
            patch_weight,
            head_weight,
        ]
        send, across, along = pl.pallas_call(
            reward_kernel,
            out_shape=message,
            in_specs=[SMEM] + [FAR] * len(arrays),
            out_specs=[VMEM] * 3,
            scratch_shapes=[
                (pltpu.SMEM if x.dtype == jnp.int32 else pltpu.VMEM)(x.shape, x.dtype) for x in arrays
            ]
            + [pltpu.SemaphoreType.DMA((len(arrays) + 16,))],
            compiler_params=params(0),
            name="reward",
        )(position, *[far(x) for x in arrays])
    else:
        count = height // PATCH
        normed, inv_spread, partial = pl.pallas_call(
            forward_kernel,
            out_shape=(
                jax.ShapeDtypeStruct((token_rows_of(height), width), F32),
                jax.ShapeDtypeStruct((token_rows_of(height), LANES), F32),
                jax.ShapeDtypeStruct((1, width), F32),
            ),
            compiler_params=params(cells),
            name="reward_forward",
        )(turned_frames, bias, gain, patch_weight)
        members = [[b * per_frame + i for i in range(per_frame)] for b in range(FRAMES)]
        pooled = lax.psum(partial, "row", axis_index_groups=members) / (count * per_frame)
        send, across, along = pl.pallas_call(
            functools.partial(backward_kernel, height=height, per_frame=per_frame),
            out_shape=message,
            in_specs=[SMEM] * 3 + [VMEM] * 9,
            out_specs=[VMEM] * 3,
            compiler_params=params(cells),
            name="reward_backward",
        )(
            frame_owner,
            picks,
            position,
            hidden_state,
            gain,
            head_bias_row,
            head_out_row,
            normed,
            inv_spread,
            pooled,
            patch_weight,
            head_weight,
        )
    arrived = lax.all_to_all(send, "row", 0, 0, tiled=True)
    direct, edge_slopes, stats, sums = pl.pallas_call(
        slope_kernel,
        out_shape=slope_outs,
        in_specs=[SMEM] + [VMEM] * 5,
        scratch_shapes=[
            pltpu.VMEM((own_rows, cells, channels), F32),
            pltpu.VMEM((4 * devices, LANES), F32),
        ],
        compiler_params=params(cells),
        name="slope",
    )(frame_owner, near(arrived), *early, near(wide))
    swaps = [(2 * i, 2 * i + 1) for i in range(devices // 2)]
    across = lax.ppermute(across, "row", swaps + [(b, a) for a, b in swaps])
    swaps = [(2 * i - 1, 2 * i) for i in range(1, devices // 2)]
    along = lax.ppermute(along, "row", swaps + [(b, a) for a, b in swaps])
    summed = lax.all_to_all(sums, "row", 0, 0, tiled=True)
    edge_direct, edge_states, turned = pl.pallas_call(
        late_kernel,
        out_shape=(
            pltpu.VMEM((2, cells, channels), F32),
            pltpu.VMEM((2,) + hidden_state.shape[1:], BF16),
            pltpu.VMEM((9 * channels, 3 * channels), BF16),
        ),
        in_specs=[SMEM] + [VMEM] * 6 + [FAR],
        scratch_shapes=[pltpu.VMEM(inner_weight.shape, BF16), pltpu.SemaphoreType.DMA((1,))],
        input_output_aliases={3: 0},
        compiler_params=params(cells),
        name="late",
    )(position, near(across), near(along), near(edge_slopes), near(stats), *early[1:3], far(inner_weight))
    return pl.pallas_call(
        functools.partial(inner_kernel, devices=devices),
        out_shape=jax.ShapeDtypeStruct(hidden_state.shape, BF16),
        in_specs=[SMEM] + [VMEM] * 7,
        out_specs=FAR,
        scratch_shapes=[
            pltpu.VMEM((own_rows + 2, cells + 2 * frame_width, 3 * channels), BF16),
            pltpu.VMEM(hidden_state.shape, BF16),
            pltpu.SemaphoreType.DMA((own_rows,)),
        ],
        compiler_params=params(cells),
        name="inner",
    )(
        position,
        near(summed),
        near(stats),
        near(direct),
        early[0],
        near(edge_direct),
        near(edge_states),
        near(turned),
    )


def solution(mesh):
    return jax.shard_map(
        per_device,
        mesh=mesh,
        in_specs=(
            P(None, None, ("clip", "row")),
            P("clip"),
            P("clip"),
            P(),
            P(),
            P(),
            P(),
            P(),
            P(),
            P(("clip", "row"), None, None, None),
            P(),
            P(),
            P(),
            P(),
        ),
        out_specs=P(("clip", "row"), None, None, None),
        check_vma=False,
    )
```

```python
import functools

import jax
import jax.numpy as jnp
from jax import lax
from jax.experimental import pallas as pl
from jax.experimental.pallas import tpu as pltpu
from jax.sharding import PartitionSpec as P

PATCH = 16
GROUPS = 32
FRAMES = 16
LANES = 128
SLOTS = LANES // PATCH
eps_norm = 1e-06
BF16 = jnp.bfloat16
F32 = jnp.float32

SMEM = pl.BlockSpec(memory_space=pltpu.SMEM)
VMEM = pl.BlockSpec(memory_space=pltpu.VMEM)
FAR = pl.BlockSpec(memory_space=pl.ANY)


def iota(shape, dim):
    return lax.broadcasted_iota(jnp.int32, shape, dim)


def div(values, count):
    if count & (count - 1):
        return values // count
    return values >> (count.bit_length() - 1)


def mod(values, count):
    if count & (count - 1):
        return values % count
    return values & (count - 1)


def ones_where(condition):
    return jnp.where(condition, 1.0, 0.0).astype(BF16)


def matmul(left, right):
    return jnp.dot(left, right, preferred_element_type=F32)


def matmul_t(left, right):
    return lax.dot_general(left, right, (((1,), (1,)), ((), ())), preferred_element_type=F32)


def cut_in_three(values):
    high = values.astype(BF16)
    rest = values - high.astype(F32)
    middle = rest.astype(BF16)
    low = (rest - middle.astype(F32)).astype(BF16)
    return high, middle, low


def exact_rows(rows, product):
    place = iota((16, rows[0].shape[1]), 0)
    stacked = jnp.zeros(place.shape, F32)
    for index, row in enumerate(rows):
        for step, piece in enumerate(cut_in_three(row)):
            stacked = jnp.where(place == 3 * index + step, piece.astype(F32), stacked)
    result = product(stacked.astype(BF16))
    return [
        result[3 * i : 3 * i + 1] + result[3 * i + 1 : 3 * i + 2] + result[3 * i + 2 : 3 * i + 3]
        for i in range(len(rows))
    ]


def silu_slope(values):
    sigmoid = jax.nn.sigmoid(values)
    return sigmoid * (1.0 + values * (1.0 - sigmoid))


def token_rows_of(height):
    return -(-(height // PATCH) // 16) * 16


def to_tokens(pixels):
    channels, columns, height = pixels.shape
    rows = channels * columns
    token_rows = token_rows_of(height)
    flat = pixels.reshape(rows, height)
    width = channels * PATCH * columns
    lane = iota((1, width), 1)
    place = iota((rows, 1), 0)
    mine = place == div(lane, PATCH * columns) * columns + mod(lane, columns)
    in_patch = mod(div(lane, columns), PATCH)
    pixel_row = iota((height, 1), 0)
    token = iota((token_rows, 1), 0)
    tokens = jnp.zeros((token_rows, width), F32)
    for t in range(height // PATCH):
        tiled = matmul(flat, ones_where(pixel_row == in_patch + t * PATCH))
        row = jnp.sum(jnp.where(mine, tiled, 0.0), axis=0, keepdims=True)
        tokens = jnp.where(token == t, row, tokens)
    return tokens.astype(BF16)


def forward_part(tokens, count, bias, gain, load_patch):
    embedded = bias[...]
    for low, high, weight in load_patch():
        embedded = embedded + matmul(tokens[:, low:high], weight)
    centred = embedded - jnp.mean(embedded, axis=1, keepdims=True)
    inv_spread = lax.rsqrt(jnp.mean(centred * centred, axis=1, keepdims=True) + eps_norm)
    normed = centred * inv_spread
    weighted = normed * gain[...]
    inside = iota((tokens.shape[0], 1), 0) < count
    pooled = jnp.sum(jnp.where(inside, weighted, 0.0), axis=0, keepdims=True)
    return normed, inv_spread, pooled


def message_shape(devices):
    return jax.ShapeDtypeStruct((devices, 4, LANES), F32)


def write_windows(patch_grad, sums, own_rows, height, send):
    span = PATCH * PATCH
    line = jnp.concatenate(
        [
            jnp.concatenate([patch_grad[t : t + 1, k * span : (k + 1) * span] for t in range(height // PATCH)], axis=1)
            for k in range(3)
        ]
        + [jnp.zeros((1, height * PATCH), F32)],
        axis=0,
    )
    line = jnp.concatenate([jnp.zeros((4, LANES), F32), line, jnp.zeros((4, LANES), F32)], axis=1)
    used = iota((4, LANES), 1) < (own_rows + 4) * PATCH
    colour = iota((4, LANES), 0)
    for index in range(send.shape[0]):
        d = send.shape[0] - 1 - index
        start = LANES + (d * own_rows - 2) * PATCH
        window = jnp.where(used, line[:, start : start + LANES], 0.0)
        send[index] = jnp.where(colour < 3, window, sums[:4])


def channel_sums(hidden):
    values = hidden.reshape(-1, hidden.shape[-1]).astype(F32)
    return jnp.sum(values, axis=0, keepdims=True), jnp.sum(values * values, axis=0, keepdims=True)


def over_group(values, size):
    lane = iota(values.shape, 1)
    lanes = values.shape[1]
    step = 1
    while step < size:
        later = pltpu.roll(values, lanes - step, 1)
        earlier = pltpu.roll(values, step, 1)
        values = values + jnp.where((lane & step) == 0, later, earlier)
        step *= 2
    return values


def group_sums(hidden):
    channels = hidden.shape[-1]
    size = channels // GROUPS
    first, second = [
        over_group(jnp.broadcast_to(x, (8, channels)), size) for x in channel_sums(hidden)
    ]
    lane = mod(iota((8, channels), 1), size)
    return jnp.where(lane == 0, first, jnp.where(lane == 1, second, 0.0))


def pull_back(row, weight):
    parts = []
    for low in range(0, weight.shape[0], LANES):
        product = weight[low : low + LANES, :].astype(F32) * row
        folded = product[:, :LANES]
        for start in range(LANES, weight.shape[1], LANES):
            folded = folded + product[:, start : start + LANES]
        parts.append(jnp.sum(folded.T, axis=0, keepdims=True))
    return jnp.concatenate(parts, axis=1)


def backward_part(
    owner, picks, gain, head_bias, head_out, normed, inv_spread, pooled, weight, head, slot, own_rows, height, sums, send
):
    (before,) = exact_rows([pooled], lambda rows: matmul(rows, head[...]))
    slope = head_out[...] * silu_slope(before + head_bias[...])
    pulled = pull_back(slope, head)
    wanted = owner[slot]
    picked = jnp.int32(0)
    for k in range(picks.shape[0]):
        picked = picked + jnp.where(picks[k] == wanted, 1, 0)
    scaled = gain[...] * (picked.astype(F32) * pulled)
    token_grad = inv_spread * (
        scaled
        - jnp.mean(scaled, axis=1, keepdims=True)
        - normed * jnp.mean(scaled * normed, axis=1, keepdims=True)
    )
    patch_grad = matmul_t(token_grad.astype(BF16), weight[...]).astype(BF16).astype(F32)
    write_windows(patch_grad, sums, own_rows, height, send)


def write_edges(place, hidden, across, along):
    last = hidden.shape[0] - 1
    even = place[0] % 2 == 0
    across[0] = hidden[jnp.where(even, last, 0)]
    along[0] = hidden[jnp.where(even, 0, last)]


def reward_kernel(place, *refs):
    count = 8
    far, send, across, along = refs[: count + 2], refs[count + 2], refs[count + 3], refs[count + 4]
    near, sems = refs[count + 5 : 2 * count + 7], refs[-1]
    frames, bias, gain, owner, picks, head_bias, head_out, hidden, patch, head = near
    depth, depths = 256, (128, 256)
    small = [pltpu.make_async_copy(far[i], near[i], sems.at[i]) for i in range(count)]
    pieces = []
    used = count
    for index, rows in enumerate(depths):
        source, target = far[count + index], near[count + index]
        parts = []
        for low in range(0, target.shape[0], rows):
            part = pl.ds(low, rows)
            parts.append(pltpu.make_async_copy(source.at[part], target.at[part], sems.at[used]))
            used += 1
        pieces.append(parts)
    for copy in small[:2] + pieces[0] + small[2:7] + pieces[1] + small[7:]:
        copy.start()

    def load_patch():
        for low in range(0, patch.shape[0], depth):
            for copy in pieces[0][low // depths[0] : (low + depth) // depths[0]]:
                copy.wait()
            yield low, low + depth, patch[low : low + depth, :]

    height = frames.shape[2]
    patches = height // PATCH
    small[0].wait()
    tokens = to_tokens(frames[...])
    small[1].wait()
    small[2].wait()
    normed, inv_spread, pooled = forward_part(tokens, patches, bias, gain, load_patch)
    for copy in small[3:] + pieces[1]:
        copy.wait()
    write_edges(place, hidden, across, along)
    backward_part(
        owner,
        picks,
        gain,
        head_bias,
        head_out,
        normed,
        inv_spread,
        pooled / patches,
        patch,
        head,
        place[0],
        hidden.shape[0],
        height,
        group_sums(hidden[...]),
        send,
    )


def forward_kernel(frames, bias, gain, patch, normed, inv_spread, pooled):
    width = patch.shape[0]
    tokens = to_tokens(frames[...])
    normed[...], spread, pooled[...] = forward_part(
        tokens, frames.shape[2] // PATCH, bias, gain, lambda: [(0, width, patch[...])]
    )
    inv_spread[...] = jnp.broadcast_to(spread, inv_spread.shape)


def backward_kernel(
    owner,
    picks,
    place,
    hidden,
    gain,
    head_bias,
    head_out,
    normed,
    inv_spread,
    pooled,
    patch,
    head,
    send,
    across,
    along,
    *,
    height,
    per_frame,
):
    write_edges(place, hidden, across, along)
    backward_part(
        owner,
        picks,
        gain,
        head_bias,
        head_out,
        normed[...],
        inv_spread[...][:, :1],
        pooled[...],
        patch,
        head,
        place[0] // per_frame,
        hidden.shape[0],
        height,
        group_sums(hidden[...]),
        send,
    )


def params(cells):
    return pltpu.CompilerParams(vmem_limit_bytes=min(16 + cells // 64, 48) * 1024 * 1024)


def near(array):
    return pltpu.with_memory_space_constraint(array, pltpu.VMEM)


def far(array):
    return pltpu.with_memory_space_constraint(array, pltpu.HBM)


def prepare_kernel(far_weight, *refs):
    count = (len(refs) - 4) // 2
    fars, wide, nears = refs[:count], refs[count], refs[count + 1 : 2 * count + 1]
    out_weight, scratch, sems = refs[2 * count + 1 :]
    copies = [pltpu.make_async_copy(far_weight, out_weight, sems.at[count])]
    copies += [pltpu.make_async_copy(fars[i], nears[i], sems.at[i]) for i in range(count)]
    for copy in copies:
        copy.start()
    block = scratch.shape[0] // 3
    amount = scratch.shape[1] // LANES
    span = 3 * (amount + 2)
    scratch[...] = jnp.zeros_like(scratch)
    copies[0].wait()
    for a in range(3):
        for e in range(3):
            for b in range(3):
                piece = out_weight[a, b, e].astype(F32)
                for i in range(amount):
                    start = a * block + e * span + 3 * (i - b + 2)
                    scratch[start : start + 3, i * LANES : (i + 1) * LANES] = piece
    wide[...] = scratch[...].astype(BF16)
    for copy in copies[1:]:
        copy.wait()


def norm_constants(totals, cell_total):
    channels = totals.shape[1]
    size = channels // GROUPS
    totals = jnp.broadcast_to(totals, (8, channels))
    lane = mod(iota((8, channels), 1), size)
    first, second = [over_group(jnp.where(lane == i, totals, 0.0), size)[:1] for i in range(2)]
    mean = first / cell_total
    return mean, lax.rsqrt(second / cell_total - mean * mean + eps_norm)


def norm_slopes(state, mean, inverse, gain, shift):
    normed = (state - mean) * inverse
    return normed, silu_slope(normed * gain + shift) * gain


def slope_kernel(
    owner, arrived, hidden, gain, shift, wide, direct, edge_slopes, stats, sums, slopes_own, received
):
    devices, message_rows, _ = arrived.shape
    own_rows, frame_count, width, channels = hidden.shape
    cells = frame_count * width
    per_frame = devices // frame_count
    received[...] = arrived[...].reshape(received.shape)

    def from_all(row):
        return received[pl.ds(row, devices, stride=message_rows), :]

    totals = jnp.sum(from_all(3), axis=0, keepdims=True)
    mean, inverse = norm_constants(totals, own_rows * devices * cells * (channels // GROUPS))
    for i in range(own_rows):
        state = hidden[i].reshape(cells, channels).astype(F32)
        slopes_own[i] = norm_slopes(state, mean, inverse, gain[...], shift[...])[1]

    lines = jnp.concatenate([from_all(k) for k in range(3)], axis=1).astype(BF16)
    source = devices - 1 - iota((1, devices), 1)
    home = jnp.zeros((1, devices), jnp.int32)
    for b in range(frame_count):
        home = jnp.where(div(source, per_frame) == b, owner[b] * per_frame, home)
    home = home + mod(source, per_frame)
    cell = iota((cells, 1), 0)
    column = mod(cell, width)
    frame_strip = div(cell, width) * per_frame
    lane = mod(iota((1, 3 * LANES), 1), PATCH)
    kept = []
    placed = None
    for e in range(3):
        wanted = column - e + 1
        if per_frame > 1 or placed is None:
            strip = frame_strip + div(wanted, PATCH) if per_frame > 1 else frame_strip
            placed = matmul(ones_where(home == strip), lines)
        inside = jnp.where((wanted >= 0) & (wanted < width), mod(wanted, PATCH), -1)
        kept.append(jnp.where(lane == inside, placed, 0.0).astype(BF16))
    block = wide.shape[0] // 3
    span = 3 * (own_rows + 4)
    entry = iota((3 * LANES, 1), 0)
    entry = div(mod(entry, LANES), PATCH) * 3 + div(entry, LANES)
    entry = jnp.where(entry < span, entry, -3 * span)
    tap = iota((1, block), 1)
    folds = jnp.concatenate([ones_where(tap == entry + e * span) for e in range(3)], axis=0)
    taps = matmul(jnp.concatenate(kept, axis=1), folds).astype(BF16)
    later = []
    for a in range(3):
        skip = (2 - a) * width
        later.append(
            jnp.concatenate([taps[skip:], jnp.zeros((skip, block), BF16)], axis=0) if skip else taps
        )
    result = matmul(jnp.concatenate(later, axis=1), wide[...])

    first = jnp.zeros((1, channels), F32)
    second = jnp.zeros((1, channels), F32)
    for i in range(own_rows):
        state = hidden[i].reshape(cells, channels).astype(F32)
        up = result[:, (i + 1) * channels : (i + 2) * channels] * slopes_own[i]
        direct[i] = up * inverse
        first = first + jnp.sum(up, axis=0, keepdims=True)
        second = second + jnp.sum(up * ((state - mean) * inverse), axis=0, keepdims=True)
    edge_slopes[0] = result[:, :channels]
    edge_slopes[1] = result[:, (own_rows + 1) * channels :]
    stats[0:1, :] = mean
    stats[1:2, :] = inverse
    both = jnp.where(iota((2, channels), 0) == 0, first, second)
    sums[...] = jnp.broadcast_to(both[None], sums.shape)


def late_kernel(
    place, across, along, slopes, stats, gain, shift, far_weight, direct, states, turned, inner_weight, sem
):
    copy = pltpu.make_async_copy(far_weight, inner_weight, sem.at[0])
    copy.start()
    cells, channels = slopes.shape[1:]
    odd = place[0] % 2 == 1
    mean = stats[0:1, :]
    inverse = stats[1:2, :]
    for i in range(2):
        state = jnp.where(odd == (i == 0), across[0], along[0])
        states[i] = state
        values = state.reshape(cells, channels).astype(F32)
        direct[i] = slopes[i] * norm_slopes(values, mean, inverse, gain[...], shift[...])[1] * inverse
    copy.wait()
    size = inner_weight.shape[3]
    for b in range(3):
        for a in range(3):
            for e in range(3):
                at = (a * 3 + e) * size
                turned[at : at + size, b * size : (b + 1) * size] = inner_weight[a, b, e].T


def inner_kernel(
    place, arrived, stats, direct, hidden, edge_direct, edge_states, turned, far_out, padded, out, sems, *, devices
):
    own_rows, frame_count, width, channels = out.shape
    cells = frame_count * width
    totals = jnp.sum(arrived[...], axis=0)
    cell_total = own_rows * devices * cells * (channels // GROUPS)
    place_row = iota((8, channels), 0)
    both = jnp.where(place_row == 0, totals[0:1], totals[1:2])
    both = over_group(both, channels // GROUPS)
    first, second = both[0:1], both[1:2]
    mean = stats[0:1, :]
    inverse = stats[1:2, :]
    constant = first / cell_total * inverse
    factor = second / cell_total * inverse * inverse
    position = place[0]
    in_frame = mod(iota((cells, 1), 0), width)
    for i in range(own_rows + 2):
        if 0 < i < own_rows + 1:
            state, part = hidden[i - 1], direct[i - 1]
        else:
            state, part = edge_states[min(i, 1)], edge_direct[min(i, 1)]
        grad = part - constant - (state.reshape(cells, channels).astype(F32) - mean) * factor
        if i == 0:
            grad = jnp.where(position > 0, grad, 0.0)
        if i == own_rows + 1:
            grad = jnp.where(position < devices - 1, grad, 0.0)
        after = jnp.where(in_frame < width - 1, pltpu.roll(grad, cells - 1, 0), 0.0)
        prior = jnp.where(in_frame > 0, pltpu.roll(grad, 1, 0), 0.0)
        padded[i, :cells, 0:channels] = after.astype(BF16)
        padded[i, :cells, channels : 2 * channels] = grad.astype(BF16)
        padded[i, :cells, 2 * channels :] = prior.astype(BF16)
        padded[i, cells:, :] = jnp.zeros((2 * width, 3 * channels), BF16)
    results = [jnp.zeros((cells, channels), F32) for _ in range(own_rows)]
    copies = []
    for i in range(own_rows + 2):
        joined = jnp.concatenate(
            [padded[i, (2 - a) * width : (2 - a) * width + cells, :] for a in range(3)], axis=1
        )
        taps = [b for b in range(3) if 0 <= i + b - 2 < own_rows]
        for low in range(0, len(taps), 2):
            some = taps[low : low + 2]
            product = matmul(joined, turned[:, some[0] * channels : (some[-1] + 1) * channels])
            for step, b in enumerate(some):
                results[i + b - 2] = results[i + b - 2] + product[:, step * channels : (step + 1) * channels]
        if i >= 2:
            out[i - 2] = results[i - 2].reshape(frame_count, width, channels).astype(BF16)
            copies.append(pltpu.make_async_copy(out.at[i - 2], far_out.at[i - 2], sems.at[i - 2]))
            copies[-1].start()
    for copy in copies:
        copy.wait()


def per_device(
    frames,
    frame_owner,
    picks,
    patch_weight,
    patch_bias,
    norm_gain,
    head_weight,
    head_bias,
    head_out,
    hidden_state,
    group_gain,
    group_shift,
    out_weight,
    inner_weight,
):
    devices = lax.axis_size("row")
    position = lax.axis_index("row").astype(jnp.int32).reshape(1)
    per_frame = devices // FRAMES
    height = frames.shape[1]
    own_rows, _, frame_width, channels = hidden_state.shape
    cells = FRAMES * frame_width
    width = patch_weight.shape[1]
    turned_frames = jnp.transpose(frames, (0, 2, 1))
    bias = patch_bias.reshape(1, width)
    gain = norm_gain.reshape(1, width)
    head_bias_row = head_bias.reshape(1, width)
    head_out_row = head_out.reshape(1, width)
    state_rows = own_rows + 2
    tap_rows = -(-9 * (own_rows + 4) // LANES) * LANES
    edge = jax.ShapeDtypeStruct((1,) + hidden_state.shape[1:], BF16)
    message = (message_shape(devices), edge, edge)
    gain_row = group_gain.reshape(1, channels)
    shift_row = group_shift.reshape(1, channels)
    early = [hidden_state, gain_row, shift_row]
    wide, *early = pl.pallas_call(
        prepare_kernel,
        out_shape=(
            pltpu.VMEM((3 * tap_rows, state_rows * channels), BF16),
            *[pltpu.VMEM(x.shape, x.dtype) for x in early],
        ),
        in_specs=[FAR] * (1 + len(early)),
        scratch_shapes=[
            pltpu.VMEM(out_weight.shape, BF16),
            pltpu.VMEM((3 * tap_rows, state_rows * channels), F32),
            pltpu.SemaphoreType.DMA((1 + len(early),)),
        ],
        compiler_params=params(cells),
        name="prepare",
    )(far(out_weight), *[far(x) for x in early])
    early = [near(x) for x in early]
    slope_outs = (
        pltpu.VMEM((own_rows, cells, channels), F32),
        pltpu.VMEM((2, cells, channels), F32),
        pltpu.VMEM((8, channels), F32),
        jax.ShapeDtypeStruct((devices, 2, channels), F32),
    )
    if per_frame == 1:
        arrays = [
            turned_frames,
            bias,
            gain,
            frame_owner,
            picks,
            head_bias_row,
            head_out_row,
            hidden_state,
            patch_weight,
            head_weight,
        ]
        send, across, along = pl.pallas_call(
            reward_kernel,
            out_shape=message,
            in_specs=[SMEM] + [FAR] * len(arrays),
            out_specs=[VMEM] * 3,
            scratch_shapes=[
                (pltpu.SMEM if x.dtype == jnp.int32 else pltpu.VMEM)(x.shape, x.dtype) for x in arrays
            ]
            + [pltpu.SemaphoreType.DMA((len(arrays) + 16,))],
            compiler_params=params(0),
            name="reward",
        )(position, *[far(x) for x in arrays])
    else:
        count = height // PATCH
        normed, inv_spread, partial = pl.pallas_call(
            forward_kernel,
            out_shape=(
                jax.ShapeDtypeStruct((token_rows_of(height), width), F32),
                jax.ShapeDtypeStruct((token_rows_of(height), LANES), F32),
                jax.ShapeDtypeStruct((1, width), F32),
            ),
            compiler_params=params(cells),
            name="reward_forward",
        )(turned_frames, bias, gain, patch_weight)
        members = [[b * per_frame + i for i in range(per_frame)] for b in range(FRAMES)]
        pooled = lax.psum(partial, "row", axis_index_groups=members) / (count * per_frame)
        send, across, along = pl.pallas_call(
            functools.partial(backward_kernel, height=height, per_frame=per_frame),
            out_shape=message,
            in_specs=[SMEM] * 3 + [VMEM] * 9,
            out_specs=[VMEM] * 3,
            compiler_params=params(cells),
            name="reward_backward",
        )(
            frame_owner,
            picks,
            position,
            hidden_state,
            gain,
            head_bias_row,
            head_out_row,
            normed,
            inv_spread,
            pooled,
            patch_weight,
            head_weight,
        )
    turned_row = [list(reversed(range(devices)))]
    arrived = lax.all_to_all(send, "row", 0, 0, axis_index_groups=turned_row, tiled=True)
    direct, edge_slopes, stats, sums = pl.pallas_call(
        slope_kernel,
        out_shape=slope_outs,
        in_specs=[SMEM] + [VMEM] * 5,
        scratch_shapes=[
            pltpu.VMEM((own_rows, cells, channels), F32),
            pltpu.VMEM((4 * devices, LANES), F32),
        ],
        compiler_params=params(cells),
        name="slope",
    )(frame_owner, near(arrived), *early, near(wide))
    swaps = [(2 * i, 2 * i + 1) for i in range(devices // 2)]
    across = lax.ppermute(across, "row", swaps + [(b, a) for a, b in swaps])
    swaps = [(2 * i - 1, 2 * i) for i in range(1, devices // 2)]
    along = lax.ppermute(along, "row", swaps + [(b, a) for a, b in swaps])
    summed = lax.all_to_all(sums, "row", 0, 0, axis_index_groups=turned_row, tiled=True)
    edge_direct, edge_states, turned = pl.pallas_call(
        late_kernel,
        out_shape=(
            pltpu.VMEM((2, cells, channels), F32),
            pltpu.VMEM((2,) + hidden_state.shape[1:], BF16),
            pltpu.VMEM((9 * channels, 3 * channels), BF16),
        ),
        in_specs=[SMEM] + [VMEM] * 6 + [FAR],
        scratch_shapes=[pltpu.VMEM(inner_weight.shape, BF16), pltpu.SemaphoreType.DMA((1,))],
        input_output_aliases={3: 0},
        compiler_params=params(cells),
        name="late",
    )(position, near(across), near(along), near(edge_slopes), near(stats), *early[1:3], far(inner_weight))
    return pl.pallas_call(
        functools.partial(inner_kernel, devices=devices),
        out_shape=jax.ShapeDtypeStruct(hidden_state.shape, BF16),
        in_specs=[SMEM] + [VMEM] * 7,
        out_specs=FAR,
        scratch_shapes=[
            pltpu.VMEM((own_rows + 2, cells + 2 * frame_width, 3 * channels), BF16),
            pltpu.VMEM(hidden_state.shape, BF16),
            pltpu.SemaphoreType.DMA((own_rows,)),
        ],
        compiler_params=params(cells),
        name="inner",
    )(
        position,
        near(summed),
        near(stats),
        near(direct),
        early[0],
        near(edge_direct),
        near(edge_states),
        near(turned),
    )


def solution(mesh):
    return jax.shard_map(
        per_device,
        mesh=mesh,
        in_specs=(
            P(None, None, ("clip", "row")),
            P("clip"),
            P("clip"),
            P(),
            P(),
            P(),
            P(),
            P(),
            P(),
            P(("clip", "row"), None, None, None),
            P(),
            P(),
            P(),
            P(),
        ),
        out_specs=P(("clip", "row"), None, None, None),
        check_vma=False,
    )
```

```python
import functools

import jax
import jax.numpy as jnp
from jax import lax
from jax.experimental import pallas as pl
from jax.experimental.pallas import tpu as pltpu
from jax.sharding import PartitionSpec as P

PATCH = 16
GROUPS = 32
FRAMES = 16
LANES = 128
SLOTS = LANES // PATCH
eps_norm = 1e-06
BF16 = jnp.bfloat16
F32 = jnp.float32

SMEM = pl.BlockSpec(memory_space=pltpu.SMEM)
VMEM = pl.BlockSpec(memory_space=pltpu.VMEM)
FAR = pl.BlockSpec(memory_space=pl.ANY)


def iota(shape, dim):
    return lax.broadcasted_iota(jnp.int32, shape, dim)


def div(values, count):
    if count & (count - 1):
        return values // count
    return values >> (count.bit_length() - 1)


def mod(values, count):
    if count & (count - 1):
        return values % count
    return values & (count - 1)


def ones_where(condition):
    return jnp.where(condition, 1.0, 0.0).astype(BF16)


def matmul(left, right):
    return jnp.dot(left, right, preferred_element_type=F32)


def matmul_t(left, right):
    return lax.dot_general(left, right, (((1,), (1,)), ((), ())), preferred_element_type=F32)


def cut_in_three(values):
    high = values.astype(BF16)
    rest = values - high.astype(F32)
    middle = rest.astype(BF16)
    low = (rest - middle.astype(F32)).astype(BF16)
    return high, middle, low


def exact_rows(rows, product):
    place = iota((16, rows[0].shape[1]), 0)
    stacked = jnp.zeros(place.shape, F32)
    for index, row in enumerate(rows):
        for step, piece in enumerate(cut_in_three(row)):
            stacked = jnp.where(place == 3 * index + step, piece.astype(F32), stacked)
    result = product(stacked.astype(BF16))
    return [
        result[3 * i : 3 * i + 1] + result[3 * i + 1 : 3 * i + 2] + result[3 * i + 2 : 3 * i + 3]
        for i in range(len(rows))
    ]


def silu_slope(values):
    sigmoid = jax.nn.sigmoid(values)
    return sigmoid * (1.0 + values * (1.0 - sigmoid))


def token_rows_of(height):
    return -(-(height // PATCH) // 16) * 16


def to_tokens(pixels):
    channels, columns, height = pixels.shape
    rows = channels * columns
    token_rows = token_rows_of(height)
    flat = pixels.reshape(rows, height)
    width = channels * PATCH * columns
    lane = iota((1, width), 1)
    place = iota((rows, 1), 0)
    mine = place == div(lane, PATCH * columns) * columns + mod(lane, columns)
    in_patch = mod(div(lane, columns), PATCH)
    pixel_row = iota((height, 1), 0)
    token = iota((token_rows, 1), 0)
    tokens = jnp.zeros((token_rows, width), F32)
    for t in range(height // PATCH):
        tiled = matmul(flat, ones_where(pixel_row == in_patch + t * PATCH))
        row = jnp.sum(jnp.where(mine, tiled, 0.0), axis=0, keepdims=True)
        tokens = jnp.where(token == t, row, tokens)
    return tokens.astype(BF16)


def forward_part(tokens, count, bias, gain, load_patch):
    embedded = bias[...]
    for low, high, weight in load_patch():
        embedded = embedded + matmul(tokens[:, low:high], weight)
    centred = embedded - jnp.mean(embedded, axis=1, keepdims=True)
    inv_spread = lax.rsqrt(jnp.mean(centred * centred, axis=1, keepdims=True) + eps_norm)
    normed = centred * inv_spread
    weighted = normed * gain[...]
    inside = iota((tokens.shape[0], 1), 0) < count
    pooled = jnp.sum(jnp.where(inside, weighted, 0.0), axis=0, keepdims=True)
    return normed, inv_spread, pooled


def led_by(leader, devices):
    return [leader] + [d for d in reversed(range(devices)) if d != leader]


def first_order(devices):
    return led_by(devices * 5 // 8, devices)


def message_shape(devices):
    return jax.ShapeDtypeStruct((devices, 4, LANES), F32)


def write_windows(patch_grad, sums, own_rows, height, send):
    span = PATCH * PATCH
    line = jnp.concatenate(
        [
            jnp.concatenate([patch_grad[t : t + 1, k * span : (k + 1) * span] for t in range(height // PATCH)], axis=1)
            for k in range(3)
        ]
        + [jnp.zeros((1, height * PATCH), F32)],
        axis=0,
    )
    line = jnp.concatenate([jnp.zeros((4, LANES), F32), line, jnp.zeros((4, LANES), F32)], axis=1)
    used = iota((4, LANES), 1) < (own_rows + 4) * PATCH
    colour = iota((4, LANES), 0)
    for index, d in enumerate(first_order(send.shape[0])):
        start = LANES + (d * own_rows - 2) * PATCH
        window = jnp.where(used, line[:, start : start + LANES], 0.0)
        send[index] = jnp.where(colour < 3, window, sums[:4])


def channel_sums(hidden):
    values = hidden.reshape(-1, hidden.shape[-1]).astype(F32)
    return jnp.sum(values, axis=0, keepdims=True), jnp.sum(values * values, axis=0, keepdims=True)


def over_group(values, size):
    lane = iota(values.shape, 1)
    lanes = values.shape[1]
    step = 1
    while step < size:
        later = pltpu.roll(values, lanes - step, 1)
        earlier = pltpu.roll(values, step, 1)
        values = values + jnp.where((lane & step) == 0, later, earlier)
        step *= 2
    return values


def group_sums(hidden):
    channels = hidden.shape[-1]
    size = channels // GROUPS
    first, second = [
        over_group(jnp.broadcast_to(x, (8, channels)), size) for x in channel_sums(hidden)
    ]
    lane = mod(iota((8, channels), 1), size)
    return jnp.where(lane == 0, first, jnp.where(lane == 1, second, 0.0))


def pull_back(row, weight):
    parts = []
    for low in range(0, weight.shape[0], LANES):
        product = weight[low : low + LANES, :].astype(F32) * row
        folded = product[:, :LANES]
        for start in range(LANES, weight.shape[1], LANES):
            folded = folded + product[:, start : start + LANES]
        parts.append(jnp.sum(folded.T, axis=0, keepdims=True))
    return jnp.concatenate(parts, axis=1)


def backward_part(
    owner, picks, gain, head_bias, head_out, normed, inv_spread, pooled, weight, head, slot, own_rows, height, sums, send
):
    (before,) = exact_rows([pooled], lambda rows: matmul(rows, head[...]))
    slope = head_out[...] * silu_slope(before + head_bias[...])
    pulled = pull_back(slope, head)
    wanted = owner[slot]
    picked = jnp.int32(0)
    for k in range(picks.shape[0]):
        picked = picked + jnp.where(picks[k] == wanted, 1, 0)
    scaled = gain[...] * (picked.astype(F32) * pulled)
    token_grad = inv_spread * (
        scaled
        - jnp.mean(scaled, axis=1, keepdims=True)
        - normed * jnp.mean(scaled * normed, axis=1, keepdims=True)
    )
    patch_grad = matmul_t(token_grad.astype(BF16), weight[...]).astype(BF16).astype(F32)
    write_windows(patch_grad, sums, own_rows, height, send)


def write_edges(place, hidden, across, along):
    last = hidden.shape[0] - 1
    even = place[0] % 2 == 0
    across[0] = hidden[jnp.where(even, last, 0)]
    along[0] = hidden[jnp.where(even, 0, last)]


def reward_kernel(place, *refs):
    count = 8
    far, send, across, along = refs[: count + 2], refs[count + 2], refs[count + 3], refs[count + 4]
    near, sems = refs[count + 5 : 2 * count + 7], refs[-1]
    frames, bias, gain, owner, picks, head_bias, head_out, hidden, patch, head = near
    depth, depths = 256, (128, 256)
    small = [pltpu.make_async_copy(far[i], near[i], sems.at[i]) for i in range(count)]
    pieces = []
    used = count
    for index, rows in enumerate(depths):
        source, target = far[count + index], near[count + index]
        parts = []
        for low in range(0, target.shape[0], rows):
            part = pl.ds(low, rows)
            parts.append(pltpu.make_async_copy(source.at[part], target.at[part], sems.at[used]))
            used += 1
        pieces.append(parts)
    for copy in small[:2] + pieces[0] + small[2:7] + pieces[1] + small[7:]:
        copy.start()

    def load_patch():
        for low in range(0, patch.shape[0], depth):
            for copy in pieces[0][low // depths[0] : (low + depth) // depths[0]]:
                copy.wait()
            yield low, low + depth, patch[low : low + depth, :]

    height = frames.shape[2]
    patches = height // PATCH
    small[0].wait()
    tokens = to_tokens(frames[...])
    small[1].wait()
    small[2].wait()
    normed, inv_spread, pooled = forward_part(tokens, patches, bias, gain, load_patch)
    for copy in small[3:] + pieces[1]:
        copy.wait()
    write_edges(place, hidden, across, along)
    backward_part(
        owner,
        picks,
        gain,
        head_bias,
        head_out,
        normed,
        inv_spread,
        pooled / patches,
        patch,
        head,
        place[0],
        hidden.shape[0],
        height,
        group_sums(hidden[...]),
        send,
    )


def forward_kernel(frames, bias, gain, patch, normed, inv_spread, pooled):
    width = patch.shape[0]
    tokens = to_tokens(frames[...])
    normed[...], spread, pooled[...] = forward_part(
        tokens, frames.shape[2] // PATCH, bias, gain, lambda: [(0, width, patch[...])]
    )
    inv_spread[...] = jnp.broadcast_to(spread, inv_spread.shape)


def backward_kernel(
    owner,
    picks,
    place,
    hidden,
    gain,
    head_bias,
    head_out,
    normed,
    inv_spread,
    pooled,
    patch,
    head,
    send,
    across,
    along,
    *,
    height,
    per_frame,
):
    write_edges(place, hidden, across, along)
    backward_part(
        owner,
        picks,
        gain,
        head_bias,
        head_out,
        normed[...],
        inv_spread[...][:, :1],
        pooled[...],
        patch,
        head,
        place[0] // per_frame,
        hidden.shape[0],
        height,
        group_sums(hidden[...]),
        send,
    )


def params(cells):
    return pltpu.CompilerParams(vmem_limit_bytes=min(16 + cells // 64, 48) * 1024 * 1024)


def near(array):
    return pltpu.with_memory_space_constraint(array, pltpu.VMEM)


def far(array):
    return pltpu.with_memory_space_constraint(array, pltpu.HBM)


def prepare_kernel(far_weight, *refs):
    count = (len(refs) - 4) // 2
    fars, wide, nears = refs[:count], refs[count], refs[count + 1 : 2 * count + 1]
    out_weight, scratch, sems = refs[2 * count + 1 :]
    copies = [pltpu.make_async_copy(far_weight, out_weight, sems.at[count])]
    copies += [pltpu.make_async_copy(fars[i], nears[i], sems.at[i]) for i in range(count)]
    for copy in copies:
        copy.start()
    block = scratch.shape[0] // 3
    amount = scratch.shape[1] // LANES
    span = 3 * (amount + 2)
    scratch[...] = jnp.zeros_like(scratch)
    copies[0].wait()
    for a in range(3):
        for e in range(3):
            for b in range(3):
                piece = out_weight[a, b, e].astype(F32)
                for i in range(amount):
                    start = a * block + e * span + 3 * (i - b + 2)
                    scratch[start : start + 3, i * LANES : (i + 1) * LANES] = piece
    wide[...] = scratch[...].astype(BF16)
    for copy in copies[1:]:
        copy.wait()


def norm_constants(totals, cell_total):
    channels = totals.shape[1]
    size = channels // GROUPS
    totals = jnp.broadcast_to(totals, (8, channels))
    lane = mod(iota((8, channels), 1), size)
    first, second = [over_group(jnp.where(lane == i, totals, 0.0), size)[:1] for i in range(2)]
    mean = first / cell_total
    return mean, lax.rsqrt(second / cell_total - mean * mean + eps_norm)


def norm_slopes(state, mean, inverse, gain, shift):
    normed = (state - mean) * inverse
    return normed, silu_slope(normed * gain + shift) * gain


def slope_kernel(
    owner, arrived, hidden, gain, shift, wide, direct, edge_slopes, stats, sums, slopes_own, received
):
    devices, message_rows, _ = arrived.shape
    own_rows, frame_count, width, channels = hidden.shape
    cells = frame_count * width
    per_frame = devices // frame_count
    received[...] = arrived[...].reshape(received.shape)

    def from_all(row):
        return received[pl.ds(row, devices, stride=message_rows), :]

    totals = jnp.sum(from_all(3), axis=0, keepdims=True)
    mean, inverse = norm_constants(totals, own_rows * devices * cells * (channels // GROUPS))
    for i in range(own_rows):
        state = hidden[i].reshape(cells, channels).astype(F32)
        slopes_own[i] = norm_slopes(state, mean, inverse, gain[...], shift[...])[1]

    lines = jnp.concatenate([from_all(k) for k in range(3)], axis=1).astype(BF16)
    place = iota((1, devices), 1)
    source = jnp.zeros_like(place)
    for index, d in enumerate(first_order(devices)):
        source = jnp.where(place == index, d, source)
    home = jnp.zeros((1, devices), jnp.int32)
    for b in range(frame_count):
        home = jnp.where(div(source, per_frame) == b, owner[b] * per_frame, home)
    home = home + mod(source, per_frame)
    cell = iota((cells, 1), 0)
    column = mod(cell, width)
    frame_strip = div(cell, width) * per_frame
    lane = mod(iota((1, 3 * LANES), 1), PATCH)
    kept = []
    placed = None
    for e in range(3):
        wanted = column - e + 1
        if per_frame > 1 or placed is None:
            strip = frame_strip + div(wanted, PATCH) if per_frame > 1 else frame_strip
            placed = matmul(ones_where(home == strip), lines)
        inside = jnp.where((wanted >= 0) & (wanted < width), mod(wanted, PATCH), -1)
        kept.append(jnp.where(lane == inside, placed, 0.0).astype(BF16))
    block = wide.shape[0] // 3
    span = 3 * (own_rows + 4)
    entry = iota((3 * LANES, 1), 0)
    entry = div(mod(entry, LANES), PATCH) * 3 + div(entry, LANES)
    entry = jnp.where(entry < span, entry, -3 * span)
    tap = iota((1, block), 1)
    folds = jnp.concatenate([ones_where(tap == entry + e * span) for e in range(3)], axis=0)
    taps = matmul(jnp.concatenate(kept, axis=1), folds).astype(BF16)
    later = []
    for a in range(3):
        skip = (2 - a) * width
        later.append(
            jnp.concatenate([taps[skip:], jnp.zeros((skip, block), BF16)], axis=0) if skip else taps
        )
    result = matmul(jnp.concatenate(later, axis=1), wide[...])

    first = jnp.zeros((1, channels), F32)
    second = jnp.zeros((1, channels), F32)
    for i in range(own_rows):
        state = hidden[i].reshape(cells, channels).astype(F32)
        up = result[:, (i + 1) * channels : (i + 2) * channels] * slopes_own[i]
        direct[i] = up * inverse
        first = first + jnp.sum(up, axis=0, keepdims=True)
        second = second + jnp.sum(up * ((state - mean) * inverse), axis=0, keepdims=True)
    edge_slopes[0] = result[:, :channels]
    edge_slopes[1] = result[:, (own_rows + 1) * channels :]
    stats[0:1, :] = mean
    stats[1:2, :] = inverse
    both = jnp.where(iota((2, channels), 0) == 0, first, second)
    sums[...] = jnp.broadcast_to(both[None], sums.shape)


def late_kernel(
    place, across, along, slopes, stats, gain, shift, far_weight, direct, states, turned, inner_weight, sem
):
    copy = pltpu.make_async_copy(far_weight, inner_weight, sem.at[0])
    copy.start()
    cells, channels = slopes.shape[1:]
    odd = place[0] % 2 == 1
    mean = stats[0:1, :]
    inverse = stats[1:2, :]
    for i in range(2):
        state = jnp.where(odd == (i == 0), across[0], along[0])
        states[i] = state
        values = state.reshape(cells, channels).astype(F32)
        direct[i] = slopes[i] * norm_slopes(values, mean, inverse, gain[...], shift[...])[1] * inverse
    copy.wait()
    size = inner_weight.shape[3]
    for b in range(3):
        for a in range(3):
            for e in range(3):
                at = (a * 3 + e) * size
                turned[at : at + size, b * size : (b + 1) * size] = inner_weight[a, b, e].T


def inner_kernel(
    place, arrived, stats, direct, hidden, edge_direct, edge_states, turned, far_out, padded, out, sems, *, devices
):
    own_rows, frame_count, width, channels = out.shape
    cells = frame_count * width
    totals = jnp.sum(arrived[...], axis=0)
    cell_total = own_rows * devices * cells * (channels // GROUPS)
    place_row = iota((8, channels), 0)
    both = jnp.where(place_row == 0, totals[0:1], totals[1:2])
    both = over_group(both, channels // GROUPS)
    first, second = both[0:1], both[1:2]
    mean = stats[0:1, :]
    inverse = stats[1:2, :]
    constant = first / cell_total * inverse
    factor = second / cell_total * inverse * inverse
    position = place[0]
    in_frame = mod(iota((cells, 1), 0), width)
    for i in range(own_rows + 2):
        if 0 < i < own_rows + 1:
            state, part = hidden[i - 1], direct[i - 1]
        else:
            state, part = edge_states[min(i, 1)], edge_direct[min(i, 1)]
        grad = part - constant - (state.reshape(cells, channels).astype(F32) - mean) * factor
        if i == 0:
            grad = jnp.where(position > 0, grad, 0.0)
        if i == own_rows + 1:
            grad = jnp.where(position < devices - 1, grad, 0.0)
        after = jnp.where(in_frame < width - 1, pltpu.roll(grad, cells - 1, 0), 0.0)
        prior = jnp.where(in_frame > 0, pltpu.roll(grad, 1, 0), 0.0)
        padded[i, :cells, 0:channels] = after.astype(BF16)
        padded[i, :cells, channels : 2 * channels] = grad.astype(BF16)
        padded[i, :cells, 2 * channels :] = prior.astype(BF16)
        padded[i, cells:, :] = jnp.zeros((2 * width, 3 * channels), BF16)
    results = [jnp.zeros((cells, channels), F32) for _ in range(own_rows)]
    copies = []
    for i in range(own_rows + 2):
        joined = jnp.concatenate(
            [padded[i, (2 - a) * width : (2 - a) * width + cells, :] for a in range(3)], axis=1
        )
        taps = [b for b in range(3) if 0 <= i + b - 2 < own_rows]
        for low in range(0, len(taps), 2):
            some = taps[low : low + 2]
            product = matmul(joined, turned[:, some[0] * channels : (some[-1] + 1) * channels])
            for step, b in enumerate(some):
                results[i + b - 2] = results[i + b - 2] + product[:, step * channels : (step + 1) * channels]
        if i >= 2:
            out[i - 2] = results[i - 2].reshape(frame_count, width, channels).astype(BF16)
            copies.append(pltpu.make_async_copy(out.at[i - 2], far_out.at[i - 2], sems.at[i - 2]))
            copies[-1].start()
    for copy in copies:
        copy.wait()


def per_device(
    frames,
    frame_owner,
    picks,
    patch_weight,
    patch_bias,
    norm_gain,
    head_weight,
    head_bias,
    head_out,
    hidden_state,
    group_gain,
    group_shift,
    out_weight,
    inner_weight,
):
    devices = lax.axis_size("row")
    position = lax.axis_index("row").astype(jnp.int32).reshape(1)
    per_frame = devices // FRAMES
    height = frames.shape[1]
    own_rows, _, frame_width, channels = hidden_state.shape
    cells = FRAMES * frame_width
    width = patch_weight.shape[1]
    turned_frames = jnp.transpose(frames, (0, 2, 1))
    bias = patch_bias.reshape(1, width)
    gain = norm_gain.reshape(1, width)
    head_bias_row = head_bias.reshape(1, width)
    head_out_row = head_out.reshape(1, width)
    state_rows = own_rows + 2
    tap_rows = -(-9 * (own_rows + 4) // LANES) * LANES
    edge = jax.ShapeDtypeStruct((1,) + hidden_state.shape[1:], BF16)
    message = (message_shape(devices), edge, edge)
    gain_row = group_gain.reshape(1, channels)
    shift_row = group_shift.reshape(1, channels)
    early = [hidden_state, gain_row, shift_row]
    wide, *early = pl.pallas_call(
        prepare_kernel,
        out_shape=(
            pltpu.VMEM((3 * tap_rows, state_rows * channels), BF16),
            *[pltpu.VMEM(x.shape, x.dtype) for x in early],
        ),
        in_specs=[FAR] * (1 + len(early)),
        scratch_shapes=[
            pltpu.VMEM(out_weight.shape, BF16),
            pltpu.VMEM((3 * tap_rows, state_rows * channels), F32),
            pltpu.SemaphoreType.DMA((1 + len(early),)),
        ],
        compiler_params=params(cells),
        name="prepare",
    )(far(out_weight), *[far(x) for x in early])
    early = [near(x) for x in early]
    slope_outs = (
        pltpu.VMEM((own_rows, cells, channels), F32),
        pltpu.VMEM((2, cells, channels), F32),
        pltpu.VMEM((8, channels), F32),
        jax.ShapeDtypeStruct((devices, 2, channels), F32),
    )
    if per_frame == 1:
        arrays = [
            turned_frames,
            bias,
            gain,
            frame_owner,
            picks,
            head_bias_row,
            head_out_row,
            hidden_state,
            patch_weight,
            head_weight,
        ]
        send, across, along = pl.pallas_call(
            reward_kernel,
            out_shape=message,
            in_specs=[SMEM] + [FAR] * len(arrays),
            out_specs=[VMEM] * 3,
            scratch_shapes=[
                (pltpu.SMEM if x.dtype == jnp.int32 else pltpu.VMEM)(x.shape, x.dtype) for x in arrays
            ]
            + [pltpu.SemaphoreType.DMA((len(arrays) + 16,))],
            compiler_params=params(0),
            name="reward",
        )(position, *[far(x) for x in arrays])
    else:
        count = height // PATCH
        normed, inv_spread, partial = pl.pallas_call(
            forward_kernel,
            out_shape=(
                jax.ShapeDtypeStruct((token_rows_of(height), width), F32),
                jax.ShapeDtypeStruct((token_rows_of(height), LANES), F32),
                jax.ShapeDtypeStruct((1, width), F32),
            ),
            compiler_params=params(cells),
            name="reward_forward",
        )(turned_frames, bias, gain, patch_weight)
        members = [[b * per_frame + i for i in range(per_frame)] for b in range(FRAMES)]
        pooled = lax.psum(partial, "row", axis_index_groups=members) / (count * per_frame)
        send, across, along = pl.pallas_call(
            functools.partial(backward_kernel, height=height, per_frame=per_frame),
            out_shape=message,
            in_specs=[SMEM] * 3 + [VMEM] * 9,
            out_specs=[VMEM] * 3,
            compiler_params=params(cells),
            name="reward_backward",
        )(
            frame_owner,
            picks,
            position,
            hidden_state,
            gain,
            head_bias_row,
            head_out_row,
            normed,
            inv_spread,
            pooled,
            patch_weight,
            head_weight,
        )
    arrived = lax.all_to_all(send, "row", 0, 0, axis_index_groups=[first_order(devices)], tiled=True)
    direct, edge_slopes, stats, sums = pl.pallas_call(
        slope_kernel,
        out_shape=slope_outs,
        in_specs=[SMEM] + [VMEM] * 5,
        scratch_shapes=[
            pltpu.VMEM((own_rows, cells, channels), F32),
            pltpu.VMEM((4 * devices, LANES), F32),
        ],
        compiler_params=params(cells),
        name="slope",
    )(frame_owner, near(arrived), *early, near(wide))
    swaps = [(2 * i, 2 * i + 1) for i in range(devices // 2)]
    across = lax.ppermute(across, "row", swaps + [(b, a) for a, b in swaps])
    swaps = [(2 * i - 1, 2 * i) for i in range(1, devices // 2)]
    along = lax.ppermute(along, "row", swaps + [(b, a) for a, b in swaps])
    summed = lax.all_to_all(sums, "row", 0, 0, axis_index_groups=[led_by(devices - 1, devices)], tiled=True)
    edge_direct, edge_states, turned = pl.pallas_call(
        late_kernel,
        out_shape=(
            pltpu.VMEM((2, cells, channels), F32),
            pltpu.VMEM((2,) + hidden_state.shape[1:], BF16),
            pltpu.VMEM((9 * channels, 3 * channels), BF16),
        ),
        in_specs=[SMEM] + [VMEM] * 6 + [FAR],
        scratch_shapes=[pltpu.VMEM(inner_weight.shape, BF16), pltpu.SemaphoreType.DMA((1,))],
        input_output_aliases={3: 0},
        compiler_params=params(cells),
        name="late",
    )(position, near(across), near(along), near(edge_slopes), near(stats), *early[1:3], far(inner_weight))
    return pl.pallas_call(
        functools.partial(inner_kernel, devices=devices),
        out_shape=jax.ShapeDtypeStruct(hidden_state.shape, BF16),
        in_specs=[SMEM] + [VMEM] * 7,
        out_specs=FAR,
        scratch_shapes=[
            pltpu.VMEM((own_rows + 2, cells + 2 * frame_width, 3 * channels), BF16),
            pltpu.VMEM(hidden_state.shape, BF16),
            pltpu.SemaphoreType.DMA((own_rows,)),
        ],
        compiler_params=params(cells),
        name="inner",
    )(
        position,
        near(summed),
        near(stats),
        near(direct),
        early[0],
        near(edge_direct),
        near(edge_states),
        near(turned),
    )


def solution(mesh):
    return jax.shard_map(
        per_device,
        mesh=mesh,
        in_specs=(
            P(None, None, ("clip", "row")),
            P("clip"),
            P("clip"),
            P(),
            P(),
            P(),
            P(),
            P(),
            P(),
            P(("clip", "row"), None, None, None),
            P(),
            P(),
            P(),
            P(),
        ),
        out_specs=P(("clip", "row"), None, None, None),
        check_vma=False,
    )
```

```python
import functools

import jax
import jax.numpy as jnp
from jax import lax
from jax.experimental import pallas as pl
from jax.experimental.pallas import tpu as pltpu
from jax.sharding import PartitionSpec as P

PATCH = 16
GROUPS = 32
FRAMES = 16
LANES = 128
SLOTS = LANES // PATCH
eps_norm = 1e-06
BF16 = jnp.bfloat16
F32 = jnp.float32

SMEM = pl.BlockSpec(memory_space=pltpu.SMEM)
VMEM = pl.BlockSpec(memory_space=pltpu.VMEM)
FAR = pl.BlockSpec(memory_space=pl.ANY)


def iota(shape, dim):
    return lax.broadcasted_iota(jnp.int32, shape, dim)


def div(values, count):
    if count & (count - 1):
        return values // count
    return values >> (count.bit_length() - 1)


def mod(values, count):
    if count & (count - 1):
        return values % count
    return values & (count - 1)


def ones_where(condition):
    return jnp.where(condition, 1.0, 0.0).astype(BF16)


def matmul(left, right):
    return jnp.dot(left, right, preferred_element_type=F32)


def matmul_t(left, right):
    return lax.dot_general(left, right, (((1,), (1,)), ((), ())), preferred_element_type=F32)


def cut_in_three(values):
    high = values.astype(BF16)
    rest = values - high.astype(F32)
    middle = rest.astype(BF16)
    low = (rest - middle.astype(F32)).astype(BF16)
    return high, middle, low


def exact_rows(rows, product):
    place = iota((16, rows[0].shape[1]), 0)
    stacked = jnp.zeros(place.shape, F32)
    for index, row in enumerate(rows):
        for step, piece in enumerate(cut_in_three(row)):
            stacked = jnp.where(place == 3 * index + step, piece.astype(F32), stacked)
    result = product(stacked.astype(BF16))
    return [
        result[3 * i : 3 * i + 1] + result[3 * i + 1 : 3 * i + 2] + result[3 * i + 2 : 3 * i + 3]
        for i in range(len(rows))
    ]


def silu_slope(values):
    sigmoid = jax.nn.sigmoid(values)
    return sigmoid * (1.0 + values * (1.0 - sigmoid))


def token_rows_of(height):
    return -(-(height // PATCH) // 16) * 16


def to_tokens(pixels):
    channels, columns, height = pixels.shape
    rows = channels * columns
    token_rows = token_rows_of(height)
    flat = pixels.reshape(rows, height)
    width = channels * PATCH * columns
    lane = iota((1, width), 1)
    place = iota((rows, 1), 0)
    mine = place == div(lane, PATCH * columns) * columns + mod(lane, columns)
    in_patch = mod(div(lane, columns), PATCH)
    pixel_row = iota((height, 1), 0)
    token = iota((token_rows, 1), 0)
    tokens = jnp.zeros((token_rows, width), F32)
    for t in range(height // PATCH):
        tiled = matmul(flat, ones_where(pixel_row == in_patch + t * PATCH))
        row = jnp.sum(jnp.where(mine, tiled, 0.0), axis=0, keepdims=True)
        tokens = jnp.where(token == t, row, tokens)
    return tokens.astype(BF16)


def forward_part(tokens, count, bias, gain, load_patch):
    embedded = bias[...]
    for low, high, weight in load_patch():
        embedded = embedded + matmul(tokens[:, low:high], weight)
    centred = embedded - jnp.mean(embedded, axis=1, keepdims=True)
    inv_spread = lax.rsqrt(jnp.mean(centred * centred, axis=1, keepdims=True) + eps_norm)
    normed = centred * inv_spread
    weighted = normed * gain[...]
    inside = iota((tokens.shape[0], 1), 0) < count
    pooled = jnp.sum(jnp.where(inside, weighted, 0.0), axis=0, keepdims=True)
    return normed, inv_spread, pooled


def led_by(leader, devices):
    return [leader] + [d for d in reversed(range(devices)) if d != leader]


def first_order(devices):
    return led_by(devices * 9 // 16, devices)


def message_shape(devices):
    return jax.ShapeDtypeStruct((devices, 4, LANES), F32)


def write_windows(patch_grad, sums, own_rows, height, send):
    span = PATCH * PATCH
    line = jnp.concatenate(
        [
            jnp.concatenate([patch_grad[t : t + 1, k * span : (k + 1) * span] for t in range(height // PATCH)], axis=1)
            for k in range(3)
        ]
        + [jnp.zeros((1, height * PATCH), F32)],
        axis=0,
    )
    line = jnp.concatenate([jnp.zeros((4, LANES), F32), line, jnp.zeros((4, LANES), F32)], axis=1)
    used = iota((4, LANES), 1) < (own_rows + 4) * PATCH
    colour = iota((4, LANES), 0)
    for index, d in enumerate(first_order(send.shape[0])):
        start = LANES + (d * own_rows - 2) * PATCH
        window = jnp.where(used, line[:, start : start + LANES], 0.0)
        send[index] = jnp.where(colour < 3, window, sums[:4])


def channel_sums(hidden):
    values = hidden.reshape(-1, hidden.shape[-1]).astype(F32)
    return jnp.sum(values, axis=0, keepdims=True), jnp.sum(values * values, axis=0, keepdims=True)


def over_group(values, size):
    lane = iota(values.shape, 1)
    lanes = values.shape[1]
    step = 1
    while step < size:
        later = pltpu.roll(values, lanes - step, 1)
        earlier = pltpu.roll(values, step, 1)
        values = values + jnp.where((lane & step) == 0, later, earlier)
        step *= 2
    return values


def group_sums(hidden):
    channels = hidden.shape[-1]
    size = channels // GROUPS
    first, second = [
        over_group(jnp.broadcast_to(x, (8, channels)), size) for x in channel_sums(hidden)
    ]
    lane = mod(iota((8, channels), 1), size)
    return jnp.where(lane == 0, first, jnp.where(lane == 1, second, 0.0))


def pull_back(row, weight):
    parts = []
    for low in range(0, weight.shape[0], LANES):
        product = weight[low : low + LANES, :].astype(F32) * row
        folded = product[:, :LANES]
        for start in range(LANES, weight.shape[1], LANES):
            folded = folded + product[:, start : start + LANES]
        parts.append(jnp.sum(folded.T, axis=0, keepdims=True))
    return jnp.concatenate(parts, axis=1)


def backward_part(
    owner, picks, gain, head_bias, head_out, normed, inv_spread, pooled, weight, head, slot, own_rows, height, sums, send
):
    (before,) = exact_rows([pooled], lambda rows: matmul(rows, head[...]))
    slope = head_out[...] * silu_slope(before + head_bias[...])
    pulled = pull_back(slope, head)
    wanted = owner[slot]
    picked = jnp.int32(0)
    for k in range(picks.shape[0]):
        picked = picked + jnp.where(picks[k] == wanted, 1, 0)
    scaled = gain[...] * (picked.astype(F32) * pulled)
    token_grad = inv_spread * (
        scaled
        - jnp.mean(scaled, axis=1, keepdims=True)
        - normed * jnp.mean(scaled * normed, axis=1, keepdims=True)
    )
    patch_grad = matmul_t(token_grad.astype(BF16), weight[...]).astype(BF16).astype(F32)
    write_windows(patch_grad, sums, own_rows, height, send)


def write_edges(place, hidden, across, along):
    last = hidden.shape[0] - 1
    even = place[0] % 2 == 0
    across[0] = hidden[jnp.where(even, last, 0)]
    along[0] = hidden[jnp.where(even, 0, last)]


def reward_kernel(place, *refs):
    count, kept = 7, 4
    far, refs = refs[: count + kept + 2], refs[count + kept + 2 :]
    send, across, along = refs[:3]
    near = refs[3 + kept : 3 + kept + count] + refs[3 : 3 + kept] + refs[3 + kept + count : -1]
    sems = refs[-1]
    frames, bias, gain, owner, picks, head_bias, head_out, hidden, _, _, _, patch, head = near
    count += kept
    depth, depths = 256, (128, 256)
    small = [pltpu.make_async_copy(far[i], near[i], sems.at[i]) for i in range(count)]
    pieces = []
    used = count
    for index, rows in enumerate(depths):
        source, target = far[count + index], near[count + index]
        parts = []
        for low in range(0, target.shape[0], rows):
            part = pl.ds(low, rows)
            parts.append(pltpu.make_async_copy(source.at[part], target.at[part], sems.at[used]))
            used += 1
        pieces.append(parts)
    for copy in [small[0], small[7], small[1]] + pieces[0] + small[2:7] + pieces[1] + small[8:]:
        copy.start()

    def load_patch():
        for low in range(0, patch.shape[0], depth):
            for copy in pieces[0][low // depths[0] : (low + depth) // depths[0]]:
                copy.wait()
            yield low, low + depth, patch[low : low + depth, :]

    height = frames.shape[2]
    patches = height // PATCH
    small[0].wait()
    small[7].wait()
    tokens = to_tokens(frames[...])
    sums = group_sums(hidden[...])
    write_edges(place, hidden, across, along)
    small[1].wait()
    small[2].wait()
    normed, inv_spread, pooled = forward_part(tokens, patches, bias, gain, load_patch)
    for copy in small[3:7] + pieces[1]:
        copy.wait()
    backward_part(
        owner,
        picks,
        gain,
        head_bias,
        head_out,
        normed,
        inv_spread,
        pooled / patches,
        patch,
        head,
        place[0],
        hidden.shape[0],
        height,
        sums,
        send,
    )
    for copy in small[8:]:
        copy.wait()


def forward_kernel(frames, bias, gain, patch, normed, inv_spread, pooled):
    width = patch.shape[0]
    tokens = to_tokens(frames[...])
    normed[...], spread, pooled[...] = forward_part(
        tokens, frames.shape[2] // PATCH, bias, gain, lambda: [(0, width, patch[...])]
    )
    inv_spread[...] = jnp.broadcast_to(spread, inv_spread.shape)


def backward_kernel(
    owner,
    picks,
    place,
    hidden,
    gain,
    head_bias,
    head_out,
    normed,
    inv_spread,
    pooled,
    patch,
    head,
    send,
    across,
    along,
    *,
    height,
    per_frame,
):
    write_edges(place, hidden, across, along)
    backward_part(
        owner,
        picks,
        gain,
        head_bias,
        head_out,
        normed[...],
        inv_spread[...][:, :1],
        pooled[...],
        patch,
        head,
        place[0] // per_frame,
        hidden.shape[0],
        height,
        group_sums(hidden[...]),
        send,
    )


def params(cells):
    return pltpu.CompilerParams(vmem_limit_bytes=min(16 + cells // 64, 48) * 1024 * 1024)


def near(array):
    return pltpu.with_memory_space_constraint(array, pltpu.VMEM)


def far(array):
    return pltpu.with_memory_space_constraint(array, pltpu.HBM)


def prepare_kernel(out_weight, wide, scratch):
    block = scratch.shape[0] // 3
    amount = scratch.shape[1] // LANES
    span = 3 * (amount + 2)
    scratch[...] = jnp.zeros_like(scratch)
    for a in range(3):
        for e in range(3):
            for b in range(3):
                piece = out_weight[a, b, e].astype(F32)
                for i in range(amount):
                    start = a * block + e * span + 3 * (i - b + 2)
                    scratch[start : start + 3, i * LANES : (i + 1) * LANES] = piece
    wide[...] = scratch[...].astype(BF16)


def norm_constants(totals, cell_total):
    channels = totals.shape[1]
    size = channels // GROUPS
    totals = jnp.broadcast_to(totals, (8, channels))
    lane = mod(iota((8, channels), 1), size)
    first, second = [over_group(jnp.where(lane == i, totals, 0.0), size)[:1] for i in range(2)]
    mean = first / cell_total
    return mean, lax.rsqrt(second / cell_total - mean * mean + eps_norm)


def norm_slopes(state, mean, inverse, gain, shift):
    normed = (state - mean) * inverse
    return normed, silu_slope(normed * gain + shift) * gain


def slope_kernel(
    owner, arrived, hidden, gain, shift, wide, direct, edge_slopes, stats, sums, slopes_own, received
):
    devices, message_rows, _ = arrived.shape
    own_rows, frame_count, width, channels = hidden.shape
    cells = frame_count * width
    per_frame = devices // frame_count
    received[...] = arrived[...].reshape(received.shape)

    def from_all(row):
        return received[pl.ds(row, devices, stride=message_rows), :]

    totals = jnp.sum(from_all(3), axis=0, keepdims=True)
    mean, inverse = norm_constants(totals, own_rows * devices * cells * (channels // GROUPS))
    for i in range(own_rows):
        state = hidden[i].reshape(cells, channels).astype(F32)
        slopes_own[i] = norm_slopes(state, mean, inverse, gain[...], shift[...])[1]

    lines = jnp.concatenate([from_all(k) for k in range(3)], axis=1).astype(BF16)
    place = iota((1, devices), 1)
    source = jnp.zeros_like(place)
    for index, d in enumerate(first_order(devices)):
        source = jnp.where(place == index, d, source)
    home = jnp.zeros((1, devices), jnp.int32)
    for b in range(frame_count):
        home = jnp.where(div(source, per_frame) == b, owner[b] * per_frame, home)
    home = home + mod(source, per_frame)
    cell = iota((cells, 1), 0)
    column = mod(cell, width)
    frame_strip = div(cell, width) * per_frame
    lane = mod(iota((1, 3 * LANES), 1), PATCH)
    kept = []
    placed = None
    for e in range(3):
        wanted = column - e + 1
        if per_frame > 1 or placed is None:
            strip = frame_strip + div(wanted, PATCH) if per_frame > 1 else frame_strip
            placed = matmul(ones_where(home == strip), lines)
        inside = jnp.where((wanted >= 0) & (wanted < width), mod(wanted, PATCH), -1)
        kept.append(jnp.where(lane == inside, placed, 0.0).astype(BF16))
    block = wide.shape[0] // 3
    span = 3 * (own_rows + 4)
    entry = iota((3 * LANES, 1), 0)
    entry = div(mod(entry, LANES), PATCH) * 3 + div(entry, LANES)
    entry = jnp.where(entry < span, entry, -3 * span)
    tap = iota((1, block), 1)
    folds = jnp.concatenate([ones_where(tap == entry + e * span) for e in range(3)], axis=0)
    taps = matmul(jnp.concatenate(kept, axis=1), folds).astype(BF16)
    later = []
    for a in range(3):
        skip = (2 - a) * width
        later.append(
            jnp.concatenate([taps[skip:], jnp.zeros((skip, block), BF16)], axis=0) if skip else taps
        )
    result = matmul(jnp.concatenate(later, axis=1), wide[...])

    first = jnp.zeros((1, channels), F32)
    second = jnp.zeros((1, channels), F32)
    for i in range(own_rows):
        state = hidden[i].reshape(cells, channels).astype(F32)
        up = result[:, (i + 1) * channels : (i + 2) * channels] * slopes_own[i]
        direct[i] = up * inverse
        first = first + jnp.sum(up, axis=0, keepdims=True)
        second = second + jnp.sum(up * ((state - mean) * inverse), axis=0, keepdims=True)
    edge_slopes[0] = result[:, :channels]
    edge_slopes[1] = result[:, (own_rows + 1) * channels :]
    stats[0:1, :] = mean
    stats[1:2, :] = inverse
    both = jnp.where(iota((2, channels), 0) == 0, first, second)
    sums[...] = jnp.broadcast_to(both[None], sums.shape)


def late_kernel(
    place, across, along, slopes, stats, gain, shift, far_weight, direct, states, turned, inner_weight, sem
):
    copy = pltpu.make_async_copy(far_weight, inner_weight, sem.at[0])
    copy.start()
    cells, channels = slopes.shape[1:]
    odd = place[0] % 2 == 1
    mean = stats[0:1, :]
    inverse = stats[1:2, :]
    for i in range(2):
        state = jnp.where(odd == (i == 0), across[0], along[0])
        states[i] = state
        values = state.reshape(cells, channels).astype(F32)
        direct[i] = slopes[i] * norm_slopes(values, mean, inverse, gain[...], shift[...])[1] * inverse
    copy.wait()
    size = inner_weight.shape[3]
    for b in range(3):
        for a in range(3):
            for e in range(3):
                at = (a * 3 + e) * size
                turned[at : at + size, b * size : (b + 1) * size] = inner_weight[a, b, e].T


def inner_kernel(
    place, arrived, stats, direct, hidden, edge_direct, edge_states, turned, far_out, padded, out, sems, *, devices
):
    own_rows, frame_count, width, channels = out.shape
    cells = frame_count * width
    totals = jnp.sum(arrived[...], axis=0)
    cell_total = own_rows * devices * cells * (channels // GROUPS)
    place_row = iota((8, channels), 0)
    both = jnp.where(place_row == 0, totals[0:1], totals[1:2])
    both = over_group(both, channels // GROUPS)
    first, second = both[0:1], both[1:2]
    mean = stats[0:1, :]
    inverse = stats[1:2, :]
    constant = first / cell_total * inverse
    factor = second / cell_total * inverse * inverse
    position = place[0]
    in_frame = mod(iota((cells, 1), 0), width)
    for i in range(own_rows + 2):
        if 0 < i < own_rows + 1:
            state, part = hidden[i - 1], direct[i - 1]
        else:
            state, part = edge_states[min(i, 1)], edge_direct[min(i, 1)]
        grad = part - constant - (state.reshape(cells, channels).astype(F32) - mean) * factor
        if i == 0:
            grad = jnp.where(position > 0, grad, 0.0)
        if i == own_rows + 1:
            grad = jnp.where(position < devices - 1, grad, 0.0)
        after = jnp.where(in_frame < width - 1, pltpu.roll(grad, cells - 1, 0), 0.0)
        prior = jnp.where(in_frame > 0, pltpu.roll(grad, 1, 0), 0.0)
        padded[i, :cells, 0:channels] = after.astype(BF16)
        padded[i, :cells, channels : 2 * channels] = grad.astype(BF16)
        padded[i, :cells, 2 * channels :] = prior.astype(BF16)
        padded[i, cells:, :] = jnp.zeros((2 * width, 3 * channels), BF16)
    results = [jnp.zeros((cells, channels), F32) for _ in range(own_rows)]
    copies = []
    for i in range(own_rows + 2):
        joined = jnp.concatenate(
            [padded[i, (2 - a) * width : (2 - a) * width + cells, :] for a in range(3)], axis=1
        )
        taps = [b for b in range(3) if 0 <= i + b - 2 < own_rows]
        for low in range(0, len(taps), 2):
            some = taps[low : low + 2]
            product = matmul(joined, turned[:, some[0] * channels : (some[-1] + 1) * channels])
            for step, b in enumerate(some):
                results[i + b - 2] = results[i + b - 2] + product[:, step * channels : (step + 1) * channels]
        if i >= 2:
            out[i - 2] = results[i - 2].reshape(frame_count, width, channels).astype(BF16)
            copies.append(pltpu.make_async_copy(out.at[i - 2], far_out.at[i - 2], sems.at[i - 2]))
            copies[-1].start()
    for copy in copies:
        copy.wait()


def per_device(
    frames,
    frame_owner,
    picks,
    patch_weight,
    patch_bias,
    norm_gain,
    head_weight,
    head_bias,
    head_out,
    hidden_state,
    group_gain,
    group_shift,
    out_weight,
    inner_weight,
):
    devices = lax.axis_size("row")
    position = lax.axis_index("row").astype(jnp.int32).reshape(1)
    per_frame = devices // FRAMES
    height = frames.shape[1]
    own_rows, _, frame_width, channels = hidden_state.shape
    cells = FRAMES * frame_width
    width = patch_weight.shape[1]
    turned_frames = jnp.transpose(frames, (0, 2, 1))
    bias = patch_bias.reshape(1, width)
    gain = norm_gain.reshape(1, width)
    head_bias_row = head_bias.reshape(1, width)
    head_out_row = head_out.reshape(1, width)
    state_rows = own_rows + 2
    tap_rows = -(-9 * (own_rows + 4) // LANES) * LANES
    edge = jax.ShapeDtypeStruct((1,) + hidden_state.shape[1:], BF16)
    message = (message_shape(devices), edge, edge)
    gain_row = group_gain.reshape(1, channels)
    shift_row = group_shift.reshape(1, channels)
    early = [hidden_state, gain_row, shift_row, out_weight]
    slope_outs = (
        pltpu.VMEM((own_rows, cells, channels), F32),
        pltpu.VMEM((2, cells, channels), F32),
        pltpu.VMEM((8, channels), F32),
        jax.ShapeDtypeStruct((devices, 2, channels), F32),
    )
    if per_frame == 1:
        arrays = [turned_frames, bias, gain, frame_owner, picks, head_bias_row, head_out_row]
        weights = [patch_weight, head_weight]

        def scratch(x):
            return (pltpu.SMEM if x.dtype == jnp.int32 else pltpu.VMEM)(x.shape, x.dtype)

        send, across, along, *early = pl.pallas_call(
            reward_kernel,
            out_shape=message + tuple(pltpu.VMEM(x.shape, x.dtype) for x in early),
            in_specs=[SMEM] + [FAR] * (len(arrays) + len(early) + len(weights)),
            out_specs=[VMEM] * (3 + len(early)),
            scratch_shapes=[scratch(x) for x in arrays + weights] + [pltpu.SemaphoreType.DMA((32,))],
            compiler_params=params(0),
            name="reward",
        )(position, *[far(x) for x in arrays + early + weights])
    else:
        count = height // PATCH
        normed, inv_spread, partial = pl.pallas_call(
            forward_kernel,
            out_shape=(
                jax.ShapeDtypeStruct((token_rows_of(height), width), F32),
                jax.ShapeDtypeStruct((token_rows_of(height), LANES), F32),
                jax.ShapeDtypeStruct((1, width), F32),
            ),
            compiler_params=params(cells),
            name="reward_forward",
        )(turned_frames, bias, gain, patch_weight)
        members = [[b * per_frame + i for i in range(per_frame)] for b in range(FRAMES)]
        pooled = lax.psum(partial, "row", axis_index_groups=members) / (count * per_frame)
        send, across, along = pl.pallas_call(
            functools.partial(backward_kernel, height=height, per_frame=per_frame),
            out_shape=message,
            in_specs=[SMEM] * 3 + [VMEM] * 9,
            out_specs=[VMEM] * 3,
            compiler_params=params(cells),
            name="reward_backward",
        )(
            frame_owner,
            picks,
            position,
            hidden_state,
            gain,
            head_bias_row,
            head_out_row,
            normed,
            inv_spread,
            pooled,
            patch_weight,
            head_weight,
        )
    early = [near(x) for x in early]
    wide = pl.pallas_call(
        prepare_kernel,
        out_shape=pltpu.VMEM((3 * tap_rows, state_rows * channels), BF16),
        in_specs=[VMEM],
        scratch_shapes=[pltpu.VMEM((3 * tap_rows, state_rows * channels), F32)],
        compiler_params=params(cells),
        name="prepare",
    )(early[3])
    arrived = lax.all_to_all(send, "row", 0, 0, axis_index_groups=[first_order(devices)], tiled=True)
    direct, edge_slopes, stats, sums = pl.pallas_call(
        slope_kernel,
        out_shape=slope_outs,
        in_specs=[SMEM] + [VMEM] * 5,
        scratch_shapes=[
            pltpu.VMEM((own_rows, cells, channels), F32),
            pltpu.VMEM((4 * devices, LANES), F32),
        ],
        compiler_params=params(cells),
        name="slope",
    )(frame_owner, near(arrived), *early[:3], near(wide))
    swaps = [(2 * i, 2 * i + 1) for i in range(devices // 2)]
    across = lax.ppermute(across, "row", swaps + [(b, a) for a, b in swaps])
    swaps = [(2 * i - 1, 2 * i) for i in range(1, devices // 2)]
    along = lax.ppermute(along, "row", swaps + [(b, a) for a, b in swaps])
    summed = lax.all_to_all(sums, "row", 0, 0, axis_index_groups=[led_by(devices - 1, devices)], tiled=True)
    edge_direct, edge_states, turned = pl.pallas_call(
        late_kernel,
        out_shape=(
            pltpu.VMEM((2, cells, channels), F32),
            pltpu.VMEM((2,) + hidden_state.shape[1:], BF16),
            pltpu.VMEM((9 * channels, 3 * channels), BF16),
        ),
        in_specs=[SMEM] + [VMEM] * 6 + [FAR],
        scratch_shapes=[pltpu.VMEM(inner_weight.shape, BF16), pltpu.SemaphoreType.DMA((1,))],
        input_output_aliases={3: 0},
        compiler_params=params(cells),
        name="late",
    )(position, near(across), near(along), near(edge_slopes), near(stats), *early[1:3], far(inner_weight))
    return pl.pallas_call(
        functools.partial(inner_kernel, devices=devices),
        out_shape=jax.ShapeDtypeStruct(hidden_state.shape, BF16),
        in_specs=[SMEM] + [VMEM] * 7,
        out_specs=FAR,
        scratch_shapes=[
            pltpu.VMEM((own_rows + 2, cells + 2 * frame_width, 3 * channels), BF16),
            pltpu.VMEM(hidden_state.shape, BF16),
            pltpu.SemaphoreType.DMA((own_rows,)),
        ],
        compiler_params=params(cells),
        name="inner",
    )(
        position,
        near(summed),
        near(stats),
        near(direct),
        early[0],
        near(edge_direct),
        near(edge_states),
        near(turned),
    )


def solution(mesh):
    return jax.shard_map(
        per_device,
        mesh=mesh,
        in_specs=(
            P(None, None, ("clip", "row")),
            P("clip"),
            P("clip"),
            P(),
            P(),
            P(),
            P(),
            P(),
            P(),
            P(("clip", "row"), None, None, None),
            P(),
            P(),
            P(),
            P(),
        ),
        out_specs=P(("clip", "row"), None, None, None),
        check_vma=False,
    )
```

```python
import functools

import jax
import jax.numpy as jnp
from jax import lax
from jax.experimental import pallas as pl
from jax.experimental.pallas import tpu as pltpu
from jax.sharding import PartitionSpec as P

PATCH = 16
GROUPS = 32
FRAMES = 16
LANES = 128
SLOTS = LANES // PATCH
eps_norm = 1e-06
BF16 = jnp.bfloat16
F32 = jnp.float32

SMEM = pl.BlockSpec(memory_space=pltpu.SMEM)
VMEM = pl.BlockSpec(memory_space=pltpu.VMEM)
FAR = pl.BlockSpec(memory_space=pl.ANY)


def iota(shape, dim):
    return lax.broadcasted_iota(jnp.int32, shape, dim)


def div(values, count):
    if count & (count - 1):
        return values // count
    return values >> (count.bit_length() - 1)


def mod(values, count):
    if count & (count - 1):
        return values % count
    return values & (count - 1)


def ones_where(condition):
    return jnp.where(condition, 1.0, 0.0).astype(BF16)


def matmul(left, right):
    return jnp.dot(left, right, preferred_element_type=F32)


def matmul_t(left, right):
    return lax.dot_general(left, right, (((1,), (1,)), ((), ())), preferred_element_type=F32)


def cut_in_three(values):
    high = values.astype(BF16)
    rest = values - high.astype(F32)
    middle = rest.astype(BF16)
    low = (rest - middle.astype(F32)).astype(BF16)
    return high, middle, low


def exact_rows(rows, product):
    place = iota((16, rows[0].shape[1]), 0)
    stacked = jnp.zeros(place.shape, F32)
    for index, row in enumerate(rows):
        for step, piece in enumerate(cut_in_three(row)):
            stacked = jnp.where(place == 3 * index + step, piece.astype(F32), stacked)
    result = product(stacked.astype(BF16))
    return [
        result[3 * i : 3 * i + 1] + result[3 * i + 1 : 3 * i + 2] + result[3 * i + 2 : 3 * i + 3]
        for i in range(len(rows))
    ]


def silu_slope(values):
    sigmoid = 0.5 + 0.5 * jnp.tanh(0.5 * values)
    return sigmoid * (1.0 + values * (1.0 - sigmoid))


def token_rows_of(height):
    return -(-(height // PATCH) // 16) * 16


def to_tokens(pixels):
    channels, columns, height = pixels.shape
    rows = channels * columns
    token_rows = token_rows_of(height)
    flat = pixels.reshape(rows, height)
    width = channels * PATCH * columns
    lane = iota((1, width), 1)
    place = iota((rows, 1), 0)
    mine = place == div(lane, PATCH * columns) * columns + mod(lane, columns)
    in_patch = mod(div(lane, columns), PATCH)
    pixel_row = iota((height, 1), 0)
    token = iota((token_rows, 1), 0)
    tokens = jnp.zeros((token_rows, width), F32)
    for t in range(height // PATCH):
        tiled = matmul(flat, ones_where(pixel_row == in_patch + t * PATCH))
        row = jnp.sum(jnp.where(mine, tiled, 0.0), axis=0, keepdims=True)
        tokens = jnp.where(token == t, row, tokens)
    return tokens.astype(BF16)


def forward_part(tokens, count, bias, gain, load_patch):
    embedded = bias[...]
    for low, high, weight in load_patch():
        embedded = embedded + matmul(tokens[:, low:high], weight)
    centred = embedded - jnp.mean(embedded, axis=1, keepdims=True)
    inv_spread = lax.rsqrt(jnp.mean(centred * centred, axis=1, keepdims=True) + eps_norm)
    normed = centred * inv_spread
    weighted = normed * gain[...]
    inside = iota((tokens.shape[0], 1), 0) < count
    pooled = jnp.sum(jnp.where(inside, weighted, 0.0), axis=0, keepdims=True)
    return normed, inv_spread, pooled


def led_by(leader, devices):
    return [leader] + [d for d in reversed(range(devices)) if d != leader]


def first_order(devices):
    return led_by(devices * 9 // 16, devices)


def message_shape(devices):
    return jax.ShapeDtypeStruct((devices, 4, LANES), F32)


def write_windows(patch_grad, sums, own_rows, height, send):
    span = PATCH * PATCH
    line = jnp.concatenate(
        [
            jnp.concatenate([patch_grad[t : t + 1, k * span : (k + 1) * span] for t in range(height // PATCH)], axis=1)
            for k in range(3)
        ]
        + [jnp.zeros((1, height * PATCH), F32)],
        axis=0,
    )
    line = jnp.concatenate([jnp.zeros((4, LANES), F32), line, jnp.zeros((4, LANES), F32)], axis=1)
    used = iota((4, LANES), 1) < (own_rows + 4) * PATCH
    colour = iota((4, LANES), 0)
    for index, d in enumerate(first_order(send.shape[0])):
        start = LANES + (d * own_rows - 2) * PATCH
        window = jnp.where(used, line[:, start : start + LANES], 0.0)
        send[index] = jnp.where(colour < 3, window, sums[:4])


def channel_sums(hidden):
    values = hidden.reshape(-1, hidden.shape[-1]).astype(F32)
    return jnp.sum(values, axis=0, keepdims=True), jnp.sum(values * values, axis=0, keepdims=True)


def over_group(values, size):
    lane = iota(values.shape, 1)
    lanes = values.shape[1]
    step = 1
    while step < size:
        later = pltpu.roll(values, lanes - step, 1)
        earlier = pltpu.roll(values, step, 1)
        values = values + jnp.where((lane & step) == 0, later, earlier)
        step *= 2
    return values


def group_sums(hidden):
    channels = hidden.shape[-1]
    size = channels // GROUPS
    first, second = [
        over_group(jnp.broadcast_to(x, (8, channels)), size) for x in channel_sums(hidden)
    ]
    lane = mod(iota((8, channels), 1), size)
    return jnp.where(lane == 0, first, jnp.where(lane == 1, second, 0.0))


def pull_back(rows, weight):
    parts = [[] for _ in rows]
    for low in range(0, weight.shape[0], LANES):
        block = weight[low : low + LANES, :].astype(F32)
        for row, found in zip(rows, parts):
            product = block * row
            folded = product[:, :LANES]
            for start in range(LANES, weight.shape[1], LANES):
                folded = folded + product[:, start : start + LANES]
            found.append(jnp.sum(folded.T, axis=0, keepdims=True))
    return [jnp.concatenate(found, axis=1) for found in parts]


def backward_part(
    owner, picks, gain, head_bias, head_out, normed, inv_spread, pooled, weight, head, slot, own_rows, height, sums, send
):
    (before,) = exact_rows([pooled], lambda rows: matmul(rows, head[...]))
    slope = head_out[...] * silu_slope(before + head_bias[...])
    split = head.shape[0] * 5 // 8 // LANES * LANES
    (held,) = exact_rows([slope], lambda rows: matmul_t(rows, head[split:, :]))
    pulled = jnp.concatenate(pull_back([slope], head[:split, :]) + [held], axis=1)
    wanted = owner[slot]
    picked = jnp.int32(0)
    for k in range(picks.shape[0]):
        picked = picked + jnp.where(picks[k] == wanted, 1, 0)
    scaled = gain[...] * (picked.astype(F32) * pulled)
    token_grad = inv_spread * (
        scaled
        - jnp.mean(scaled, axis=1, keepdims=True)
        - normed * jnp.mean(scaled * normed, axis=1, keepdims=True)
    )
    token_grad = token_grad.astype(BF16)
    count = height // PATCH
    split = weight.shape[0] * 2 // 3 if count <= 4 else weight.shape[0]
    patch_grad = matmul_t(token_grad, weight[:split, :])
    if split < weight.shape[0]:
        some = token_grad.astype(F32)
        rest = pull_back([some[t : t + 1] for t in range(count)], weight[split:, :])
        patch_grad = jnp.concatenate([patch_grad[:count], jnp.concatenate(rest, axis=0)], axis=1)
    patch_grad = patch_grad.astype(BF16).astype(F32)
    write_windows(patch_grad, sums, own_rows, height, send)


def write_edges(place, hidden, across, along):
    last = hidden.shape[0] - 1
    even = place[0] % 2 == 0
    across[0] = hidden[jnp.where(even, last, 0)]
    along[0] = hidden[jnp.where(even, 0, last)]


def reward_kernel(place, *refs):
    count, kept = 7, 4
    far, refs = refs[: count + kept + 2], refs[count + kept + 2 :]
    send, across, along = refs[:3]
    near = refs[3 + kept : 3 + kept + count] + refs[3 : 3 + kept] + refs[3 + kept + count : -1]
    sems = refs[-1]
    frames, bias, gain, owner, picks, head_bias, head_out, hidden, _, _, _, patch, head = near
    count += kept
    depth, depths = 256, (128, 256)
    small = [pltpu.make_async_copy(far[i], near[i], sems.at[i]) for i in range(count)]
    pieces = []
    used = count
    for index, rows in enumerate(depths):
        source, target = far[count + index], near[count + index]
        parts = []
        for low in range(0, target.shape[0], rows):
            part = pl.ds(low, rows)
            parts.append(pltpu.make_async_copy(source.at[part], target.at[part], sems.at[used]))
            used += 1
        pieces.append(parts)
    for copy in [small[0], small[7], small[1]] + pieces[0] + small[2:7] + pieces[1] + small[8:]:
        copy.start()

    def load_patch():
        for low in range(0, patch.shape[0], depth):
            for copy in pieces[0][low // depths[0] : (low + depth) // depths[0]]:
                copy.wait()
            yield low, low + depth, patch[low : low + depth, :]

    height = frames.shape[2]
    patches = height // PATCH
    small[0].wait()
    small[7].wait()
    tokens = to_tokens(frames[...])
    sums = group_sums(hidden[...])
    write_edges(place, hidden, across, along)
    small[1].wait()
    small[2].wait()
    normed, inv_spread, pooled = forward_part(tokens, patches, bias, gain, load_patch)
    for copy in small[3:7] + pieces[1]:
        copy.wait()
    backward_part(
        owner,
        picks,
        gain,
        head_bias,
        head_out,
        normed,
        inv_spread,
        pooled / patches,
        patch,
        head,
        place[0],
        hidden.shape[0],
        height,
        sums,
        send,
    )
    for copy in small[8:]:
        copy.wait()


def forward_kernel(frames, bias, gain, patch, normed, inv_spread, pooled):
    width = patch.shape[0]
    tokens = to_tokens(frames[...])
    normed[...], spread, pooled[...] = forward_part(
        tokens, frames.shape[2] // PATCH, bias, gain, lambda: [(0, width, patch[...])]
    )
    inv_spread[...] = jnp.broadcast_to(spread, inv_spread.shape)


def backward_kernel(
    owner,
    picks,
    place,
    hidden,
    gain,
    head_bias,
    head_out,
    normed,
    inv_spread,
    pooled,
    patch,
    head,
    send,
    across,
    along,
    *,
    height,
    per_frame,
):
    write_edges(place, hidden, across, along)
    backward_part(
        owner,
        picks,
        gain,
        head_bias,
        head_out,
        normed[...],
        inv_spread[...][:, :1],
        pooled[...],
        patch,
        head,
        place[0] // per_frame,
        hidden.shape[0],
        height,
        group_sums(hidden[...]),
        send,
    )


def params(cells):
    return pltpu.CompilerParams(vmem_limit_bytes=min(16 + cells // 64, 48) * 1024 * 1024)


def near(array):
    return pltpu.with_memory_space_constraint(array, pltpu.VMEM)


def far(array):
    return pltpu.with_memory_space_constraint(array, pltpu.HBM)


def prepare_kernel(out_weight, wide, scratch):
    block = scratch.shape[0] // 3
    amount = scratch.shape[1] // LANES
    span = 3 * (amount + 2)
    scratch[...] = jnp.zeros_like(scratch)
    for a in range(3):
        for e in range(3):
            for b in range(3):
                piece = out_weight[a, b, e].astype(F32)
                for i in range(amount):
                    start = a * block + e * span + 3 * (i - b + 2)
                    scratch[start : start + 3, i * LANES : (i + 1) * LANES] = piece
    wide[...] = scratch[...].astype(BF16)


def norm_constants(totals, cell_total):
    channels = totals.shape[1]
    size = channels // GROUPS
    totals = jnp.broadcast_to(totals, (8, channels))
    lane = mod(iota((8, channels), 1), size)
    first, second = [over_group(jnp.where(lane == i, totals, 0.0), size)[:1] for i in range(2)]
    mean = first / cell_total
    return mean, lax.rsqrt(second / cell_total - mean * mean + eps_norm)


def norm_slopes(state, mean, inverse, gain, shift):
    normed = (state - mean) * inverse
    return normed, silu_slope(normed * gain + shift) * gain


def slope_kernel(
    owner, arrived, hidden, gain, shift, wide, direct, edge_slopes, stats, sums, slopes_own, received
):
    devices, message_rows, _ = arrived.shape
    own_rows, frame_count, width, channels = hidden.shape
    cells = frame_count * width
    per_frame = devices // frame_count
    received[...] = arrived[...].reshape(received.shape)

    def from_all(row):
        return received[pl.ds(row, devices, stride=message_rows), :]

    totals = jnp.sum(from_all(3), axis=0, keepdims=True)
    mean, inverse = norm_constants(totals, own_rows * devices * cells * (channels // GROUPS))
    for i in range(own_rows):
        state = hidden[i].reshape(cells, channels).astype(F32)
        slopes_own[i] = norm_slopes(state, mean, inverse, gain[...], shift[...])[1]

    lines = jnp.concatenate([from_all(k) for k in range(3)], axis=1).astype(BF16)
    place = iota((1, devices), 1)
    source = jnp.zeros_like(place)
    for index, d in enumerate(first_order(devices)):
        source = jnp.where(place == index, d, source)
    home = jnp.zeros((1, devices), jnp.int32)
    for b in range(frame_count):
        home = jnp.where(div(source, per_frame) == b, owner[b] * per_frame, home)
    home = home + mod(source, per_frame)
    cell = iota((cells, 1), 0)
    column = mod(cell, width)
    frame_strip = div(cell, width) * per_frame
    lane = mod(iota((1, 3 * LANES), 1), PATCH)
    kept = []
    placed = None
    for e in range(3):
        wanted = column - e + 1
        if per_frame > 1 or placed is None:
            strip = frame_strip + div(wanted, PATCH) if per_frame > 1 else frame_strip
            placed = matmul(ones_where(home == strip), lines)
        inside = jnp.where((wanted >= 0) & (wanted < width), mod(wanted, PATCH), -1)
        kept.append(jnp.where(lane == inside, placed, 0.0).astype(BF16))
    block = wide.shape[0] // 3
    span = 3 * (own_rows + 4)
    entry = iota((3 * LANES, 1), 0)
    entry = div(mod(entry, LANES), PATCH) * 3 + div(entry, LANES)
    entry = jnp.where(entry < span, entry, -3 * span)
    tap = iota((1, block), 1)
    folds = jnp.concatenate([ones_where(tap == entry + e * span) for e in range(3)], axis=0)
    taps = matmul(jnp.concatenate(kept, axis=1), folds).astype(BF16)
    later = []
    for a in range(3):
        skip = (2 - a) * width
        later.append(
            jnp.concatenate([taps[skip:], jnp.zeros((skip, block), BF16)], axis=0) if skip else taps
        )
    result = matmul(jnp.concatenate(later, axis=1), wide[...])

    first = jnp.zeros((1, channels), F32)
    second = jnp.zeros((1, channels), F32)
    for i in range(own_rows):
        state = hidden[i].reshape(cells, channels).astype(F32)
        up = result[:, (i + 1) * channels : (i + 2) * channels] * slopes_own[i]
        direct[i] = up * inverse
        first = first + jnp.sum(up, axis=0, keepdims=True)
        second = second + jnp.sum(up * ((state - mean) * inverse), axis=0, keepdims=True)
    edge_slopes[0] = result[:, :channels]
    edge_slopes[1] = result[:, (own_rows + 1) * channels :]
    stats[0:1, :] = mean
    stats[1:2, :] = inverse
    both = jnp.where(iota((2, channels), 0) == 0, first, second)
    sums[...] = jnp.broadcast_to(both[None], sums.shape)


def late_kernel(
    place, across, along, slopes, stats, gain, shift, far_weight, direct, states, turned, inner_weight, sem
):
    copy = pltpu.make_async_copy(far_weight, inner_weight, sem.at[0])
    copy.start()
    cells, channels = slopes.shape[1:]
    odd = place[0] % 2 == 1
    mean = stats[0:1, :]
    inverse = stats[1:2, :]
    for i in range(2):
        state = jnp.where(odd == (i == 0), across[0], along[0])
        states[i] = state
        values = state.reshape(cells, channels).astype(F32)
        direct[i] = slopes[i] * norm_slopes(values, mean, inverse, gain[...], shift[...])[1] * inverse
    copy.wait()
    size = inner_weight.shape[3]
    for b in range(3):
        for a in range(3):
            for e in range(3):
                at = (a * 3 + e) * size
                turned[at : at + size, b * size : (b + 1) * size] = inner_weight[a, b, e].T


def inner_kernel(
    place, arrived, stats, direct, hidden, edge_direct, edge_states, turned, far_out, padded, out, sems, *, devices
):
    own_rows, frame_count, width, channels = out.shape
    cells = frame_count * width
    totals = jnp.sum(arrived[...], axis=0)
    cell_total = own_rows * devices * cells * (channels // GROUPS)
    place_row = iota((8, channels), 0)
    both = jnp.where(place_row == 0, totals[0:1], totals[1:2])
    both = over_group(both, channels // GROUPS)
    first, second = both[0:1], both[1:2]
    mean = stats[0:1, :]
    inverse = stats[1:2, :]
    constant = first / cell_total * inverse
    factor = second / cell_total * inverse * inverse
    position = place[0]
    in_frame = mod(iota((cells, 1), 0), width)
    for i in range(own_rows + 2):
        if 0 < i < own_rows + 1:
            state, part = hidden[i - 1], direct[i - 1]
        else:
            state, part = edge_states[min(i, 1)], edge_direct[min(i, 1)]
        grad = part - constant - (state.reshape(cells, channels).astype(F32) - mean) * factor
        if i == 0:
            grad = jnp.where(position > 0, grad, 0.0)
        if i == own_rows + 1:
            grad = jnp.where(position < devices - 1, grad, 0.0)
        after = jnp.where(in_frame < width - 1, pltpu.roll(grad, cells - 1, 0), 0.0)
        prior = jnp.where(in_frame > 0, pltpu.roll(grad, 1, 0), 0.0)
        padded[i, :cells, 0:channels] = after.astype(BF16)
        padded[i, :cells, channels : 2 * channels] = grad.astype(BF16)
        padded[i, :cells, 2 * channels :] = prior.astype(BF16)
        padded[i, cells:, :] = jnp.zeros((2 * width, 3 * channels), BF16)
    results = [jnp.zeros((cells, channels), F32) for _ in range(own_rows)]
    copies = []
    for i in range(own_rows + 2):
        joined = jnp.concatenate(
            [padded[i, (2 - a) * width : (2 - a) * width + cells, :] for a in range(3)], axis=1
        )
        taps = [b for b in range(3) if 0 <= i + b - 2 < own_rows]
        for low in range(0, len(taps), 2):
            some = taps[low : low + 2]
            product = matmul(joined, turned[:, some[0] * channels : (some[-1] + 1) * channels])
            for step, b in enumerate(some):
                results[i + b - 2] = results[i + b - 2] + product[:, step * channels : (step + 1) * channels]
        if i >= 2:
            out[i - 2] = results[i - 2].reshape(frame_count, width, channels).astype(BF16)
            copies.append(pltpu.make_async_copy(out.at[i - 2], far_out.at[i - 2], sems.at[i - 2]))
            copies[-1].start()
    for copy in copies:
        copy.wait()


def per_device(
    frames,
    frame_owner,
    picks,
    patch_weight,
    patch_bias,
    norm_gain,
    head_weight,
    head_bias,
    head_out,
    hidden_state,
    group_gain,
    group_shift,
    out_weight,
    inner_weight,
):
    devices = lax.axis_size("row")
    position = lax.axis_index("row").astype(jnp.int32).reshape(1)
    per_frame = devices // FRAMES
    height = frames.shape[1]
    own_rows, _, frame_width, channels = hidden_state.shape
    cells = FRAMES * frame_width
    width = patch_weight.shape[1]
    turned_frames = jnp.transpose(frames, (0, 2, 1))
    bias = patch_bias.reshape(1, width)
    gain = norm_gain.reshape(1, width)
    head_bias_row = head_bias.reshape(1, width)
    head_out_row = head_out.reshape(1, width)
    state_rows = own_rows + 2
    tap_rows = -(-9 * (own_rows + 4) // LANES) * LANES
    edge = jax.ShapeDtypeStruct((1,) + hidden_state.shape[1:], BF16)
    message = (message_shape(devices), edge, edge)
    gain_row = group_gain.reshape(1, channels)
    shift_row = group_shift.reshape(1, channels)
    early = [hidden_state, gain_row, shift_row, out_weight]
    slope_outs = (
        pltpu.VMEM((own_rows, cells, channels), F32),
        pltpu.VMEM((2, cells, channels), F32),
        pltpu.VMEM((8, channels), F32),
        jax.ShapeDtypeStruct((devices, 2, channels), F32),
    )
    if per_frame == 1:
        arrays = [turned_frames, bias, gain, frame_owner, picks, head_bias_row, head_out_row]
        weights = [patch_weight, head_weight]

        def scratch(x):
            return (pltpu.SMEM if x.dtype == jnp.int32 else pltpu.VMEM)(x.shape, x.dtype)

        send, across, along, *early = pl.pallas_call(
            reward_kernel,
            out_shape=message + tuple(pltpu.VMEM(x.shape, x.dtype) for x in early),
            in_specs=[SMEM] + [FAR] * (len(arrays) + len(early) + len(weights)),
            out_specs=[VMEM] * (3 + len(early)),
            scratch_shapes=[scratch(x) for x in arrays + weights] + [pltpu.SemaphoreType.DMA((32,))],
            compiler_params=params(0),
            name="reward",
        )(position, *[far(x) for x in arrays + early + weights])
    else:
        count = height // PATCH
        normed, inv_spread, partial = pl.pallas_call(
            forward_kernel,
            out_shape=(
                jax.ShapeDtypeStruct((token_rows_of(height), width), F32),
                jax.ShapeDtypeStruct((token_rows_of(height), LANES), F32),
                jax.ShapeDtypeStruct((1, width), F32),
            ),
            compiler_params=params(cells),
            name="reward_forward",
        )(turned_frames, bias, gain, patch_weight)
        members = [[b * per_frame + i for i in range(per_frame)] for b in range(FRAMES)]
        pooled = lax.psum(partial, "row", axis_index_groups=members) / (count * per_frame)
        send, across, along = pl.pallas_call(
            functools.partial(backward_kernel, height=height, per_frame=per_frame),
            out_shape=message,
            in_specs=[SMEM] * 3 + [VMEM] * 9,
            out_specs=[VMEM] * 3,
            compiler_params=params(cells),
            name="reward_backward",
        )(
            frame_owner,
            picks,
            position,
            hidden_state,
            gain,
            head_bias_row,
            head_out_row,
            normed,
            inv_spread,
            pooled,
            patch_weight,
            head_weight,
        )
    early = [near(x) for x in early]
    wide = pl.pallas_call(
        prepare_kernel,
        out_shape=pltpu.VMEM((3 * tap_rows, state_rows * channels), BF16),
        in_specs=[VMEM],
        scratch_shapes=[pltpu.VMEM((3 * tap_rows, state_rows * channels), F32)],
        compiler_params=params(cells),
        name="prepare",
    )(early[3])
    arrived = lax.all_to_all(send, "row", 0, 0, axis_index_groups=[first_order(devices)], tiled=True)
    direct, edge_slopes, stats, sums = pl.pallas_call(
        slope_kernel,
        out_shape=slope_outs,
        in_specs=[SMEM] + [VMEM] * 5,
        scratch_shapes=[
            pltpu.VMEM((own_rows, cells, channels), F32),
            pltpu.VMEM((4 * devices, LANES), F32),
        ],
        compiler_params=params(cells),
        name="slope",
    )(frame_owner, near(arrived), *early[:3], near(wide))
    swaps = [(2 * i, 2 * i + 1) for i in range(devices // 2)]
    across = lax.ppermute(across, "row", swaps + [(b, a) for a, b in swaps])
    swaps = [(2 * i - 1, 2 * i) for i in range(1, devices // 2)]
    along = lax.ppermute(along, "row", swaps + [(b, a) for a, b in swaps])
    summed = lax.all_to_all(sums, "row", 0, 0, axis_index_groups=[led_by(devices - 1, devices)], tiled=True)
    edge_direct, edge_states, turned = pl.pallas_call(
        late_kernel,
        out_shape=(
            pltpu.VMEM((2, cells, channels), F32),
            pltpu.VMEM((2,) + hidden_state.shape[1:], BF16),
            pltpu.VMEM((9 * channels, 3 * channels), BF16),
        ),
        in_specs=[SMEM] + [VMEM] * 6 + [FAR],
        scratch_shapes=[pltpu.VMEM(inner_weight.shape, BF16), pltpu.SemaphoreType.DMA((1,))],
        input_output_aliases={3: 0},
        compiler_params=params(cells),
        name="late",
    )(position, near(across), near(along), near(edge_slopes), near(stats), *early[1:3], far(inner_weight))
    return pl.pallas_call(
        functools.partial(inner_kernel, devices=devices),
        out_shape=jax.ShapeDtypeStruct(hidden_state.shape, BF16),
        in_specs=[SMEM] + [VMEM] * 7,
        out_specs=FAR,
        scratch_shapes=[
            pltpu.VMEM((own_rows + 2, cells + 2 * frame_width, 3 * channels), BF16),
            pltpu.VMEM(hidden_state.shape, BF16),
            pltpu.SemaphoreType.DMA((own_rows,)),
        ],
        compiler_params=params(cells),
        name="inner",
    )(
        position,
        near(summed),
        near(stats),
        near(direct),
        early[0],
        near(edge_direct),
        near(edge_states),
        near(turned),
    )


def solution(mesh):
    return jax.shard_map(
        per_device,
        mesh=mesh,
        in_specs=(
            P(None, None, ("clip", "row")),
            P("clip"),
            P("clip"),
            P(),
            P(),
            P(),
            P(),
            P(),
            P(),
            P(("clip", "row"), None, None, None),
            P(),
            P(),
            P(),
            P(),
        ),
        out_specs=P(("clip", "row"), None, None, None),
        check_vma=False,
    )
```

```python
import functools

import jax
import jax.numpy as jnp
from jax import lax
from jax.experimental import pallas as pl
from jax.experimental.pallas import tpu as pltpu
from jax.sharding import PartitionSpec as P

PATCH = 16
GROUPS = 32
FRAMES = 16
LANES = 128
SLOTS = LANES // PATCH
eps_norm = 1e-06
BF16 = jnp.bfloat16
F32 = jnp.float32

SMEM = pl.BlockSpec(memory_space=pltpu.SMEM)
VMEM = pl.BlockSpec(memory_space=pltpu.VMEM)
FAR = pl.BlockSpec(memory_space=pl.ANY)


def iota(shape, dim):
    return lax.broadcasted_iota(jnp.int32, shape, dim)


def div(values, count):
    if count & (count - 1):
        return values // count
    return values >> (count.bit_length() - 1)


def mod(values, count):
    if count & (count - 1):
        return values % count
    return values & (count - 1)


def ones_where(condition):
    return jnp.where(condition, 1.0, 0.0).astype(BF16)


def matmul(left, right):
    return jnp.dot(left, right, preferred_element_type=F32)


def matmul_t(left, right):
    return lax.dot_general(left, right, (((1,), (1,)), ((), ())), preferred_element_type=F32)


def cut_in_three(values):
    high = values.astype(BF16)
    rest = values - high.astype(F32)
    middle = rest.astype(BF16)
    low = (rest - middle.astype(F32)).astype(BF16)
    return high, middle, low


def exact_rows(rows, product):
    place = iota((16, rows[0].shape[1]), 0)
    stacked = jnp.zeros(place.shape, F32)
    for index, row in enumerate(rows):
        for step, piece in enumerate(cut_in_three(row)):
            stacked = jnp.where(place == 3 * index + step, piece.astype(F32), stacked)
    result = product(stacked.astype(BF16))
    return [
        result[3 * i : 3 * i + 1] + result[3 * i + 1 : 3 * i + 2] + result[3 * i + 2 : 3 * i + 3]
        for i in range(len(rows))
    ]


def silu_slope(values):
    sigmoid = jax.nn.sigmoid(values)
    return sigmoid * (1.0 + values * (1.0 - sigmoid))


def token_rows_of(height):
    return -(-(height // PATCH) // 16) * 16


def to_tokens(pixels):
    channels, columns, height = pixels.shape
    rows = channels * columns
    token_rows = token_rows_of(height)
    flat = pixels.reshape(rows, height)
    width = channels * PATCH * columns
    lane = iota((1, width), 1)
    place = iota((rows, 1), 0)
    mine = place == div(lane, PATCH * columns) * columns + mod(lane, columns)
    in_patch = mod(div(lane, columns), PATCH)
    pixel_row = iota((height, 1), 0)
    token = iota((token_rows, 1), 0)
    tokens = jnp.zeros((token_rows, width), F32)
    for t in range(height // PATCH):
        tiled = matmul(flat, ones_where(pixel_row == in_patch + t * PATCH))
        row = jnp.sum(jnp.where(mine, tiled, 0.0), axis=0, keepdims=True)
        tokens = jnp.where(token == t, row, tokens)
    return tokens.astype(BF16)


def forward_part(tokens, count, bias, gain, load_patch):
    embedded = bias[...]
    for low, high, weight in load_patch():
        embedded = embedded + matmul(tokens[:, low:high], weight)
    centred = embedded - jnp.mean(embedded, axis=1, keepdims=True)
    inv_spread = lax.rsqrt(jnp.mean(centred * centred, axis=1, keepdims=True) + eps_norm)
    normed = centred * inv_spread
    weighted = normed * gain[...]
    inside = iota((tokens.shape[0], 1), 0) < count
    pooled = jnp.sum(jnp.where(inside, weighted, 0.0), axis=0, keepdims=True)
    return normed, inv_spread, pooled


def led_by(leader, devices):
    return [leader] + [d for d in reversed(range(devices)) if d != leader]


def first_order(devices):
    return led_by(devices * 9 // 16, devices)


def message_shape(devices):
    return jax.ShapeDtypeStruct((devices, 4, LANES), F32)


def write_windows(patch_grad, sums, own_rows, height, send):
    span = PATCH * PATCH
    line = jnp.concatenate(
        [
            jnp.concatenate([patch_grad[t : t + 1, k * span : (k + 1) * span] for t in range(height // PATCH)], axis=1)
            for k in range(3)
        ]
        + [jnp.zeros((1, height * PATCH), F32)],
        axis=0,
    )
    line = jnp.concatenate([jnp.zeros((4, LANES), F32), line, jnp.zeros((4, LANES), F32)], axis=1)
    used = iota((4, LANES), 1) < (own_rows + 4) * PATCH
    colour = iota((4, LANES), 0)
    for index, d in enumerate(first_order(send.shape[0])):
        start = LANES + (d * own_rows - 2) * PATCH
        window = jnp.where(used, line[:, start : start + LANES], 0.0)
        send[index] = jnp.where(colour < 3, window, sums[:4])


def channel_sums(hidden):
    values = hidden.reshape(-1, hidden.shape[-1]).astype(F32)
    return jnp.sum(values, axis=0, keepdims=True), jnp.sum(values * values, axis=0, keepdims=True)


def over_group(values, size):
    lane = iota(values.shape, 1)
    lanes = values.shape[1]
    step = 1
    while step < size:
        later = pltpu.roll(values, lanes - step, 1)
        earlier = pltpu.roll(values, step, 1)
        values = values + jnp.where((lane & step) == 0, later, earlier)
        step *= 2
    return values


def group_sums(hidden):
    channels = hidden.shape[-1]
    size = channels // GROUPS
    first, second = [
        over_group(jnp.broadcast_to(x, (8, channels)), size) for x in channel_sums(hidden)
    ]
    lane = mod(iota((8, channels), 1), size)
    return jnp.where(lane == 0, first, jnp.where(lane == 1, second, 0.0))


def pull_back(row, weight):
    parts = []
    for low in range(0, weight.shape[0], LANES):
        product = weight[low : low + LANES, :].astype(F32) * row
        folded = product[:, :LANES]
        for start in range(LANES, weight.shape[1], LANES):
            folded = folded + product[:, start : start + LANES]
        parts.append(jnp.sum(folded.T, axis=0, keepdims=True))
    return jnp.concatenate(parts, axis=1)


def backward_part(
    owner, picks, gain, head_bias, head_out, normed, inv_spread, pooled, weight, head, through_head, slot, own_rows, height, sums, send
):
    (before,) = exact_rows([pooled], through_head)
    slope = head_out[...] * silu_slope(before + head_bias[...])
    pulled = pull_back(slope, head)
    wanted = owner[slot]
    picked = jnp.int32(0)
    for k in range(picks.shape[0]):
        picked = picked + jnp.where(picks[k] == wanted, 1, 0)
    scaled = gain[...] * (picked.astype(F32) * pulled)
    token_grad = inv_spread * (
        scaled
        - jnp.mean(scaled, axis=1, keepdims=True)
        - normed * jnp.mean(scaled * normed, axis=1, keepdims=True)
    )
    patch_grad = matmul_t(token_grad.astype(BF16), weight[...]).astype(BF16).astype(F32)
    write_windows(patch_grad, sums, own_rows, height, send)


def write_edges(place, hidden, across, along):
    last = hidden.shape[0] - 1
    even = place[0] % 2 == 0
    across[0] = hidden[jnp.where(even, last, 0)]
    along[0] = hidden[jnp.where(even, 0, last)]


def reward_kernel(place, *refs):
    count, kept = 7, 4
    far, refs = refs[: count + kept + 2], refs[count + kept + 2 :]
    send, across, along = refs[:3]
    near = refs[3 + kept : 3 + kept + count] + refs[3 : 3 + kept] + refs[3 + kept + count : -1]
    sems = refs[-1]
    frames, bias, gain, owner, picks, head_bias, head_out, hidden, _, _, _, patch, head = near
    count += kept
    depth, depths = 256, (128, 256)
    small = [pltpu.make_async_copy(far[i], near[i], sems.at[i]) for i in range(count)]
    pieces = []
    used = count
    for index, rows in enumerate(depths):
        source, target = far[count + index], near[count + index]
        parts = []
        for low in range(0, target.shape[0], rows):
            part = pl.ds(low, rows)
            parts.append(pltpu.make_async_copy(source.at[part], target.at[part], sems.at[used]))
            used += 1
        pieces.append(parts)
    for copy in [small[0], small[7], small[1]] + pieces[0] + small[2:7] + pieces[1] + small[8:]:
        copy.start()

    def load_patch():
        for low in range(0, patch.shape[0], depth):
            for copy in pieces[0][low // depths[0] : (low + depth) // depths[0]]:
                copy.wait()
            yield low, low + depth, patch[low : low + depth, :]

    height = frames.shape[2]
    patches = height // PATCH
    small[0].wait()
    small[7].wait()
    tokens = to_tokens(frames[...])
    sums = group_sums(hidden[...])
    write_edges(place, hidden, across, along)
    small[1].wait()
    small[2].wait()
    normed, inv_spread, pooled = forward_part(tokens, patches, bias, gain, load_patch)
    for copy in small[3:7]:
        copy.wait()

    def through_head(rows):
        total = jnp.zeros((rows.shape[0], head.shape[1]), F32)
        for index, low in enumerate(range(0, head.shape[0], depths[1])):
            pieces[1][index].wait()
            total = total + matmul(rows[:, low : low + depths[1]], head[low : low + depths[1], :])
        return total

    backward_part(
        owner,
        picks,
        gain,
        head_bias,
        head_out,
        normed,
        inv_spread,
        pooled / patches,
        patch,
        head,
        through_head,
        place[0],
        hidden.shape[0],
        height,
        sums,
        send,
    )
    for copy in small[8:]:
        copy.wait()


def forward_kernel(frames, bias, gain, patch, normed, inv_spread, pooled):
    width = patch.shape[0]
    tokens = to_tokens(frames[...])
    normed[...], spread, pooled[...] = forward_part(
        tokens, frames.shape[2] // PATCH, bias, gain, lambda: [(0, width, patch[...])]
    )
    inv_spread[...] = jnp.broadcast_to(spread, inv_spread.shape)


def backward_kernel(
    owner,
    picks,
    place,
    hidden,
    gain,
    head_bias,
    head_out,
    normed,
    inv_spread,
    pooled,
    patch,
    head,
    send,
    across,
    along,
    *,
    height,
    per_frame,
):
    write_edges(place, hidden, across, along)
    backward_part(
        owner,
        picks,
        gain,
        head_bias,
        head_out,
        normed[...],
        inv_spread[...][:, :1],
        pooled[...],
        patch,
        head,
        lambda rows: matmul(rows, head[...]),
        place[0] // per_frame,
        hidden.shape[0],
        height,
        group_sums(hidden[...]),
        send,
    )


def params(cells):
    return pltpu.CompilerParams(vmem_limit_bytes=min(16 + cells // 64, 48) * 1024 * 1024)


def near(array):
    return pltpu.with_memory_space_constraint(array, pltpu.VMEM)


def far(array):
    return pltpu.with_memory_space_constraint(array, pltpu.HBM)


def prepare_kernel(out_weight, wide, scratch):
    block = scratch.shape[0] // 3
    amount = scratch.shape[1] // LANES
    span = 3 * (amount + 2)
    scratch[...] = jnp.zeros_like(scratch)
    for a in range(3):
        for e in range(3):
            for b in range(3):
                piece = out_weight[a, b, e].astype(F32)
                for i in range(amount):
                    start = a * block + e * span + 3 * (i - b + 2)
                    scratch[start : start + 3, i * LANES : (i + 1) * LANES] = piece
    wide[...] = scratch[...].astype(BF16)


def norm_constants(totals, cell_total):
    channels = totals.shape[1]
    size = channels // GROUPS
    totals = jnp.broadcast_to(totals, (8, channels))
    lane = mod(iota((8, channels), 1), size)
    first, second = [over_group(jnp.where(lane == i, totals, 0.0), size)[:1] for i in range(2)]
    mean = first / cell_total
    return mean, lax.rsqrt(second / cell_total - mean * mean + eps_norm)


def norm_slopes(state, mean, inverse, gain, shift):
    normed = (state - mean) * inverse
    return normed, silu_slope(normed * gain + shift) * gain


def slope_kernel(
    owner, arrived, hidden, gain, shift, wide, direct, edge_slopes, stats, sums, slopes_own, received
):
    devices, message_rows, _ = arrived.shape
    own_rows, frame_count, width, channels = hidden.shape
    cells = frame_count * width
    per_frame = devices // frame_count
    received[...] = arrived[...].reshape(received.shape)

    def from_all(row):
        return received[pl.ds(row, devices, stride=message_rows), :]

    totals = jnp.sum(from_all(3), axis=0, keepdims=True)
    mean, inverse = norm_constants(totals, own_rows * devices * cells * (channels // GROUPS))
    for i in range(own_rows):
        state = hidden[i].reshape(cells, channels).astype(F32)
        slopes_own[i] = norm_slopes(state, mean, inverse, gain[...], shift[...])[1]

    lines = jnp.concatenate([from_all(k) for k in range(3)], axis=1).astype(BF16)
    place = iota((1, devices), 1)
    source = jnp.zeros_like(place)
    for index, d in enumerate(first_order(devices)):
        source = jnp.where(place == index, d, source)
    home = jnp.zeros((1, devices), jnp.int32)
    for b in range(frame_count):
        home = jnp.where(div(source, per_frame) == b, owner[b] * per_frame, home)
    home = home + mod(source, per_frame)
    cell = iota((cells, 1), 0)
    column = mod(cell, width)
    frame_strip = div(cell, width) * per_frame
    lane = mod(iota((1, 3 * LANES), 1), PATCH)
    kept = []
    placed = None
    for e in range(3):
        wanted = column - e + 1
        if per_frame > 1 or placed is None:
            strip = frame_strip + div(wanted, PATCH) if per_frame > 1 else frame_strip
            placed = matmul(ones_where(home == strip), lines)
        inside = jnp.where((wanted >= 0) & (wanted < width), mod(wanted, PATCH), -1)
        kept.append(jnp.where(lane == inside, placed, 0.0).astype(BF16))
    block = wide.shape[0] // 3
    span = 3 * (own_rows + 4)
    entry = iota((3 * LANES, 1), 0)
    entry = div(mod(entry, LANES), PATCH) * 3 + div(entry, LANES)
    entry = jnp.where(entry < span, entry, -3 * span)
    tap = iota((1, block), 1)
    folds = jnp.concatenate([ones_where(tap == entry + e * span) for e in range(3)], axis=0)
    taps = matmul(jnp.concatenate(kept, axis=1), folds).astype(BF16)
    later = []
    for a in range(3):
        skip = (2 - a) * width
        later.append(
            jnp.concatenate([taps[skip:], jnp.zeros((skip, block), BF16)], axis=0) if skip else taps
        )
    result = matmul(jnp.concatenate(later, axis=1), wide[...])

    first = jnp.zeros((1, channels), F32)
    second = jnp.zeros((1, channels), F32)
    for i in range(own_rows):
        state = hidden[i].reshape(cells, channels).astype(F32)
        up = result[:, (i + 1) * channels : (i + 2) * channels] * slopes_own[i]
        direct[i] = up * inverse
        first = first + jnp.sum(up, axis=0, keepdims=True)
        second = second + jnp.sum(up * ((state - mean) * inverse), axis=0, keepdims=True)
    edge_slopes[0] = result[:, :channels]
    edge_slopes[1] = result[:, (own_rows + 1) * channels :]
    stats[0:1, :] = mean
    stats[1:2, :] = inverse
    both = jnp.where(iota((2, channels), 0) == 0, first, second)
    sums[...] = jnp.broadcast_to(both[None], sums.shape)


def late_kernel(
    place, across, along, slopes, stats, gain, shift, far_weight, direct, states, turned, inner_weight, sem
):
    copy = pltpu.make_async_copy(far_weight, inner_weight, sem.at[0])
    copy.start()
    cells, channels = slopes.shape[1:]
    odd = place[0] % 2 == 1
    mean = stats[0:1, :]
    inverse = stats[1:2, :]
    for i in range(2):
        state = jnp.where(odd == (i == 0), across[0], along[0])
        states[i] = state
        values = state.reshape(cells, channels).astype(F32)
        direct[i] = slopes[i] * norm_slopes(values, mean, inverse, gain[...], shift[...])[1] * inverse
    copy.wait()
    size = inner_weight.shape[3]
    for b in range(3):
        for a in range(3):
            for e in range(3):
                at = (a * 3 + e) * size
                turned[at : at + size, b * size : (b + 1) * size] = inner_weight[a, b, e].T


def inner_kernel(
    place, arrived, stats, direct, hidden, edge_direct, edge_states, turned, far_out, padded, out, sems, *, devices
):
    own_rows, frame_count, width, channels = out.shape
    cells = frame_count * width
    totals = jnp.sum(arrived[...], axis=0)
    cell_total = own_rows * devices * cells * (channels // GROUPS)
    place_row = iota((8, channels), 0)
    both = jnp.where(place_row == 0, totals[0:1], totals[1:2])
    both = over_group(both, channels // GROUPS)
    first, second = both[0:1], both[1:2]
    mean = stats[0:1, :]
    inverse = stats[1:2, :]
    constant = first / cell_total * inverse
    factor = second / cell_total * inverse * inverse
    position = place[0]
    in_frame = mod(iota((cells, 1), 0), width)
    for i in range(own_rows + 2):
        if 0 < i < own_rows + 1:
            state, part = hidden[i - 1], direct[i - 1]
        else:
            state, part = edge_states[min(i, 1)], edge_direct[min(i, 1)]
        grad = part - constant - (state.reshape(cells, channels).astype(F32) - mean) * factor
        if i == 0:
            grad = jnp.where(position > 0, grad, 0.0)
        if i == own_rows + 1:
            grad = jnp.where(position < devices - 1, grad, 0.0)
        after = jnp.where(in_frame < width - 1, pltpu.roll(grad, cells - 1, 0), 0.0)
        prior = jnp.where(in_frame > 0, pltpu.roll(grad, 1, 0), 0.0)
        padded[i, :cells, 0:channels] = after.astype(BF16)
        padded[i, :cells, channels : 2 * channels] = grad.astype(BF16)
        padded[i, :cells, 2 * channels :] = prior.astype(BF16)
        padded[i, cells:, :] = jnp.zeros((2 * width, 3 * channels), BF16)
    results = [jnp.zeros((cells, channels), F32) for _ in range(own_rows)]
    copies = []
    for i in range(own_rows + 2):
        joined = jnp.concatenate(
            [padded[i, (2 - a) * width : (2 - a) * width + cells, :] for a in range(3)], axis=1
        )
        taps = [b for b in range(3) if 0 <= i + b - 2 < own_rows]
        for low in range(0, len(taps), 2):
            some = taps[low : low + 2]
            product = matmul(joined, turned[:, some[0] * channels : (some[-1] + 1) * channels])
            for step, b in enumerate(some):
                results[i + b - 2] = results[i + b - 2] + product[:, step * channels : (step + 1) * channels]
        if i >= 2:
            out[i - 2] = results[i - 2].reshape(frame_count, width, channels).astype(BF16)
            copies.append(pltpu.make_async_copy(out.at[i - 2], far_out.at[i - 2], sems.at[i - 2]))
            copies[-1].start()
    for copy in copies:
        copy.wait()


def per_device(
    frames,
    frame_owner,
    picks,
    patch_weight,
    patch_bias,
    norm_gain,
    head_weight,
    head_bias,
    head_out,
    hidden_state,
    group_gain,
    group_shift,
    out_weight,
    inner_weight,
):
    devices = lax.axis_size("row")
    position = lax.axis_index("row").astype(jnp.int32).reshape(1)
    per_frame = devices // FRAMES
    height = frames.shape[1]
    own_rows, _, frame_width, channels = hidden_state.shape
    cells = FRAMES * frame_width
    width = patch_weight.shape[1]
    turned_frames = jnp.transpose(frames, (0, 2, 1))
    bias = patch_bias.reshape(1, width)
    gain = norm_gain.reshape(1, width)
    head_bias_row = head_bias.reshape(1, width)
    head_out_row = head_out.reshape(1, width)
    state_rows = own_rows + 2
    tap_rows = -(-9 * (own_rows + 4) // LANES) * LANES
    edge = jax.ShapeDtypeStruct((1,) + hidden_state.shape[1:], BF16)
    message = (message_shape(devices), edge, edge)
    gain_row = group_gain.reshape(1, channels)
    shift_row = group_shift.reshape(1, channels)
    early = [hidden_state, gain_row, shift_row, out_weight]
    slope_outs = (
        pltpu.VMEM((own_rows, cells, channels), F32),
        pltpu.VMEM((2, cells, channels), F32),
        pltpu.VMEM((8, channels), F32),
        jax.ShapeDtypeStruct((devices, 2, channels), F32),
    )
    if per_frame == 1:
        arrays = [turned_frames, bias, gain, frame_owner, picks, head_bias_row, head_out_row]
        weights = [patch_weight, head_weight]

        def scratch(x):
            return (pltpu.SMEM if x.dtype == jnp.int32 else pltpu.VMEM)(x.shape, x.dtype)

        send, across, along, *early = pl.pallas_call(
            reward_kernel,
            out_shape=message + tuple(pltpu.VMEM(x.shape, x.dtype) for x in early),
            in_specs=[SMEM] + [FAR] * (len(arrays) + len(early) + len(weights)),
            out_specs=[VMEM] * (3 + len(early)),
            scratch_shapes=[scratch(x) for x in arrays + weights] + [pltpu.SemaphoreType.DMA((32,))],
            compiler_params=params(0),
            name="reward",
        )(position, *[far(x) for x in arrays + early + weights])
    else:
        count = height // PATCH
        normed, inv_spread, partial = pl.pallas_call(
            forward_kernel,
            out_shape=(
                jax.ShapeDtypeStruct((token_rows_of(height), width), F32),
                jax.ShapeDtypeStruct((token_rows_of(height), LANES), F32),
                jax.ShapeDtypeStruct((1, width), F32),
            ),
            compiler_params=params(cells),
            name="reward_forward",
        )(turned_frames, bias, gain, patch_weight)
        members = [[b * per_frame + i for i in range(per_frame)] for b in range(FRAMES)]
        pooled = lax.psum(partial, "row", axis_index_groups=members) / (count * per_frame)
        send, across, along = pl.pallas_call(
            functools.partial(backward_kernel, height=height, per_frame=per_frame),
            out_shape=message,
            in_specs=[SMEM] * 3 + [VMEM] * 9,
            out_specs=[VMEM] * 3,
            compiler_params=params(cells),
            name="reward_backward",
        )(
            frame_owner,
            picks,
            position,
            hidden_state,
            gain,
            head_bias_row,
            head_out_row,
            normed,
            inv_spread,
            pooled,
            patch_weight,
            head_weight,
        )
    early = [near(x) for x in early]
    wide = pl.pallas_call(
        prepare_kernel,
        out_shape=pltpu.VMEM((3 * tap_rows, state_rows * channels), BF16),
        in_specs=[VMEM],
        scratch_shapes=[pltpu.VMEM((3 * tap_rows, state_rows * channels), F32)],
        compiler_params=params(cells),
        name="prepare",
    )(early[3])
    arrived = lax.all_to_all(send, "row", 0, 0, axis_index_groups=[first_order(devices)], tiled=True)
    direct, edge_slopes, stats, sums = pl.pallas_call(
        slope_kernel,
        out_shape=slope_outs,
        in_specs=[SMEM] + [VMEM] * 5,
        scratch_shapes=[
            pltpu.VMEM((own_rows, cells, channels), F32),
            pltpu.VMEM((4 * devices, LANES), F32),
        ],
        compiler_params=params(cells),
        name="slope",
    )(frame_owner, near(arrived), *early[:3], near(wide))
    swaps = [(2 * i, 2 * i + 1) for i in range(devices // 2)]
    across = lax.ppermute(across, "row", swaps + [(b, a) for a, b in swaps])
    swaps = [(2 * i - 1, 2 * i) for i in range(1, devices // 2)]
    along = lax.ppermute(along, "row", swaps + [(b, a) for a, b in swaps])
    summed = lax.all_to_all(sums, "row", 0, 0, axis_index_groups=[led_by(devices - 1, devices)], tiled=True)
    edge_direct, edge_states, turned = pl.pallas_call(
        late_kernel,
        out_shape=(
            pltpu.VMEM((2, cells, channels), F32),
            pltpu.VMEM((2,) + hidden_state.shape[1:], BF16),
            pltpu.VMEM((9 * channels, 3 * channels), BF16),
        ),
        in_specs=[SMEM] + [VMEM] * 6 + [FAR],
        scratch_shapes=[pltpu.VMEM(inner_weight.shape, BF16), pltpu.SemaphoreType.DMA((1,))],
        input_output_aliases={3: 0},
        compiler_params=params(cells),
        name="late",
    )(position, near(across), near(along), near(edge_slopes), near(stats), *early[1:3], far(inner_weight))
    return pl.pallas_call(
        functools.partial(inner_kernel, devices=devices),
        out_shape=jax.ShapeDtypeStruct(hidden_state.shape, BF16),
        in_specs=[SMEM] + [VMEM] * 7,
        out_specs=FAR,
        scratch_shapes=[
            pltpu.VMEM((own_rows + 2, cells + 2 * frame_width, 3 * channels), BF16),
            pltpu.VMEM(hidden_state.shape, BF16),
            pltpu.SemaphoreType.DMA((own_rows,)),
        ],
        compiler_params=params(cells),
        name="inner",
    )(
        position,
        near(summed),
        near(stats),
        near(direct),
        early[0],
        near(edge_direct),
        near(edge_states),
        near(turned),
    )


def solution(mesh):
    return jax.shard_map(
        per_device,
        mesh=mesh,
        in_specs=(
            P(None, None, ("clip", "row")),
            P("clip"),
            P("clip"),
            P(),
            P(),
            P(),
            P(),
            P(),
            P(),
            P(("clip", "row"), None, None, None),
            P(),
            P(),
            P(),
            P(),
        ),
        out_specs=P(("clip", "row"), None, None, None),
        check_vma=False,
    )
```

```python
import functools

import jax
import jax.numpy as jnp
from jax import lax
from jax.experimental import pallas as pl
from jax.experimental.pallas import tpu as pltpu
from jax.sharding import PartitionSpec as P

PATCH = 16
GROUPS = 32
FRAMES = 16
LANES = 128
SLOTS = LANES // PATCH
eps_norm = 1e-06
BF16 = jnp.bfloat16
F32 = jnp.float32

SMEM = pl.BlockSpec(memory_space=pltpu.SMEM)
VMEM = pl.BlockSpec(memory_space=pltpu.VMEM)
FAR = pl.BlockSpec(memory_space=pl.ANY)


def iota(shape, dim):
    return lax.broadcasted_iota(jnp.int32, shape, dim)


def div(values, count):
    if count & (count - 1):
        return values // count
    return values >> (count.bit_length() - 1)


def mod(values, count):
    if count & (count - 1):
        return values % count
    return values & (count - 1)


def ones_where(condition):
    return jnp.where(condition, 1.0, 0.0).astype(BF16)


def matmul(left, right):
    return jnp.dot(left, right, preferred_element_type=F32)


def matmul_t(left, right):
    return lax.dot_general(left, right, (((1,), (1,)), ((), ())), preferred_element_type=F32)


def cut_in_three(values):
    high = values.astype(BF16)
    rest = values - high.astype(F32)
    middle = rest.astype(BF16)
    low = (rest - middle.astype(F32)).astype(BF16)
    return high, middle, low


def exact_rows(rows, product):
    place = iota((16, rows[0].shape[1]), 0)
    stacked = jnp.zeros(place.shape, F32)
    for index, row in enumerate(rows):
        for step, piece in enumerate(cut_in_three(row)):
            stacked = jnp.where(place == 3 * index + step, piece.astype(F32), stacked)
    result = product(stacked.astype(BF16))
    return [
        result[3 * i : 3 * i + 1] + result[3 * i + 1 : 3 * i + 2] + result[3 * i + 2 : 3 * i + 3]
        for i in range(len(rows))
    ]


def silu_slope(values):
    sigmoid = jax.nn.sigmoid(values)
    return sigmoid * (1.0 + values * (1.0 - sigmoid))


def token_rows_of(height):
    return -(-(height // PATCH) // 16) * 16


def to_tokens(pixels):
    channels, columns, height = pixels.shape
    rows = channels * columns
    token_rows = token_rows_of(height)
    flat = pixels.reshape(rows, height)
    width = channels * PATCH * columns
    lane = iota((1, width), 1)
    place = iota((rows, 1), 0)
    mine = place == div(lane, PATCH * columns) * columns + mod(lane, columns)
    in_patch = mod(div(lane, columns), PATCH)
    pixel_row = iota((height, 1), 0)
    token = iota((token_rows, 1), 0)
    tokens = jnp.zeros((token_rows, width), F32)
    for t in range(height // PATCH):
        tiled = matmul(flat, ones_where(pixel_row == in_patch + t * PATCH))
        row = jnp.sum(jnp.where(mine, tiled, 0.0), axis=0, keepdims=True)
        tokens = jnp.where(token == t, row, tokens)
    return tokens.astype(BF16)


def forward_part(tokens, count, bias, gain, load_patch):
    embedded = bias[...]
    for low, high, weight in load_patch():
        embedded = embedded + matmul(tokens[:, low:high], weight)
    centred = embedded - jnp.mean(embedded, axis=1, keepdims=True)
    inv_spread = lax.rsqrt(jnp.mean(centred * centred, axis=1, keepdims=True) + eps_norm)
    normed = centred * inv_spread
    weighted = normed * gain[...]
    inside = iota((tokens.shape[0], 1), 0) < count
    pooled = jnp.sum(jnp.where(inside, weighted, 0.0), axis=0, keepdims=True)
    return normed, inv_spread, pooled


def led_by(leader, devices):
    return [leader] + [d for d in reversed(range(devices)) if d != leader]


def first_order(devices):
    return led_by(devices * 9 // 16, devices)


def message_shape(devices):
    return jax.ShapeDtypeStruct((devices, 4, LANES), F32)


def write_windows(patch_grad, sums, own_rows, height, send):
    span = PATCH * PATCH
    line = jnp.concatenate(
        [
            jnp.concatenate([patch_grad[t : t + 1, k * span : (k + 1) * span] for t in range(height // PATCH)], axis=1)
            for k in range(3)
        ]
        + [jnp.zeros((1, height * PATCH), F32)],
        axis=0,
    )
    line = jnp.concatenate([jnp.zeros((4, LANES), F32), line, jnp.zeros((4, LANES), F32)], axis=1)
    used = iota((4, LANES), 1) < (own_rows + 4) * PATCH
    colour = iota((4, LANES), 0)
    for index, d in enumerate(first_order(send.shape[0])):
        start = LANES + (d * own_rows - 2) * PATCH
        window = jnp.where(used, line[:, start : start + LANES], 0.0)
        send[index] = jnp.where(colour < 3, window, sums[:4])


def channel_sums(hidden):
    values = hidden.reshape(-1, hidden.shape[-1]).astype(F32)
    return jnp.sum(values, axis=0, keepdims=True), jnp.sum(values * values, axis=0, keepdims=True)


def over_group(values, size):
    lane = iota(values.shape, 1)
    lanes = values.shape[1]
    step = 1
    while step < size:
        later = pltpu.roll(values, lanes - step, 1)
        earlier = pltpu.roll(values, step, 1)
        values = values + jnp.where((lane & step) == 0, later, earlier)
        step *= 2
    return values


def group_sums(hidden):
    channels = hidden.shape[-1]
    size = channels // GROUPS
    first, second = [
        over_group(jnp.broadcast_to(x, (8, channels)), size) for x in channel_sums(hidden)
    ]
    lane = mod(iota((8, channels), 1), size)
    return jnp.where(lane == 0, first, jnp.where(lane == 1, second, 0.0))


def pull_back(row, weight):
    parts = []
    for low in range(0, weight.shape[0], LANES):
        product = weight[low : low + LANES, :].astype(F32) * row
        folded = product[:, :LANES]
        for start in range(LANES, weight.shape[1], LANES):
            folded = folded + product[:, start : start + LANES]
        parts.append(jnp.sum(folded.T, axis=0, keepdims=True))
    return jnp.concatenate(parts, axis=1)


def backward_part(
    owner, picks, gain, head_bias, head_out, normed, inv_spread, pooled, weight, head, through_head, slot, own_rows, height, sums, send
):
    (before,) = exact_rows([pooled], through_head)
    slope = head_out[...] * silu_slope(before + head_bias[...])
    pulled = pull_back(slope, head)
    wanted = owner[slot]
    picked = jnp.int32(0)
    for k in range(picks.shape[0]):
        picked = picked + jnp.where(picks[k] == wanted, 1, 0)
    scaled = gain[...] * (picked.astype(F32) * pulled)
    token_grad = inv_spread * (
        scaled
        - jnp.mean(scaled, axis=1, keepdims=True)
        - normed * jnp.mean(scaled * normed, axis=1, keepdims=True)
    )
    patch_grad = matmul_t(token_grad.astype(BF16), weight[...]).astype(BF16).astype(F32)
    write_windows(patch_grad, sums, own_rows, height, send)


def write_edges(place, hidden, across, along):
    last = hidden.shape[0] - 1
    even = place[0] % 2 == 0
    across[0] = hidden[jnp.where(even, last, 0)]
    along[0] = hidden[jnp.where(even, 0, last)]


def reward_kernel(place, *refs):
    count, kept = 7, 4
    far, refs = refs[: count + kept + 2], refs[count + kept + 2 :]
    send, across, along = refs[:3]
    near = refs[3 + kept : 3 + kept + count] + refs[3 : 3 + kept] + refs[3 + kept + count : -1]
    sems = refs[-1]
    frames, bias, gain, owner, picks, head_bias, head_out, hidden, _, _, _, patch, head = near
    count += kept
    depth, depths = 256, (128, 256)
    small = [pltpu.make_async_copy(far[i], near[i], sems.at[i]) for i in range(count)]
    pieces = []
    used = count
    for index, rows in enumerate(depths):
        source, target = far[count + index], near[count + index]
        parts = []
        for low in range(0, target.shape[0], rows):
            part = pl.ds(low, rows)
            parts.append(pltpu.make_async_copy(source.at[part], target.at[part], sems.at[used]))
            used += 1
        pieces.append(parts)
    for copy in [small[0], small[7], small[1]] + pieces[0] + small[2:7] + pieces[1] + small[8:]:
        copy.start()

    def load_patch():
        for low in range(0, patch.shape[0], depth):
            for copy in pieces[0][low // depths[0] : (low + depth) // depths[0]]:
                copy.wait()
            yield low, low + depth, patch[low : low + depth, :]

    height = frames.shape[2]
    patches = height // PATCH
    small[0].wait()
    small[7].wait()
    tokens = to_tokens(frames[...])
    sums = group_sums(hidden[...])
    write_edges(place, hidden, across, along)
    small[1].wait()
    small[2].wait()
    normed, inv_spread, pooled = forward_part(tokens, patches, bias, gain, load_patch)
    for copy in small[3:7]:
        copy.wait()

    def through_head(rows):
        total = jnp.zeros((rows.shape[0], head.shape[1]), F32)
        for index, low in enumerate(range(0, head.shape[0], depths[1])):
            pieces[1][index].wait()
            total = total + matmul(rows[:, low : low + depths[1]], head[low : low + depths[1], :])
        return total

    backward_part(
        owner,
        picks,
        gain,
        head_bias,
        head_out,
        normed,
        inv_spread,
        pooled / patches,
        patch,
        head,
        through_head,
        place[0],
        hidden.shape[0],
        height,
        sums,
        send,
    )
    for copy in small[8:]:
        copy.wait()


def forward_kernel(frames, bias, gain, patch, normed, inv_spread, pooled):
    width = patch.shape[0]
    tokens = to_tokens(frames[...])
    normed[...], spread, pooled[...] = forward_part(
        tokens, frames.shape[2] // PATCH, bias, gain, lambda: [(0, width, patch[...])]
    )
    inv_spread[...] = jnp.broadcast_to(spread, inv_spread.shape)


def backward_kernel(
    owner,
    picks,
    place,
    hidden,
    gain,
    head_bias,
    head_out,
    normed,
    inv_spread,
    pooled,
    patch,
    head,
    send,
    across,
    along,
    *,
    height,
    per_frame,
):
    write_edges(place, hidden, across, along)
    backward_part(
        owner,
        picks,
        gain,
        head_bias,
        head_out,
        normed[...],
        inv_spread[...][:, :1],
        pooled[...],
        patch,
        head,
        lambda rows: matmul(rows, head[...]),
        place[0] // per_frame,
        hidden.shape[0],
        height,
        group_sums(hidden[...]),
        send,
    )


def params(cells):
    return pltpu.CompilerParams(vmem_limit_bytes=min(16 + cells // 64, 48) * 1024 * 1024)


def near(array):
    return pltpu.with_memory_space_constraint(array, pltpu.VMEM)


def far(array):
    return pltpu.with_memory_space_constraint(array, pltpu.HBM)


def tap_lane(j, k, e):
    return (j + 1) * PATCH + 4 * k + e


def prepare_kernel(out_weight, wide, scratch):
    amount = scratch.shape[1] // LANES
    scratch[...] = jnp.zeros_like(scratch)
    for a in range(3):
        for e in range(3):
            for b in range(3):
                piece = out_weight[a, b, e].astype(F32)
                for i in range(amount):
                    for k in range(3):
                        at = a * LANES + tap_lane(i - b + 2, k, e)
                        scratch[at : at + 1, i * LANES : (i + 1) * LANES] = piece[k : k + 1]
    wide[...] = scratch[...].astype(BF16)


def norm_constants(totals, cell_total):
    channels = totals.shape[1]
    size = channels // GROUPS
    totals = jnp.broadcast_to(totals, (8, channels))
    lane = mod(iota((8, channels), 1), size)
    first, second = [over_group(jnp.where(lane == i, totals, 0.0), size)[:1] for i in range(2)]
    mean = first / cell_total
    return mean, lax.rsqrt(second / cell_total - mean * mean + eps_norm)


def norm_slopes(state, mean, inverse, gain, shift):
    normed = (state - mean) * inverse
    return normed, silu_slope(normed * gain + shift) * gain


def slope_kernel(
    owner, arrived, hidden, gain, shift, wide, direct, edge_slopes, stats, sums, slopes_own, received, taps
):
    devices, message_rows, _ = arrived.shape
    own_rows, frame_count, width, channels = hidden.shape
    cells = frame_count * width
    per_frame = devices // frame_count
    got = arrived[...].reshape(received.shape)
    kind = mod(iota((got.shape[0], 1), 0), message_rows)
    totals = jnp.sum(jnp.where(kind == 3, got, 0.0), axis=0, keepdims=True)
    mean, inverse = norm_constants(totals, own_rows * devices * cells * (channels // GROUPS))
    for i in range(own_rows):
        state = hidden[i].reshape(cells, channels).astype(F32)
        slopes_own[i] = norm_slopes(state, mean, inverse, gain[...], shift[...])[1]

    if per_frame == 1:
        lane = iota((1, LANES), 1)
        entry = iota((LANES, 1), 0)
        turned = ones_where(entry - mod(entry, PATCH) + PATCH - 1 - mod(entry, PATCH) == lane)
        received[...] = matmul(jnp.where(kind < 3, got, 0.0).astype(BF16), turned)
        lane = mod(iota((PATCH, LANES), 1), PATCH)
        column = iota((PATCH, LANES), 0)
        marks = []
        for k in range(3):
            e = lane - 4 * k
            wanted = column - e + 1
            marks.append((e >= 0) & (e < 3) & (wanted >= 0) & (wanted < PATCH))
        for d in range(devices):
            row = first_order(devices)[d]
            block = jnp.zeros((PATCH, LANES), F32)
            for k in range(3):
                line = jnp.broadcast_to(received[d * message_rows + k : d * message_rows + k + 1, :], (PATCH, LANES))
                line = pltpu.roll(line, 4 * k + 2, 1, stride=1, stride_axis=0)
                block = jnp.where(marks[k], line, block)
            start = pl.multiple_of(owner[row] * PATCH, PATCH)
            taps[pl.ds(start, PATCH), :] = block.astype(BF16)
    else:
        received[...] = got
        lines = [received[pl.ds(k, devices, stride=message_rows), :] for k in range(3)]
        lines = jnp.concatenate(lines, axis=1).astype(BF16)
        place = iota((1, devices), 1)
        source = jnp.zeros_like(place)
        for index, d in enumerate(first_order(devices)):
            source = jnp.where(place == index, d, source)
        home = jnp.zeros((1, devices), jnp.int32)
        for b in range(frame_count):
            home = jnp.where(div(source, per_frame) == b, owner[b] * per_frame, home)
        home = home + mod(source, per_frame)
        cell = iota((cells, 1), 0)
        column = mod(cell, width)
        lane = mod(iota((1, 3 * LANES), 1), PATCH)
        entry = iota((3 * LANES, 1), 0)
        window_row = div(mod(entry, LANES), PATCH)
        found = jnp.zeros((cells, LANES), F32)
        for e in range(3):
            wanted = column - e + 1
            strip = div(cell, width) * per_frame + div(wanted, PATCH)
            placed = matmul(ones_where(home == strip), lines)
            inside = jnp.where((wanted >= 0) & (wanted < width), mod(wanted, PATCH), -1)
            kept = jnp.where(lane == inside, placed, 0.0).astype(BF16)
            target = jnp.where(
                window_row < own_rows + 4, tap_lane(window_row, div(entry, LANES), e), -1
            )
            found = found + matmul(kept, ones_where(target == iota((1, LANES), 1)))
        taps[:cells, :] = found.astype(BF16)
    taps[cells:, :] = jnp.zeros((2 * width, LANES), BF16)
    steps = [taps[(2 - a) * width : (2 - a) * width + cells, :] for a in range(3)]
    result = matmul(jnp.concatenate(steps, axis=1), wide[...])

    first = jnp.zeros((1, channels), F32)
    second = jnp.zeros((1, channels), F32)
    for i in range(own_rows):
        state = hidden[i].reshape(cells, channels).astype(F32)
        up = result[:, (i + 1) * channels : (i + 2) * channels] * slopes_own[i]
        direct[i] = up * inverse
        first = first + jnp.sum(up, axis=0, keepdims=True)
        second = second + jnp.sum(up * ((state - mean) * inverse), axis=0, keepdims=True)
    edge_slopes[0] = result[:, :channels]
    edge_slopes[1] = result[:, (own_rows + 1) * channels :]
    stats[0:1, :] = mean
    stats[1:2, :] = inverse
    both = jnp.where(iota((2, channels), 0) == 0, first, second)
    sums[...] = jnp.broadcast_to(both[None], sums.shape)


def late_kernel(
    place, across, along, slopes, stats, gain, shift, far_weight, direct, states, turned, inner_weight, sem
):
    copy = pltpu.make_async_copy(far_weight, inner_weight, sem.at[0])
    copy.start()
    cells, channels = slopes.shape[1:]
    odd = place[0] % 2 == 1
    mean = stats[0:1, :]
    inverse = stats[1:2, :]
    for i in range(2):
        state = jnp.where(odd == (i == 0), across[0], along[0])
        states[i] = state
        values = state.reshape(cells, channels).astype(F32)
        direct[i] = slopes[i] * norm_slopes(values, mean, inverse, gain[...], shift[...])[1] * inverse
    copy.wait()
    size = inner_weight.shape[3]
    for b in range(3):
        for a in range(3):
            for e in range(3):
                at = (a * 3 + e) * size
                turned[at : at + size, b * size : (b + 1) * size] = inner_weight[a, b, e].T


def inner_kernel(
    place, arrived, stats, direct, hidden, edge_direct, edge_states, turned, far_out, padded, out, sems, *, devices
):
    own_rows, frame_count, width, channels = out.shape
    cells = frame_count * width
    totals = jnp.sum(arrived[...], axis=0)
    cell_total = own_rows * devices * cells * (channels // GROUPS)
    place_row = iota((8, channels), 0)
    both = jnp.where(place_row == 0, totals[0:1], totals[1:2])
    both = over_group(both, channels // GROUPS)
    first, second = both[0:1], both[1:2]
    mean = stats[0:1, :]
    inverse = stats[1:2, :]
    constant = first / cell_total * inverse
    factor = second / cell_total * inverse * inverse
    position = place[0]
    in_frame = mod(iota((cells, 1), 0), width)
    for i in range(own_rows + 2):
        if 0 < i < own_rows + 1:
            state, part = hidden[i - 1], direct[i - 1]
        else:
            state, part = edge_states[min(i, 1)], edge_direct[min(i, 1)]
        grad = part - constant - (state.reshape(cells, channels).astype(F32) - mean) * factor
        if i == 0:
            grad = jnp.where(position > 0, grad, 0.0)
        if i == own_rows + 1:
            grad = jnp.where(position < devices - 1, grad, 0.0)
        after = jnp.where(in_frame < width - 1, pltpu.roll(grad, cells - 1, 0), 0.0)
        prior = jnp.where(in_frame > 0, pltpu.roll(grad, 1, 0), 0.0)
        padded[i, :cells, 0:channels] = after.astype(BF16)
        padded[i, :cells, channels : 2 * channels] = grad.astype(BF16)
        padded[i, :cells, 2 * channels :] = prior.astype(BF16)
        padded[i, cells:, :] = jnp.zeros((2 * width, 3 * channels), BF16)
    results = [jnp.zeros((cells, channels), F32) for _ in range(own_rows)]
    copies = []
    for i in range(own_rows + 2):
        joined = jnp.concatenate(
            [padded[i, (2 - a) * width : (2 - a) * width + cells, :] for a in range(3)], axis=1
        )
        taps = [b for b in range(3) if 0 <= i + b - 2 < own_rows]
        for low in range(0, len(taps), 2):
            some = taps[low : low + 2]
            product = matmul(joined, turned[:, some[0] * channels : (some[-1] + 1) * channels])
            for step, b in enumerate(some):
                results[i + b - 2] = results[i + b - 2] + product[:, step * channels : (step + 1) * channels]
        if i >= 2:
            out[i - 2] = results[i - 2].reshape(frame_count, width, channels).astype(BF16)
            copies.append(pltpu.make_async_copy(out.at[i - 2], far_out.at[i - 2], sems.at[i - 2]))
            copies[-1].start()
    for copy in copies:
        copy.wait()


def per_device(
    frames,
    frame_owner,
    picks,
    patch_weight,
    patch_bias,
    norm_gain,
    head_weight,
    head_bias,
    head_out,
    hidden_state,
    group_gain,
    group_shift,
    out_weight,
    inner_weight,
):
    devices = lax.axis_size("row")
    position = lax.axis_index("row").astype(jnp.int32).reshape(1)
    per_frame = devices // FRAMES
    height = frames.shape[1]
    own_rows, _, frame_width, channels = hidden_state.shape
    cells = FRAMES * frame_width
    width = patch_weight.shape[1]
    turned_frames = jnp.transpose(frames, (0, 2, 1))
    bias = patch_bias.reshape(1, width)
    gain = norm_gain.reshape(1, width)
    head_bias_row = head_bias.reshape(1, width)
    head_out_row = head_out.reshape(1, width)
    state_rows = own_rows + 2
    edge = jax.ShapeDtypeStruct((1,) + hidden_state.shape[1:], BF16)
    message = (message_shape(devices), edge, edge)
    gain_row = group_gain.reshape(1, channels)
    shift_row = group_shift.reshape(1, channels)
    early = [hidden_state, gain_row, shift_row, out_weight]
    slope_outs = (
        pltpu.VMEM((own_rows, cells, channels), F32),
        pltpu.VMEM((2, cells, channels), F32),
        pltpu.VMEM((8, channels), F32),
        jax.ShapeDtypeStruct((devices, 2, channels), F32),
    )
    if per_frame == 1:
        arrays = [turned_frames, bias, gain, frame_owner, picks, head_bias_row, head_out_row]
        weights = [patch_weight, head_weight]

        def scratch(x):
            return (pltpu.SMEM if x.dtype == jnp.int32 else pltpu.VMEM)(x.shape, x.dtype)

        send, across, along, *early = pl.pallas_call(
            reward_kernel,
            out_shape=message + tuple(pltpu.VMEM(x.shape, x.dtype) for x in early),
            in_specs=[SMEM] + [FAR] * (len(arrays) + len(early) + len(weights)),
            out_specs=[VMEM] * (3 + len(early)),
            scratch_shapes=[scratch(x) for x in arrays + weights] + [pltpu.SemaphoreType.DMA((32,))],
            compiler_params=params(0),
            name="reward",
        )(position, *[far(x) for x in arrays + early + weights])
    else:
        count = height // PATCH
        normed, inv_spread, partial = pl.pallas_call(
            forward_kernel,
            out_shape=(
                jax.ShapeDtypeStruct((token_rows_of(height), width), F32),
                jax.ShapeDtypeStruct((token_rows_of(height), LANES), F32),
                jax.ShapeDtypeStruct((1, width), F32),
            ),
            compiler_params=params(cells),
            name="reward_forward",
        )(turned_frames, bias, gain, patch_weight)
        members = [[b * per_frame + i for i in range(per_frame)] for b in range(FRAMES)]
        pooled = lax.psum(partial, "row", axis_index_groups=members) / (count * per_frame)
        send, across, along = pl.pallas_call(
            functools.partial(backward_kernel, height=height, per_frame=per_frame),
            out_shape=message,
            in_specs=[SMEM] * 3 + [VMEM] * 9,
            out_specs=[VMEM] * 3,
            compiler_params=params(cells),
            name="reward_backward",
        )(
            frame_owner,
            picks,
            position,
            hidden_state,
            gain,
            head_bias_row,
            head_out_row,
            normed,
            inv_spread,
            pooled,
            patch_weight,
            head_weight,
        )
    early = [near(x) for x in early]
    wide = pl.pallas_call(
        prepare_kernel,
        out_shape=pltpu.VMEM((3 * LANES, state_rows * channels), BF16),
        in_specs=[VMEM],
        scratch_shapes=[pltpu.VMEM((3 * LANES, state_rows * channels), F32)],
        compiler_params=params(cells),
        name="prepare",
    )(early[3])
    arrived = lax.all_to_all(send, "row", 0, 0, axis_index_groups=[first_order(devices)], tiled=True)
    direct, edge_slopes, stats, sums = pl.pallas_call(
        slope_kernel,
        out_shape=slope_outs,
        in_specs=[SMEM] + [VMEM] * 5,
        scratch_shapes=[
            pltpu.VMEM((own_rows, cells, channels), F32),
            pltpu.VMEM((4 * devices, LANES), F32),
            pltpu.VMEM((cells + 2 * frame_width, LANES), BF16),
        ],
        compiler_params=params(cells),
        name="slope",
    )(frame_owner, near(arrived), *early[:3], near(wide))
    swaps = [(2 * i, 2 * i + 1) for i in range(devices // 2)]
    across = lax.ppermute(across, "row", swaps + [(b, a) for a, b in swaps])
    swaps = [(2 * i - 1, 2 * i) for i in range(1, devices // 2)]
    along = lax.ppermute(along, "row", swaps + [(b, a) for a, b in swaps])
    summed = lax.all_to_all(sums, "row", 0, 0, axis_index_groups=[led_by(devices - 1, devices)], tiled=True)
    edge_direct, edge_states, turned = pl.pallas_call(
        late_kernel,
        out_shape=(
            pltpu.VMEM((2, cells, channels), F32),
            pltpu.VMEM((2,) + hidden_state.shape[1:], BF16),
            pltpu.VMEM((9 * channels, 3 * channels), BF16),
        ),
        in_specs=[SMEM] + [VMEM] * 6 + [FAR],
        scratch_shapes=[pltpu.VMEM(inner_weight.shape, BF16), pltpu.SemaphoreType.DMA((1,))],
        input_output_aliases={3: 0},
        compiler_params=params(cells),
        name="late",
    )(position, near(across), near(along), near(edge_slopes), near(stats), *early[1:3], far(inner_weight))
    return pl.pallas_call(
        functools.partial(inner_kernel, devices=devices),
        out_shape=jax.ShapeDtypeStruct(hidden_state.shape, BF16),
        in_specs=[SMEM] + [VMEM] * 7,
        out_specs=FAR,
        scratch_shapes=[
            pltpu.VMEM((own_rows + 2, cells + 2 * frame_width, 3 * channels), BF16),
            pltpu.VMEM(hidden_state.shape, BF16),
            pltpu.SemaphoreType.DMA((own_rows,)),
        ],
        compiler_params=params(cells),
        name="inner",
    )(
        position,
        near(summed),
        near(stats),
        near(direct),
        early[0],
        near(edge_direct),
        near(edge_states),
        near(turned),
    )


def solution(mesh):
    return jax.shard_map(
        per_device,
        mesh=mesh,
        in_specs=(
            P(None, None, ("clip", "row")),
            P("clip"),
            P("clip"),
            P(),
            P(),
            P(),
            P(),
            P(),
            P(),
            P(("clip", "row"), None, None, None),
            P(),
            P(),
            P(),
            P(),
        ),
        out_specs=P(("clip", "row"), None, None, None),
        check_vma=False,
    )
```

```python
import functools

import jax
import jax.numpy as jnp
from jax import lax
from jax.experimental import pallas as pl
from jax.experimental.pallas import tpu as pltpu
from jax.sharding import PartitionSpec as P

PATCH = 16
GROUPS = 32
FRAMES = 16
LANES = 128
SLOTS = LANES // PATCH
eps_norm = 1e-06
BF16 = jnp.bfloat16
F32 = jnp.float32

SMEM = pl.BlockSpec(memory_space=pltpu.SMEM)
VMEM = pl.BlockSpec(memory_space=pltpu.VMEM)
FAR = pl.BlockSpec(memory_space=pl.ANY)


def iota(shape, dim):
    return lax.broadcasted_iota(jnp.int32, shape, dim)


def div(values, count):
    if count & (count - 1):
        return values // count
    return values >> (count.bit_length() - 1)


def mod(values, count):
    if count & (count - 1):
        return values % count
    return values & (count - 1)


def ones_where(condition):
    return jnp.where(condition, 1.0, 0.0).astype(BF16)


def matmul(left, right):
    return jnp.dot(left, right, preferred_element_type=F32)


def matmul_t(left, right):
    return lax.dot_general(left, right, (((1,), (1,)), ((), ())), preferred_element_type=F32)


def cut_in_three(values):
    high = values.astype(BF16)
    rest = values - high.astype(F32)
    middle = rest.astype(BF16)
    low = (rest - middle.astype(F32)).astype(BF16)
    return high, middle, low


def exact_rows(rows, product):
    place = iota((16, rows[0].shape[1]), 0)
    stacked = jnp.zeros(place.shape, F32)
    for index, row in enumerate(rows):
        for step, piece in enumerate(cut_in_three(row)):
            stacked = jnp.where(place == 3 * index + step, piece.astype(F32), stacked)
    result = product(stacked.astype(BF16))
    return [
        result[3 * i : 3 * i + 1] + result[3 * i + 1 : 3 * i + 2] + result[3 * i + 2 : 3 * i + 3]
        for i in range(len(rows))
    ]


def silu_slope(values):
    sigmoid = jax.nn.sigmoid(values)
    return sigmoid * (1.0 + values * (1.0 - sigmoid))


def token_rows_of(height):
    return -(-(height // PATCH) // 16) * 16


def to_tokens(pixels):
    channels, columns, height = pixels.shape
    rows = channels * columns
    token_rows = token_rows_of(height)
    flat = pixels.reshape(rows, height)
    width = channels * PATCH * columns
    lane = iota((1, width), 1)
    place = iota((rows, 1), 0)
    mine = place == div(lane, PATCH * columns) * columns + mod(lane, columns)
    in_patch = mod(div(lane, columns), PATCH)
    pixel_row = iota((height, 1), 0)
    token = iota((token_rows, 1), 0)
    tokens = jnp.zeros((token_rows, width), F32)
    for t in range(height // PATCH):
        tiled = matmul(flat, ones_where(pixel_row == in_patch + t * PATCH))
        row = jnp.sum(jnp.where(mine, tiled, 0.0), axis=0, keepdims=True)
        tokens = jnp.where(token == t, row, tokens)
    return tokens.astype(BF16)


def forward_part(tokens, count, bias, gain, load_patch):
    embedded = jnp.zeros((tokens.shape[0], bias.shape[1]), F32)
    for low, high, weight in load_patch():
        embedded = embedded + matmul(tokens[:, low:high], weight)
    embedded = embedded + bias[...]
    centred = embedded - jnp.mean(embedded, axis=1, keepdims=True)
    inv_spread = lax.rsqrt(jnp.mean(centred * centred, axis=1, keepdims=True) + eps_norm)
    normed = centred * inv_spread
    weighted = normed * gain[...]
    inside = iota((tokens.shape[0], 1), 0) < count
    pooled = jnp.sum(jnp.where(inside, weighted, 0.0), axis=0, keepdims=True)
    return normed, inv_spread, pooled


def led_by(leader, devices):
    return [leader] + [d for d in reversed(range(devices)) if d != leader]


def first_order(devices):
    return led_by(devices * 9 // 16, devices)


def message_shape(devices):
    return jax.ShapeDtypeStruct((devices, 4, LANES), F32)


def write_windows(patch_grad, sums, own_rows, height, send):
    span = PATCH * PATCH
    line = jnp.concatenate(
        [
            jnp.concatenate([patch_grad[t : t + 1, k * span : (k + 1) * span] for t in range(height // PATCH)], axis=1)
            for k in range(3)
        ]
        + [jnp.zeros((1, height * PATCH), F32)],
        axis=0,
    )
    line = jnp.concatenate([jnp.zeros((4, LANES), F32), line, jnp.zeros((4, LANES), F32)], axis=1)
    used = iota((4, LANES), 1) < (own_rows + 4) * PATCH
    colour = iota((4, LANES), 0)
    for index, d in enumerate(first_order(send.shape[0])):
        start = LANES + (d * own_rows - 2) * PATCH
        window = jnp.where(used, line[:, start : start + LANES], 0.0)
        send[index] = jnp.where(colour < 3, window, sums[:4])


def channel_sums(hidden):
    values = hidden.reshape(-1, hidden.shape[-1]).astype(F32)
    return jnp.sum(values, axis=0, keepdims=True), jnp.sum(values * values, axis=0, keepdims=True)


def over_group(values, size):
    lane = iota(values.shape, 1)
    lanes = values.shape[1]
    step = 1
    while step < size:
        later = pltpu.roll(values, lanes - step, 1)
        earlier = pltpu.roll(values, step, 1)
        values = values + jnp.where((lane & step) == 0, later, earlier)
        step *= 2
    return values


def group_sums(hidden):
    channels = hidden.shape[-1]
    size = channels // GROUPS
    first, second = [
        over_group(jnp.broadcast_to(x, (8, channels)), size) for x in channel_sums(hidden)
    ]
    lane = mod(iota((8, channels), 1), size)
    return jnp.where(lane == 0, first, jnp.where(lane == 1, second, 0.0))


def pull_back(row, weight):
    parts = []
    for low in range(0, weight.shape[0], LANES):
        product = weight[low : low + LANES, :].astype(F32) * row
        folded = product[:, :LANES]
        for start in range(LANES, weight.shape[1], LANES):
            folded = folded + product[:, start : start + LANES]
        parts.append(jnp.sum(folded.T, axis=0, keepdims=True))
    return jnp.concatenate(parts, axis=1)


def backward_part(
    owner, picks, gain, head_bias, head_out, normed, inv_spread, pooled, weight, head, through_head, slot, own_rows, height, sums, send
):
    (before,) = exact_rows([pooled], through_head)
    slope = head_out[...] * silu_slope(before + head_bias[...])
    pulled = pull_back(slope, head)
    wanted = owner[slot]
    picked = jnp.int32(0)
    for k in range(picks.shape[0]):
        picked = picked + jnp.where(picks[k] == wanted, 1, 0)
    scaled = gain[...] * (picked.astype(F32) * pulled)
    token_grad = inv_spread * (
        scaled
        - jnp.mean(scaled, axis=1, keepdims=True)
        - normed * jnp.mean(scaled * normed, axis=1, keepdims=True)
    )
    patch_grad = matmul_t(token_grad.astype(BF16), weight[...]).astype(BF16).astype(F32)
    write_windows(patch_grad, sums, own_rows, height, send)


def write_edges(position, hidden, across, along):
    last = hidden.shape[0] - 1
    even = position % 2 == 0
    across[0] = hidden[jnp.where(even, last, 0)]
    along[0] = hidden[jnp.where(even, 0, last)]


def reward_kernel(*refs):
    position = lax.axis_index("row")
    count, kept = 7, 4
    far, refs = refs[: count + kept + 2], refs[count + kept + 2 :]
    send, across, along = refs[:3]
    near = refs[3 + kept : 3 + kept + count] + refs[3 : 3 + kept] + refs[3 + kept + count : -1]
    sems = refs[-1]
    frames, bias, gain, owner, picks, head_bias, head_out, hidden, _, _, _, patch, head = near
    count += kept
    depth, depths = 256, (256, 256)
    small = [pltpu.make_async_copy(far[i], near[i], sems.at[i]) for i in range(count)]
    pieces = []
    used = count
    for index, rows in enumerate(depths):
        source, target = far[count + index], near[count + index]
        parts = []
        for low in range(0, target.shape[0], rows):
            part = pl.ds(low, rows)
            parts.append(pltpu.make_async_copy(source.at[part], target.at[part], sems.at[used]))
            used += 1
        pieces.append(parts)
    for copy in [small[0], small[7]] + pieces[0] + small[1:7] + pieces[1] + small[8:]:
        copy.start()

    def load_patch():
        for low in range(0, patch.shape[0], depth):
            for copy in pieces[0][low // depths[0] : (low + depth) // depths[0]]:
                copy.wait()
            yield low, low + depth, patch[low : low + depth, :]
        small[1].wait()
        small[2].wait()

    height = frames.shape[2]
    patches = height // PATCH
    small[0].wait()
    small[7].wait()
    tokens = to_tokens(frames[...])
    sums = group_sums(hidden[...])
    write_edges(position, hidden, across, along)
    normed, inv_spread, pooled = forward_part(tokens, patches, bias, gain, load_patch)
    for copy in small[3:7]:
        copy.wait()

    def through_head(rows):
        total = jnp.zeros((rows.shape[0], head.shape[1]), F32)
        for index, low in enumerate(range(0, head.shape[0], depths[1])):
            pieces[1][index].wait()
            total = total + matmul(rows[:, low : low + depths[1]], head[low : low + depths[1], :])
        return total

    backward_part(
        owner,
        picks,
        gain,
        head_bias,
        head_out,
        normed,
        inv_spread,
        pooled / patches,
        patch,
        head,
        through_head,
        position,
        hidden.shape[0],
        height,
        sums,
        send,
    )
    for copy in small[8:]:
        copy.wait()


def forward_kernel(frames, bias, gain, patch, normed, inv_spread, pooled):
    width = patch.shape[0]
    tokens = to_tokens(frames[...])
    normed[...], spread, pooled[...] = forward_part(
        tokens, frames.shape[2] // PATCH, bias, gain, lambda: [(0, width, patch[...])]
    )
    inv_spread[...] = jnp.broadcast_to(spread, inv_spread.shape)


def backward_kernel(
    owner,
    picks,
    hidden,
    gain,
    head_bias,
    head_out,
    normed,
    inv_spread,
    pooled,
    patch,
    head,
    send,
    across,
    along,
    *,
    height,
    per_frame,
):
    position = lax.axis_index("row")
    write_edges(position, hidden, across, along)
    backward_part(
        owner,
        picks,
        gain,
        head_bias,
        head_out,
        normed[...],
        inv_spread[...][:, :1],
        pooled[...],
        patch,
        head,
        lambda rows: matmul(rows, head[...]),
        position // per_frame,
        hidden.shape[0],
        height,
        group_sums(hidden[...]),
        send,
    )


def params(cells):
    return pltpu.CompilerParams(vmem_limit_bytes=min(16 + cells // 64, 48) * 1024 * 1024)


def near(array):
    return pltpu.with_memory_space_constraint(array, pltpu.VMEM)


def far(array):
    return pltpu.with_memory_space_constraint(array, pltpu.HBM)


def tap_lane(j, k, e):
    return (j + 1) * PATCH + 4 * k + e


def prepare_kernel(out_weight, wide, scratch):
    amount = scratch.shape[1] // LANES
    scratch[...] = jnp.zeros_like(scratch)
    for a in range(3):
        for e in range(3):
            for b in range(3):
                piece = out_weight[a, b, e].astype(F32)
                for i in range(amount):
                    for k in range(3):
                        at = a * LANES + tap_lane(i - b + 2, k, e)
                        scratch[at : at + 1, i * LANES : (i + 1) * LANES] = piece[k : k + 1]
    wide[...] = scratch[...].astype(BF16)


def norm_constants(totals, cell_total):
    channels = totals.shape[1]
    size = channels // GROUPS
    totals = jnp.broadcast_to(totals, (8, channels))
    lane = mod(iota((8, channels), 1), size)
    first, second = [over_group(jnp.where(lane == i, totals, 0.0), size)[:1] for i in range(2)]
    mean = first / cell_total
    return mean, lax.rsqrt(second / cell_total - mean * mean + eps_norm)


def norm_slopes(state, mean, inverse, gain, shift):
    normed = (state - mean) * inverse
    return normed, silu_slope(normed * gain + shift) * gain


def slope_kernel(
    arrived,
    hidden,
    gain,
    shift,
    wide,
    far_owner,
    direct,
    edge_slopes,
    stats,
    sums,
    slopes_own,
    received,
    taps,
    owner,
    sem,
):
    copy = pltpu.make_async_copy(far_owner, owner, sem.at[0])
    copy.start()
    devices, message_rows, _ = arrived.shape
    own_rows, frame_count, width, channels = hidden.shape
    cells = frame_count * width
    per_frame = devices // frame_count
    got = arrived[...].reshape(received.shape)
    kind = mod(iota((got.shape[0], 1), 0), message_rows)
    totals = jnp.sum(jnp.where(kind == 3, got, 0.0), axis=0, keepdims=True)
    mean, inverse = norm_constants(totals, own_rows * devices * cells * (channels // GROUPS))
    for i in range(own_rows):
        state = hidden[i].reshape(cells, channels).astype(F32)
        slopes_own[i] = norm_slopes(state, mean, inverse, gain[...], shift[...])[1] * inverse

    if per_frame == 1:
        lane = iota((1, LANES), 1)
        entry = iota((LANES, 1), 0)
        turned = ones_where(entry - mod(entry, PATCH) + PATCH - 1 - mod(entry, PATCH) == lane)
        received[...] = matmul(jnp.where(kind < 3, got, 0.0).astype(BF16), turned)
        lane = mod(iota((PATCH, LANES), 1), PATCH)
        column = iota((PATCH, LANES), 0)
        marks = []
        for k in range(3):
            e = lane - 4 * k
            wanted = column - e + 1
            marks.append((e >= 0) & (e < 3) & (wanted >= 0) & (wanted < PATCH))
        copy.wait()
        for d in range(devices):
            row = first_order(devices)[d]
            block = jnp.zeros((PATCH, LANES), F32)
            for k in range(3):
                line = jnp.broadcast_to(received[d * message_rows + k : d * message_rows + k + 1, :], (PATCH, LANES))
                line = pltpu.roll(line, 4 * k + 2, 1, stride=1, stride_axis=0)
                block = jnp.where(marks[k], line, block)
            start = pl.multiple_of(owner[row] * PATCH, PATCH)
            taps[pl.ds(start, PATCH), :] = block.astype(BF16)
    else:
        copy.wait()
        received[...] = got
        lines = [received[pl.ds(k, devices, stride=message_rows), :] for k in range(3)]
        lines = jnp.concatenate(lines, axis=1).astype(BF16)
        place = iota((1, devices), 1)
        source = jnp.zeros_like(place)
        for index, d in enumerate(first_order(devices)):
            source = jnp.where(place == index, d, source)
        home = jnp.zeros((1, devices), jnp.int32)
        for b in range(frame_count):
            home = jnp.where(div(source, per_frame) == b, owner[b] * per_frame, home)
        home = home + mod(source, per_frame)
        cell = iota((cells, 1), 0)
        column = mod(cell, width)
        lane = mod(iota((1, 3 * LANES), 1), PATCH)
        entry = iota((3 * LANES, 1), 0)
        window_row = div(mod(entry, LANES), PATCH)
        found = jnp.zeros((cells, LANES), F32)
        for e in range(3):
            wanted = column - e + 1
            strip = div(cell, width) * per_frame + div(wanted, PATCH)
            placed = matmul(ones_where(home == strip), lines)
            inside = jnp.where((wanted >= 0) & (wanted < width), mod(wanted, PATCH), -1)
            kept = jnp.where(lane == inside, placed, 0.0).astype(BF16)
            target = jnp.where(
                window_row < own_rows + 4, tap_lane(window_row, div(entry, LANES), e), -1
            )
            found = found + matmul(kept, ones_where(target == iota((1, LANES), 1)))
        taps[:cells, :] = found.astype(BF16)
    taps[cells:, :] = jnp.zeros((2 * width, LANES), BF16)
    steps = [taps[(2 - a) * width : (2 - a) * width + cells, :] for a in range(3)]
    result = matmul(jnp.concatenate(steps, axis=1), wide[...])

    first = jnp.zeros((1, channels), F32)
    second = jnp.zeros((1, channels), F32)
    for i in range(own_rows):
        state = hidden[i].reshape(cells, channels).astype(F32)
        part = result[:, (i + 1) * channels : (i + 2) * channels] * slopes_own[i]
        direct[i] = part
        first = first + jnp.sum(part, axis=0, keepdims=True)
        second = second + jnp.sum(part * (state - mean), axis=0, keepdims=True)
    first = first / inverse
    edge_slopes[0] = result[:, :channels]
    edge_slopes[1] = result[:, (own_rows + 1) * channels :]
    stats[0:1, :] = mean
    stats[1:2, :] = inverse
    both = jnp.where(iota((2, channels), 0) == 0, first, second)
    sums[...] = jnp.broadcast_to(both[None], sums.shape)


def late_kernel(
    across, along, slopes, stats, gain, shift, far_weight, direct, states, turned, inner_weight, sem
):
    copy = pltpu.make_async_copy(far_weight, inner_weight, sem.at[0])
    copy.start()
    cells, channels = slopes.shape[1:]
    odd = lax.axis_index("row") % 2 == 1
    mean = stats[0:1, :]
    inverse = stats[1:2, :]
    for i in range(2):
        state = jnp.where(odd == (i == 0), across[0], along[0])
        states[i] = state
        values = state.reshape(cells, channels).astype(F32)
        direct[i] = slopes[i] * norm_slopes(values, mean, inverse, gain[...], shift[...])[1] * inverse
    copy.wait()
    size = inner_weight.shape[3]
    for b in range(3):
        for a in range(3):
            for e in range(3):
                at = (a * 3 + e) * size
                turned[at : at + size, b * size : (b + 1) * size] = inner_weight[a, b, e].T


def inner_kernel(
    arrived, stats, direct, hidden, edge_direct, edge_states, turned, far_out, padded, out, sems, *, devices
):
    own_rows, frame_count, width, channels = out.shape
    cells = frame_count * width
    totals = jnp.sum(arrived[...], axis=0)
    cell_total = own_rows * devices * cells * (channels // GROUPS)
    place_row = iota((8, channels), 0)
    both = jnp.where(place_row == 0, totals[0:1], totals[1:2])
    both = over_group(both, channels // GROUPS)
    first, second = both[0:1], both[1:2]
    mean = stats[0:1, :]
    inverse = stats[1:2, :]
    constant = first / cell_total * inverse
    factor = second / cell_total * inverse * inverse
    position = lax.axis_index("row")
    in_frame = mod(iota((cells, 1), 0), width)
    for i in range(own_rows + 2):
        if 0 < i < own_rows + 1:
            state, part = hidden[i - 1], direct[i - 1]
        else:
            state, part = edge_states[min(i, 1)], edge_direct[min(i, 1)]
        grad = part - constant - (state.reshape(cells, channels).astype(F32) - mean) * factor
        if i == 0:
            grad = jnp.where(position > 0, grad, 0.0)
        if i == own_rows + 1:
            grad = jnp.where(position < devices - 1, grad, 0.0)
        after = jnp.where(in_frame < width - 1, pltpu.roll(grad, cells - 1, 0), 0.0)
        prior = jnp.where(in_frame > 0, pltpu.roll(grad, 1, 0), 0.0)
        padded[i, :cells, 0:channels] = after.astype(BF16)
        padded[i, :cells, channels : 2 * channels] = grad.astype(BF16)
        padded[i, :cells, 2 * channels :] = prior.astype(BF16)
        padded[i, cells:, :] = jnp.zeros((2 * width, 3 * channels), BF16)
    results = [jnp.zeros((cells, channels), F32) for _ in range(own_rows)]
    copies = []
    for i in range(own_rows + 2):
        joined = jnp.concatenate(
            [padded[i, (2 - a) * width : (2 - a) * width + cells, :] for a in range(3)], axis=1
        )
        taps = [b for b in range(3) if 0 <= i + b - 2 < own_rows]
        for low in range(0, len(taps), 2):
            some = taps[low : low + 2]
            product = matmul(joined, turned[:, some[0] * channels : (some[-1] + 1) * channels])
            for step, b in enumerate(some):
                results[i + b - 2] = results[i + b - 2] + product[:, step * channels : (step + 1) * channels]
        if i >= 2:
            out[i - 2] = results[i - 2].reshape(frame_count, width, channels).astype(BF16)
            copies.append(pltpu.make_async_copy(out.at[i - 2], far_out.at[i - 2], sems.at[i - 2]))
            copies[-1].start()
    for copy in copies:
        copy.wait()


def per_device(
    frames,
    frame_owner,
    picks,
    patch_weight,
    patch_bias,
    norm_gain,
    head_weight,
    head_bias,
    head_out,
    hidden_state,
    group_gain,
    group_shift,
    out_weight,
    inner_weight,
):
    devices = lax.axis_size("row")
    per_frame = devices // FRAMES
    height = frames.shape[1]
    own_rows, _, frame_width, channels = hidden_state.shape
    cells = FRAMES * frame_width
    width = patch_weight.shape[1]
    turned_frames = jnp.transpose(frames, (0, 2, 1))
    bias = patch_bias.reshape(1, width)
    gain = norm_gain.reshape(1, width)
    head_bias_row = head_bias.reshape(1, width)
    head_out_row = head_out.reshape(1, width)
    state_rows = own_rows + 2
    edge = jax.ShapeDtypeStruct((1,) + hidden_state.shape[1:], BF16)
    message = (message_shape(devices), edge, edge)
    gain_row = group_gain.reshape(1, channels)
    shift_row = group_shift.reshape(1, channels)
    early = [hidden_state, gain_row, shift_row, out_weight]
    slope_outs = (
        pltpu.VMEM((own_rows, cells, channels), F32),
        pltpu.VMEM((2, cells, channels), F32),
        pltpu.VMEM((8, channels), F32),
        jax.ShapeDtypeStruct((devices, 2, channels), F32),
    )
    if per_frame == 1:
        arrays = [turned_frames, bias, gain, frame_owner, picks, head_bias_row, head_out_row]
        weights = [patch_weight, head_weight]

        def scratch(x):
            return (pltpu.SMEM if x.dtype == jnp.int32 else pltpu.VMEM)(x.shape, x.dtype)

        send, across, along, *early = pl.pallas_call(
            reward_kernel,
            out_shape=message + tuple(pltpu.VMEM(x.shape, x.dtype) for x in early),
            in_specs=[FAR] * (len(arrays) + len(early) + len(weights)),
            out_specs=[VMEM] * (3 + len(early)),
            scratch_shapes=[scratch(x) for x in arrays + weights] + [pltpu.SemaphoreType.DMA((32,))],
            compiler_params=params(0),
            name="reward",
        )(*[far(x) for x in arrays + early + weights])
    else:
        count = height // PATCH
        normed, inv_spread, partial = pl.pallas_call(
            forward_kernel,
            out_shape=(
                jax.ShapeDtypeStruct((token_rows_of(height), width), F32),
                jax.ShapeDtypeStruct((token_rows_of(height), LANES), F32),
                jax.ShapeDtypeStruct((1, width), F32),
            ),
            compiler_params=params(cells),
            name="reward_forward",
        )(turned_frames, bias, gain, patch_weight)
        members = [[b * per_frame + i for i in range(per_frame)] for b in range(FRAMES)]
        pooled = lax.psum(partial, "row", axis_index_groups=members) / (count * per_frame)
        send, across, along = pl.pallas_call(
            functools.partial(backward_kernel, height=height, per_frame=per_frame),
            out_shape=message,
            in_specs=[SMEM] * 2 + [VMEM] * 9,
            out_specs=[VMEM] * 3,
            compiler_params=params(cells),
            name="reward_backward",
        )(
            frame_owner,
            picks,
            hidden_state,
            gain,
            head_bias_row,
            head_out_row,
            normed,
            inv_spread,
            pooled,
            patch_weight,
            head_weight,
        )
    early = [near(x) for x in early]
    wide = pl.pallas_call(
        prepare_kernel,
        out_shape=pltpu.VMEM((3 * LANES, state_rows * channels), BF16),
        in_specs=[VMEM],
        scratch_shapes=[pltpu.VMEM((3 * LANES, state_rows * channels), F32)],
        compiler_params=params(cells),
        name="prepare",
    )(early[3])
    arrived = lax.all_to_all(send, "row", 0, 0, axis_index_groups=[first_order(devices)], tiled=True)
    direct, edge_slopes, stats, sums = pl.pallas_call(
        slope_kernel,
        out_shape=slope_outs,
        in_specs=[VMEM] * 5 + [FAR],
        scratch_shapes=[
            pltpu.VMEM((own_rows, cells, channels), F32),
            pltpu.VMEM((4 * devices, LANES), F32),
            pltpu.VMEM((cells + 2 * frame_width, LANES), BF16),
            pltpu.SMEM(frame_owner.shape, jnp.int32),
            pltpu.SemaphoreType.DMA((1,)),
        ],
        compiler_params=params(cells),
        name="slope",
    )(near(arrived), *early[:3], near(wide), far(frame_owner))
    swaps = [(2 * i, 2 * i + 1) for i in range(devices // 2)]
    across = lax.ppermute(across, "row", swaps + [(b, a) for a, b in swaps])
    swaps = [(2 * i - 1, 2 * i) for i in range(1, devices // 2)]
    along = lax.ppermute(along, "row", swaps + [(b, a) for a, b in swaps])
    summed = lax.all_to_all(sums, "row", 0, 0, axis_index_groups=[led_by(devices - 1, devices)], tiled=True)
    edge_direct, edge_states, turned = pl.pallas_call(
        late_kernel,
        out_shape=(
            pltpu.VMEM((2, cells, channels), F32),
            pltpu.VMEM((2,) + hidden_state.shape[1:], BF16),
            pltpu.VMEM((9 * channels, 3 * channels), BF16),
        ),
        in_specs=[VMEM] * 6 + [FAR],
        scratch_shapes=[pltpu.VMEM(inner_weight.shape, BF16), pltpu.SemaphoreType.DMA((1,))],
        input_output_aliases={2: 0},
        compiler_params=params(cells),
        name="late",
    )(near(across), near(along), near(edge_slopes), near(stats), *early[1:3], far(inner_weight))
    return pl.pallas_call(
        functools.partial(inner_kernel, devices=devices),
        out_shape=jax.ShapeDtypeStruct(hidden_state.shape, BF16),
        in_specs=[VMEM] * 7,
        out_specs=FAR,
        scratch_shapes=[
            pltpu.VMEM((own_rows + 2, cells + 2 * frame_width, 3 * channels), BF16),
            pltpu.VMEM(hidden_state.shape, BF16),
            pltpu.SemaphoreType.DMA((own_rows,)),
        ],
        compiler_params=params(cells),
        name="inner",
    )(
        near(summed),
        near(stats),
        near(direct),
        early[0],
        near(edge_direct),
        near(edge_states),
        near(turned),
    )


def solution(mesh):
    return jax.shard_map(
        per_device,
        mesh=mesh,
        in_specs=(
            P(None, None, ("clip", "row")),
            P("clip"),
            P("clip"),
            P(),
            P(),
            P(),
            P(),
            P(),
            P(),
            P(("clip", "row"), None, None, None),
            P(),
            P(),
            P(),
            P(),
        ),
        out_specs=P(("clip", "row"), None, None, None),
        check_vma=False,
    )
```

```python
import functools

import jax
import jax.numpy as jnp
from jax import lax
from jax.experimental import pallas as pl
from jax.experimental.pallas import tpu as pltpu
from jax.sharding import PartitionSpec as P

PATCH = 16
GROUPS = 32
FRAMES = 16
LANES = 128
SLOTS = LANES // PATCH
eps_norm = 1e-06
BF16 = jnp.bfloat16
F32 = jnp.float32

SMEM = pl.BlockSpec(memory_space=pltpu.SMEM)
VMEM = pl.BlockSpec(memory_space=pltpu.VMEM)
FAR = pl.BlockSpec(memory_space=pl.ANY)


def iota(shape, dim):
    return lax.broadcasted_iota(jnp.int32, shape, dim)


def div(values, count):
    if count & (count - 1):
        return values // count
    return values >> (count.bit_length() - 1)


def mod(values, count):
    if count & (count - 1):
        return values % count
    return values & (count - 1)


def ones_where(condition):
    return jnp.where(condition, 1.0, 0.0).astype(BF16)


def matmul(left, right):
    return jnp.dot(left, right, preferred_element_type=F32)


def matmul_t(left, right):
    return lax.dot_general(left, right, (((1,), (1,)), ((), ())), preferred_element_type=F32)


def cut_in_three(values):
    high = values.astype(BF16)
    rest = values - high.astype(F32)
    middle = rest.astype(BF16)
    low = (rest - middle.astype(F32)).astype(BF16)
    return high, middle, low


def exact_rows(rows, product):
    place = iota((16, rows[0].shape[1]), 0)
    stacked = jnp.zeros(place.shape, F32)
    for index, row in enumerate(rows):
        for step, piece in enumerate(cut_in_three(row)):
            stacked = jnp.where(place == 3 * index + step, piece.astype(F32), stacked)
    result = product(stacked.astype(BF16))
    return [
        result[3 * i : 3 * i + 1] + result[3 * i + 1 : 3 * i + 2] + result[3 * i + 2 : 3 * i + 3]
        for i in range(len(rows))
    ]


def silu_slope(values):
    sigmoid = jax.nn.sigmoid(values)
    return sigmoid * (1.0 + values * (1.0 - sigmoid))


def token_rows_of(height):
    return -(-(height // PATCH) // 16) * 16


def to_tokens(pixels):
    channels, columns, height = pixels.shape
    rows = channels * columns
    token_rows = token_rows_of(height)
    flat = pixels.reshape(rows, height)
    width = channels * PATCH * columns
    lane = iota((1, width), 1)
    place = iota((rows, 1), 0)
    mine = place == div(lane, PATCH * columns) * columns + mod(lane, columns)
    in_patch = mod(div(lane, columns), PATCH)
    pixel_row = iota((height, 1), 0)
    token = iota((token_rows, 1), 0)
    tokens = jnp.zeros((token_rows, width), F32)
    for t in range(height // PATCH):
        tiled = matmul(flat, ones_where(pixel_row == in_patch + t * PATCH))
        row = jnp.sum(jnp.where(mine, tiled, 0.0), axis=0, keepdims=True)
        tokens = jnp.where(token == t, row, tokens)
    return tokens.astype(BF16)


def forward_part(tokens, count, bias, gain, load_patch):
    embedded = jnp.zeros((tokens.shape[0], bias.shape[1]), F32)
    for low, high, weight in load_patch():
        embedded = embedded + matmul(tokens[:, low:high], weight)
    embedded = embedded + bias[...]
    centred = embedded - jnp.mean(embedded, axis=1, keepdims=True)
    inv_spread = lax.rsqrt(jnp.mean(centred * centred, axis=1, keepdims=True) + eps_norm)
    normed = centred * inv_spread
    weighted = normed * gain[...]
    inside = iota((tokens.shape[0], 1), 0) < count
    pooled = jnp.sum(jnp.where(inside, weighted, 0.0), axis=0, keepdims=True)
    return normed, inv_spread, pooled


def led_by(leader, devices):
    return [leader] + [d for d in reversed(range(devices)) if d != leader]


def first_order(devices):
    return led_by(devices * 9 // 16, devices)


def message_shape(devices):
    return jax.ShapeDtypeStruct((devices, 4, LANES), F32)


def write_windows(patch_grad, sums, own_rows, height, send):
    span = PATCH * PATCH
    line = jnp.concatenate(
        [
            jnp.concatenate([patch_grad[t : t + 1, k * span : (k + 1) * span] for t in range(height // PATCH)], axis=1)
            for k in range(3)
        ]
        + [jnp.zeros((1, height * PATCH), F32)],
        axis=0,
    )
    line = jnp.concatenate([jnp.zeros((4, LANES), F32), line, jnp.zeros((4, LANES), F32)], axis=1)
    used = iota((4, LANES), 1) < (own_rows + 4) * PATCH
    colour = iota((4, LANES), 0)
    for index, d in enumerate(first_order(send.shape[0])):
        start = LANES + (d * own_rows - 2) * PATCH
        window = jnp.where(used, line[:, start : start + LANES], 0.0)
        send[index] = jnp.where(colour < 3, window, sums[:4])


def channel_sums(hidden):
    values = hidden.reshape(-1, hidden.shape[-1]).astype(F32)
    return jnp.sum(values, axis=0, keepdims=True), jnp.sum(values * values, axis=0, keepdims=True)


def over_group(values, size):
    lane = iota(values.shape, 1)
    lanes = values.shape[1]
    step = 1
    while step < size:
        later = pltpu.roll(values, lanes - step, 1)
        earlier = pltpu.roll(values, step, 1)
        values = values + jnp.where((lane & step) == 0, later, earlier)
        step *= 2
    return values


def group_sums(hidden):
    channels = hidden.shape[-1]
    size = channels // GROUPS
    first, second = [
        over_group(jnp.broadcast_to(x, (8, channels)), size) for x in channel_sums(hidden)
    ]
    lane = mod(iota((8, channels), 1), size)
    return jnp.where(lane == 0, first, jnp.where(lane == 1, second, 0.0))


def pull_back(row, weight):
    parts = []
    for low in range(0, weight.shape[0], LANES):
        product = weight[low : low + LANES, :].astype(F32) * row
        folded = product[:, :LANES]
        for start in range(LANES, weight.shape[1], LANES):
            folded = folded + product[:, start : start + LANES]
        parts.append(jnp.sum(folded.T, axis=0, keepdims=True))
    return jnp.concatenate(parts, axis=1)


def backward_part(
    owner, picks, gain, head_bias, head_out, normed, inv_spread, pooled, through_patch, head, through_head, slot, own_rows, height, sums, send
):
    (before,) = exact_rows([pooled], through_head)
    slope = head_out[...] * silu_slope(before + head_bias[...])
    pulled = pull_back(slope, head)
    wanted = owner[slot]
    picked = jnp.int32(0)
    for k in range(picks.shape[0]):
        picked = picked + jnp.where(picks[k] == wanted, 1, 0)
    scaled = gain[...] * (picked.astype(F32) * pulled)
    token_grad = inv_spread * (
        scaled
        - jnp.mean(scaled, axis=1, keepdims=True)
        - normed * jnp.mean(scaled * normed, axis=1, keepdims=True)
    )
    patch_grad = through_patch(token_grad.astype(BF16)).astype(BF16).astype(F32)
    write_windows(patch_grad, sums, own_rows, height, send)


def write_edges(position, hidden, across, along):
    last = hidden.shape[0] - 1
    even = position % 2 == 0
    across[0] = hidden[jnp.where(even, last, 0)]
    along[0] = hidden[jnp.where(even, 0, last)]


def reward_kernel(*refs):
    position = lax.axis_index("row")
    count, kept = 7, 4
    far, refs = refs[: count + kept + 2], refs[count + kept + 2 :]
    send, across, along = refs[:3]
    near = refs[3 + kept : 3 + kept + count] + refs[3 : 3 + kept] + refs[3 + kept + count : -2]
    turned, sems = refs[-2:]
    frames, bias, gain, owner, picks, head_bias, head_out, hidden, _, _, _, patch, head = near
    count += kept
    depth, depths = 256, (256, 256)
    small = [pltpu.make_async_copy(far[i], near[i], sems.at[i]) for i in range(count)]
    pieces = []
    used = count
    for index, rows in enumerate(depths):
        source, target = far[count + index], near[count + index]
        parts = []
        for low in range(0, target.shape[0], rows):
            part = pl.ds(low, rows)
            parts.append(pltpu.make_async_copy(source.at[part], target.at[part], sems.at[used]))
            used += 1
        pieces.append(parts)
    for copy in [small[0], small[7]] + pieces[0] + small[1:7] + pieces[1] + small[8:]:
        copy.start()

    def load_patch():
        for low in range(0, patch.shape[0], depth):
            for copy in pieces[0][low // depths[0] : (low + depth) // depths[0]]:
                copy.wait()
            yield low, low + depth, patch[low : low + depth, :]
        small[1].wait()
        small[2].wait()
        for low in range(0, patch.shape[0], LANES):
            for start in range(0, patch.shape[1], LANES):
                block = patch[low : low + LANES, start : start + LANES]
                turned[start : start + LANES, low : low + LANES] = block.T

    height = frames.shape[2]
    patches = height // PATCH
    small[0].wait()
    small[7].wait()
    tokens = to_tokens(frames[...])
    sums = group_sums(hidden[...])
    write_edges(position, hidden, across, along)
    normed, inv_spread, pooled = forward_part(tokens, patches, bias, gain, load_patch)
    for copy in small[3:7]:
        copy.wait()

    def through_head(rows):
        total = jnp.zeros((rows.shape[0], head.shape[1]), F32)
        for index, low in enumerate(range(0, head.shape[0], depths[1])):
            pieces[1][index].wait()
            total = total + matmul(rows[:, low : low + depths[1]], head[low : low + depths[1], :])
        return total

    backward_part(
        owner,
        picks,
        gain,
        head_bias,
        head_out,
        normed,
        inv_spread,
        pooled / patches,
        lambda rows: matmul(rows, turned[...]),
        head,
        through_head,
        position,
        hidden.shape[0],
        height,
        sums,
        send,
    )
    for copy in small[8:]:
        copy.wait()


def forward_kernel(frames, bias, gain, patch, normed, inv_spread, pooled):
    width = patch.shape[0]
    tokens = to_tokens(frames[...])
    normed[...], spread, pooled[...] = forward_part(
        tokens, frames.shape[2] // PATCH, bias, gain, lambda: [(0, width, patch[...])]
    )
    inv_spread[...] = jnp.broadcast_to(spread, inv_spread.shape)


def backward_kernel(
    owner,
    picks,
    hidden,
    gain,
    head_bias,
    head_out,
    normed,
    inv_spread,
    pooled,
    patch,
    head,
    send,
    across,
    along,
    *,
    height,
    per_frame,
):
    position = lax.axis_index("row")
    write_edges(position, hidden, across, along)
    backward_part(
        owner,
        picks,
        gain,
        head_bias,
        head_out,
        normed[...],
        inv_spread[...][:, :1],
        pooled[...],
        lambda rows: matmul_t(rows, patch[...]),
        head,
        lambda rows: matmul(rows, head[...]),
        position // per_frame,
        hidden.shape[0],
        height,
        group_sums(hidden[...]),
        send,
    )


def params(cells):
    return pltpu.CompilerParams(vmem_limit_bytes=min(16 + cells // 64, 48) * 1024 * 1024)


def near(array):
    return pltpu.with_memory_space_constraint(array, pltpu.VMEM)


def far(array):
    return pltpu.with_memory_space_constraint(array, pltpu.HBM)


def tap_lane(j, k, e):
    return (j + 1) * PATCH + 4 * k + e


def prepare_kernel(out_weight, wide, scratch):
    amount = scratch.shape[1] // LANES
    scratch[...] = jnp.zeros_like(scratch)
    for a in range(3):
        for e in range(3):
            for b in range(3):
                piece = out_weight[a, b, e].astype(F32)
                for i in range(amount):
                    for k in range(3):
                        at = a * LANES + tap_lane(i - b + 2, k, e)
                        scratch[at : at + 1, i * LANES : (i + 1) * LANES] = piece[k : k + 1]
    wide[...] = scratch[...].astype(BF16)


def norm_constants(totals, cell_total):
    channels = totals.shape[1]
    size = channels // GROUPS
    totals = jnp.broadcast_to(totals, (8, channels))
    lane = mod(iota((8, channels), 1), size)
    first, second = [over_group(jnp.where(lane == i, totals, 0.0), size)[:1] for i in range(2)]
    mean = first / cell_total
    return mean, lax.rsqrt(second / cell_total - mean * mean + eps_norm)


def norm_slopes(state, mean, inverse, gain, shift):
    normed = (state - mean) * inverse
    return normed, silu_slope(normed * gain + shift) * gain


def slope_kernel(
    arrived,
    hidden,
    gain,
    shift,
    wide,
    far_owner,
    direct,
    edge_slopes,
    stats,
    sums,
    slopes_own,
    received,
    taps,
    owner,
    sem,
):
    copy = pltpu.make_async_copy(far_owner, owner, sem.at[0])
    copy.start()
    devices, message_rows, _ = arrived.shape
    own_rows, frame_count, width, channels = hidden.shape
    cells = frame_count * width
    per_frame = devices // frame_count
    got = arrived[...].reshape(received.shape)
    kind = mod(iota((got.shape[0], 1), 0), message_rows)
    totals = jnp.sum(jnp.where(kind == 3, got, 0.0), axis=0, keepdims=True)
    mean, inverse = norm_constants(totals, own_rows * devices * cells * (channels // GROUPS))
    for i in range(own_rows):
        state = hidden[i].reshape(cells, channels).astype(F32)
        slopes_own[i] = norm_slopes(state, mean, inverse, gain[...], shift[...])[1] * inverse

    if per_frame == 1:
        lane = iota((1, LANES), 1)
        entry = iota((LANES, 1), 0)
        turned = ones_where(entry - mod(entry, PATCH) + PATCH - 1 - mod(entry, PATCH) == lane)
        received[...] = matmul(jnp.where(kind < 3, got, 0.0).astype(BF16), turned)
        lane = mod(iota((PATCH, LANES), 1), PATCH)
        column = iota((PATCH, LANES), 0)
        marks = []
        for k in range(3):
            e = lane - 4 * k
            wanted = column - e + 1
            marks.append((e >= 0) & (e < 3) & (wanted >= 0) & (wanted < PATCH))
        copy.wait()
        for d in range(devices):
            row = first_order(devices)[d]
            block = jnp.zeros((PATCH, LANES), F32)
            for k in range(3):
                line = jnp.broadcast_to(received[d * message_rows + k : d * message_rows + k + 1, :], (PATCH, LANES))
                line = pltpu.roll(line, 4 * k + 2, 1, stride=1, stride_axis=0)
                block = jnp.where(marks[k], line, block)
            start = pl.multiple_of(owner[row] * PATCH, PATCH)
            taps[pl.ds(start, PATCH), :] = block.astype(BF16)
    else:
        copy.wait()
        received[...] = got
        lines = [received[pl.ds(k, devices, stride=message_rows), :] for k in range(3)]
        lines = jnp.concatenate(lines, axis=1).astype(BF16)
        place = iota((1, devices), 1)
        source = jnp.zeros_like(place)
        for index, d in enumerate(first_order(devices)):
            source = jnp.where(place == index, d, source)
        home = jnp.zeros((1, devices), jnp.int32)
        for b in range(frame_count):
            home = jnp.where(div(source, per_frame) == b, owner[b] * per_frame, home)
        home = home + mod(source, per_frame)
        cell = iota((cells, 1), 0)
        column = mod(cell, width)
        lane = mod(iota((1, 3 * LANES), 1), PATCH)
        entry = iota((3 * LANES, 1), 0)
        window_row = div(mod(entry, LANES), PATCH)
        found = jnp.zeros((cells, LANES), F32)
        for e in range(3):
            wanted = column - e + 1
            strip = div(cell, width) * per_frame + div(wanted, PATCH)
            placed = matmul(ones_where(home == strip), lines)
            inside = jnp.where((wanted >= 0) & (wanted < width), mod(wanted, PATCH), -1)
            kept = jnp.where(lane == inside, placed, 0.0).astype(BF16)
            target = jnp.where(
                window_row < own_rows + 4, tap_lane(window_row, div(entry, LANES), e), -1
            )
            found = found + matmul(kept, ones_where(target == iota((1, LANES), 1)))
        taps[:cells, :] = found.astype(BF16)
    taps[cells:, :] = jnp.zeros((2 * width, LANES), BF16)
    steps = [taps[(2 - a) * width : (2 - a) * width + cells, :] for a in range(3)]
    result = matmul(jnp.concatenate(steps, axis=1), wide[...])

    first = jnp.zeros((1, channels), F32)
    second = jnp.zeros((1, channels), F32)
    for i in range(own_rows):
        state = hidden[i].reshape(cells, channels).astype(F32)
        part = result[:, (i + 1) * channels : (i + 2) * channels] * slopes_own[i]
        direct[i] = part
        first = first + jnp.sum(part, axis=0, keepdims=True)
        second = second + jnp.sum(part * (state - mean), axis=0, keepdims=True)
    first = first / inverse
    edge_slopes[0] = result[:, :channels]
    edge_slopes[1] = result[:, (own_rows + 1) * channels :]
    stats[0:1, :] = mean
    stats[1:2, :] = inverse
    both = jnp.where(iota((2, channels), 0) == 0, first, second)
    sums[...] = jnp.broadcast_to(both[None], sums.shape)


def late_kernel(
    across, along, slopes, stats, gain, shift, far_weight, direct, states, turned, inner_weight, sem
):
    copy = pltpu.make_async_copy(far_weight, inner_weight, sem.at[0])
    copy.start()
    cells, channels = slopes.shape[1:]
    odd = lax.axis_index("row") % 2 == 1
    mean = stats[0:1, :]
    inverse = stats[1:2, :]
    for i in range(2):
        state = jnp.where(odd == (i == 0), across[0], along[0])
        states[i] = state
        values = state.reshape(cells, channels).astype(F32)
        direct[i] = slopes[i] * norm_slopes(values, mean, inverse, gain[...], shift[...])[1] * inverse
    copy.wait()
    size = inner_weight.shape[3]
    for b in range(3):
        for a in range(3):
            for e in range(3):
                at = (a * 3 + e) * size
                turned[at : at + size, b * size : (b + 1) * size] = inner_weight[a, b, e].T


def inner_kernel(
    arrived, stats, direct, hidden, edge_direct, edge_states, turned, far_out, padded, out, sems, *, devices
):
    own_rows, frame_count, width, channels = out.shape
    cells = frame_count * width
    totals = jnp.sum(arrived[...], axis=0)
    cell_total = own_rows * devices * cells * (channels // GROUPS)
    place_row = iota((8, channels), 0)
    both = jnp.where(place_row == 0, totals[0:1], totals[1:2])
    both = over_group(both, channels // GROUPS)
    first, second = both[0:1], both[1:2]
    mean = stats[0:1, :]
    inverse = stats[1:2, :]
    constant = first / cell_total * inverse
    factor = second / cell_total * inverse * inverse
    position = lax.axis_index("row")
    in_frame = mod(iota((cells, 1), 0), width)
    for i in range(own_rows + 2):
        if 0 < i < own_rows + 1:
            state, part = hidden[i - 1], direct[i - 1]
        else:
            state, part = edge_states[min(i, 1)], edge_direct[min(i, 1)]
        grad = part - constant - (state.reshape(cells, channels).astype(F32) - mean) * factor
        if i == 0:
            grad = jnp.where(position > 0, grad, 0.0)
        if i == own_rows + 1:
            grad = jnp.where(position < devices - 1, grad, 0.0)
        after = jnp.where(in_frame < width - 1, pltpu.roll(grad, cells - 1, 0), 0.0)
        prior = jnp.where(in_frame > 0, pltpu.roll(grad, 1, 0), 0.0)
        padded[i, :cells, 0:channels] = after.astype(BF16)
        padded[i, :cells, channels : 2 * channels] = grad.astype(BF16)
        padded[i, :cells, 2 * channels :] = prior.astype(BF16)
        padded[i, cells:, :] = jnp.zeros((2 * width, 3 * channels), BF16)
    results = [jnp.zeros((cells, channels), F32) for _ in range(own_rows)]
    copies = []
    for i in range(own_rows + 2):
        joined = jnp.concatenate(
            [padded[i, (2 - a) * width : (2 - a) * width + cells, :] for a in range(3)], axis=1
        )
        taps = [b for b in range(3) if 0 <= i + b - 2 < own_rows]
        for low in range(0, len(taps), 2):
            some = taps[low : low + 2]
            product = matmul(joined, turned[:, some[0] * channels : (some[-1] + 1) * channels])
            for step, b in enumerate(some):
                results[i + b - 2] = results[i + b - 2] + product[:, step * channels : (step + 1) * channels]
        if i >= 2:
            out[i - 2] = results[i - 2].reshape(frame_count, width, channels).astype(BF16)
            copies.append(pltpu.make_async_copy(out.at[i - 2], far_out.at[i - 2], sems.at[i - 2]))
            copies[-1].start()
    for copy in copies:
        copy.wait()


def per_device(
    frames,
    frame_owner,
    picks,
    patch_weight,
    patch_bias,
    norm_gain,
    head_weight,
    head_bias,
    head_out,
    hidden_state,
    group_gain,
    group_shift,
    out_weight,
    inner_weight,
):
    devices = lax.axis_size("row")
    per_frame = devices // FRAMES
    height = frames.shape[1]
    own_rows, _, frame_width, channels = hidden_state.shape
    cells = FRAMES * frame_width
    width = patch_weight.shape[1]
    turned_frames = jnp.transpose(frames, (0, 2, 1))
    bias = patch_bias.reshape(1, width)
    gain = norm_gain.reshape(1, width)
    head_bias_row = head_bias.reshape(1, width)
    head_out_row = head_out.reshape(1, width)
    state_rows = own_rows + 2
    edge = jax.ShapeDtypeStruct((1,) + hidden_state.shape[1:], BF16)
    message = (message_shape(devices), edge, edge)
    gain_row = group_gain.reshape(1, channels)
    shift_row = group_shift.reshape(1, channels)
    early = [hidden_state, gain_row, shift_row, out_weight]
    slope_outs = (
        pltpu.VMEM((own_rows, cells, channels), F32),
        pltpu.VMEM((2, cells, channels), F32),
        pltpu.VMEM((8, channels), F32),
        jax.ShapeDtypeStruct((devices, 2, channels), F32),
    )
    if per_frame == 1:
        arrays = [turned_frames, bias, gain, frame_owner, picks, head_bias_row, head_out_row]
        weights = [patch_weight, head_weight]

        def scratch(x):
            return (pltpu.SMEM if x.dtype == jnp.int32 else pltpu.VMEM)(x.shape, x.dtype)

        send, across, along, *early = pl.pallas_call(
            reward_kernel,
            out_shape=message + tuple(pltpu.VMEM(x.shape, x.dtype) for x in early),
            in_specs=[FAR] * (len(arrays) + len(early) + len(weights)),
            out_specs=[VMEM] * (3 + len(early)),
            scratch_shapes=[scratch(x) for x in arrays + weights]
            + [pltpu.VMEM(patch_weight.shape[::-1], BF16), pltpu.SemaphoreType.DMA((32,))],
            compiler_params=params(0),
            name="reward",
        )(*[far(x) for x in arrays + early + weights])
    else:
        count = height // PATCH
        normed, inv_spread, partial = pl.pallas_call(
            forward_kernel,
            out_shape=(
                jax.ShapeDtypeStruct((token_rows_of(height), width), F32),
                jax.ShapeDtypeStruct((token_rows_of(height), LANES), F32),
                jax.ShapeDtypeStruct((1, width), F32),
            ),
            compiler_params=params(cells),
            name="reward_forward",
        )(turned_frames, bias, gain, patch_weight)
        members = [[b * per_frame + i for i in range(per_frame)] for b in range(FRAMES)]
        pooled = lax.psum(partial, "row", axis_index_groups=members) / (count * per_frame)
        send, across, along = pl.pallas_call(
            functools.partial(backward_kernel, height=height, per_frame=per_frame),
            out_shape=message,
            in_specs=[SMEM] * 2 + [VMEM] * 9,
            out_specs=[VMEM] * 3,
            compiler_params=params(cells),
            name="reward_backward",
        )(
            frame_owner,
            picks,
            hidden_state,
            gain,
            head_bias_row,
            head_out_row,
            normed,
            inv_spread,
            pooled,
            patch_weight,
            head_weight,
        )
    early = [near(x) for x in early]
    wide = pl.pallas_call(
        prepare_kernel,
        out_shape=pltpu.VMEM((3 * LANES, state_rows * channels), BF16),
        in_specs=[VMEM],
        scratch_shapes=[pltpu.VMEM((3 * LANES, state_rows * channels), F32)],
        compiler_params=params(cells),
        name="prepare",
    )(early[3])
    arrived = lax.all_to_all(send, "row", 0, 0, axis_index_groups=[first_order(devices)], tiled=True)
    direct, edge_slopes, stats, sums = pl.pallas_call(
        slope_kernel,
        out_shape=slope_outs,
        in_specs=[VMEM] * 5 + [FAR],
        scratch_shapes=[
            pltpu.VMEM((own_rows, cells, channels), F32),
            pltpu.VMEM((4 * devices, LANES), F32),
            pltpu.VMEM((cells + 2 * frame_width, LANES), BF16),
            pltpu.SMEM(frame_owner.shape, jnp.int32),
            pltpu.SemaphoreType.DMA((1,)),
        ],
        compiler_params=params(cells),
        name="slope",
    )(near(arrived), *early[:3], near(wide), far(frame_owner))
    swaps = [(2 * i, 2 * i + 1) for i in range(devices // 2)]
    across = lax.ppermute(across, "row", swaps + [(b, a) for a, b in swaps])
    swaps = [(2 * i - 1, 2 * i) for i in range(1, devices // 2)]
    along = lax.ppermute(along, "row", swaps + [(b, a) for a, b in swaps])
    summed = lax.all_to_all(sums, "row", 0, 0, axis_index_groups=[led_by(devices - 1, devices)], tiled=True)
    edge_direct, edge_states, turned = pl.pallas_call(
        late_kernel,
        out_shape=(
            pltpu.VMEM((2, cells, channels), F32),
            pltpu.VMEM((2,) + hidden_state.shape[1:], BF16),
            pltpu.VMEM((9 * channels, 3 * channels), BF16),
        ),
        in_specs=[VMEM] * 6 + [FAR],
        scratch_shapes=[pltpu.VMEM(inner_weight.shape, BF16), pltpu.SemaphoreType.DMA((1,))],
        input_output_aliases={2: 0},
        compiler_params=params(cells),
        name="late",
    )(near(across), near(along), near(edge_slopes), near(stats), *early[1:3], far(inner_weight))
    return pl.pallas_call(
        functools.partial(inner_kernel, devices=devices),
        out_shape=jax.ShapeDtypeStruct(hidden_state.shape, BF16),
        in_specs=[VMEM] * 7,
        out_specs=FAR,
        scratch_shapes=[
            pltpu.VMEM((own_rows + 2, cells + 2 * frame_width, 3 * channels), BF16),
            pltpu.VMEM(hidden_state.shape, BF16),
            pltpu.SemaphoreType.DMA((own_rows,)),
        ],
        compiler_params=params(cells),
        name="inner",
    )(
        near(summed),
        near(stats),
        near(direct),
        early[0],
        near(edge_direct),
        near(edge_states),
        near(turned),
    )


def solution(mesh):
    return jax.shard_map(
        per_device,
        mesh=mesh,
        in_specs=(
            P(None, None, ("clip", "row")),
            P("clip"),
            P("clip"),
            P(),
            P(),
            P(),
            P(),
            P(),
            P(),
            P(("clip", "row"), None, None, None),
            P(),
            P(),
            P(),
            P(),
        ),
        out_specs=P(("clip", "row"), None, None, None),
        check_vma=False,
    )
```

```python
import functools

import jax
import jax.numpy as jnp
from jax import lax
from jax.experimental import pallas as pl
from jax.experimental.pallas import tpu as pltpu
from jax.sharding import PartitionSpec as P

PATCH = 16
GROUPS = 32
FRAMES = 16
LANES = 128
SLOTS = LANES // PATCH
eps_norm = 1e-06
BF16 = jnp.bfloat16
F32 = jnp.float32

SMEM = pl.BlockSpec(memory_space=pltpu.SMEM)
VMEM = pl.BlockSpec(memory_space=pltpu.VMEM)
FAR = pl.BlockSpec(memory_space=pl.ANY)


def iota(shape, dim):
    return lax.broadcasted_iota(jnp.int32, shape, dim)


def div(values, count):
    if count & (count - 1):
        return values // count
    return values >> (count.bit_length() - 1)


def mod(values, count):
    if count & (count - 1):
        return values % count
    return values & (count - 1)


def ones_where(condition):
    return jnp.where(condition, 1.0, 0.0).astype(BF16)


def matmul(left, right):
    return jnp.dot(left, right, preferred_element_type=F32)


def matmul_t(left, right):
    return lax.dot_general(left, right, (((1,), (1,)), ((), ())), preferred_element_type=F32)


def cut_in_three(values):
    high = values.astype(BF16)
    rest = values - high.astype(F32)
    middle = rest.astype(BF16)
    low = (rest - middle.astype(F32)).astype(BF16)
    return high, middle, low


def exact_rows(rows, product):
    place = iota((16, rows[0].shape[1]), 0)
    stacked = jnp.zeros(place.shape, F32)
    for index, row in enumerate(rows):
        for step, piece in enumerate(cut_in_three(row)):
            stacked = jnp.where(place == 3 * index + step, piece.astype(F32), stacked)
    result = product(stacked.astype(BF16))
    return [
        result[3 * i : 3 * i + 1] + result[3 * i + 1 : 3 * i + 2] + result[3 * i + 2 : 3 * i + 3]
        for i in range(len(rows))
    ]


def silu_slope(values):
    sigmoid = jax.nn.sigmoid(values)
    return sigmoid * (1.0 + values * (1.0 - sigmoid))


def token_rows_of(height):
    return -(-(height // PATCH) // 16) * 16


def to_tokens(pixels):
    channels, columns, height = pixels.shape
    rows = channels * columns
    token_rows = token_rows_of(height)
    flat = pixels.reshape(rows, height)
    width = channels * PATCH * columns
    lane = iota((1, width), 1)
    place = iota((rows, 1), 0)
    mine = place == div(lane, PATCH * columns) * columns + mod(lane, columns)
    in_patch = mod(div(lane, columns), PATCH)
    pixel_row = iota((height, 1), 0)
    token = iota((token_rows, 1), 0)
    tokens = jnp.zeros((token_rows, width), F32)
    for t in range(height // PATCH):
        tiled = matmul(flat, ones_where(pixel_row == in_patch + t * PATCH))
        row = jnp.sum(jnp.where(mine, tiled, 0.0), axis=0, keepdims=True)
        tokens = jnp.where(token == t, row, tokens)
    return tokens.astype(BF16)


def forward_part(tokens, count, bias, gain, load_patch):
    embedded = jnp.zeros((tokens.shape[0], bias.shape[1]), F32)
    for low, high, weight in load_patch():
        embedded = embedded + matmul(tokens[:, low:high], weight)
    embedded = embedded + bias[...]
    centred = embedded - jnp.mean(embedded, axis=1, keepdims=True)
    inv_spread = lax.rsqrt(jnp.mean(centred * centred, axis=1, keepdims=True) + eps_norm)
    normed = centred * inv_spread
    weighted = normed * gain[...]
    inside = iota((tokens.shape[0], 1), 0) < count
    pooled = jnp.sum(jnp.where(inside, weighted, 0.0), axis=0, keepdims=True)
    return normed, inv_spread, pooled


def led_by(leader, devices):
    return [leader] + [d for d in reversed(range(devices)) if d != leader]


def first_order(devices):
    return led_by(devices * 13 // 16, devices)


def message_shape(devices):
    return jax.ShapeDtypeStruct((devices, 4, LANES), F32)


def write_windows(patch_grad, sums, own_rows, height, send):
    span = PATCH * PATCH
    line = jnp.concatenate(
        [
            jnp.concatenate([patch_grad[t : t + 1, k * span : (k + 1) * span] for t in range(height // PATCH)], axis=1)
            for k in range(3)
        ]
        + [jnp.zeros((1, height * PATCH), F32)],
        axis=0,
    )
    line = jnp.concatenate([jnp.zeros((4, LANES), F32), line, jnp.zeros((4, LANES), F32)], axis=1)
    used = iota((4, LANES), 1) < (own_rows + 4) * PATCH
    colour = iota((4, LANES), 0)
    for index, d in enumerate(first_order(send.shape[0])):
        start = LANES + (d * own_rows - 2) * PATCH
        window = jnp.where(used, line[:, start : start + LANES], 0.0)
        send[index] = jnp.where(colour < 3, window, sums[:4])


def channel_sums(hidden):
    values = hidden.reshape(-1, hidden.shape[-1]).astype(F32)
    return jnp.sum(values, axis=0, keepdims=True), jnp.sum(values * values, axis=0, keepdims=True)


def over_group(values, size):
    lane = iota(values.shape, 1)
    lanes = values.shape[1]
    step = 1
    while step < size:
        later = pltpu.roll(values, lanes - step, 1)
        earlier = pltpu.roll(values, step, 1)
        values = values + jnp.where((lane & step) == 0, later, earlier)
        step *= 2
    return values


def group_sums(hidden):
    channels = hidden.shape[-1]
    size = channels // GROUPS
    first, second = [
        over_group(jnp.broadcast_to(x, (8, channels)), size) for x in channel_sums(hidden)
    ]
    lane = mod(iota((8, channels), 1), size)
    return jnp.where(lane == 0, first, jnp.where(lane == 1, second, 0.0))


def pull_back(row, weight):
    parts = []
    for low in range(0, weight.shape[0], LANES):
        product = weight[low : low + LANES, :].astype(F32) * row
        folded = product[:, :LANES]
        for start in range(LANES, weight.shape[1], LANES):
            folded = folded + product[:, start : start + LANES]
        parts.append(jnp.sum(folded.T, axis=0, keepdims=True))
    return jnp.concatenate(parts, axis=1)


def backward_part(
    owner, picks, gain, head_bias, head_out, normed, inv_spread, pooled, weight, head, through_head, slot, own_rows, height, sums, send
):
    (before,) = exact_rows([pooled], through_head)
    slope = head_out[...] * silu_slope(before + head_bias[...])
    pulled = pull_back(slope, head)
    wanted = owner[slot]
    picked = jnp.int32(0)
    for k in range(picks.shape[0]):
        picked = picked + jnp.where(picks[k] == wanted, 1, 0)
    scaled = gain[...] * (picked.astype(F32) * pulled)
    token_grad = inv_spread * (
        scaled
        - jnp.mean(scaled, axis=1, keepdims=True)
        - normed * jnp.mean(scaled * normed, axis=1, keepdims=True)
    )
    patch_grad = matmul_t(token_grad.astype(BF16), weight[...]).astype(BF16).astype(F32)
    write_windows(patch_grad, sums, own_rows, height, send)


def write_edges(position, hidden, across, along):
    last = hidden.shape[0] - 1
    even = position % 2 == 0
    across[0] = hidden[jnp.where(even, last, 0)]
    along[0] = hidden[jnp.where(even, 0, last)]


def reward_kernel(*refs):
    position = lax.axis_index("row")
    count, kept = 7, 4
    far, refs = refs[: count + kept + 2], refs[count + kept + 2 :]
    send, across, along = refs[:3]
    near = refs[3 + kept : 3 + kept + count] + refs[3 : 3 + kept] + refs[3 + kept + count : -1]
    sems = refs[-1]
    frames, bias, gain, owner, picks, head_bias, head_out, hidden, _, _, _, patch, head = near
    count += kept
    depth, depths = 256, (256, 256)
    small = [pltpu.make_async_copy(far[i], near[i], sems.at[i]) for i in range(count)]
    pieces = []
    used = count
    for index, rows in enumerate(depths):
        source, target = far[count + index], near[count + index]
        parts = []
        for low in range(0, target.shape[0], rows):
            part = pl.ds(low, rows)
            parts.append(pltpu.make_async_copy(source.at[part], target.at[part], sems.at[used]))
            used += 1
        pieces.append(parts)
    for copy in [small[0], small[7]] + pieces[0] + small[1:7] + pieces[1] + small[8:]:
        copy.start()

    def load_patch():
        for low in range(0, patch.shape[0], depth):
            for copy in pieces[0][low // depths[0] : (low + depth) // depths[0]]:
                copy.wait()
            yield low, low + depth, patch[low : low + depth, :]
        small[1].wait()
        small[2].wait()

    height = frames.shape[2]
    patches = height // PATCH
    small[0].wait()
    small[7].wait()
    tokens = to_tokens(frames[...])
    sums = group_sums(hidden[...])
    write_edges(position, hidden, across, along)
    normed, inv_spread, pooled = forward_part(tokens, patches, bias, gain, load_patch)
    for copy in small[3:7]:
        copy.wait()

    def through_head(rows):
        total = jnp.zeros((rows.shape[0], head.shape[1]), F32)
        for index, low in enumerate(range(0, head.shape[0], depths[1])):
            pieces[1][index].wait()
            total = total + matmul(rows[:, low : low + depths[1]], head[low : low + depths[1], :])
        return total

    backward_part(
        owner,
        picks,
        gain,
        head_bias,
        head_out,
        normed,
        inv_spread,
        pooled / patches,
        patch,
        head,
        through_head,
        position,
        hidden.shape[0],
        height,
        sums,
        send,
    )
    for copy in small[8:]:
        copy.wait()


def forward_kernel(frames, bias, gain, patch, normed, inv_spread, pooled):
    width = patch.shape[0]
    tokens = to_tokens(frames[...])
    normed[...], spread, pooled[...] = forward_part(
        tokens, frames.shape[2] // PATCH, bias, gain, lambda: [(0, width, patch[...])]
    )
    inv_spread[...] = jnp.broadcast_to(spread, inv_spread.shape)


def backward_kernel(
    owner,
    picks,
    hidden,
    gain,
    head_bias,
    head_out,
    normed,
    inv_spread,
    pooled,
    patch,
    head,
    send,
    across,
    along,
    *,
    height,
    per_frame,
):
    position = lax.axis_index("row")
    write_edges(position, hidden, across, along)
    backward_part(
        owner,
        picks,
        gain,
        head_bias,
        head_out,
        normed[...],
        inv_spread[...][:, :1],
        pooled[...],
        patch,
        head,
        lambda rows: matmul(rows, head[...]),
        position // per_frame,
        hidden.shape[0],
        height,
        group_sums(hidden[...]),
        send,
    )


def params(cells):
    return pltpu.CompilerParams(vmem_limit_bytes=min(16 + cells // 64, 48) * 1024 * 1024)


def near(array):
    return pltpu.with_memory_space_constraint(array, pltpu.VMEM)


def far(array):
    return pltpu.with_memory_space_constraint(array, pltpu.HBM)


def tap_lane(j, k, e):
    return (j + 1) * PATCH + 4 * k + e


def prepare_kernel(out_weight, wide, scratch):
    amount = scratch.shape[1] // LANES
    scratch[...] = jnp.zeros_like(scratch)
    for a in range(3):
        for e in range(3):
            for b in range(3):
                piece = out_weight[a, b, e].astype(F32)
                for i in range(amount):
                    for k in range(3):
                        at = a * LANES + tap_lane(i - b + 2, k, e)
                        scratch[at : at + 1, i * LANES : (i + 1) * LANES] = piece[k : k + 1]
    wide[...] = scratch[...].astype(BF16)


def norm_constants(totals, cell_total):
    channels = totals.shape[1]
    size = channels // GROUPS
    totals = jnp.broadcast_to(totals, (8, channels))
    lane = mod(iota((8, channels), 1), size)
    first, second = [over_group(jnp.where(lane == i, totals, 0.0), size)[:1] for i in range(2)]
    mean = first / cell_total
    return mean, lax.rsqrt(second / cell_total - mean * mean + eps_norm)


def norm_slopes(state, mean, inverse, gain, shift):
    normed = (state - mean) * inverse
    return normed, silu_slope(normed * gain + shift) * gain


def slope_kernel(
    arrived,
    hidden,
    gain,
    shift,
    wide,
    far_owner,
    direct,
    edge_slopes,
    stats,
    sums,
    slopes_own,
    received,
    taps,
    owner,
    sem,
):
    copy = pltpu.make_async_copy(far_owner, owner, sem.at[0])
    copy.start()
    devices, message_rows, _ = arrived.shape
    own_rows, frame_count, width, channels = hidden.shape
    cells = frame_count * width
    per_frame = devices // frame_count
    got = arrived[...].reshape(received.shape)
    kind = mod(iota((got.shape[0], 1), 0), message_rows)
    totals = jnp.sum(jnp.where(kind == 3, got, 0.0), axis=0, keepdims=True)
    mean, inverse = norm_constants(totals, own_rows * devices * cells * (channels // GROUPS))
    for i in range(own_rows):
        state = hidden[i].reshape(cells, channels).astype(F32)
        slopes_own[i] = norm_slopes(state, mean, inverse, gain[...], shift[...])[1] * inverse

    if per_frame == 1:
        lane = iota((1, LANES), 1)
        entry = iota((LANES, 1), 0)
        turned = ones_where(entry - mod(entry, PATCH) + PATCH - 1 - mod(entry, PATCH) == lane)
        received[...] = matmul(jnp.where(kind < 3, got, 0.0).astype(BF16), turned)
        lane = mod(iota((PATCH, LANES), 1), PATCH)
        column = iota((PATCH, LANES), 0)
        marks = []
        for k in range(3):
            e = lane - 4 * k
            wanted = column - e + 1
            marks.append((e >= 0) & (e < 3) & (wanted >= 0) & (wanted < PATCH))
        copy.wait()
        for d in range(devices):
            row = first_order(devices)[d]
            block = jnp.zeros((PATCH, LANES), F32)
            for k in range(3):
                line = jnp.broadcast_to(received[d * message_rows + k : d * message_rows + k + 1, :], (PATCH, LANES))
                line = pltpu.roll(line, 4 * k + 2, 1, stride=1, stride_axis=0)
                block = jnp.where(marks[k], line, block)
            start = pl.multiple_of(owner[row] * PATCH, PATCH)
            taps[pl.ds(start, PATCH), :] = block.astype(BF16)
    else:
        copy.wait()
        received[...] = got
        lines = [received[pl.ds(k, devices, stride=message_rows), :] for k in range(3)]
        lines = jnp.concatenate(lines, axis=1).astype(BF16)
        place = iota((1, devices), 1)
        source = jnp.zeros_like(place)
        for index, d in enumerate(first_order(devices)):
            source = jnp.where(place == index, d, source)
        home = jnp.zeros((1, devices), jnp.int32)
        for b in range(frame_count):
            home = jnp.where(div(source, per_frame) == b, owner[b] * per_frame, home)
        home = home + mod(source, per_frame)
        cell = iota((cells, 1), 0)
        column = mod(cell, width)
        lane = mod(iota((1, 3 * LANES), 1), PATCH)
        entry = iota((3 * LANES, 1), 0)
        window_row = div(mod(entry, LANES), PATCH)
        found = jnp.zeros((cells, LANES), F32)
        for e in range(3):
            wanted = column - e + 1
            strip = div(cell, width) * per_frame + div(wanted, PATCH)
            placed = matmul(ones_where(home == strip), lines)
            inside = jnp.where((wanted >= 0) & (wanted < width), mod(wanted, PATCH), -1)
            kept = jnp.where(lane == inside, placed, 0.0).astype(BF16)
            target = jnp.where(
                window_row < own_rows + 4, tap_lane(window_row, div(entry, LANES), e), -1
            )
            found = found + matmul(kept, ones_where(target == iota((1, LANES), 1)))
        taps[:cells, :] = found.astype(BF16)
    taps[cells:, :] = jnp.zeros((2 * width, LANES), BF16)
    steps = [taps[(2 - a) * width : (2 - a) * width + cells, :] for a in range(3)]
    result = matmul(jnp.concatenate(steps, axis=1), wide[...])

    first = jnp.zeros((1, channels), F32)
    second = jnp.zeros((1, channels), F32)
    for i in range(own_rows):
        state = hidden[i].reshape(cells, channels).astype(F32)
        part = result[:, (i + 1) * channels : (i + 2) * channels] * slopes_own[i]
        direct[i] = part
        first = first + jnp.sum(part, axis=0, keepdims=True)
        second = second + jnp.sum(part * (state - mean), axis=0, keepdims=True)
    first = first / inverse
    edge_slopes[0] = result[:, :channels]
    edge_slopes[1] = result[:, (own_rows + 1) * channels :]
    stats[0:1, :] = mean
    stats[1:2, :] = inverse
    both = jnp.where(iota((2, channels), 0) == 0, first, second)
    sums[...] = jnp.broadcast_to(both[None], sums.shape)


def late_kernel(
    across, along, slopes, stats, gain, shift, far_weight, direct, states, turned, inner_weight, sem
):
    copy = pltpu.make_async_copy(far_weight, inner_weight, sem.at[0])
    copy.start()
    cells, channels = slopes.shape[1:]
    odd = lax.axis_index("row") % 2 == 1
    mean = stats[0:1, :]
    inverse = stats[1:2, :]
    for i in range(2):
        state = jnp.where(odd == (i == 0), across[0], along[0])
        states[i] = state
        values = state.reshape(cells, channels).astype(F32)
        direct[i] = slopes[i] * norm_slopes(values, mean, inverse, gain[...], shift[...])[1] * inverse
    copy.wait()
    size = inner_weight.shape[3]
    for b in range(3):
        for a in range(3):
            for e in range(3):
                at = (a * 3 + e) * size
                turned[at : at + size, b * size : (b + 1) * size] = inner_weight[a, b, e].T


def inner_kernel(
    arrived, stats, direct, hidden, edge_direct, edge_states, turned, far_out, padded, out, sems, *, devices
):
    own_rows, frame_count, width, channels = out.shape
    cells = frame_count * width
    totals = jnp.sum(arrived[...], axis=0)
    cell_total = own_rows * devices * cells * (channels // GROUPS)
    place_row = iota((8, channels), 0)
    both = jnp.where(place_row == 0, totals[0:1], totals[1:2])
    both = over_group(both, channels // GROUPS)
    first, second = both[0:1], both[1:2]
    mean = stats[0:1, :]
    inverse = stats[1:2, :]
    constant = first / cell_total * inverse
    factor = second / cell_total * inverse * inverse
    position = lax.axis_index("row")
    in_frame = mod(iota((cells, 1), 0), width)
    for i in range(own_rows + 2):
        if 0 < i < own_rows + 1:
            state, part = hidden[i - 1], direct[i - 1]
        else:
            state, part = edge_states[min(i, 1)], edge_direct[min(i, 1)]
        grad = part - constant - (state.reshape(cells, channels).astype(F32) - mean) * factor
        if i == 0:
            grad = jnp.where(position > 0, grad, 0.0)
        if i == own_rows + 1:
            grad = jnp.where(position < devices - 1, grad, 0.0)
        after = jnp.where(in_frame < width - 1, pltpu.roll(grad, cells - 1, 0), 0.0)
        prior = jnp.where(in_frame > 0, pltpu.roll(grad, 1, 0), 0.0)
        padded[i, :cells, 0:channels] = after.astype(BF16)
        padded[i, :cells, channels : 2 * channels] = grad.astype(BF16)
        padded[i, :cells, 2 * channels :] = prior.astype(BF16)
        padded[i, cells:, :] = jnp.zeros((2 * width, 3 * channels), BF16)
    results = [jnp.zeros((cells, channels), F32) for _ in range(own_rows)]
    copies = []
    for i in range(own_rows + 2):
        joined = jnp.concatenate(
            [padded[i, (2 - a) * width : (2 - a) * width + cells, :] for a in range(3)], axis=1
        )
        taps = [b for b in range(3) if 0 <= i + b - 2 < own_rows]
        for low in range(0, len(taps), 2):
            some = taps[low : low + 2]
            product = matmul(joined, turned[:, some[0] * channels : (some[-1] + 1) * channels])
            for step, b in enumerate(some):
                results[i + b - 2] = results[i + b - 2] + product[:, step * channels : (step + 1) * channels]
        if i >= 2:
            out[i - 2] = results[i - 2].reshape(frame_count, width, channels).astype(BF16)
            copies.append(pltpu.make_async_copy(out.at[i - 2], far_out.at[i - 2], sems.at[i - 2]))
            copies[-1].start()
    for copy in copies:
        copy.wait()


def per_device(
    frames,
    frame_owner,
    picks,
    patch_weight,
    patch_bias,
    norm_gain,
    head_weight,
    head_bias,
    head_out,
    hidden_state,
    group_gain,
    group_shift,
    out_weight,
    inner_weight,
):
    devices = lax.axis_size("row")
    per_frame = devices // FRAMES
    height = frames.shape[1]
    own_rows, _, frame_width, channels = hidden_state.shape
    cells = FRAMES * frame_width
    width = patch_weight.shape[1]
    turned_frames = jnp.transpose(frames, (0, 2, 1))
    bias = patch_bias.reshape(1, width)
    gain = norm_gain.reshape(1, width)
    head_bias_row = head_bias.reshape(1, width)
    head_out_row = head_out.reshape(1, width)
    state_rows = own_rows + 2
    edge = jax.ShapeDtypeStruct((1,) + hidden_state.shape[1:], BF16)
    message = (message_shape(devices), edge, edge)
    gain_row = group_gain.reshape(1, channels)
    shift_row = group_shift.reshape(1, channels)
    early = [hidden_state, gain_row, shift_row, out_weight]
    slope_outs = (
        pltpu.VMEM((own_rows, cells, channels), F32),
        pltpu.VMEM((2, cells, channels), F32),
        pltpu.VMEM((8, channels), F32),
        jax.ShapeDtypeStruct((devices, 2, channels), F32),
    )
    if per_frame == 1:
        arrays = [turned_frames, bias, gain, frame_owner, picks, head_bias_row, head_out_row]
        weights = [patch_weight, head_weight]

        def scratch(x):
            return (pltpu.SMEM if x.dtype == jnp.int32 else pltpu.VMEM)(x.shape, x.dtype)

        send, across, along, *early = pl.pallas_call(
            reward_kernel,
            out_shape=message + tuple(pltpu.VMEM(x.shape, x.dtype) for x in early),
            in_specs=[FAR] * (len(arrays) + len(early) + len(weights)),
            out_specs=[VMEM] * (3 + len(early)),
            scratch_shapes=[scratch(x) for x in arrays + weights] + [pltpu.SemaphoreType.DMA((32,))],
            compiler_params=params(0),
            name="reward",
        )(*[far(x) for x in arrays + early + weights])
    else:
        count = height // PATCH
        normed, inv_spread, partial = pl.pallas_call(
            forward_kernel,
            out_shape=(
                jax.ShapeDtypeStruct((token_rows_of(height), width), F32),
                jax.ShapeDtypeStruct((token_rows_of(height), LANES), F32),
                jax.ShapeDtypeStruct((1, width), F32),
            ),
            compiler_params=params(cells),
            name="reward_forward",
        )(turned_frames, bias, gain, patch_weight)
        members = [[b * per_frame + i for i in range(per_frame)] for b in range(FRAMES)]
        pooled = lax.psum(partial, "row", axis_index_groups=members) / (count * per_frame)
        send, across, along = pl.pallas_call(
            functools.partial(backward_kernel, height=height, per_frame=per_frame),
            out_shape=message,
            in_specs=[SMEM] * 2 + [VMEM] * 9,
            out_specs=[VMEM] * 3,
            compiler_params=params(cells),
            name="reward_backward",
        )(
            frame_owner,
            picks,
            hidden_state,
            gain,
            head_bias_row,
            head_out_row,
            normed,
            inv_spread,
            pooled,
            patch_weight,
            head_weight,
        )
    early = [near(x) for x in early]
    wide = pl.pallas_call(
        prepare_kernel,
        out_shape=pltpu.VMEM((3 * LANES, state_rows * channels), BF16),
        in_specs=[VMEM],
        scratch_shapes=[pltpu.VMEM((3 * LANES, state_rows * channels), F32)],
        compiler_params=params(cells),
        name="prepare",
    )(early[3])
    arrived = lax.all_to_all(send, "row", 0, 0, axis_index_groups=[first_order(devices)], tiled=True)
    direct, edge_slopes, stats, sums = pl.pallas_call(
        slope_kernel,
        out_shape=slope_outs,
        in_specs=[VMEM] * 5 + [FAR],
        scratch_shapes=[
            pltpu.VMEM((own_rows, cells, channels), F32),
            pltpu.VMEM((4 * devices, LANES), F32),
            pltpu.VMEM((cells + 2 * frame_width, LANES), BF16),
            pltpu.SMEM(frame_owner.shape, jnp.int32),
            pltpu.SemaphoreType.DMA((1,)),
        ],
        compiler_params=params(cells),
        name="slope",
    )(near(arrived), *early[:3], near(wide), far(frame_owner))
    swaps = [(2 * i, 2 * i + 1) for i in range(devices // 2)]
    across = lax.ppermute(across, "row", swaps + [(b, a) for a, b in swaps])
    swaps = [(2 * i - 1, 2 * i) for i in range(1, devices // 2)]
    along = lax.ppermute(along, "row", swaps + [(b, a) for a, b in swaps])
    summed = lax.all_to_all(sums, "row", 0, 0, axis_index_groups=[led_by(devices - 1, devices)], tiled=True)
    edge_direct, edge_states, turned = pl.pallas_call(
        late_kernel,
        out_shape=(
            pltpu.VMEM((2, cells, channels), F32),
            pltpu.VMEM((2,) + hidden_state.shape[1:], BF16),
            pltpu.VMEM((9 * channels, 3 * channels), BF16),
        ),
        in_specs=[VMEM] * 6 + [FAR],
        scratch_shapes=[pltpu.VMEM(inner_weight.shape, BF16), pltpu.SemaphoreType.DMA((1,))],
        input_output_aliases={2: 0},
        compiler_params=params(cells),
        name="late",
    )(near(across), near(along), near(edge_slopes), near(stats), *early[1:3], far(inner_weight))
    return pl.pallas_call(
        functools.partial(inner_kernel, devices=devices),
        out_shape=jax.ShapeDtypeStruct(hidden_state.shape, BF16),
        in_specs=[VMEM] * 7,
        out_specs=FAR,
        scratch_shapes=[
            pltpu.VMEM((own_rows + 2, cells + 2 * frame_width, 3 * channels), BF16),
            pltpu.VMEM(hidden_state.shape, BF16),
            pltpu.SemaphoreType.DMA((own_rows,)),
        ],
        compiler_params=params(cells),
        name="inner",
    )(
        near(summed),
        near(stats),
        near(direct),
        early[0],
        near(edge_direct),
        near(edge_states),
        near(turned),
    )


def solution(mesh):
    return jax.shard_map(
        per_device,
        mesh=mesh,
        in_specs=(
            P(None, None, ("clip", "row")),
            P("clip"),
            P("clip"),
            P(),
            P(),
            P(),
            P(),
            P(),
            P(),
            P(("clip", "row"), None, None, None),
            P(),
            P(),
            P(),
            P(),
        ),
        out_specs=P(("clip", "row"), None, None, None),
        check_vma=False,
    )
```

```python
import functools

import jax
import jax.numpy as jnp
from jax import lax
from jax.experimental import pallas as pl
from jax.experimental.pallas import tpu as pltpu
from jax.sharding import PartitionSpec as P

PATCH = 16
GROUPS = 32
FRAMES = 16
LANES = 128
SLOTS = LANES // PATCH
eps_norm = 1e-06
BF16 = jnp.bfloat16
F32 = jnp.float32

SMEM = pl.BlockSpec(memory_space=pltpu.SMEM)
VMEM = pl.BlockSpec(memory_space=pltpu.VMEM)
FAR = pl.BlockSpec(memory_space=pl.ANY)


def iota(shape, dim):
    return lax.broadcasted_iota(jnp.int32, shape, dim)


def div(values, count):
    if count & (count - 1):
        return values // count
    return values >> (count.bit_length() - 1)


def mod(values, count):
    if count & (count - 1):
        return values % count
    return values & (count - 1)


def ones_where(condition):
    return jnp.where(condition, 1.0, 0.0).astype(BF16)


def matmul(left, right):
    return jnp.dot(left, right, preferred_element_type=F32)


def matmul_t(left, right):
    return lax.dot_general(left, right, (((1,), (1,)), ((), ())), preferred_element_type=F32)


def cut_in_three(values):
    high = values.astype(BF16)
    rest = values - high.astype(F32)
    middle = rest.astype(BF16)
    low = (rest - middle.astype(F32)).astype(BF16)
    return high, middle, low


def exact_rows(rows, product):
    place = iota((8, rows[0].shape[1]), 0)
    stacked = jnp.zeros(place.shape, F32)
    for index, row in enumerate(rows):
        for step, piece in enumerate(cut_in_three(row)):
            stacked = jnp.where(place == 3 * index + step, piece.astype(F32), stacked)
    result = product(jnp.concatenate([stacked, jnp.zeros_like(stacked)], axis=0).astype(BF16))
    return [
        result[3 * i : 3 * i + 1] + result[3 * i + 1 : 3 * i + 2] + result[3 * i + 2 : 3 * i + 3]
        for i in range(len(rows))
    ]


def silu_slope(values):
    sigmoid = jax.nn.sigmoid(values)
    return sigmoid * (1.0 + values * (1.0 - sigmoid))


def token_rows_of(height):
    return -(-(height // PATCH) // 16) * 16


def to_tokens(pixels):
    channels, columns, height = pixels.shape
    rows = channels * columns
    token_rows = token_rows_of(height)
    flat = pixels.reshape(rows, height)
    width = channels * PATCH * columns
    lane = iota((1, width), 1)
    place = iota((rows, 1), 0)
    mine = place == div(lane, PATCH * columns) * columns + mod(lane, columns)
    in_patch = mod(div(lane, columns), PATCH)
    pixel_row = iota((height, 1), 0)
    token = iota((token_rows, 1), 0)
    tokens = jnp.zeros((token_rows, width), F32)
    for t in range(height // PATCH):
        tiled = matmul(flat, ones_where(pixel_row == in_patch + t * PATCH))
        row = jnp.sum(jnp.where(mine, tiled, 0.0), axis=0, keepdims=True)
        tokens = jnp.where(token == t, row, tokens)
    return tokens.astype(BF16)


def forward_part(tokens, count, bias, gain, load_patch):
    embedded = jnp.zeros((tokens.shape[0], bias.shape[1]), F32)
    for low, high, weight in load_patch():
        embedded = embedded + matmul(tokens[:, low:high], weight)
    rows = -(-count // 8) * 8
    embedded = embedded[:rows] + bias[...]
    centred = embedded - jnp.mean(embedded, axis=1, keepdims=True)
    inv_spread = lax.rsqrt(jnp.mean(centred * centred, axis=1, keepdims=True) + eps_norm)
    normed = centred * inv_spread
    weighted = normed * gain[...]
    inside = iota((rows, 1), 0) < count
    pooled = jnp.sum(jnp.where(inside, weighted, 0.0), axis=0, keepdims=True)
    return normed, inv_spread, pooled


def led_by(leader, devices):
    return [leader] + [d for d in reversed(range(devices)) if d != leader]


def first_order(devices):
    return led_by(devices * 13 // 16, devices)


def message_shape(devices):
    return jax.ShapeDtypeStruct((devices, 4, LANES), F32)


def write_windows(patch_grad, sums, own_rows, height, send):
    span = PATCH * PATCH
    line = jnp.concatenate(
        [
            jnp.concatenate([patch_grad[t : t + 1, k * span : (k + 1) * span] for t in range(height // PATCH)], axis=1)
            for k in range(3)
        ]
        + [jnp.zeros((1, height * PATCH), F32)],
        axis=0,
    )
    line = jnp.concatenate([jnp.zeros((4, LANES), F32), line, jnp.zeros((4, LANES), F32)], axis=1)
    used = iota((4, LANES), 1) < (own_rows + 4) * PATCH
    colour = iota((4, LANES), 0)
    for index, d in enumerate(first_order(send.shape[0])):
        start = LANES + (d * own_rows - 2) * PATCH
        window = jnp.where(used, line[:, start : start + LANES], 0.0)
        send[index] = jnp.where(colour < 3, window, sums[:4])


def channel_sums(hidden):
    values = hidden.reshape(-1, hidden.shape[-1]).astype(F32)
    return jnp.sum(values, axis=0, keepdims=True), jnp.sum(values * values, axis=0, keepdims=True)


def over_group(values, size):
    lane = iota(values.shape, 1)
    lanes = values.shape[1]
    step = 1
    while step < size:
        later = pltpu.roll(values, lanes - step, 1)
        earlier = pltpu.roll(values, step, 1)
        values = values + jnp.where((lane & step) == 0, later, earlier)
        step *= 2
    return values


def group_sums(hidden):
    channels = hidden.shape[-1]
    size = channels // GROUPS
    first, second = [
        over_group(jnp.broadcast_to(x, (8, channels)), size) for x in channel_sums(hidden)
    ]
    lane = mod(iota((8, channels), 1), size)
    return jnp.where(lane == 0, first, jnp.where(lane == 1, second, 0.0))


def pull_back(row, weight):
    parts = []
    for low in range(0, weight.shape[0], LANES):
        product = weight[low : low + LANES, :].astype(F32) * row
        folded = product[:, :LANES]
        for start in range(LANES, weight.shape[1], LANES):
            folded = folded + product[:, start : start + LANES]
        parts.append(jnp.sum(folded.T, axis=0, keepdims=True))
    return jnp.concatenate(parts, axis=1)


def backward_part(
    owner, picks, gain, head_bias, head_out, normed, inv_spread, pooled, weight, head, through_head, slot, own_rows, height, sums, send
):
    (before,) = exact_rows([pooled], through_head)
    slope = head_out[...] * silu_slope(before + head_bias[...])
    pulled = pull_back(slope, head)
    wanted = owner[slot]
    picked = jnp.int32(0)
    for k in range(picks.shape[0]):
        picked = picked + jnp.where(picks[k] == wanted, 1, 0)
    scaled = gain[...] * (picked.astype(F32) * pulled)
    token_grad = inv_spread * (
        scaled
        - jnp.mean(scaled, axis=1, keepdims=True)
        - normed * jnp.mean(scaled * normed, axis=1, keepdims=True)
    )
    filler = jnp.zeros((-token_grad.shape[0] % 16, token_grad.shape[1]), F32)
    token_grad = jnp.concatenate([token_grad, filler], axis=0).astype(BF16)
    patch_grad = matmul_t(token_grad, weight[...]).astype(BF16).astype(F32)
    write_windows(patch_grad, sums, own_rows, height, send)


def write_edges(position, hidden, across, along):
    last = hidden.shape[0] - 1
    even = position % 2 == 0
    across[0] = hidden[jnp.where(even, last, 0)]
    along[0] = hidden[jnp.where(even, 0, last)]


def reward_kernel(*refs):
    position = lax.axis_index("row")
    count, kept = 7, 4
    far, refs = refs[: count + kept + 2], refs[count + kept + 2 :]
    send, across, along = refs[:3]
    near = refs[3 + kept : 3 + kept + count] + refs[3 : 3 + kept] + refs[3 + kept + count : -1]
    sems = refs[-1]
    frames, bias, gain, owner, picks, head_bias, head_out, hidden, _, _, _, patch, head = near
    count += kept
    depths = (256, 256)
    small = [pltpu.make_async_copy(far[i], near[i], sems.at[i]) for i in range(count)]
    pieces = []
    used = count
    for index, rows in enumerate(depths):
        source, target = far[count + index], near[count + index]
        parts = []
        for low in range(0, target.shape[0], rows):
            part = pl.ds(low, rows)
            parts.append(pltpu.make_async_copy(source.at[part], target.at[part], sems.at[used]))
            used += 1
        pieces.append(parts)
    for copy in [small[0], small[7]] + pieces[0] + small[1:7] + pieces[1] + small[8:]:
        copy.start()

    def load_patch():
        for copy in pieces[0] + small[1:3]:
            copy.wait()
        yield 0, patch.shape[0], patch[...]

    height = frames.shape[2]
    patches = height // PATCH
    small[0].wait()
    small[7].wait()
    tokens = to_tokens(frames[...])
    sums = group_sums(hidden[...])
    write_edges(position, hidden, across, along)
    normed, inv_spread, pooled = forward_part(tokens, patches, bias, gain, load_patch)
    for copy in small[3:7]:
        copy.wait()

    def through_head(rows):
        total = jnp.zeros((rows.shape[0], head.shape[1]), F32)
        for index, low in enumerate(range(0, head.shape[0], depths[1])):
            pieces[1][index].wait()
            total = total + matmul(rows[:, low : low + depths[1]], head[low : low + depths[1], :])
        return total

    backward_part(
        owner,
        picks,
        gain,
        head_bias,
        head_out,
        normed,
        inv_spread,
        pooled / patches,
        patch,
        head,
        through_head,
        position,
        hidden.shape[0],
        height,
        sums,
        send,
    )
    for copy in small[8:]:
        copy.wait()


def forward_kernel(frames, bias, gain, patch, normed, inv_spread, pooled):
    width = patch.shape[0]
    tokens = to_tokens(frames[...])
    normed[...], spread, pooled[...] = forward_part(
        tokens, frames.shape[2] // PATCH, bias, gain, lambda: [(0, width, patch[...])]
    )
    inv_spread[...] = jnp.broadcast_to(spread, inv_spread.shape)


def backward_kernel(
    owner,
    picks,
    hidden,
    gain,
    head_bias,
    head_out,
    normed,
    inv_spread,
    pooled,
    patch,
    head,
    send,
    across,
    along,
    *,
    height,
    per_frame,
):
    position = lax.axis_index("row")
    write_edges(position, hidden, across, along)
    backward_part(
        owner,
        picks,
        gain,
        head_bias,
        head_out,
        normed[...],
        inv_spread[...][:, :1],
        pooled[...],
        patch,
        head,
        lambda rows: matmul(rows, head[...]),
        position // per_frame,
        hidden.shape[0],
        height,
        group_sums(hidden[...]),
        send,
    )


def params(cells):
    return pltpu.CompilerParams(vmem_limit_bytes=min(16 + cells // 64, 48) * 1024 * 1024)


def near(array):
    return pltpu.with_memory_space_constraint(array, pltpu.VMEM)


def far(array):
    return pltpu.with_memory_space_constraint(array, pltpu.HBM)


def tap_lane(j, k, e):
    return (j + 1) * PATCH + 4 * k + e


def prepare_kernel(out_weight, wide, scratch):
    amount = scratch.shape[1] // LANES
    scratch[...] = jnp.zeros_like(scratch)
    for a in range(3):
        for e in range(3):
            for b in range(3):
                piece = out_weight[a, b, e].astype(F32)
                for i in range(amount):
                    for k in range(3):
                        at = a * LANES + tap_lane(i - b + 2, k, e)
                        scratch[at : at + 1, i * LANES : (i + 1) * LANES] = piece[k : k + 1]
    wide[...] = scratch[...].astype(BF16)


def norm_constants(totals, cell_total):
    channels = totals.shape[1]
    size = channels // GROUPS
    totals = jnp.broadcast_to(totals, (8, channels))
    lane = mod(iota((8, channels), 1), size)
    first, second = [over_group(jnp.where(lane == i, totals, 0.0), size)[:1] for i in range(2)]
    mean = first / cell_total
    return mean, lax.rsqrt(second / cell_total - mean * mean + eps_norm)


def norm_slopes(state, mean, inverse, gain, shift):
    normed = (state - mean) * inverse
    return normed, silu_slope(normed * gain + shift) * gain


def slope_kernel(
    arrived,
    hidden,
    gain,
    shift,
    wide,
    far_owner,
    direct,
    edge_slopes,
    stats,
    sums,
    slopes_own,
    received,
    taps,
    owner,
    sem,
):
    copy = pltpu.make_async_copy(far_owner, owner, sem.at[0])
    copy.start()
    devices, message_rows, _ = arrived.shape
    own_rows, frame_count, width, channels = hidden.shape
    cells = frame_count * width
    per_frame = devices // frame_count
    got = arrived[...].reshape(received.shape)
    kind = mod(iota((got.shape[0], 1), 0), message_rows)
    totals = jnp.sum(jnp.where(kind == 3, got, 0.0), axis=0, keepdims=True)
    mean, inverse = norm_constants(totals, own_rows * devices * cells * (channels // GROUPS))
    for i in range(own_rows):
        state = hidden[i].reshape(cells, channels).astype(F32)
        slopes_own[i] = norm_slopes(state, mean, inverse, gain[...], shift[...])[1] * inverse

    if per_frame == 1:
        lane = iota((1, LANES), 1)
        entry = iota((LANES, 1), 0)
        turned = ones_where(entry - mod(entry, PATCH) + PATCH - 1 - mod(entry, PATCH) == lane)
        received[...] = matmul(jnp.where(kind < 3, got, 0.0).astype(BF16), turned)
        lane = mod(iota((PATCH, LANES), 1), PATCH)
        column = iota((PATCH, LANES), 0)
        marks = []
        for k in range(3):
            e = lane - 4 * k
            wanted = column - e + 1
            marks.append((e >= 0) & (e < 3) & (wanted >= 0) & (wanted < PATCH))
        copy.wait()
        for d in range(devices):
            row = first_order(devices)[d]
            block = jnp.zeros((PATCH, LANES), F32)
            for k in range(3):
                line = jnp.broadcast_to(received[d * message_rows + k : d * message_rows + k + 1, :], (PATCH, LANES))
                line = pltpu.roll(line, 4 * k + 2, 1, stride=1, stride_axis=0)
                block = jnp.where(marks[k], line, block)
            start = pl.multiple_of(owner[row] * PATCH, PATCH)
            taps[pl.ds(start, PATCH), :] = block.astype(BF16)
    else:
        copy.wait()
        received[...] = got
        lines = [received[pl.ds(k, devices, stride=message_rows), :] for k in range(3)]
        lines = jnp.concatenate(lines, axis=1).astype(BF16)
        place = iota((1, devices), 1)
        source = jnp.zeros_like(place)
        for index, d in enumerate(first_order(devices)):
            source = jnp.where(place == index, d, source)
        home = jnp.zeros((1, devices), jnp.int32)
        for b in range(frame_count):
            home = jnp.where(div(source, per_frame) == b, owner[b] * per_frame, home)
        home = home + mod(source, per_frame)
        cell = iota((cells, 1), 0)
        column = mod(cell, width)
        lane = mod(iota((1, 3 * LANES), 1), PATCH)
        entry = iota((3 * LANES, 1), 0)
        window_row = div(mod(entry, LANES), PATCH)
        found = jnp.zeros((cells, LANES), F32)
        for e in range(3):
            wanted = column - e + 1
            strip = div(cell, width) * per_frame + div(wanted, PATCH)
            placed = matmul(ones_where(home == strip), lines)
            inside = jnp.where((wanted >= 0) & (wanted < width), mod(wanted, PATCH), -1)
            kept = jnp.where(lane == inside, placed, 0.0).astype(BF16)
            target = jnp.where(
                window_row < own_rows + 4, tap_lane(window_row, div(entry, LANES), e), -1
            )
            found = found + matmul(kept, ones_where(target == iota((1, LANES), 1)))
        taps[:cells, :] = found.astype(BF16)
    taps[cells:, :] = jnp.zeros((2 * width, LANES), BF16)
    steps = [taps[(2 - a) * width : (2 - a) * width + cells, :] for a in range(3)]
    result = matmul(jnp.concatenate(steps, axis=1), wide[...])

    first = jnp.zeros((1, channels), F32)
    second = jnp.zeros((1, channels), F32)
    for i in range(own_rows):
        state = hidden[i].reshape(cells, channels).astype(F32)
        part = result[:, (i + 1) * channels : (i + 2) * channels] * slopes_own[i]
        direct[i] = part
        first = first + jnp.sum(part, axis=0, keepdims=True)
        second = second + jnp.sum(part * (state - mean), axis=0, keepdims=True)
    first = first / inverse
    edge_slopes[0] = result[:, :channels]
    edge_slopes[1] = result[:, (own_rows + 1) * channels :]
    stats[0:1, :] = mean
    stats[1:2, :] = inverse
    both = jnp.where(iota((2, channels), 0) == 0, first, second)
    sums[...] = jnp.broadcast_to(both[None], sums.shape)


def late_kernel(
    across, along, slopes, stats, gain, shift, far_weight, direct, states, turned, inner_weight, sem
):
    copy = pltpu.make_async_copy(far_weight, inner_weight, sem.at[0])
    copy.start()
    cells, channels = slopes.shape[1:]
    odd = lax.axis_index("row") % 2 == 1
    mean = stats[0:1, :]
    inverse = stats[1:2, :]
    for i in range(2):
        state = jnp.where(odd == (i == 0), across[0], along[0])
        states[i] = state
        values = state.reshape(cells, channels).astype(F32)
        direct[i] = slopes[i] * norm_slopes(values, mean, inverse, gain[...], shift[...])[1] * inverse
    copy.wait()
    size = inner_weight.shape[3]
    for b in range(3):
        for a in range(3):
            for e in range(3):
                at = (a * 3 + e) * size
                turned[at : at + size, b * size : (b + 1) * size] = inner_weight[a, b, e].T


def inner_kernel(
    arrived, stats, direct, hidden, edge_direct, edge_states, turned, far_out, padded, out, sems, *, devices
):
    own_rows, frame_count, width, channels = out.shape
    cells = frame_count * width
    totals = jnp.sum(arrived[...], axis=0)
    cell_total = own_rows * devices * cells * (channels // GROUPS)
    place_row = iota((8, channels), 0)
    both = jnp.where(place_row == 0, totals[0:1], totals[1:2])
    both = over_group(both, channels // GROUPS)
    first, second = both[0:1], both[1:2]
    mean = stats[0:1, :]
    inverse = stats[1:2, :]
    constant = first / cell_total * inverse
    factor = second / cell_total * inverse * inverse
    position = lax.axis_index("row")
    in_frame = mod(iota((cells, 1), 0), width)
    for i in range(own_rows + 2):
        if 0 < i < own_rows + 1:
            state, part = hidden[i - 1], direct[i - 1]
        else:
            state, part = edge_states[min(i, 1)], edge_direct[min(i, 1)]
        grad = part - constant - (state.reshape(cells, channels).astype(F32) - mean) * factor
        if i == 0:
            grad = jnp.where(position > 0, grad, 0.0)
        if i == own_rows + 1:
            grad = jnp.where(position < devices - 1, grad, 0.0)
        after = jnp.where(in_frame < width - 1, pltpu.roll(grad, cells - 1, 0), 0.0)
        prior = jnp.where(in_frame > 0, pltpu.roll(grad, 1, 0), 0.0)
        padded[i, :cells, 0:channels] = after.astype(BF16)
        padded[i, :cells, channels : 2 * channels] = grad.astype(BF16)
        padded[i, :cells, 2 * channels :] = prior.astype(BF16)
        padded[i, cells:, :] = jnp.zeros((2 * width, 3 * channels), BF16)
    results = [jnp.zeros((cells, channels), F32) for _ in range(own_rows)]
    copies = []
    for i in range(own_rows + 2):
        joined = jnp.concatenate(
            [padded[i, (2 - a) * width : (2 - a) * width + cells, :] for a in range(3)], axis=1
        )
        taps = [b for b in range(3) if 0 <= i + b - 2 < own_rows]
        for low in range(0, len(taps), 2):
            some = taps[low : low + 2]
            product = matmul(joined, turned[:, some[0] * channels : (some[-1] + 1) * channels])
            for step, b in enumerate(some):
                results[i + b - 2] = results[i + b - 2] + product[:, step * channels : (step + 1) * channels]
        if i >= 2:
            out[i - 2] = results[i - 2].reshape(frame_count, width, channels).astype(BF16)
            copies.append(pltpu.make_async_copy(out.at[i - 2], far_out.at[i - 2], sems.at[i - 2]))
            copies[-1].start()
    for copy in copies:
        copy.wait()


def per_device(
    frames,
    frame_owner,
    picks,
    patch_weight,
    patch_bias,
    norm_gain,
    head_weight,
    head_bias,
    head_out,
    hidden_state,
    group_gain,
    group_shift,
    out_weight,
    inner_weight,
):
    devices = lax.axis_size("row")
    per_frame = devices // FRAMES
    height = frames.shape[1]
    own_rows, _, frame_width, channels = hidden_state.shape
    cells = FRAMES * frame_width
    width = patch_weight.shape[1]
    turned_frames = jnp.transpose(frames, (0, 2, 1))
    bias = patch_bias.reshape(1, width)
    gain = norm_gain.reshape(1, width)
    head_bias_row = head_bias.reshape(1, width)
    head_out_row = head_out.reshape(1, width)
    state_rows = own_rows + 2
    edge = jax.ShapeDtypeStruct((1,) + hidden_state.shape[1:], BF16)
    message = (message_shape(devices), edge, edge)
    gain_row = group_gain.reshape(1, channels)
    shift_row = group_shift.reshape(1, channels)
    early = [hidden_state, gain_row, shift_row, out_weight]
    slope_outs = (
        pltpu.VMEM((own_rows, cells, channels), F32),
        pltpu.VMEM((2, cells, channels), F32),
        pltpu.VMEM((8, channels), F32),
        jax.ShapeDtypeStruct((devices, 2, channels), F32),
    )
    if per_frame == 1:
        arrays = [turned_frames, bias, gain, frame_owner, picks, head_bias_row, head_out_row]
        weights = [patch_weight, head_weight]

        def scratch(x):
            return (pltpu.SMEM if x.dtype == jnp.int32 else pltpu.VMEM)(x.shape, x.dtype)

        send, across, along, *early = pl.pallas_call(
            reward_kernel,
            out_shape=message + tuple(pltpu.VMEM(x.shape, x.dtype) for x in early),
            in_specs=[FAR] * (len(arrays) + len(early) + len(weights)),
            out_specs=[VMEM] * (3 + len(early)),
            scratch_shapes=[scratch(x) for x in arrays + weights] + [pltpu.SemaphoreType.DMA((32,))],
            compiler_params=params(0),
            name="reward",
        )(*[far(x) for x in arrays + early + weights])
    else:
        count = height // PATCH
        normed, inv_spread, partial = pl.pallas_call(
            forward_kernel,
            out_shape=(
                jax.ShapeDtypeStruct((-(-count // 8) * 8, width), F32),
                jax.ShapeDtypeStruct((-(-count // 8) * 8, LANES), F32),
                jax.ShapeDtypeStruct((1, width), F32),
            ),
            compiler_params=params(cells),
            name="reward_forward",
        )(turned_frames, bias, gain, patch_weight)
        members = [[b * per_frame + i for i in range(per_frame)] for b in range(FRAMES)]
        pooled = lax.psum(partial, "row", axis_index_groups=members) / (count * per_frame)
        send, across, along = pl.pallas_call(
            functools.partial(backward_kernel, height=height, per_frame=per_frame),
            out_shape=message,
            in_specs=[SMEM] * 2 + [VMEM] * 9,
            out_specs=[VMEM] * 3,
            compiler_params=params(cells),
            name="reward_backward",
        )(
            frame_owner,
            picks,
            hidden_state,
            gain,
            head_bias_row,
            head_out_row,
            normed,
            inv_spread,
            pooled,
            patch_weight,
            head_weight,
        )
    early = [near(x) for x in early]
    wide = pl.pallas_call(
        prepare_kernel,
        out_shape=pltpu.VMEM((3 * LANES, state_rows * channels), BF16),
        in_specs=[VMEM],
        scratch_shapes=[pltpu.VMEM((3 * LANES, state_rows * channels), F32)],
        compiler_params=params(cells),
        name="prepare",
    )(early[3])
    arrived = lax.all_to_all(send, "row", 0, 0, axis_index_groups=[first_order(devices)], tiled=True)
    direct, edge_slopes, stats, sums = pl.pallas_call(
        slope_kernel,
        out_shape=slope_outs,
        in_specs=[VMEM] * 5 + [FAR],
        scratch_shapes=[
            pltpu.VMEM((own_rows, cells, channels), F32),
            pltpu.VMEM((4 * devices, LANES), F32),
            pltpu.VMEM((cells + 2 * frame_width, LANES), BF16),
            pltpu.SMEM(frame_owner.shape, jnp.int32),
            pltpu.SemaphoreType.DMA((1,)),
        ],
        compiler_params=params(cells),
        name="slope",
    )(near(arrived), *early[:3], near(wide), far(frame_owner))
    swaps = [(2 * i, 2 * i + 1) for i in range(devices // 2)]
    across = lax.ppermute(across, "row", swaps + [(b, a) for a, b in swaps])
    swaps = [(2 * i - 1, 2 * i) for i in range(1, devices // 2)]
    along = lax.ppermute(along, "row", swaps + [(b, a) for a, b in swaps])
    summed = lax.all_to_all(sums, "row", 0, 0, axis_index_groups=[led_by(devices - 1, devices)], tiled=True)
    edge_direct, edge_states, turned = pl.pallas_call(
        late_kernel,
        out_shape=(
            pltpu.VMEM((2, cells, channels), F32),
            pltpu.VMEM((2,) + hidden_state.shape[1:], BF16),
            pltpu.VMEM((9 * channels, 3 * channels), BF16),
        ),
        in_specs=[VMEM] * 6 + [FAR],
        scratch_shapes=[pltpu.VMEM(inner_weight.shape, BF16), pltpu.SemaphoreType.DMA((1,))],
        input_output_aliases={2: 0},
        compiler_params=params(cells),
        name="late",
    )(near(across), near(along), near(edge_slopes), near(stats), *early[1:3], far(inner_weight))
    return pl.pallas_call(
        functools.partial(inner_kernel, devices=devices),
        out_shape=jax.ShapeDtypeStruct(hidden_state.shape, BF16),
        in_specs=[VMEM] * 7,
        out_specs=FAR,
        scratch_shapes=[
            pltpu.VMEM((own_rows + 2, cells + 2 * frame_width, 3 * channels), BF16),
            pltpu.VMEM(hidden_state.shape, BF16),
            pltpu.SemaphoreType.DMA((own_rows,)),
        ],
        compiler_params=params(cells),
        name="inner",
    )(
        near(summed),
        near(stats),
        near(direct),
        early[0],
        near(edge_direct),
        near(edge_states),
        near(turned),
    )


def solution(mesh):
    return jax.shard_map(
        per_device,
        mesh=mesh,
        in_specs=(
            P(None, None, ("clip", "row")),
            P("clip"),
            P("clip"),
            P(),
            P(),
            P(),
            P(),
            P(),
            P(),
            P(("clip", "row"), None, None, None),
            P(),
            P(),
            P(),
            P(),
        ),
        out_specs=P(("clip", "row"), None, None, None),
        check_vma=False,
    )
```

```python
import functools

import jax
import jax.numpy as jnp
from jax import lax
from jax.experimental import pallas as pl
from jax.experimental.pallas import tpu as pltpu
from jax.sharding import PartitionSpec as P

PATCH = 16
GROUPS = 32
FRAMES = 16
LANES = 128
SLOTS = LANES // PATCH
eps_norm = 1e-06
BF16 = jnp.bfloat16
F32 = jnp.float32

SMEM = pl.BlockSpec(memory_space=pltpu.SMEM)
VMEM = pl.BlockSpec(memory_space=pltpu.VMEM)
FAR = pl.BlockSpec(memory_space=pl.ANY)


def iota(shape, dim):
    return lax.broadcasted_iota(jnp.int32, shape, dim)


def div(values, count):
    if count & (count - 1):
        return values // count
    return values >> (count.bit_length() - 1)


def mod(values, count):
    if count & (count - 1):
        return values % count
    return values & (count - 1)


def ones_where(condition):
    return jnp.where(condition, 1.0, 0.0).astype(BF16)


def matmul(left, right):
    return jnp.dot(left, right, preferred_element_type=F32)


def matmul_t(left, right):
    return lax.dot_general(left, right, (((1,), (1,)), ((), ())), preferred_element_type=F32)


def cut_in_three(values):
    high = values.astype(BF16)
    rest = values - high.astype(F32)
    middle = rest.astype(BF16)
    low = (rest - middle.astype(F32)).astype(BF16)
    return high, middle, low


def three_pieces(row):
    place = iota((8, row.shape[1]), 0)
    stacked = jnp.zeros(place.shape, F32)
    for step, piece in enumerate(cut_in_three(row)):
        stacked = jnp.where(place == step, piece.astype(F32), stacked)
    return jnp.concatenate([stacked, jnp.zeros_like(stacked)], axis=0).astype(BF16)


def silu_slope(values):
    sigmoid = jax.nn.sigmoid(values)
    return sigmoid * (1.0 + values * (1.0 - sigmoid))


def token_rows_of(height):
    return -(-(height // PATCH) // 16) * 16


def to_tokens(pixels):
    channels, columns, height = pixels.shape
    rows = channels * columns
    token_rows = token_rows_of(height)
    flat = pixels.reshape(rows, height)
    width = channels * PATCH * columns
    lane = iota((1, width), 1)
    place = iota((rows, 1), 0)
    mine = place == div(lane, PATCH * columns) * columns + mod(lane, columns)
    in_patch = mod(div(lane, columns), PATCH)
    pixel_row = iota((height, 1), 0)
    token = iota((token_rows, 1), 0)
    tokens = jnp.zeros((token_rows, width), F32)
    for t in range(height // PATCH):
        tiled = matmul(flat, ones_where(pixel_row == in_patch + t * PATCH))
        row = jnp.sum(jnp.where(mine, tiled, 0.0), axis=0, keepdims=True)
        tokens = jnp.where(token == t, row, tokens)
    return tokens.astype(BF16)


def forward_part(tokens, count, bias, gain, load_patch):
    embedded = jnp.zeros((tokens.shape[0], bias.shape[1]), F32)
    for low, high, weight in load_patch():
        embedded = embedded + matmul(tokens[:, low:high], weight)
    rows = -(-count // 8) * 8
    embedded = embedded[:rows] + bias[...]
    centred = embedded - jnp.mean(embedded, axis=1, keepdims=True)
    inv_spread = lax.rsqrt(jnp.mean(centred * centred, axis=1, keepdims=True) + eps_norm)
    normed = centred * inv_spread
    weighted = normed * gain[...]
    inside = iota((rows, 1), 0) < count
    pooled = jnp.sum(jnp.where(inside, weighted, 0.0), axis=0, keepdims=True)
    return normed, inv_spread, pooled


def led_by(leader, devices):
    return [leader] + [d for d in reversed(range(devices)) if d != leader]


def first_order(devices):
    return led_by(devices * 13 // 16, devices)


def message_shape(devices):
    return jax.ShapeDtypeStruct((devices, 4, LANES), F32)


def write_windows(patch_grad, sums, own_rows, height, send):
    span = PATCH * PATCH
    line = jnp.concatenate(
        [
            jnp.concatenate([patch_grad[t : t + 1, k * span : (k + 1) * span] for t in range(height // PATCH)], axis=1)
            for k in range(3)
        ]
        + [jnp.zeros((1, height * PATCH), F32)],
        axis=0,
    )
    line = jnp.concatenate([jnp.zeros((4, LANES), F32), line, jnp.zeros((4, LANES), F32)], axis=1)
    used = iota((4, LANES), 1) < (own_rows + 4) * PATCH
    colour = iota((4, LANES), 0)
    for index, d in enumerate(first_order(send.shape[0])):
        start = LANES + (d * own_rows - 2) * PATCH
        window = jnp.where(used, line[:, start : start + LANES], 0.0)
        send[index] = jnp.where(colour < 3, window, sums[:4])


def channel_sums(hidden):
    values = hidden.reshape(-1, hidden.shape[-1]).astype(F32)
    return jnp.sum(values, axis=0, keepdims=True), jnp.sum(values * values, axis=0, keepdims=True)


def over_group(values, size):
    lane = iota(values.shape, 1)
    lanes = values.shape[1]
    step = 1
    while step < size:
        later = pltpu.roll(values, lanes - step, 1)
        earlier = pltpu.roll(values, step, 1)
        values = values + jnp.where((lane & step) == 0, later, earlier)
        step *= 2
    return values


def group_sums(hidden):
    channels = hidden.shape[-1]
    size = channels // GROUPS
    first, second = [
        over_group(jnp.broadcast_to(x, (8, channels)), size) for x in channel_sums(hidden)
    ]
    lane = mod(iota((8, channels), 1), size)
    return jnp.where(lane == 0, first, jnp.where(lane == 1, second, 0.0))


def there_and_back(pooled, bias, head_out, head, ready, folded):
    rows, columns = head.shape
    stacked = three_pieces(pooled)
    block = columns // len(ready)
    for index, wait in enumerate(ready):
        wait()
        part = slice(index * block, (index + 1) * block)
        result = matmul(stacked, head[:, part])
        before = result[0:1] + result[1:2] + result[2:3] + bias[:, part]
        slope = head_out[:, part] * silu_slope(before)
        for low in range(0, rows, LANES):
            product = head[low : low + LANES, part].astype(F32) * slope
            total = product[:, :LANES]
            for start in range(LANES, block, LANES):
                total = total + product[:, start : start + LANES]
            if index:
                total = total + folded[low : low + LANES, :]
            folded[low : low + LANES, :] = total
    return jnp.concatenate(
        [
            jnp.sum(folded[low : low + LANES, :].T, axis=0, keepdims=True)
            for low in range(0, rows, LANES)
        ],
        axis=1,
    )


def backward_part(
    owner, picks, gain, head_bias, head_out, normed, inv_spread, pooled, weight, head, ready, folded, slot, own_rows, height, sums, send
):
    pulled = there_and_back(pooled, head_bias, head_out, head, ready, folded)
    wanted = owner[slot]
    picked = jnp.int32(0)
    for k in range(picks.shape[0]):
        picked = picked + jnp.where(picks[k] == wanted, 1, 0)
    scaled = gain[...] * (picked.astype(F32) * pulled)
    token_grad = inv_spread * (
        scaled
        - jnp.mean(scaled, axis=1, keepdims=True)
        - normed * jnp.mean(scaled * normed, axis=1, keepdims=True)
    )
    filler = jnp.zeros((-token_grad.shape[0] % 16, token_grad.shape[1]), F32)
    token_grad = jnp.concatenate([token_grad, filler], axis=0).astype(BF16)
    patch_grad = matmul_t(token_grad, weight[...]).astype(BF16).astype(F32)
    write_windows(patch_grad, sums, own_rows, height, send)


def write_edges(position, hidden, across, along):
    last = hidden.shape[0] - 1
    even = position % 2 == 0
    across[0] = hidden[jnp.where(even, last, 0)]
    along[0] = hidden[jnp.where(even, 0, last)]


def reward_kernel(*refs):
    position = lax.axis_index("row")
    count, kept = 7, 4
    far, refs = refs[: count + kept + 2], refs[count + kept + 2 :]
    send, across, along = refs[:3]
    near = refs[3 + kept : 3 + kept + count] + refs[3 : 3 + kept] + refs[3 + kept + count : -2]
    folded, sems = refs[-2:]
    frames, bias, gain, owner, picks, head_bias, head_out, hidden, _, _, _, patch, head = near
    count += kept
    small = [pltpu.make_async_copy(far[i], near[i], sems.at[i]) for i in range(count)]
    block = 256
    used = count
    pieces = [[], []]
    for low in range(0, patch.shape[0], block):
        part = pl.ds(low, block)
        pieces[0].append(pltpu.make_async_copy(far[count].at[part], patch.at[part], sems.at[used]))
        used += 1
    for low in range(0, head.shape[1], block):
        part = pl.ds(low, block)
        pieces[1].append(
            pltpu.make_async_copy(far[count + 1].at[:, part], head.at[:, part], sems.at[used])
        )
        used += 1
    for copy in [small[0], small[7]] + pieces[0] + small[1:7] + pieces[1] + small[8:]:
        copy.start()

    def load_patch():
        for copy in pieces[0] + small[1:3]:
            copy.wait()
        yield 0, patch.shape[0], patch[...]

    height = frames.shape[2]
    patches = height // PATCH
    small[0].wait()
    small[7].wait()
    tokens = to_tokens(frames[...])
    sums = group_sums(hidden[...])
    write_edges(position, hidden, across, along)
    normed, inv_spread, pooled = forward_part(tokens, patches, bias, gain, load_patch)
    for copy in small[3:7]:
        copy.wait()

    backward_part(
        owner,
        picks,
        gain,
        head_bias,
        head_out,
        normed,
        inv_spread,
        pooled / patches,
        patch,
        head,
        [copy.wait for copy in pieces[1]],
        folded,
        position,
        hidden.shape[0],
        height,
        sums,
        send,
    )
    for copy in small[8:]:
        copy.wait()


def forward_kernel(frames, bias, gain, patch, normed, inv_spread, pooled):
    width = patch.shape[0]
    tokens = to_tokens(frames[...])
    normed[...], spread, pooled[...] = forward_part(
        tokens, frames.shape[2] // PATCH, bias, gain, lambda: [(0, width, patch[...])]
    )
    inv_spread[...] = jnp.broadcast_to(spread, inv_spread.shape)


def backward_kernel(
    owner,
    picks,
    hidden,
    gain,
    head_bias,
    head_out,
    normed,
    inv_spread,
    pooled,
    patch,
    head,
    send,
    across,
    along,
    folded,
    *,
    height,
    per_frame,
):
    position = lax.axis_index("row")
    write_edges(position, hidden, across, along)
    backward_part(
        owner,
        picks,
        gain,
        head_bias,
        head_out,
        normed[...],
        inv_spread[...][:, :1],
        pooled[...],
        patch,
        head,
        [lambda: None],
        folded,
        position // per_frame,
        hidden.shape[0],
        height,
        group_sums(hidden[...]),
        send,
    )


def params(cells):
    return pltpu.CompilerParams(vmem_limit_bytes=min(16 + cells // 64, 48) * 1024 * 1024)


def near(array):
    return pltpu.with_memory_space_constraint(array, pltpu.VMEM)


def far(array):
    return pltpu.with_memory_space_constraint(array, pltpu.HBM)


def tap_lane(j, k, e):
    return (j + 1) * PATCH + 4 * k + e


def prepare_kernel(out_weight, wide, scratch):
    amount = scratch.shape[1] // LANES
    scratch[...] = jnp.zeros_like(scratch)
    for a in range(3):
        for e in range(3):
            for b in range(3):
                piece = out_weight[a, b, e].astype(F32)
                for i in range(amount):
                    for k in range(3):
                        at = a * LANES + tap_lane(i - b + 2, k, e)
                        scratch[at : at + 1, i * LANES : (i + 1) * LANES] = piece[k : k + 1]
    wide[...] = scratch[...].astype(BF16)


def norm_constants(totals, cell_total):
    channels = totals.shape[1]
    size = channels // GROUPS
    totals = jnp.broadcast_to(totals, (8, channels))
    lane = mod(iota((8, channels), 1), size)
    first, second = [over_group(jnp.where(lane == i, totals, 0.0), size)[:1] for i in range(2)]
    mean = first / cell_total
    return mean, lax.rsqrt(second / cell_total - mean * mean + eps_norm)


def norm_slopes(state, mean, inverse, gain, shift):
    normed = (state - mean) * inverse
    return normed, silu_slope(normed * gain + shift) * gain


def slope_kernel(
    arrived,
    hidden,
    gain,
    shift,
    wide,
    far_owner,
    direct,
    edge_slopes,
    stats,
    sums,
    slopes_own,
    received,
    taps,
    owner,
    sem,
):
    copy = pltpu.make_async_copy(far_owner, owner, sem.at[0])
    copy.start()
    devices, message_rows, _ = arrived.shape
    own_rows, frame_count, width, channels = hidden.shape
    cells = frame_count * width
    per_frame = devices // frame_count
    got = arrived[...].reshape(received.shape)
    kind = mod(iota((got.shape[0], 1), 0), message_rows)
    totals = jnp.sum(jnp.where(kind == 3, got, 0.0), axis=0, keepdims=True)
    mean, inverse = norm_constants(totals, own_rows * devices * cells * (channels // GROUPS))
    for i in range(own_rows):
        state = hidden[i].reshape(cells, channels).astype(F32)
        slopes_own[i] = norm_slopes(state, mean, inverse, gain[...], shift[...])[1] * inverse

    if per_frame == 1:
        lane = iota((1, LANES), 1)
        entry = iota((LANES, 1), 0)
        turned = ones_where(entry - mod(entry, PATCH) + PATCH - 1 - mod(entry, PATCH) == lane)
        received[...] = matmul(jnp.where(kind < 3, got, 0.0).astype(BF16), turned)
        lane = mod(iota((PATCH, LANES), 1), PATCH)
        column = iota((PATCH, LANES), 0)
        marks = []
        for k in range(3):
            e = lane - 4 * k
            wanted = column - e + 1
            marks.append((e >= 0) & (e < 3) & (wanted >= 0) & (wanted < PATCH))
        copy.wait()
        for d in range(devices):
            row = first_order(devices)[d]
            block = jnp.zeros((PATCH, LANES), F32)
            for k in range(3):
                line = jnp.broadcast_to(received[d * message_rows + k : d * message_rows + k + 1, :], (PATCH, LANES))
                line = pltpu.roll(line, 4 * k + 2, 1, stride=1, stride_axis=0)
                block = jnp.where(marks[k], line, block)
            start = pl.multiple_of(owner[row] * PATCH, PATCH)
            taps[pl.ds(start, PATCH), :] = block.astype(BF16)
    else:
        copy.wait()
        received[...] = got
        lines = [received[pl.ds(k, devices, stride=message_rows), :] for k in range(3)]
        lines = jnp.concatenate(lines, axis=1).astype(BF16)
        place = iota((1, devices), 1)
        source = jnp.zeros_like(place)
        for index, d in enumerate(first_order(devices)):
            source = jnp.where(place == index, d, source)
        home = jnp.zeros((1, devices), jnp.int32)
        for b in range(frame_count):
            home = jnp.where(div(source, per_frame) == b, owner[b] * per_frame, home)
        home = home + mod(source, per_frame)
        cell = iota((cells, 1), 0)
        column = mod(cell, width)
        lane = mod(iota((1, 3 * LANES), 1), PATCH)
        entry = iota((3 * LANES, 1), 0)
        window_row = div(mod(entry, LANES), PATCH)
        found = jnp.zeros((cells, LANES), F32)
        for e in range(3):
            wanted = column - e + 1
            strip = div(cell, width) * per_frame + div(wanted, PATCH)
            placed = matmul(ones_where(home == strip), lines)
            inside = jnp.where((wanted >= 0) & (wanted < width), mod(wanted, PATCH), -1)
            kept = jnp.where(lane == inside, placed, 0.0).astype(BF16)
            target = jnp.where(
                window_row < own_rows + 4, tap_lane(window_row, div(entry, LANES), e), -1
            )
            found = found + matmul(kept, ones_where(target == iota((1, LANES), 1)))
        taps[:cells, :] = found.astype(BF16)
    taps[cells:, :] = jnp.zeros((2 * width, LANES), BF16)
    steps = [taps[(2 - a) * width : (2 - a) * width + cells, :] for a in range(3)]
    result = matmul(jnp.concatenate(steps, axis=1), wide[...])

    first = jnp.zeros((1, channels), F32)
    second = jnp.zeros((1, channels), F32)
    for i in range(own_rows):
        state = hidden[i].reshape(cells, channels).astype(F32)
        part = result[:, (i + 1) * channels : (i + 2) * channels] * slopes_own[i]
        direct[i] = part
        first = first + jnp.sum(part, axis=0, keepdims=True)
        second = second + jnp.sum(part * (state - mean), axis=0, keepdims=True)
    first = first / inverse
    edge_slopes[0] = result[:, :channels]
    edge_slopes[1] = result[:, (own_rows + 1) * channels :]
    stats[0:1, :] = mean
    stats[1:2, :] = inverse
    both = jnp.where(iota((2, channels), 0) == 0, first, second)
    sums[...] = jnp.broadcast_to(both[None], sums.shape)


def late_kernel(
    across, along, slopes, stats, gain, shift, far_weight, direct, states, turned, inner_weight, sem
):
    copy = pltpu.make_async_copy(far_weight, inner_weight, sem.at[0])
    copy.start()
    cells, channels = slopes.shape[1:]
    odd = lax.axis_index("row") % 2 == 1
    mean = stats[0:1, :]
    inverse = stats[1:2, :]
    for i in range(2):
        state = jnp.where(odd == (i == 0), across[0], along[0])
        states[i] = state
        values = state.reshape(cells, channels).astype(F32)
        direct[i] = slopes[i] * norm_slopes(values, mean, inverse, gain[...], shift[...])[1] * inverse
    copy.wait()
    size = inner_weight.shape[3]
    for b in range(3):
        for a in range(3):
            for e in range(3):
                at = (a * 3 + e) * size
                turned[at : at + size, b * size : (b + 1) * size] = inner_weight[a, b, e].T


def inner_kernel(
    arrived, stats, direct, hidden, edge_direct, edge_states, turned, far_out, padded, out, sems, *, devices
):
    own_rows, frame_count, width, channels = out.shape
    cells = frame_count * width
    totals = jnp.sum(arrived[...], axis=0)
    cell_total = own_rows * devices * cells * (channels // GROUPS)
    place_row = iota((8, channels), 0)
    both = jnp.where(place_row == 0, totals[0:1], totals[1:2])
    both = over_group(both, channels // GROUPS)
    first, second = both[0:1], both[1:2]
    mean = stats[0:1, :]
    inverse = stats[1:2, :]
    constant = first / cell_total * inverse
    factor = second / cell_total * inverse * inverse
    position = lax.axis_index("row")
    in_frame = mod(iota((cells, 1), 0), width)
    for i in range(own_rows + 2):
        if 0 < i < own_rows + 1:
            state, part = hidden[i - 1], direct[i - 1]
        else:
            state, part = edge_states[min(i, 1)], edge_direct[min(i, 1)]
        grad = part - constant - (state.reshape(cells, channels).astype(F32) - mean) * factor
        if i == 0:
            grad = jnp.where(position > 0, grad, 0.0)
        if i == own_rows + 1:
            grad = jnp.where(position < devices - 1, grad, 0.0)
        after = jnp.where(in_frame < width - 1, pltpu.roll(grad, cells - 1, 0), 0.0)
        prior = jnp.where(in_frame > 0, pltpu.roll(grad, 1, 0), 0.0)
        padded[i, :cells, 0:channels] = after.astype(BF16)
        padded[i, :cells, channels : 2 * channels] = grad.astype(BF16)
        padded[i, :cells, 2 * channels :] = prior.astype(BF16)
        padded[i, cells:, :] = jnp.zeros((2 * width, 3 * channels), BF16)
    results = [jnp.zeros((cells, channels), F32) for _ in range(own_rows)]
    copies = []
    for i in range(own_rows + 2):
        joined = jnp.concatenate(
            [padded[i, (2 - a) * width : (2 - a) * width + cells, :] for a in range(3)], axis=1
        )
        taps = [b for b in range(3) if 0 <= i + b - 2 < own_rows]
        for low in range(0, len(taps), 2):
            some = taps[low : low + 2]
            product = matmul(joined, turned[:, some[0] * channels : (some[-1] + 1) * channels])
            for step, b in enumerate(some):
                results[i + b - 2] = results[i + b - 2] + product[:, step * channels : (step + 1) * channels]
        if i >= 2:
            out[i - 2] = results[i - 2].reshape(frame_count, width, channels).astype(BF16)
            copies.append(pltpu.make_async_copy(out.at[i - 2], far_out.at[i - 2], sems.at[i - 2]))
            copies[-1].start()
    for copy in copies:
        copy.wait()


def per_device(
    frames,
    frame_owner,
    picks,
    patch_weight,
    patch_bias,
    norm_gain,
    head_weight,
    head_bias,
    head_out,
    hidden_state,
    group_gain,
    group_shift,
    out_weight,
    inner_weight,
):
    devices = lax.axis_size("row")
    per_frame = devices // FRAMES
    height = frames.shape[1]
    own_rows, _, frame_width, channels = hidden_state.shape
    cells = FRAMES * frame_width
    width = patch_weight.shape[1]
    turned_frames = jnp.transpose(frames, (0, 2, 1))
    bias = patch_bias.reshape(1, width)
    gain = norm_gain.reshape(1, width)
    head_bias_row = head_bias.reshape(1, width)
    head_out_row = head_out.reshape(1, width)
    state_rows = own_rows + 2
    edge = jax.ShapeDtypeStruct((1,) + hidden_state.shape[1:], BF16)
    message = (message_shape(devices), edge, edge)
    gain_row = group_gain.reshape(1, channels)
    shift_row = group_shift.reshape(1, channels)
    early = [hidden_state, gain_row, shift_row, out_weight]
    slope_outs = (
        pltpu.VMEM((own_rows, cells, channels), F32),
        pltpu.VMEM((2, cells, channels), F32),
        pltpu.VMEM((8, channels), F32),
        jax.ShapeDtypeStruct((devices, 2, channels), F32),
    )
    if per_frame == 1:
        arrays = [turned_frames, bias, gain, frame_owner, picks, head_bias_row, head_out_row]
        weights = [patch_weight, head_weight]

        def scratch(x):
            return (pltpu.SMEM if x.dtype == jnp.int32 else pltpu.VMEM)(x.shape, x.dtype)

        send, across, along, *early = pl.pallas_call(
            reward_kernel,
            out_shape=message + tuple(pltpu.VMEM(x.shape, x.dtype) for x in early),
            in_specs=[FAR] * (len(arrays) + len(early) + len(weights)),
            out_specs=[VMEM] * (3 + len(early)),
            scratch_shapes=[scratch(x) for x in arrays + weights]
            + [pltpu.VMEM((head_weight.shape[0], LANES), F32), pltpu.SemaphoreType.DMA((32,))],
            compiler_params=params(0),
            name="reward",
        )(*[far(x) for x in arrays + early + weights])
    else:
        count = height // PATCH
        normed, inv_spread, partial = pl.pallas_call(
            forward_kernel,
            out_shape=(
                jax.ShapeDtypeStruct((-(-count // 8) * 8, width), F32),
                jax.ShapeDtypeStruct((-(-count // 8) * 8, LANES), F32),
                jax.ShapeDtypeStruct((1, width), F32),
            ),
            compiler_params=params(cells),
            name="reward_forward",
        )(turned_frames, bias, gain, patch_weight)
        members = [[b * per_frame + i for i in range(per_frame)] for b in range(FRAMES)]
        pooled = lax.psum(partial, "row", axis_index_groups=members) / (count * per_frame)
        send, across, along = pl.pallas_call(
            functools.partial(backward_kernel, height=height, per_frame=per_frame),
            out_shape=message,
            in_specs=[SMEM] * 2 + [VMEM] * 9,
            out_specs=[VMEM] * 3,
            scratch_shapes=[pltpu.VMEM((head_weight.shape[0], LANES), F32)],
            compiler_params=params(cells),
            name="reward_backward",
        )(
            frame_owner,
            picks,
            hidden_state,
            gain,
            head_bias_row,
            head_out_row,
            normed,
            inv_spread,
            pooled,
            patch_weight,
            head_weight,
        )
    early = [near(x) for x in early]
    wide = pl.pallas_call(
        prepare_kernel,
        out_shape=pltpu.VMEM((3 * LANES, state_rows * channels), BF16),
        in_specs=[VMEM],
        scratch_shapes=[pltpu.VMEM((3 * LANES, state_rows * channels), F32)],
        compiler_params=params(cells),
        name="prepare",
    )(early[3])
    arrived = lax.all_to_all(send, "row", 0, 0, axis_index_groups=[first_order(devices)], tiled=True)
    direct, edge_slopes, stats, sums = pl.pallas_call(
        slope_kernel,
        out_shape=slope_outs,
        in_specs=[VMEM] * 5 + [FAR],
        scratch_shapes=[
            pltpu.VMEM((own_rows, cells, channels), F32),
            pltpu.VMEM((4 * devices, LANES), F32),
            pltpu.VMEM((cells + 2 * frame_width, LANES), BF16),
            pltpu.SMEM(frame_owner.shape, jnp.int32),
            pltpu.SemaphoreType.DMA((1,)),
        ],
        compiler_params=params(cells),
        name="slope",
    )(near(arrived), *early[:3], near(wide), far(frame_owner))
    swaps = [(2 * i, 2 * i + 1) for i in range(devices // 2)]
    across = lax.ppermute(across, "row", swaps + [(b, a) for a, b in swaps])
    swaps = [(2 * i - 1, 2 * i) for i in range(1, devices // 2)]
    along = lax.ppermute(along, "row", swaps + [(b, a) for a, b in swaps])
    summed = lax.all_to_all(sums, "row", 0, 0, axis_index_groups=[led_by(devices - 1, devices)], tiled=True)
    edge_direct, edge_states, turned = pl.pallas_call(
        late_kernel,
        out_shape=(
            pltpu.VMEM((2, cells, channels), F32),
            pltpu.VMEM((2,) + hidden_state.shape[1:], BF16),
            pltpu.VMEM((9 * channels, 3 * channels), BF16),
        ),
        in_specs=[VMEM] * 6 + [FAR],
        scratch_shapes=[pltpu.VMEM(inner_weight.shape, BF16), pltpu.SemaphoreType.DMA((1,))],
        input_output_aliases={2: 0},
        compiler_params=params(cells),
        name="late",
    )(near(across), near(along), near(edge_slopes), near(stats), *early[1:3], far(inner_weight))
    return pl.pallas_call(
        functools.partial(inner_kernel, devices=devices),
        out_shape=jax.ShapeDtypeStruct(hidden_state.shape, BF16),
        in_specs=[VMEM] * 7,
        out_specs=FAR,
        scratch_shapes=[
            pltpu.VMEM((own_rows + 2, cells + 2 * frame_width, 3 * channels), BF16),
            pltpu.VMEM(hidden_state.shape, BF16),
            pltpu.SemaphoreType.DMA((own_rows,)),
        ],
        compiler_params=params(cells),
        name="inner",
    )(
        near(summed),
        near(stats),
        near(direct),
        early[0],
        near(edge_direct),
        near(edge_states),
        near(turned),
    )


def solution(mesh):
    return jax.shard_map(
        per_device,
        mesh=mesh,
        in_specs=(
            P(None, None, ("clip", "row")),
            P("clip"),
            P("clip"),
            P(),
            P(),
            P(),
            P(),
            P(),
            P(),
            P(("clip", "row"), None, None, None),
            P(),
            P(),
            P(),
            P(),
        ),
        out_specs=P(("clip", "row"), None, None, None),
        check_vma=False,
    )
```

```python
import functools

import jax
import jax.numpy as jnp
from jax import lax
from jax.experimental import pallas as pl
from jax.experimental.pallas import tpu as pltpu
from jax.sharding import PartitionSpec as P

PATCH = 16
GROUPS = 32
FRAMES = 16
LANES = 128
SLOTS = LANES // PATCH
eps_norm = 1e-06
BF16 = jnp.bfloat16
F32 = jnp.float32

SMEM = pl.BlockSpec(memory_space=pltpu.SMEM)
VMEM = pl.BlockSpec(memory_space=pltpu.VMEM)
FAR = pl.BlockSpec(memory_space=pl.ANY)


def iota(shape, dim):
    return lax.broadcasted_iota(jnp.int32, shape, dim)


def div(values, count):
    if count & (count - 1):
        return values // count
    return values >> (count.bit_length() - 1)


def mod(values, count):
    if count & (count - 1):
        return values % count
    return values & (count - 1)


def ones_where(condition):
    return jnp.where(condition, 1.0, 0.0).astype(BF16)


def matmul(left, right):
    return jnp.dot(left, right, preferred_element_type=F32)


def matmul_t(left, right):
    return lax.dot_general(left, right, (((1,), (1,)), ((), ())), preferred_element_type=F32)


def cut_in_three(values):
    high = values.astype(BF16)
    rest = values - high.astype(F32)
    middle = rest.astype(BF16)
    low = (rest - middle.astype(F32)).astype(BF16)
    return high, middle, low


def exact_rows(rows, product):
    place = iota((8, rows[0].shape[1]), 0)
    stacked = jnp.zeros(place.shape, F32)
    for index, row in enumerate(rows):
        for step, piece in enumerate(cut_in_three(row)):
            stacked = jnp.where(place == 3 * index + step, piece.astype(F32), stacked)
    result = product(jnp.concatenate([stacked, jnp.zeros_like(stacked)], axis=0).astype(BF16))
    return [
        result[3 * i : 3 * i + 1] + result[3 * i + 1 : 3 * i + 2] + result[3 * i + 2 : 3 * i + 3]
        for i in range(len(rows))
    ]


def silu_slope(values):
    sigmoid = jax.nn.sigmoid(values)
    return sigmoid * (1.0 + values * (1.0 - sigmoid))


def token_rows_of(height):
    return -(-(height // PATCH) // 16) * 16


def to_tokens(pixels):
    channels, columns, height = pixels.shape
    rows = channels * columns
    token_rows = token_rows_of(height)
    flat = pixels.reshape(rows, height)
    width = channels * PATCH * columns
    lane = iota((1, width), 1)
    place = iota((rows, 1), 0)
    mine = place == div(lane, PATCH * columns) * columns + mod(lane, columns)
    in_patch = mod(div(lane, columns), PATCH)
    pixel_row = iota((height, 1), 0)
    token = iota((token_rows, 1), 0)
    tokens = jnp.zeros((token_rows, width), F32)
    for t in range(height // PATCH):
        tiled = matmul(flat, ones_where(pixel_row == in_patch + t * PATCH))
        row = jnp.sum(jnp.where(mine, tiled, 0.0), axis=0, keepdims=True)
        tokens = jnp.where(token == t, row, tokens)
    return tokens.astype(BF16)


def forward_part(tokens, count, bias, gain, load_patch):
    embedded = jnp.zeros((tokens.shape[0], bias.shape[1]), F32)
    for low, high, weight in load_patch():
        embedded = embedded + matmul(tokens[:, low:high], weight)
    rows = -(-count // 8) * 8
    embedded = embedded[:rows] + bias[...]
    centred = embedded - jnp.mean(embedded, axis=1, keepdims=True)
    inv_spread = lax.rsqrt(jnp.mean(centred * centred, axis=1, keepdims=True) + eps_norm)
    normed = centred * inv_spread
    weighted = normed * gain[...]
    inside = iota((rows, 1), 0) < count
    pooled = jnp.sum(jnp.where(inside, weighted, 0.0), axis=0, keepdims=True)
    return normed, inv_spread, pooled


def led_by(leader, devices):
    return [leader] + [d for d in reversed(range(devices)) if d != leader]


def first_order(devices):
    return led_by(devices * 13 // 16, devices)


def message_shape(devices):
    return jax.ShapeDtypeStruct((devices, 4, LANES), F32)


def write_windows(patch_grad, sums, own_rows, height, send):
    span = PATCH * PATCH
    line = jnp.concatenate(
        [
            jnp.concatenate([patch_grad[t : t + 1, k * span : (k + 1) * span] for t in range(height // PATCH)], axis=1)
            for k in range(3)
        ]
        + [jnp.zeros((1, height * PATCH), F32)],
        axis=0,
    )
    line = jnp.concatenate([jnp.zeros((4, LANES), F32), line, jnp.zeros((4, LANES), F32)], axis=1)
    used = iota((4, LANES), 1) < (own_rows + 4) * PATCH
    colour = iota((4, LANES), 0)
    for index, d in enumerate(first_order(send.shape[0])):
        start = LANES + (d * own_rows - 2) * PATCH
        window = jnp.where(used, line[:, start : start + LANES], 0.0)
        send[index] = jnp.where(colour < 3, window, sums[:4])


def channel_sums(hidden):
    values = hidden.reshape(-1, hidden.shape[-1]).astype(F32)
    return jnp.sum(values, axis=0, keepdims=True), jnp.sum(values * values, axis=0, keepdims=True)


def over_group(values, size):
    lane = iota(values.shape, 1)
    lanes = values.shape[1]
    step = 1
    while step < size:
        later = pltpu.roll(values, lanes - step, 1)
        earlier = pltpu.roll(values, step, 1)
        values = values + jnp.where((lane & step) == 0, later, earlier)
        step *= 2
    return values


def group_sums(hidden):
    channels = hidden.shape[-1]
    size = channels // GROUPS
    first, second = [
        over_group(jnp.broadcast_to(x, (8, channels)), size) for x in channel_sums(hidden)
    ]
    lane = mod(iota((8, channels), 1), size)
    return jnp.where(lane == 0, first, jnp.where(lane == 1, second, 0.0))


def pull_back(row, weight):
    parts = []
    for low in range(0, weight.shape[0], LANES):
        product = weight[low : low + LANES, :].astype(F32) * row
        folded = product[:, :LANES]
        for start in range(LANES, weight.shape[1], LANES):
            folded = folded + product[:, start : start + LANES]
        parts.append(jnp.sum(folded.T, axis=0, keepdims=True))
    return jnp.concatenate(parts, axis=1)


def backward_part(
    owner, picks, gain, head_bias, head_out, normed, inv_spread, pooled, weight, head, through_head, slot, own_rows, height, sums, send
):
    (before,) = exact_rows([pooled], through_head)
    slope = head_out[...] * silu_slope(before + head_bias[...])
    pulled = pull_back(slope, head)
    wanted = owner[slot]
    picked = jnp.int32(0)
    for k in range(picks.shape[0]):
        picked = picked + jnp.where(picks[k] == wanted, 1, 0)
    scaled = gain[...] * (picked.astype(F32) * pulled)
    token_grad = inv_spread * (
        scaled
        - jnp.mean(scaled, axis=1, keepdims=True)
        - normed * jnp.mean(scaled * normed, axis=1, keepdims=True)
    )
    filler = jnp.zeros((-token_grad.shape[0] % 16, token_grad.shape[1]), F32)
    token_grad = jnp.concatenate([token_grad, filler], axis=0).astype(BF16)
    patch_grad = matmul_t(token_grad, weight[...]).astype(BF16).astype(F32)
    write_windows(patch_grad, sums, own_rows, height, send)


def write_edges(position, hidden, across, along):
    last = hidden.shape[0] - 1
    even = position % 2 == 0
    across[0] = hidden[jnp.where(even, last, 0)]
    along[0] = hidden[jnp.where(even, 0, last)]


def reward_kernel(*refs):
    position = lax.axis_index("row")
    count, kept = 7, 4
    far, refs = refs[: count + kept + 2], refs[count + kept + 2 :]
    send, across, along = refs[:3]
    near = refs[3 + kept : 3 + kept + count] + refs[3 : 3 + kept] + refs[3 + kept + count : -1]
    sems = refs[-1]
    frames, bias, gain, owner, picks, head_bias, head_out, hidden, _, _, _, patch, head = near
    count += kept
    depths = (256, 256)
    small = [pltpu.make_async_copy(far[i], near[i], sems.at[i]) for i in range(count)]
    pieces = []
    used = count
    for index, rows in enumerate(depths):
        source, target = far[count + index], near[count + index]
        parts = []
        for low in range(0, target.shape[0], rows):
            part = pl.ds(low, rows)
            parts.append(pltpu.make_async_copy(source.at[part], target.at[part], sems.at[used]))
            used += 1
        pieces.append(parts)
    for copy in [small[0], small[7]] + pieces[0] + small[1:7] + pieces[1] + small[8:]:
        copy.start()

    def load_patch():
        for copy in pieces[0] + small[1:3]:
            copy.wait()
        yield 0, patch.shape[0], patch[...]

    height = frames.shape[2]
    patches = height // PATCH
    small[0].wait()
    small[7].wait()
    tokens = to_tokens(frames[...])
    sums = group_sums(hidden[...])
    write_edges(position, hidden, across, along)
    normed, inv_spread, pooled = forward_part(tokens, patches, bias, gain, load_patch)
    for copy in small[3:7]:
        copy.wait()

    def through_head(rows):
        total = jnp.zeros((rows.shape[0], head.shape[1]), F32)
        for index, low in enumerate(range(0, head.shape[0], depths[1])):
            pieces[1][index].wait()
            total = total + matmul(rows[:, low : low + depths[1]], head[low : low + depths[1], :])
        return total

    backward_part(
        owner,
        picks,
        gain,
        head_bias,
        head_out,
        normed,
        inv_spread,
        pooled / patches,
        patch,
        head,
        through_head,
        position,
        hidden.shape[0],
        height,
        sums,
        send,
    )
    for copy in small[8:]:
        copy.wait()


def forward_kernel(frames, bias, gain, patch, normed, inv_spread, pooled):
    width = patch.shape[0]
    tokens = to_tokens(frames[...])
    normed[...], spread, pooled[...] = forward_part(
        tokens, frames.shape[2] // PATCH, bias, gain, lambda: [(0, width, patch[...])]
    )
    inv_spread[...] = jnp.broadcast_to(spread, inv_spread.shape)


def backward_kernel(
    owner,
    picks,
    hidden,
    gain,
    head_bias,
    head_out,
    normed,
    inv_spread,
    pooled,
    patch,
    head,
    send,
    across,
    along,
    *,
    height,
    per_frame,
):
    position = lax.axis_index("row")
    write_edges(position, hidden, across, along)
    backward_part(
        owner,
        picks,
        gain,
        head_bias,
        head_out,
        normed[...],
        inv_spread[...][:, :1],
        pooled[...],
        patch,
        head,
        lambda rows: matmul(rows, head[...]),
        position // per_frame,
        hidden.shape[0],
        height,
        group_sums(hidden[...]),
        send,
    )


def params(cells):
    return pltpu.CompilerParams(vmem_limit_bytes=min(16 + cells // 64, 48) * 1024 * 1024)


def near(array):
    return pltpu.with_memory_space_constraint(array, pltpu.VMEM)


def far(array):
    return pltpu.with_memory_space_constraint(array, pltpu.HBM)


def tap_lane(j, k, e):
    return (j + 1) * PATCH + 4 * k + e


def prepare_kernel(out_weight, wide, scratch):
    amount = scratch.shape[1] // LANES
    scratch[...] = jnp.zeros_like(scratch)
    for a in range(3):
        for e in range(3):
            for b in range(3):
                piece = out_weight[a, b, e].astype(F32)
                for i in range(amount):
                    for k in range(3):
                        at = a * LANES + tap_lane(i - b + 2, k, e)
                        scratch[at : at + 1, i * LANES : (i + 1) * LANES] = piece[k : k + 1]
    wide[...] = scratch[...].astype(BF16)


def norm_constants(totals, cell_total):
    channels = totals.shape[1]
    size = channels // GROUPS
    totals = jnp.broadcast_to(totals, (8, channels))
    lane = mod(iota((8, channels), 1), size)
    first, second = [over_group(jnp.where(lane == i, totals, 0.0), size)[:1] for i in range(2)]
    mean = first / cell_total
    return mean, lax.rsqrt(second / cell_total - mean * mean + eps_norm)


def norm_slopes(state, mean, inverse, gain, shift):
    normed = (state - mean) * inverse
    return normed, silu_slope(normed * gain + shift) * gain


def slope_kernel(
    arrived,
    hidden,
    gain,
    shift,
    wide,
    far_owner,
    direct,
    edge_slopes,
    stats,
    sums,
    slopes_own,
    received,
    taps,
    owner,
    sem,
):
    copy = pltpu.make_async_copy(far_owner, owner, sem.at[0])
    copy.start()
    devices, message_rows, _ = arrived.shape
    own_rows, frame_count, width, channels = hidden.shape
    cells = frame_count * width
    per_frame = devices // frame_count
    got = arrived[...].reshape(received.shape)
    kind = mod(iota((got.shape[0], 1), 0), message_rows)
    totals = jnp.sum(jnp.where(kind == 3, got, 0.0), axis=0, keepdims=True)
    mean, inverse = norm_constants(totals, own_rows * devices * cells * (channels // GROUPS))
    for i in range(own_rows):
        state = hidden[i].reshape(cells, channels).astype(F32)
        slopes_own[i] = norm_slopes(state, mean, inverse, gain[...], shift[...])[1] * inverse

    if per_frame == 1:
        lane = iota((1, LANES), 1)
        entry = iota((LANES, 1), 0)
        turned = ones_where(entry - mod(entry, PATCH) + PATCH - 1 - mod(entry, PATCH) == lane)
        received[...] = matmul(jnp.where(kind < 3, got, 0.0).astype(BF16), turned)
        lane = mod(iota((PATCH, LANES), 1), PATCH)
        column = iota((PATCH, LANES), 0)
        marks = []
        for k in range(3):
            e = lane - 4 * k
            wanted = column - e + 1
            marks.append((e >= 0) & (e < 3) & (wanted >= 0) & (wanted < PATCH))
        copy.wait()
        for d in range(devices):
            row = first_order(devices)[d]
            block = jnp.zeros((PATCH, LANES), F32)
            for k in range(3):
                line = jnp.broadcast_to(received[d * message_rows + k : d * message_rows + k + 1, :], (PATCH, LANES))
                line = pltpu.roll(line, 4 * k + 2, 1, stride=1, stride_axis=0)
                block = jnp.where(marks[k], line, block)
            start = pl.multiple_of(owner[row] * PATCH, PATCH)
            taps[pl.ds(start, PATCH), :] = block.astype(BF16)
    else:
        copy.wait()
        received[...] = got
        lines = [received[pl.ds(k, devices, stride=message_rows), :] for k in range(3)]
        lines = jnp.concatenate(lines, axis=1).astype(BF16)
        place = iota((1, devices), 1)
        source = jnp.zeros_like(place)
        for index, d in enumerate(first_order(devices)):
            source = jnp.where(place == index, d, source)
        home = jnp.zeros((1, devices), jnp.int32)
        for b in range(frame_count):
            home = jnp.where(div(source, per_frame) == b, owner[b] * per_frame, home)
        home = home + mod(source, per_frame)
        cell = iota((cells, 1), 0)
        column = mod(cell, width)
        lane = mod(iota((1, 3 * LANES), 1), PATCH)
        entry = iota((3 * LANES, 1), 0)
        window_row = div(mod(entry, LANES), PATCH)
        found = jnp.zeros((cells, LANES), F32)
        for e in range(3):
            wanted = column - e + 1
            strip = div(cell, width) * per_frame + div(wanted, PATCH)
            placed = matmul(ones_where(home == strip), lines)
            inside = jnp.where((wanted >= 0) & (wanted < width), mod(wanted, PATCH), -1)
            kept = jnp.where(lane == inside, placed, 0.0).astype(BF16)
            target = jnp.where(
                window_row < own_rows + 4, tap_lane(window_row, div(entry, LANES), e), -1
            )
            found = found + matmul(kept, ones_where(target == iota((1, LANES), 1)))
        taps[:cells, :] = found.astype(BF16)
    taps[cells:, :] = jnp.zeros((2 * width, LANES), BF16)
    steps = [taps[(2 - a) * width : (2 - a) * width + cells, :] for a in range(3)]
    result = matmul(jnp.concatenate(steps, axis=1), wide[...])

    first = jnp.zeros((1, channels), F32)
    second = jnp.zeros((1, channels), F32)
    for i in range(own_rows):
        state = hidden[i].reshape(cells, channels).astype(F32)
        part = result[:, (i + 1) * channels : (i + 2) * channels] * slopes_own[i]
        direct[i] = part
        first = first + jnp.sum(part, axis=0, keepdims=True)
        second = second + jnp.sum(part * (state - mean), axis=0, keepdims=True)
    first = first / inverse
    edge_slopes[0] = result[:, :channels]
    edge_slopes[1] = result[:, (own_rows + 1) * channels :]
    stats[0:1, :] = mean
    stats[1:2, :] = inverse
    both = jnp.where(iota((2, channels), 0) == 0, first, second)
    sums[...] = jnp.broadcast_to(both[None], sums.shape)


def late_kernel(
    across, along, slopes, stats, gain, shift, far_weight, direct, states, turned, inner_weight, sem
):
    copy = pltpu.make_async_copy(far_weight, inner_weight, sem.at[0])
    copy.start()
    cells, channels = slopes.shape[1:]
    odd = lax.axis_index("row") % 2 == 1
    mean = stats[0:1, :]
    inverse = stats[1:2, :]
    for i in range(2):
        state = jnp.where(odd == (i == 0), across[0], along[0])
        states[i] = state
        values = state.reshape(cells, channels).astype(F32)
        direct[i] = slopes[i] * norm_slopes(values, mean, inverse, gain[...], shift[...])[1] * inverse
    copy.wait()
    size = inner_weight.shape[3]
    for b in range(3):
        for a in range(3):
            for e in range(3):
                at = (a * 3 + e) * size
                turned[at : at + size, b * size : (b + 1) * size] = inner_weight[a, b, e].T


def inner_kernel(
    arrived, stats, direct, hidden, edge_direct, edge_states, turned, far_out, out, sems, *, devices
):
    own_rows, frame_count, width, channels = out.shape
    cells = frame_count * width
    totals = jnp.sum(arrived[...], axis=0)
    cell_total = own_rows * devices * cells * (channels // GROUPS)
    place_row = iota((8, channels), 0)
    both = jnp.where(place_row == 0, totals[0:1], totals[1:2])
    both = over_group(both, channels // GROUPS)
    first, second = both[0:1], both[1:2]
    mean = stats[0:1, :]
    inverse = stats[1:2, :]
    constant = first / cell_total * inverse
    factor = second / cell_total * inverse * inverse
    position = lax.axis_index("row")
    in_frame = mod(iota((cells, 1), 0), width)
    results = [jnp.zeros((cells, channels), F32) for _ in range(own_rows)]
    copies = []
    for i in range(own_rows + 2):
        if 0 < i < own_rows + 1:
            state, part = hidden[i - 1], direct[i - 1]
        else:
            state, part = edge_states[min(i, 1)], edge_direct[min(i, 1)]
        grad = part - constant - (state.reshape(cells, channels).astype(F32) - mean) * factor
        if i == 0:
            grad = jnp.where(position > 0, grad, 0.0)
        if i == own_rows + 1:
            grad = jnp.where(position < devices - 1, grad, 0.0)
        after = jnp.where(in_frame < width - 1, pltpu.roll(grad, cells - 1, 0), 0.0)
        prior = jnp.where(in_frame > 0, pltpu.roll(grad, 1, 0), 0.0)
        taps = jnp.concatenate([after.astype(BF16), grad.astype(BF16), prior.astype(BF16)], axis=1)
        later = []
        for a in range(3):
            skip = (2 - a) * width
            filler = jnp.zeros((skip, taps.shape[1]), BF16)
            later.append(jnp.concatenate([taps[skip:], filler], axis=0) if skip else taps)
        joined = jnp.concatenate(later, axis=1)
        rows = [b for b in range(3) if 0 <= i + b - 2 < own_rows]
        for low in range(0, len(rows), 2):
            some = rows[low : low + 2]
            product = matmul(joined, turned[:, some[0] * channels : (some[-1] + 1) * channels])
            for step, b in enumerate(some):
                results[i + b - 2] = results[i + b - 2] + product[:, step * channels : (step + 1) * channels]
        if i >= 2:
            out[i - 2] = results[i - 2].reshape(frame_count, width, channels).astype(BF16)
            copies.append(pltpu.make_async_copy(out.at[i - 2], far_out.at[i - 2], sems.at[i - 2]))
            copies[-1].start()
    for copy in copies:
        copy.wait()


def per_device(
    frames,
    frame_owner,
    picks,
    patch_weight,
    patch_bias,
    norm_gain,
    head_weight,
    head_bias,
    head_out,
    hidden_state,
    group_gain,
    group_shift,
    out_weight,
    inner_weight,
):
    devices = lax.axis_size("row")
    per_frame = devices // FRAMES
    height = frames.shape[1]
    own_rows, _, frame_width, channels = hidden_state.shape
    cells = FRAMES * frame_width
    width = patch_weight.shape[1]
    turned_frames = jnp.transpose(frames, (0, 2, 1))
    bias = patch_bias.reshape(1, width)
    gain = norm_gain.reshape(1, width)
    head_bias_row = head_bias.reshape(1, width)
    head_out_row = head_out.reshape(1, width)
    state_rows = own_rows + 2
    edge = jax.ShapeDtypeStruct((1,) + hidden_state.shape[1:], BF16)
    message = (message_shape(devices), edge, edge)
    gain_row = group_gain.reshape(1, channels)
    shift_row = group_shift.reshape(1, channels)
    early = [hidden_state, gain_row, shift_row, out_weight]
    slope_outs = (
        pltpu.VMEM((own_rows, cells, channels), F32),
        pltpu.VMEM((2, cells, channels), F32),
        pltpu.VMEM((8, channels), F32),
        jax.ShapeDtypeStruct((devices, 2, channels), F32),
    )
    if per_frame == 1:
        arrays = [turned_frames, bias, gain, frame_owner, picks, head_bias_row, head_out_row]
        weights = [patch_weight, head_weight]

        def scratch(x):
            return (pltpu.SMEM if x.dtype == jnp.int32 else pltpu.VMEM)(x.shape, x.dtype)

        send, across, along, *early = pl.pallas_call(
            reward_kernel,
            out_shape=message + tuple(pltpu.VMEM(x.shape, x.dtype) for x in early),
            in_specs=[FAR] * (len(arrays) + len(early) + len(weights)),
            out_specs=[VMEM] * (3 + len(early)),
            scratch_shapes=[scratch(x) for x in arrays + weights] + [pltpu.SemaphoreType.DMA((32,))],
            compiler_params=params(0),
            name="reward",
        )(*[far(x) for x in arrays + early + weights])
    else:
        count = height // PATCH
        normed, inv_spread, partial = pl.pallas_call(
            forward_kernel,
            out_shape=(
                jax.ShapeDtypeStruct((-(-count // 8) * 8, width), F32),
                jax.ShapeDtypeStruct((-(-count // 8) * 8, LANES), F32),
                jax.ShapeDtypeStruct((1, width), F32),
            ),
            compiler_params=params(cells),
            name="reward_forward",
        )(turned_frames, bias, gain, patch_weight)
        members = [[b * per_frame + i for i in range(per_frame)] for b in range(FRAMES)]
        pooled = lax.psum(partial, "row", axis_index_groups=members) / (count * per_frame)
        send, across, along = pl.pallas_call(
            functools.partial(backward_kernel, height=height, per_frame=per_frame),
            out_shape=message,
            in_specs=[SMEM] * 2 + [VMEM] * 9,
            out_specs=[VMEM] * 3,
            compiler_params=params(cells),
            name="reward_backward",
        )(
            frame_owner,
            picks,
            hidden_state,
            gain,
            head_bias_row,
            head_out_row,
            normed,
            inv_spread,
            pooled,
            patch_weight,
            head_weight,
        )
    early = [near(x) for x in early]
    wide = pl.pallas_call(
        prepare_kernel,
        out_shape=pltpu.VMEM((3 * LANES, state_rows * channels), BF16),
        in_specs=[VMEM],
        scratch_shapes=[pltpu.VMEM((3 * LANES, state_rows * channels), F32)],
        compiler_params=params(cells),
        name="prepare",
    )(early[3])
    arrived = lax.all_to_all(send, "row", 0, 0, axis_index_groups=[first_order(devices)], tiled=True)
    direct, edge_slopes, stats, sums = pl.pallas_call(
        slope_kernel,
        out_shape=slope_outs,
        in_specs=[VMEM] * 5 + [FAR],
        scratch_shapes=[
            pltpu.VMEM((own_rows, cells, channels), F32),
            pltpu.VMEM((4 * devices, LANES), F32),
            pltpu.VMEM((cells + 2 * frame_width, LANES), BF16),
            pltpu.SMEM(frame_owner.shape, jnp.int32),
            pltpu.SemaphoreType.DMA((1,)),
        ],
        compiler_params=params(cells),
        name="slope",
    )(near(arrived), *early[:3], near(wide), far(frame_owner))
    swaps = [(2 * i, 2 * i + 1) for i in range(devices // 2)]
    across = lax.ppermute(across, "row", swaps + [(b, a) for a, b in swaps])
    swaps = [(2 * i - 1, 2 * i) for i in range(1, devices // 2)]
    along = lax.ppermute(along, "row", swaps + [(b, a) for a, b in swaps])
    summed = lax.all_to_all(sums, "row", 0, 0, axis_index_groups=[led_by(devices - 1, devices)], tiled=True)
    edge_direct, edge_states, turned = pl.pallas_call(
        late_kernel,
        out_shape=(
            pltpu.VMEM((2, cells, channels), F32),
            pltpu.VMEM((2,) + hidden_state.shape[1:], BF16),
            pltpu.VMEM((9 * channels, 3 * channels), BF16),
        ),
        in_specs=[VMEM] * 6 + [FAR],
        scratch_shapes=[pltpu.VMEM(inner_weight.shape, BF16), pltpu.SemaphoreType.DMA((1,))],
        input_output_aliases={2: 0},
        compiler_params=params(cells),
        name="late",
    )(near(across), near(along), near(edge_slopes), near(stats), *early[1:3], far(inner_weight))
    return pl.pallas_call(
        functools.partial(inner_kernel, devices=devices),
        out_shape=jax.ShapeDtypeStruct(hidden_state.shape, BF16),
        in_specs=[VMEM] * 7,
        out_specs=FAR,
        scratch_shapes=[
            pltpu.VMEM(hidden_state.shape, BF16),
            pltpu.SemaphoreType.DMA((own_rows,)),
        ],
        compiler_params=params(cells),
        name="inner",
    )(
        near(summed),
        near(stats),
        near(direct),
        early[0],
        near(edge_direct),
        near(edge_states),
        near(turned),
    )


def solution(mesh):
    return jax.shard_map(
        per_device,
        mesh=mesh,
        in_specs=(
            P(None, None, ("clip", "row")),
            P("clip"),
            P("clip"),
            P(),
            P(),
            P(),
            P(),
            P(),
            P(),
            P(("clip", "row"), None, None, None),
            P(),
            P(),
            P(),
            P(),
        ),
        out_specs=P(("clip", "row"), None, None, None),
        check_vma=False,
    )
```

```python
import functools

import jax
import jax.numpy as jnp
from jax import lax
from jax.experimental import pallas as pl
from jax.experimental.pallas import tpu as pltpu
from jax.sharding import PartitionSpec as P

PATCH = 16
GROUPS = 32
FRAMES = 16
LANES = 128
SLOTS = LANES // PATCH
eps_norm = 1e-06
BF16 = jnp.bfloat16
F32 = jnp.float32

SMEM = pl.BlockSpec(memory_space=pltpu.SMEM)
VMEM = pl.BlockSpec(memory_space=pltpu.VMEM)
FAR = pl.BlockSpec(memory_space=pl.ANY)


def iota(shape, dim):
    return lax.broadcasted_iota(jnp.int32, shape, dim)


def div(values, count):
    if count & (count - 1):
        return values // count
    return values >> (count.bit_length() - 1)


def mod(values, count):
    if count & (count - 1):
        return values % count
    return values & (count - 1)


def ones_where(condition):
    return jnp.where(condition, 1.0, 0.0).astype(BF16)


def matmul(left, right):
    return jnp.dot(left, right, preferred_element_type=F32)


def matmul_t(left, right):
    return lax.dot_general(left, right, (((1,), (1,)), ((), ())), preferred_element_type=F32)


def cut_in_three(values):
    high = values.astype(BF16)
    rest = values - high.astype(F32)
    middle = rest.astype(BF16)
    low = (rest - middle.astype(F32)).astype(BF16)
    return high, middle, low


def exact_rows(rows, product):
    place = iota((8, rows[0].shape[1]), 0)
    stacked = jnp.zeros(place.shape, F32)
    for index, row in enumerate(rows):
        for step, piece in enumerate(cut_in_three(row)):
            stacked = jnp.where(place == 3 * index + step, piece.astype(F32), stacked)
    result = product(jnp.concatenate([stacked, jnp.zeros_like(stacked)], axis=0).astype(BF16))
    return [
        result[3 * i : 3 * i + 1] + result[3 * i + 1 : 3 * i + 2] + result[3 * i + 2 : 3 * i + 3]
        for i in range(len(rows))
    ]


def silu_slope(values):
    sigmoid = jax.nn.sigmoid(values)
    return sigmoid * (1.0 + values * (1.0 - sigmoid))


def token_rows_of(height):
    return -(-(height // PATCH) // 16) * 16


def to_tokens(pixels):
    channels, columns, height = pixels.shape
    rows = channels * columns
    token_rows = token_rows_of(height)
    flat = pixels.reshape(rows, height)
    width = channels * PATCH * columns
    lane = iota((1, width), 1)
    place = iota((rows, 1), 0)
    mine = place == div(lane, PATCH * columns) * columns + mod(lane, columns)
    in_patch = mod(div(lane, columns), PATCH)
    pixel_row = iota((height, 1), 0)
    token = iota((token_rows, 1), 0)
    tokens = jnp.zeros((token_rows, width), F32)
    for t in range(height // PATCH):
        tiled = matmul(flat, ones_where(pixel_row == in_patch + t * PATCH))
        row = jnp.sum(jnp.where(mine, tiled, 0.0), axis=0, keepdims=True)
        tokens = jnp.where(token == t, row, tokens)
    return tokens.astype(BF16)


def forward_part(tokens, count, bias, gain, load_patch):
    embedded = jnp.zeros((tokens.shape[0], bias.shape[1]), F32)
    for low, high, weight in load_patch():
        embedded = embedded + matmul(tokens[:, low:high], weight)
    rows = -(-count // 8) * 8
    embedded = embedded[:rows] + bias[...]
    centred = embedded - jnp.mean(embedded, axis=1, keepdims=True)
    inv_spread = lax.rsqrt(jnp.mean(centred * centred, axis=1, keepdims=True) + eps_norm)
    normed = centred * inv_spread
    weighted = normed * gain[...]
    inside = iota((rows, 1), 0) < count
    pooled = jnp.sum(jnp.where(inside, weighted, 0.0), axis=0, keepdims=True)
    return normed, inv_spread, pooled


def led_by(leader, devices):
    return [leader] + [d for d in reversed(range(devices)) if d != leader]


def first_order(devices):
    return led_by(devices * 13 // 16, devices)


def message_shape(devices):
    return jax.ShapeDtypeStruct((devices, 4, LANES), F32)


def write_windows(patch_grad, sums, own_rows, height, send):
    span = PATCH * PATCH
    line = jnp.concatenate(
        [
            jnp.concatenate([patch_grad[t : t + 1, k * span : (k + 1) * span] for t in range(height // PATCH)], axis=1)
            for k in range(3)
        ]
        + [jnp.zeros((1, height * PATCH), F32)],
        axis=0,
    )
    line = jnp.concatenate([jnp.zeros((4, LANES), F32), line, jnp.zeros((4, LANES), F32)], axis=1)
    used = iota((4, LANES), 1) < (own_rows + 4) * PATCH
    colour = iota((4, LANES), 0)
    for index, d in enumerate(first_order(send.shape[0])):
        start = LANES + (d * own_rows - 2) * PATCH
        window = jnp.where(used, line[:, start : start + LANES], 0.0)
        send[index] = jnp.where(colour < 3, window, sums[:4])


def channel_sums(hidden):
    values = hidden.reshape(-1, hidden.shape[-1]).astype(F32)
    return jnp.sum(values, axis=0, keepdims=True), jnp.sum(values * values, axis=0, keepdims=True)


def over_group(values, size):
    lane = iota(values.shape, 1)
    lanes = values.shape[1]
    step = 1
    while step < size:
        later = pltpu.roll(values, lanes - step, 1)
        earlier = pltpu.roll(values, step, 1)
        values = values + jnp.where((lane & step) == 0, later, earlier)
        step *= 2
    return values


def group_sums(hidden):
    channels = hidden.shape[-1]
    size = channels // GROUPS
    first, second = [
        over_group(jnp.broadcast_to(x, (8, channels)), size) for x in channel_sums(hidden)
    ]
    lane = mod(iota((8, channels), 1), size)
    return jnp.where(lane == 0, first, jnp.where(lane == 1, second, 0.0))


def pull_back(row, weight):
    parts = []
    for low in range(0, weight.shape[0], LANES):
        product = weight[low : low + LANES, :].astype(F32) * row
        folded = product[:, :LANES]
        for start in range(LANES, weight.shape[1], LANES):
            folded = folded + product[:, start : start + LANES]
        parts.append(jnp.sum(folded.T, axis=0, keepdims=True))
    return jnp.concatenate(parts, axis=1)


def backward_part(
    owner, picks, gain, head_bias, head_out, normed, inv_spread, pooled, weight, head, through_head, slot, own_rows, height, sums, send
):
    (before,) = exact_rows([pooled], through_head)
    slope = head_out[...] * silu_slope(before + head_bias[...])
    pulled = pull_back(slope, head)
    wanted = owner[slot]
    picked = jnp.int32(0)
    for k in range(picks.shape[0]):
        picked = picked + jnp.where(picks[k] == wanted, 1, 0)
    scaled = gain[...] * (picked.astype(F32) * pulled)
    token_grad = inv_spread * (
        scaled
        - jnp.mean(scaled, axis=1, keepdims=True)
        - normed * jnp.mean(scaled * normed, axis=1, keepdims=True)
    )
    filler = jnp.zeros((-token_grad.shape[0] % 16, token_grad.shape[1]), F32)
    token_grad = jnp.concatenate([token_grad, filler], axis=0).astype(BF16)
    patch_grad = matmul_t(token_grad, weight[...]).astype(BF16).astype(F32)
    write_windows(patch_grad, sums, own_rows, height, send)


def write_edges(position, hidden, across, along):
    last = hidden.shape[0] - 1
    even = position % 2 == 0
    across[0] = hidden[jnp.where(even, last, 0)]
    along[0] = hidden[jnp.where(even, 0, last)]


def reward_kernel(*refs):
    position = lax.axis_index("row")
    count, kept = 7, 4
    far, refs = refs[: count + kept + 2], refs[count + kept + 2 :]
    send, across, along = refs[:3]
    near = refs[3 + kept : 3 + kept + count] + refs[3 : 3 + kept] + refs[3 + kept + count : -1]
    sems = refs[-1]
    frames, bias, gain, owner, picks, head_bias, head_out, hidden, _, _, _, patch, head = near
    count += kept
    depths = (256, 256)
    small = [pltpu.make_async_copy(far[i], near[i], sems.at[i]) for i in range(count)]
    pieces = []
    used = count
    for index, rows in enumerate(depths):
        source, target = far[count + index], near[count + index]
        parts = []
        for low in range(0, target.shape[0], rows):
            part = pl.ds(low, rows)
            parts.append(pltpu.make_async_copy(source.at[part], target.at[part], sems.at[used]))
            used += 1
        pieces.append(parts)
    last = hidden.shape[0] - 1
    even = position % 2 == 0
    edges = [
        pltpu.make_async_copy(far[7].at[pl.ds(jnp.where(even, last, 0), 1)], across, sems.at[used]),
        pltpu.make_async_copy(far[7].at[pl.ds(jnp.where(even, 0, last), 1)], along, sems.at[used + 1]),
    ]
    for copy in [small[0]] + pieces[0] + small[1:7] + pieces[1] + small[7:] + edges:
        copy.start()

    def load_patch():
        for copy in pieces[0] + small[1:3]:
            copy.wait()
        yield 0, patch.shape[0], patch[...]

    height = frames.shape[2]
    patches = height // PATCH
    small[0].wait()
    tokens = to_tokens(frames[...])
    normed, inv_spread, pooled = forward_part(tokens, patches, bias, gain, load_patch)
    for copy in small[3:8]:
        copy.wait()

    def through_head(rows):
        total = jnp.zeros((rows.shape[0], head.shape[1]), F32)
        for index, low in enumerate(range(0, head.shape[0], depths[1])):
            pieces[1][index].wait()
            total = total + matmul(rows[:, low : low + depths[1]], head[low : low + depths[1], :])
        return total

    backward_part(
        owner,
        picks,
        gain,
        head_bias,
        head_out,
        normed,
        inv_spread,
        pooled / patches,
        patch,
        head,
        through_head,
        position,
        hidden.shape[0],
        height,
        group_sums(hidden[...]),
        send,
    )
    for copy in small[8:] + edges:
        copy.wait()


def forward_kernel(frames, bias, gain, patch, normed, inv_spread, pooled):
    width = patch.shape[0]
    tokens = to_tokens(frames[...])
    normed[...], spread, pooled[...] = forward_part(
        tokens, frames.shape[2] // PATCH, bias, gain, lambda: [(0, width, patch[...])]
    )
    inv_spread[...] = jnp.broadcast_to(spread, inv_spread.shape)


def backward_kernel(
    owner,
    picks,
    hidden,
    gain,
    head_bias,
    head_out,
    normed,
    inv_spread,
    pooled,
    patch,
    head,
    send,
    across,
    along,
    *,
    height,
    per_frame,
):
    position = lax.axis_index("row")
    write_edges(position, hidden, across, along)
    backward_part(
        owner,
        picks,
        gain,
        head_bias,
        head_out,
        normed[...],
        inv_spread[...][:, :1],
        pooled[...],
        patch,
        head,
        lambda rows: matmul(rows, head[...]),
        position // per_frame,
        hidden.shape[0],
        height,
        group_sums(hidden[...]),
        send,
    )


def params(cells):
    return pltpu.CompilerParams(vmem_limit_bytes=min(16 + cells // 64, 48) * 1024 * 1024)


def near(array):
    return pltpu.with_memory_space_constraint(array, pltpu.VMEM)


def far(array):
    return pltpu.with_memory_space_constraint(array, pltpu.HBM)


def tap_lane(j, k, e):
    return (j + 1) * PATCH + 4 * k + e


def prepare_kernel(out_weight, wide, scratch):
    amount = scratch.shape[1] // LANES
    scratch[...] = jnp.zeros_like(scratch)
    for a in range(3):
        for e in range(3):
            for b in range(3):
                piece = out_weight[a, b, e].astype(F32)
                for i in range(amount):
                    for k in range(3):
                        at = a * LANES + tap_lane(i - b + 2, k, e)
                        scratch[at : at + 1, i * LANES : (i + 1) * LANES] = piece[k : k + 1]
    wide[...] = scratch[...].astype(BF16)


def norm_constants(totals, cell_total):
    channels = totals.shape[1]
    size = channels // GROUPS
    totals = jnp.broadcast_to(totals, (8, channels))
    lane = mod(iota((8, channels), 1), size)
    first, second = [over_group(jnp.where(lane == i, totals, 0.0), size)[:1] for i in range(2)]
    mean = first / cell_total
    return mean, lax.rsqrt(second / cell_total - mean * mean + eps_norm)


def norm_slopes(state, mean, inverse, gain, shift):
    normed = (state - mean) * inverse
    return normed, silu_slope(normed * gain + shift) * gain


def slope_kernel(
    arrived,
    hidden,
    gain,
    shift,
    wide,
    far_owner,
    direct,
    edge_slopes,
    stats,
    sums,
    slopes_own,
    received,
    taps,
    owner,
    sem,
):
    copy = pltpu.make_async_copy(far_owner, owner, sem.at[0])
    copy.start()
    devices, message_rows, _ = arrived.shape
    own_rows, frame_count, width, channels = hidden.shape
    cells = frame_count * width
    per_frame = devices // frame_count
    got = arrived[...].reshape(received.shape)
    kind = mod(iota((got.shape[0], 1), 0), message_rows)
    totals = jnp.sum(jnp.where(kind == 3, got, 0.0), axis=0, keepdims=True)
    mean, inverse = norm_constants(totals, own_rows * devices * cells * (channels // GROUPS))
    for i in range(own_rows):
        state = hidden[i].reshape(cells, channels).astype(F32)
        slopes_own[i] = norm_slopes(state, mean, inverse, gain[...], shift[...])[1] * inverse

    if per_frame == 1:
        lane = iota((1, LANES), 1)
        entry = iota((LANES, 1), 0)
        turned = ones_where(entry - mod(entry, PATCH) + PATCH - 1 - mod(entry, PATCH) == lane)
        received[...] = matmul(jnp.where(kind < 3, got, 0.0).astype(BF16), turned)
        lane = mod(iota((PATCH, LANES), 1), PATCH)
        column = iota((PATCH, LANES), 0)
        marks = []
        for k in range(3):
            e = lane - 4 * k
            wanted = column - e + 1
            marks.append((e >= 0) & (e < 3) & (wanted >= 0) & (wanted < PATCH))
        copy.wait()
        for d in range(devices):
            row = first_order(devices)[d]
            block = jnp.zeros((PATCH, LANES), F32)
            for k in range(3):
                line = jnp.broadcast_to(received[d * message_rows + k : d * message_rows + k + 1, :], (PATCH, LANES))
                line = pltpu.roll(line, 4 * k + 2, 1, stride=1, stride_axis=0)
                block = jnp.where(marks[k], line, block)
            start = pl.multiple_of(owner[row] * PATCH, PATCH)
            taps[pl.ds(start, PATCH), :] = block.astype(BF16)
    else:
        copy.wait()
        received[...] = got
        lines = [received[pl.ds(k, devices, stride=message_rows), :] for k in range(3)]
        lines = jnp.concatenate(lines, axis=1).astype(BF16)
        place = iota((1, devices), 1)
        source = jnp.zeros_like(place)
        for index, d in enumerate(first_order(devices)):
            source = jnp.where(place == index, d, source)
        home = jnp.zeros((1, devices), jnp.int32)
        for b in range(frame_count):
            home = jnp.where(div(source, per_frame) == b, owner[b] * per_frame, home)
        home = home + mod(source, per_frame)
        cell = iota((cells, 1), 0)
        column = mod(cell, width)
        lane = mod(iota((1, 3 * LANES), 1), PATCH)
        entry = iota((3 * LANES, 1), 0)
        window_row = div(mod(entry, LANES), PATCH)
        found = jnp.zeros((cells, LANES), F32)
        for e in range(3):
            wanted = column - e + 1
            strip = div(cell, width) * per_frame + div(wanted, PATCH)
            placed = matmul(ones_where(home == strip), lines)
            inside = jnp.where((wanted >= 0) & (wanted < width), mod(wanted, PATCH), -1)
            kept = jnp.where(lane == inside, placed, 0.0).astype(BF16)
            target = jnp.where(
                window_row < own_rows + 4, tap_lane(window_row, div(entry, LANES), e), -1
            )
            found = found + matmul(kept, ones_where(target == iota((1, LANES), 1)))
        taps[:cells, :] = found.astype(BF16)
    taps[cells:, :] = jnp.zeros((2 * width, LANES), BF16)
    steps = [taps[(2 - a) * width : (2 - a) * width + cells, :] for a in range(3)]
    result = matmul(jnp.concatenate(steps, axis=1), wide[...])

    first = jnp.zeros((1, channels), F32)
    second = jnp.zeros((1, channels), F32)
    for i in range(own_rows):
        state = hidden[i].reshape(cells, channels).astype(F32)
        part = result[:, (i + 1) * channels : (i + 2) * channels] * slopes_own[i]
        direct[i] = part
        first = first + jnp.sum(part, axis=0, keepdims=True)
        second = second + jnp.sum(part * (state - mean), axis=0, keepdims=True)
    first = first / inverse
    edge_slopes[0] = result[:, :channels]
    edge_slopes[1] = result[:, (own_rows + 1) * channels :]
    stats[0:1, :] = mean
    stats[1:2, :] = inverse
    both = jnp.where(iota((2, channels), 0) == 0, first, second)
    sums[...] = jnp.broadcast_to(both[None], sums.shape)


def late_kernel(
    across, along, slopes, stats, gain, shift, far_weight, direct, states, turned, inner_weight, sem
):
    copy = pltpu.make_async_copy(far_weight, inner_weight, sem.at[0])
    copy.start()
    cells, channels = slopes.shape[1:]
    odd = lax.axis_index("row") % 2 == 1
    mean = stats[0:1, :]
    inverse = stats[1:2, :]
    for i in range(2):
        state = jnp.where(odd == (i == 0), across[0], along[0])
        states[i] = state
        values = state.reshape(cells, channels).astype(F32)
        direct[i] = slopes[i] * norm_slopes(values, mean, inverse, gain[...], shift[...])[1] * inverse
    copy.wait()
    size = inner_weight.shape[3]
    for b in range(3):
        for a in range(3):
            for e in range(3):
                at = (a * 3 + e) * size
                turned[at : at + size, b * size : (b + 1) * size] = inner_weight[a, b, e].T


def inner_kernel(
    arrived, stats, direct, hidden, edge_direct, edge_states, turned, far_out, out, sems, *, devices
):
    own_rows, frame_count, width, channels = out.shape
    cells = frame_count * width
    totals = jnp.sum(arrived[...], axis=0)
    cell_total = own_rows * devices * cells * (channels // GROUPS)
    place_row = iota((8, channels), 0)
    both = jnp.where(place_row == 0, totals[0:1], totals[1:2])
    both = over_group(both, channels // GROUPS)
    first, second = both[0:1], both[1:2]
    mean = stats[0:1, :]
    inverse = stats[1:2, :]
    constant = first / cell_total * inverse
    factor = second / cell_total * inverse * inverse
    position = lax.axis_index("row")
    in_frame = mod(iota((cells, 1), 0), width)
    results = [jnp.zeros((cells, channels), F32) for _ in range(own_rows)]
    copies = []
    for i in range(own_rows + 2):
        if 0 < i < own_rows + 1:
            state, part = hidden[i - 1], direct[i - 1]
        else:
            state, part = edge_states[min(i, 1)], edge_direct[min(i, 1)]
        grad = part - constant - (state.reshape(cells, channels).astype(F32) - mean) * factor
        if i == 0:
            grad = jnp.where(position > 0, grad, 0.0)
        if i == own_rows + 1:
            grad = jnp.where(position < devices - 1, grad, 0.0)
        after = jnp.where(in_frame < width - 1, pltpu.roll(grad, cells - 1, 0), 0.0)
        prior = jnp.where(in_frame > 0, pltpu.roll(grad, 1, 0), 0.0)
        taps = jnp.concatenate([after.astype(BF16), grad.astype(BF16), prior.astype(BF16)], axis=1)
        later = []
        for a in range(3):
            skip = (2 - a) * width
            filler = jnp.zeros((skip, taps.shape[1]), BF16)
            later.append(jnp.concatenate([taps[skip:], filler], axis=0) if skip else taps)
        joined = jnp.concatenate(later, axis=1)
        rows = [b for b in range(3) if 0 <= i + b - 2 < own_rows]
        for low in range(0, len(rows), 2):
            some = rows[low : low + 2]
            product = matmul(joined, turned[:, some[0] * channels : (some[-1] + 1) * channels])
            for step, b in enumerate(some):
                results[i + b - 2] = results[i + b - 2] + product[:, step * channels : (step + 1) * channels]
        if i >= 2:
            out[i - 2] = results[i - 2].reshape(frame_count, width, channels).astype(BF16)
            copies.append(pltpu.make_async_copy(out.at[i - 2], far_out.at[i - 2], sems.at[i - 2]))
            copies[-1].start()
    for copy in copies:
        copy.wait()


def per_device(
    frames,
    frame_owner,
    picks,
    patch_weight,
    patch_bias,
    norm_gain,
    head_weight,
    head_bias,
    head_out,
    hidden_state,
    group_gain,
    group_shift,
    out_weight,
    inner_weight,
):
    devices = lax.axis_size("row")
    per_frame = devices // FRAMES
    height = frames.shape[1]
    own_rows, _, frame_width, channels = hidden_state.shape
    cells = FRAMES * frame_width
    width = patch_weight.shape[1]
    turned_frames = jnp.transpose(frames, (0, 2, 1))
    bias = patch_bias.reshape(1, width)
    gain = norm_gain.reshape(1, width)
    head_bias_row = head_bias.reshape(1, width)
    head_out_row = head_out.reshape(1, width)
    state_rows = own_rows + 2
    edge = jax.ShapeDtypeStruct((1,) + hidden_state.shape[1:], BF16)
    message = (message_shape(devices), edge, edge)
    gain_row = group_gain.reshape(1, channels)
    shift_row = group_shift.reshape(1, channels)
    early = [hidden_state, gain_row, shift_row, out_weight]
    slope_outs = (
        pltpu.VMEM((own_rows, cells, channels), F32),
        pltpu.VMEM((2, cells, channels), F32),
        pltpu.VMEM((8, channels), F32),
        jax.ShapeDtypeStruct((devices, 2, channels), F32),
    )
    if per_frame == 1:
        arrays = [turned_frames, bias, gain, frame_owner, picks, head_bias_row, head_out_row]
        weights = [patch_weight, head_weight]

        def scratch(x):
            return (pltpu.SMEM if x.dtype == jnp.int32 else pltpu.VMEM)(x.shape, x.dtype)

        send, across, along, *early = pl.pallas_call(
            reward_kernel,
            out_shape=message + tuple(pltpu.VMEM(x.shape, x.dtype) for x in early),
            in_specs=[FAR] * (len(arrays) + len(early) + len(weights)),
            out_specs=[VMEM] * (3 + len(early)),
            scratch_shapes=[scratch(x) for x in arrays + weights] + [pltpu.SemaphoreType.DMA((32,))],
            compiler_params=params(0),
            name="reward",
        )(*[far(x) for x in arrays + early + weights])
    else:
        count = height // PATCH
        normed, inv_spread, partial = pl.pallas_call(
            forward_kernel,
            out_shape=(
                jax.ShapeDtypeStruct((-(-count // 8) * 8, width), F32),
                jax.ShapeDtypeStruct((-(-count // 8) * 8, LANES), F32),
                jax.ShapeDtypeStruct((1, width), F32),
            ),
            compiler_params=params(cells),
            name="reward_forward",
        )(turned_frames, bias, gain, patch_weight)
        members = [[b * per_frame + i for i in range(per_frame)] for b in range(FRAMES)]
        pooled = lax.psum(partial, "row", axis_index_groups=members) / (count * per_frame)
        send, across, along = pl.pallas_call(
            functools.partial(backward_kernel, height=height, per_frame=per_frame),
            out_shape=message,
            in_specs=[SMEM] * 2 + [VMEM] * 9,
            out_specs=[VMEM] * 3,
            compiler_params=params(cells),
            name="reward_backward",
        )(
            frame_owner,
            picks,
            hidden_state,
            gain,
            head_bias_row,
            head_out_row,
            normed,
            inv_spread,
            pooled,
            patch_weight,
            head_weight,
        )
    early = [near(x) for x in early]
    wide = pl.pallas_call(
        prepare_kernel,
        out_shape=pltpu.VMEM((3 * LANES, state_rows * channels), BF16),
        in_specs=[VMEM],
        scratch_shapes=[pltpu.VMEM((3 * LANES, state_rows * channels), F32)],
        compiler_params=params(cells),
        name="prepare",
    )(early[3])
    arrived = lax.all_to_all(send, "row", 0, 0, axis_index_groups=[first_order(devices)], tiled=True)
    direct, edge_slopes, stats, sums = pl.pallas_call(
        slope_kernel,
        out_shape=slope_outs,
        in_specs=[VMEM] * 5 + [FAR],
        scratch_shapes=[
            pltpu.VMEM((own_rows, cells, channels), F32),
            pltpu.VMEM((4 * devices, LANES), F32),
            pltpu.VMEM((cells + 2 * frame_width, LANES), BF16),
            pltpu.SMEM(frame_owner.shape, jnp.int32),
            pltpu.SemaphoreType.DMA((1,)),
        ],
        compiler_params=params(cells),
        name="slope",
    )(near(arrived), *early[:3], near(wide), far(frame_owner))
    swaps = [(2 * i, 2 * i + 1) for i in range(devices // 2)]
    across = lax.ppermute(across, "row", swaps + [(b, a) for a, b in swaps])
    swaps = [(2 * i - 1, 2 * i) for i in range(1, devices // 2)]
    along = lax.ppermute(along, "row", swaps + [(b, a) for a, b in swaps])
    summed = lax.all_to_all(sums, "row", 0, 0, axis_index_groups=[led_by(devices - 1, devices)], tiled=True)
    edge_direct, edge_states, turned = pl.pallas_call(
        late_kernel,
        out_shape=(
            pltpu.VMEM((2, cells, channels), F32),
            pltpu.VMEM((2,) + hidden_state.shape[1:], BF16),
            pltpu.VMEM((9 * channels, 3 * channels), BF16),
        ),
        in_specs=[VMEM] * 6 + [FAR],
        scratch_shapes=[pltpu.VMEM(inner_weight.shape, BF16), pltpu.SemaphoreType.DMA((1,))],
        input_output_aliases={2: 0},
        compiler_params=params(cells),
        name="late",
    )(near(across), near(along), near(edge_slopes), near(stats), *early[1:3], far(inner_weight))
    return pl.pallas_call(
        functools.partial(inner_kernel, devices=devices),
        out_shape=jax.ShapeDtypeStruct(hidden_state.shape, BF16),
        in_specs=[VMEM] * 7,
        out_specs=FAR,
        scratch_shapes=[
            pltpu.VMEM(hidden_state.shape, BF16),
            pltpu.SemaphoreType.DMA((own_rows,)),
        ],
        compiler_params=params(cells),
        name="inner",
    )(
        near(summed),
        near(stats),
        near(direct),
        early[0],
        near(edge_direct),
        near(edge_states),
        near(turned),
    )


def solution(mesh):
    return jax.shard_map(
        per_device,
        mesh=mesh,
        in_specs=(
            P(None, None, ("clip", "row")),
            P("clip"),
            P("clip"),
            P(),
            P(),
            P(),
            P(),
            P(),
            P(),
            P(("clip", "row"), None, None, None),
            P(),
            P(),
            P(),
            P(),
        ),
        out_specs=P(("clip", "row"), None, None, None),
        check_vma=False,
    )
```

```python
import functools

import jax
import jax.numpy as jnp
from jax import lax
from jax.experimental import pallas as pl
from jax.experimental.pallas import tpu as pltpu
from jax.sharding import PartitionSpec as P

PATCH = 16
GROUPS = 32
FRAMES = 16
LANES = 128
SLOTS = LANES // PATCH
eps_norm = 1e-06
BF16 = jnp.bfloat16
F32 = jnp.float32

SMEM = pl.BlockSpec(memory_space=pltpu.SMEM)
VMEM = pl.BlockSpec(memory_space=pltpu.VMEM)
FAR = pl.BlockSpec(memory_space=pl.ANY)


def iota(shape, dim):
    return lax.broadcasted_iota(jnp.int32, shape, dim)


def div(values, count):
    if count & (count - 1):
        return values // count
    return values >> (count.bit_length() - 1)


def mod(values, count):
    if count & (count - 1):
        return values % count
    return values & (count - 1)


def ones_where(condition):
    return jnp.where(condition, 1.0, 0.0).astype(BF16)


def matmul(left, right):
    return jnp.dot(left, right, preferred_element_type=F32)


def matmul_t(left, right):
    return lax.dot_general(left, right, (((1,), (1,)), ((), ())), preferred_element_type=F32)


def cut_in_three(values):
    high = values.astype(BF16)
    rest = values - high.astype(F32)
    middle = rest.astype(BF16)
    low = (rest - middle.astype(F32)).astype(BF16)
    return high, middle, low


def exact_rows(rows, product):
    place = iota((8, rows[0].shape[1]), 0)
    stacked = jnp.zeros(place.shape, F32)
    for index, row in enumerate(rows):
        for step, piece in enumerate(cut_in_three(row)):
            stacked = jnp.where(place == 3 * index + step, piece.astype(F32), stacked)
    result = product(jnp.concatenate([stacked, jnp.zeros_like(stacked)], axis=0).astype(BF16))
    return [
        result[3 * i : 3 * i + 1] + result[3 * i + 1 : 3 * i + 2] + result[3 * i + 2 : 3 * i + 3]
        for i in range(len(rows))
    ]


def silu_slope(values):
    sigmoid = jax.nn.sigmoid(values)
    return sigmoid * (1.0 + values * (1.0 - sigmoid))


def token_rows_of(height):
    return -(-(height // PATCH) // 16) * 16


def to_tokens(pixels):
    channels, columns, height = pixels.shape
    rows = channels * columns
    token_rows = token_rows_of(height)
    flat = pixels.reshape(rows, height)
    width = channels * PATCH * columns
    lane = iota((1, width), 1)
    place = iota((rows, 1), 0)
    mine = place == div(lane, PATCH * columns) * columns + mod(lane, columns)
    in_patch = mod(div(lane, columns), PATCH)
    pixel_row = iota((height, 1), 0)
    token = iota((token_rows, 1), 0)
    tokens = jnp.zeros((token_rows, width), F32)
    for t in range(height // PATCH):
        tiled = matmul(flat, ones_where(pixel_row == in_patch + t * PATCH))
        row = jnp.sum(jnp.where(mine, tiled, 0.0), axis=0, keepdims=True)
        tokens = jnp.where(token == t, row, tokens)
    return tokens.astype(BF16)


def forward_part(tokens, count, bias, gain, load_patch):
    embedded = jnp.zeros((tokens.shape[0], bias.shape[1]), F32)
    for low, high, weight in load_patch():
        embedded = embedded + matmul(tokens[:, low:high], weight)
    rows = -(-count // 8) * 8
    embedded = embedded[:rows] + bias[...]
    centred = embedded - jnp.mean(embedded, axis=1, keepdims=True)
    inv_spread = lax.rsqrt(jnp.mean(centred * centred, axis=1, keepdims=True) + eps_norm)
    normed = centred * inv_spread
    weighted = normed * gain[...]
    inside = iota((rows, 1), 0) < count
    pooled = jnp.sum(jnp.where(inside, weighted, 0.0), axis=0, keepdims=True)
    return normed, inv_spread, pooled


def led_by(leader, devices):
    return [leader] + [d for d in reversed(range(devices)) if d != leader]


def first_order(devices):
    return led_by(devices * 13 // 16, devices)


def message_shape(devices):
    return jax.ShapeDtypeStruct((devices, 4, LANES), F32)


def write_windows(patch_grad, sums, own_rows, height, send):
    span = PATCH * PATCH
    line = jnp.concatenate(
        [
            jnp.concatenate([patch_grad[t : t + 1, k * span : (k + 1) * span] for t in range(height // PATCH)], axis=1)
            for k in range(3)
        ]
        + [jnp.zeros((1, height * PATCH), F32)],
        axis=0,
    )
    line = jnp.concatenate([jnp.zeros((4, LANES), F32), line, jnp.zeros((4, LANES), F32)], axis=1)
    used = iota((4, LANES), 1) < (own_rows + 4) * PATCH
    colour = iota((4, LANES), 0)
    for index, d in enumerate(first_order(send.shape[0])):
        start = LANES + (d * own_rows - 2) * PATCH
        window = jnp.where(used, line[:, start : start + LANES], 0.0)
        send[index] = jnp.where(colour < 3, window, sums[:4])


def channel_sums(hidden):
    values = hidden.reshape(-1, hidden.shape[-1]).astype(F32)
    return jnp.sum(values, axis=0, keepdims=True), jnp.sum(values * values, axis=0, keepdims=True)


def over_group(values, size):
    lane = iota(values.shape, 1)
    lanes = values.shape[1]
    step = 1
    while step < size:
        later = pltpu.roll(values, lanes - step, 1)
        earlier = pltpu.roll(values, step, 1)
        values = values + jnp.where((lane & step) == 0, later, earlier)
        step *= 2
    return values


def group_sums(hidden):
    channels = hidden.shape[-1]
    size = channels // GROUPS
    first, second = [
        over_group(jnp.broadcast_to(x, (8, channels)), size) for x in channel_sums(hidden)
    ]
    lane = mod(iota((8, channels), 1), size)
    return jnp.where(lane == 0, first, jnp.where(lane == 1, second, 0.0))


def pull_back(row, weight):
    parts = []
    for low in range(0, weight.shape[0], LANES):
        product = weight[low : low + LANES, :].astype(F32) * row
        folded = product[:, :LANES]
        for start in range(LANES, weight.shape[1], LANES):
            folded = folded + product[:, start : start + LANES]
        parts.append(jnp.sum(folded.T, axis=0, keepdims=True))
    return jnp.concatenate(parts, axis=1)


def backward_part(
    owner, picks, gain, head_bias, head_out, normed, inv_spread, pooled, weight, head, through_head, slot, own_rows, height, sums, send
):
    (before,) = exact_rows([pooled], through_head)
    slope = head_out[...] * silu_slope(before + head_bias[...])
    pulled = pull_back(slope, head)
    wanted = owner[slot]
    picked = jnp.int32(0)
    for k in range(picks.shape[0]):
        picked = picked + jnp.where(picks[k] == wanted, 1, 0)
    scaled = gain[...] * (picked.astype(F32) * pulled)
    token_grad = inv_spread * (
        scaled
        - jnp.mean(scaled, axis=1, keepdims=True)
        - normed * jnp.mean(scaled * normed, axis=1, keepdims=True)
    )
    filler = jnp.zeros((-token_grad.shape[0] % 16, token_grad.shape[1]), F32)
    token_grad = jnp.concatenate([token_grad, filler], axis=0).astype(BF16)
    patch_grad = matmul_t(token_grad, weight[...]).astype(BF16).astype(F32)
    write_windows(patch_grad, sums, own_rows, height, send)


def write_edges(position, hidden, across, along):
    last = hidden.shape[0] - 1
    even = position % 2 == 0
    across[0] = hidden[jnp.where(even, last, 0)]
    along[0] = hidden[jnp.where(even, 0, last)]


def reward_kernel(*refs):
    position = lax.axis_index("row")
    count, kept = 7, 4
    far, refs = refs[: count + kept + 2], refs[count + kept + 2 :]
    send, across, along = refs[:3]
    near = refs[3 + kept : 3 + kept + count] + refs[3 : 3 + kept] + refs[3 + kept + count : -1]
    sems = refs[-1]
    frames, bias, gain, owner, picks, head_bias, head_out, hidden, _, _, _, patch, head = near
    count += kept
    depths = (256, 256)
    small = [pltpu.make_async_copy(far[i], near[i], sems.at[i]) for i in range(count)]
    pieces = []
    used = count
    for index, rows in enumerate(depths):
        source, target = far[count + index], near[count + index]
        parts = []
        for low in range(0, target.shape[0], rows):
            part = pl.ds(low, rows)
            parts.append(pltpu.make_async_copy(source.at[part], target.at[part], sems.at[used]))
            used += 1
        pieces.append(parts)
    for copy in [small[0], small[7]] + pieces[0] + small[1:7]:
        copy.start()

    def load_patch():
        for copy in pieces[0] + small[1:3]:
            copy.wait()
        yield 0, patch.shape[0], patch[...]

    height = frames.shape[2]
    patches = height // PATCH
    small[0].wait()
    for copy in pieces[1] + small[8:]:
        copy.start()
    small[7].wait()
    tokens = to_tokens(frames[...])
    sums = group_sums(hidden[...])
    write_edges(position, hidden, across, along)
    normed, inv_spread, pooled = forward_part(tokens, patches, bias, gain, load_patch)
    for copy in small[3:7]:
        copy.wait()

    def through_head(rows):
        total = jnp.zeros((rows.shape[0], head.shape[1]), F32)
        for index, low in enumerate(range(0, head.shape[0], depths[1])):
            pieces[1][index].wait()
            total = total + matmul(rows[:, low : low + depths[1]], head[low : low + depths[1], :])
        return total

    backward_part(
        owner,
        picks,
        gain,
        head_bias,
        head_out,
        normed,
        inv_spread,
        pooled / patches,
        patch,
        head,
        through_head,
        position,
        hidden.shape[0],
        height,
        sums,
        send,
    )
    for copy in small[8:]:
        copy.wait()


def forward_kernel(frames, bias, gain, patch, normed, inv_spread, pooled):
    width = patch.shape[0]
    tokens = to_tokens(frames[...])
    normed[...], spread, pooled[...] = forward_part(
        tokens, frames.shape[2] // PATCH, bias, gain, lambda: [(0, width, patch[...])]
    )
    inv_spread[...] = jnp.broadcast_to(spread, inv_spread.shape)


def backward_kernel(
    owner,
    picks,
    hidden,
    gain,
    head_bias,
    head_out,
    normed,
    inv_spread,
    pooled,
    patch,
    head,
    send,
    across,
    along,
    *,
    height,
    per_frame,
):
    position = lax.axis_index("row")
    write_edges(position, hidden, across, along)
    backward_part(
        owner,
        picks,
        gain,
        head_bias,
        head_out,
        normed[...],
        inv_spread[...][:, :1],
        pooled[...],
        patch,
        head,
        lambda rows: matmul(rows, head[...]),
        position // per_frame,
        hidden.shape[0],
        height,
        group_sums(hidden[...]),
        send,
    )


def params(cells):
    return pltpu.CompilerParams(vmem_limit_bytes=min(16 + cells // 64, 48) * 1024 * 1024)


def near(array):
    return pltpu.with_memory_space_constraint(array, pltpu.VMEM)


def far(array):
    return pltpu.with_memory_space_constraint(array, pltpu.HBM)


def tap_lane(j, k, e):
    return (j + 1) * PATCH + 4 * k + e


def prepare_kernel(out_weight, wide, scratch):
    amount = scratch.shape[1] // LANES
    scratch[...] = jnp.zeros_like(scratch)
    for a in range(3):
        for e in range(3):
            for b in range(3):
                piece = out_weight[a, b, e].astype(F32)
                for i in range(amount):
                    for k in range(3):
                        at = a * LANES + tap_lane(i - b + 2, k, e)
                        scratch[at : at + 1, i * LANES : (i + 1) * LANES] = piece[k : k + 1]
    wide[...] = scratch[...].astype(BF16)


def norm_constants(totals, cell_total):
    channels = totals.shape[1]
    size = channels // GROUPS
    totals = jnp.broadcast_to(totals, (8, channels))
    lane = mod(iota((8, channels), 1), size)
    first, second = [over_group(jnp.where(lane == i, totals, 0.0), size)[:1] for i in range(2)]
    mean = first / cell_total
    return mean, lax.rsqrt(second / cell_total - mean * mean + eps_norm)


def norm_slopes(state, mean, inverse, gain, shift):
    normed = (state - mean) * inverse
    return normed, silu_slope(normed * gain + shift) * gain


def slope_kernel(
    arrived,
    hidden,
    gain,
    shift,
    wide,
    far_owner,
    direct,
    edge_slopes,
    stats,
    sums,
    slopes_own,
    received,
    taps,
    owner,
    sem,
):
    copy = pltpu.make_async_copy(far_owner, owner, sem.at[0])
    copy.start()
    devices, message_rows, _ = arrived.shape
    own_rows, frame_count, width, channels = hidden.shape
    cells = frame_count * width
    per_frame = devices // frame_count
    got = arrived[...].reshape(received.shape)
    kind = mod(iota((got.shape[0], 1), 0), message_rows)
    totals = jnp.sum(jnp.where(kind == 3, got, 0.0), axis=0, keepdims=True)
    mean, inverse = norm_constants(totals, own_rows * devices * cells * (channels // GROUPS))
    for i in range(own_rows):
        state = hidden[i].reshape(cells, channels).astype(F32)
        slopes_own[i] = norm_slopes(state, mean, inverse, gain[...], shift[...])[1] * inverse

    if per_frame == 1:
        lane = iota((1, LANES), 1)
        entry = iota((LANES, 1), 0)
        turned = ones_where(entry - mod(entry, PATCH) + PATCH - 1 - mod(entry, PATCH) == lane)
        received[...] = matmul(jnp.where(kind < 3, got, 0.0).astype(BF16), turned)
        lane = mod(iota((PATCH, LANES), 1), PATCH)
        column = iota((PATCH, LANES), 0)
        marks = []
        for k in range(3):
            e = lane - 4 * k
            wanted = column - e + 1
            marks.append((e >= 0) & (e < 3) & (wanted >= 0) & (wanted < PATCH))
        copy.wait()
        for d in range(devices):
            row = first_order(devices)[d]
            block = jnp.zeros((PATCH, LANES), F32)
            for k in range(3):
                line = jnp.broadcast_to(received[d * message_rows + k : d * message_rows + k + 1, :], (PATCH, LANES))
                line = pltpu.roll(line, 4 * k + 2, 1, stride=1, stride_axis=0)
                block = jnp.where(marks[k], line, block)
            start = pl.multiple_of(owner[row] * PATCH, PATCH)
            taps[pl.ds(start, PATCH), :] = block.astype(BF16)
    else:
        copy.wait()
        received[...] = got
        lines = [received[pl.ds(k, devices, stride=message_rows), :] for k in range(3)]
        lines = jnp.concatenate(lines, axis=1).astype(BF16)
        place = iota((1, devices), 1)
        source = jnp.zeros_like(place)
        for index, d in enumerate(first_order(devices)):
            source = jnp.where(place == index, d, source)
        home = jnp.zeros((1, devices), jnp.int32)
        for b in range(frame_count):
            home = jnp.where(div(source, per_frame) == b, owner[b] * per_frame, home)
        home = home + mod(source, per_frame)
        cell = iota((cells, 1), 0)
        column = mod(cell, width)
        lane = mod(iota((1, 3 * LANES), 1), PATCH)
        entry = iota((3 * LANES, 1), 0)
        window_row = div(mod(entry, LANES), PATCH)
        found = jnp.zeros((cells, LANES), F32)
        for e in range(3):
            wanted = column - e + 1
            strip = div(cell, width) * per_frame + div(wanted, PATCH)
            placed = matmul(ones_where(home == strip), lines)
            inside = jnp.where((wanted >= 0) & (wanted < width), mod(wanted, PATCH), -1)
            kept = jnp.where(lane == inside, placed, 0.0).astype(BF16)
            target = jnp.where(
                window_row < own_rows + 4, tap_lane(window_row, div(entry, LANES), e), -1
            )
            found = found + matmul(kept, ones_where(target == iota((1, LANES), 1)))
        taps[:cells, :] = found.astype(BF16)
    taps[cells:, :] = jnp.zeros((2 * width, LANES), BF16)
    steps = [taps[(2 - a) * width : (2 - a) * width + cells, :] for a in range(3)]
    result = matmul(jnp.concatenate(steps, axis=1), wide[...])

    first = jnp.zeros((1, channels), F32)
    second = jnp.zeros((1, channels), F32)
    for i in range(own_rows):
        state = hidden[i].reshape(cells, channels).astype(F32)
        part = result[:, (i + 1) * channels : (i + 2) * channels] * slopes_own[i]
        direct[i] = part
        first = first + jnp.sum(part, axis=0, keepdims=True)
        second = second + jnp.sum(part * (state - mean), axis=0, keepdims=True)
    first = first / inverse
    edge_slopes[0] = result[:, :channels]
    edge_slopes[1] = result[:, (own_rows + 1) * channels :]
    stats[0:1, :] = mean
    stats[1:2, :] = inverse
    both = jnp.where(iota((2, channels), 0) == 0, first, second)
    sums[...] = jnp.broadcast_to(both[None], sums.shape)


def late_kernel(
    across, along, slopes, stats, gain, shift, far_weight, direct, states, turned, inner_weight, sem
):
    copy = pltpu.make_async_copy(far_weight, inner_weight, sem.at[0])
    copy.start()
    cells, channels = slopes.shape[1:]
    odd = lax.axis_index("row") % 2 == 1
    mean = stats[0:1, :]
    inverse = stats[1:2, :]
    for i in range(2):
        state = jnp.where(odd == (i == 0), across[0], along[0])
        states[i] = state
        values = state.reshape(cells, channels).astype(F32)
        direct[i] = slopes[i] * norm_slopes(values, mean, inverse, gain[...], shift[...])[1] * inverse
    copy.wait()
    size = inner_weight.shape[3]
    for b in range(3):
        for a in range(3):
            for e in range(3):
                at = (a * 3 + e) * size
                turned[at : at + size, b * size : (b + 1) * size] = inner_weight[a, b, e].T


def inner_kernel(
    arrived, stats, direct, hidden, edge_direct, edge_states, turned, far_out, out, sems, *, devices
):
    own_rows, frame_count, width, channels = out.shape
    cells = frame_count * width
    totals = jnp.sum(arrived[...], axis=0)
    cell_total = own_rows * devices * cells * (channels // GROUPS)
    place_row = iota((8, channels), 0)
    both = jnp.where(place_row == 0, totals[0:1], totals[1:2])
    both = over_group(both, channels // GROUPS)
    first, second = both[0:1], both[1:2]
    mean = stats[0:1, :]
    inverse = stats[1:2, :]
    constant = first / cell_total * inverse
    factor = second / cell_total * inverse * inverse
    position = lax.axis_index("row")
    in_frame = mod(iota((cells, 1), 0), width)
    results = [jnp.zeros((cells, channels), F32) for _ in range(own_rows)]
    copies = []
    for i in range(own_rows + 2):
        if 0 < i < own_rows + 1:
            state, part = hidden[i - 1], direct[i - 1]
        else:
            state, part = edge_states[min(i, 1)], edge_direct[min(i, 1)]
        grad = part - constant - (state.reshape(cells, channels).astype(F32) - mean) * factor
        if i == 0:
            grad = jnp.where(position > 0, grad, 0.0)
        if i == own_rows + 1:
            grad = jnp.where(position < devices - 1, grad, 0.0)
        after = jnp.where(in_frame < width - 1, pltpu.roll(grad, cells - 1, 0), 0.0)
        prior = jnp.where(in_frame > 0, pltpu.roll(grad, 1, 0), 0.0)
        taps = jnp.concatenate([after.astype(BF16), grad.astype(BF16), prior.astype(BF16)], axis=1)
        later = []
        for a in range(3):
            skip = (2 - a) * width
            filler = jnp.zeros((skip, taps.shape[1]), BF16)
            later.append(jnp.concatenate([taps[skip:], filler], axis=0) if skip else taps)
        joined = jnp.concatenate(later, axis=1)
        rows = [b for b in range(3) if 0 <= i + b - 2 < own_rows]
        for low in range(0, len(rows), 2):
            some = rows[low : low + 2]
            product = matmul(joined, turned[:, some[0] * channels : (some[-1] + 1) * channels])
            for step, b in enumerate(some):
                results[i + b - 2] = results[i + b - 2] + product[:, step * channels : (step + 1) * channels]
        if i >= 2:
            out[i - 2] = results[i - 2].reshape(frame_count, width, channels).astype(BF16)
            copies.append(pltpu.make_async_copy(out.at[i - 2], far_out.at[i - 2], sems.at[i - 2]))
            copies[-1].start()
    for copy in copies:
        copy.wait()


def per_device(
    frames,
    frame_owner,
    picks,
    patch_weight,
    patch_bias,
    norm_gain,
    head_weight,
    head_bias,
    head_out,
    hidden_state,
    group_gain,
    group_shift,
    out_weight,
    inner_weight,
):
    devices = lax.axis_size("row")
    per_frame = devices // FRAMES
    height = frames.shape[1]
    own_rows, _, frame_width, channels = hidden_state.shape
    cells = FRAMES * frame_width
    width = patch_weight.shape[1]
    turned_frames = jnp.transpose(frames, (0, 2, 1))
    bias = patch_bias.reshape(1, width)
    gain = norm_gain.reshape(1, width)
    head_bias_row = head_bias.reshape(1, width)
    head_out_row = head_out.reshape(1, width)
    state_rows = own_rows + 2
    edge = jax.ShapeDtypeStruct((1,) + hidden_state.shape[1:], BF16)
    message = (message_shape(devices), edge, edge)
    gain_row = group_gain.reshape(1, channels)
    shift_row = group_shift.reshape(1, channels)
    early = [hidden_state, gain_row, shift_row, out_weight]
    slope_outs = (
        pltpu.VMEM((own_rows, cells, channels), F32),
        pltpu.VMEM((2, cells, channels), F32),
        pltpu.VMEM((8, channels), F32),
        jax.ShapeDtypeStruct((devices, 2, channels), F32),
    )
    if per_frame == 1:
        arrays = [turned_frames, bias, gain, frame_owner, picks, head_bias_row, head_out_row]
        weights = [patch_weight, head_weight]

        def scratch(x):
            return (pltpu.SMEM if x.dtype == jnp.int32 else pltpu.VMEM)(x.shape, x.dtype)

        send, across, along, *early = pl.pallas_call(
            reward_kernel,
            out_shape=message + tuple(pltpu.VMEM(x.shape, x.dtype) for x in early),
            in_specs=[FAR] * (len(arrays) + len(early) + len(weights)),
            out_specs=[VMEM] * (3 + len(early)),
            scratch_shapes=[scratch(x) for x in arrays + weights] + [pltpu.SemaphoreType.DMA((32,))],
            compiler_params=params(0),
            name="reward",
        )(*[far(x) for x in arrays + early + weights])
    else:
        count = height // PATCH
        normed, inv_spread, partial = pl.pallas_call(
            forward_kernel,
            out_shape=(
                jax.ShapeDtypeStruct((-(-count // 8) * 8, width), F32),
                jax.ShapeDtypeStruct((-(-count // 8) * 8, LANES), F32),
                jax.ShapeDtypeStruct((1, width), F32),
            ),
            compiler_params=params(cells),
            name="reward_forward",
        )(turned_frames, bias, gain, patch_weight)
        members = [[b * per_frame + i for i in range(per_frame)] for b in range(FRAMES)]
        pooled = lax.psum(partial, "row", axis_index_groups=members) / (count * per_frame)
        send, across, along = pl.pallas_call(
            functools.partial(backward_kernel, height=height, per_frame=per_frame),
            out_shape=message,
            in_specs=[SMEM] * 2 + [VMEM] * 9,
            out_specs=[VMEM] * 3,
            compiler_params=params(cells),
            name="reward_backward",
        )(
            frame_owner,
            picks,
            hidden_state,
            gain,
            head_bias_row,
            head_out_row,
            normed,
            inv_spread,
            pooled,
            patch_weight,
            head_weight,
        )
    early = [near(x) for x in early]
    wide = pl.pallas_call(
        prepare_kernel,
        out_shape=pltpu.VMEM((3 * LANES, state_rows * channels), BF16),
        in_specs=[VMEM],
        scratch_shapes=[pltpu.VMEM((3 * LANES, state_rows * channels), F32)],
        compiler_params=params(cells),
        name="prepare",
    )(early[3])
    arrived = lax.all_to_all(send, "row", 0, 0, axis_index_groups=[first_order(devices)], tiled=True)
    direct, edge_slopes, stats, sums = pl.pallas_call(
        slope_kernel,
        out_shape=slope_outs,
        in_specs=[VMEM] * 5 + [FAR],
        scratch_shapes=[
            pltpu.VMEM((own_rows, cells, channels), F32),
            pltpu.VMEM((4 * devices, LANES), F32),
            pltpu.VMEM((cells + 2 * frame_width, LANES), BF16),
            pltpu.SMEM(frame_owner.shape, jnp.int32),
            pltpu.SemaphoreType.DMA((1,)),
        ],
        compiler_params=params(cells),
        name="slope",
    )(near(arrived), *early[:3], near(wide), far(frame_owner))
    swaps = [(2 * i, 2 * i + 1) for i in range(devices // 2)]
    across = lax.ppermute(across, "row", swaps + [(b, a) for a, b in swaps])
    swaps = [(2 * i - 1, 2 * i) for i in range(1, devices // 2)]
    along = lax.ppermute(along, "row", swaps + [(b, a) for a, b in swaps])
    summed = lax.all_to_all(sums, "row", 0, 0, axis_index_groups=[led_by(devices - 1, devices)], tiled=True)
    edge_direct, edge_states, turned = pl.pallas_call(
        late_kernel,
        out_shape=(
            pltpu.VMEM((2, cells, channels), F32),
            pltpu.VMEM((2,) + hidden_state.shape[1:], BF16),
            pltpu.VMEM((9 * channels, 3 * channels), BF16),
        ),
        in_specs=[VMEM] * 6 + [FAR],
        scratch_shapes=[pltpu.VMEM(inner_weight.shape, BF16), pltpu.SemaphoreType.DMA((1,))],
        input_output_aliases={2: 0},
        compiler_params=params(cells),
        name="late",
    )(near(across), near(along), near(edge_slopes), near(stats), *early[1:3], far(inner_weight))
    return pl.pallas_call(
        functools.partial(inner_kernel, devices=devices),
        out_shape=jax.ShapeDtypeStruct(hidden_state.shape, BF16),
        in_specs=[VMEM] * 7,
        out_specs=FAR,
        scratch_shapes=[
            pltpu.VMEM(hidden_state.shape, BF16),
            pltpu.SemaphoreType.DMA((own_rows,)),
        ],
        compiler_params=params(cells),
        name="inner",
    )(
        near(summed),
        near(stats),
        near(direct),
        early[0],
        near(edge_direct),
        near(edge_states),
        near(turned),
    )


def solution(mesh):
    return jax.shard_map(
        per_device,
        mesh=mesh,
        in_specs=(
            P(None, None, ("clip", "row")),
            P("clip"),
            P("clip"),
            P(),
            P(),
            P(),
            P(),
            P(),
            P(),
            P(("clip", "row"), None, None, None),
            P(),
            P(),
            P(),
            P(),
        ),
        out_specs=P(("clip", "row"), None, None, None),
        check_vma=False,
    )
```

```python
import functools

import jax
import jax.numpy as jnp
from jax import lax
from jax.experimental import pallas as pl
from jax.experimental.pallas import tpu as pltpu
from jax.sharding import PartitionSpec as P

PATCH = 16
GROUPS = 32
FRAMES = 16
LANES = 128
SLOTS = LANES // PATCH
eps_norm = 1e-06
BF16 = jnp.bfloat16
F32 = jnp.float32

SMEM = pl.BlockSpec(memory_space=pltpu.SMEM)
VMEM = pl.BlockSpec(memory_space=pltpu.VMEM)
FAR = pl.BlockSpec(memory_space=pl.ANY)


def iota(shape, dim):
    return lax.broadcasted_iota(jnp.int32, shape, dim)


def div(values, count):
    if count & (count - 1):
        return values // count
    return values >> (count.bit_length() - 1)


def mod(values, count):
    if count & (count - 1):
        return values % count
    return values & (count - 1)


def ones_where(condition):
    return jnp.where(condition, 1.0, 0.0).astype(BF16)


def matmul(left, right):
    return jnp.dot(left, right, preferred_element_type=F32)


def matmul_t(left, right):
    return lax.dot_general(left, right, (((1,), (1,)), ((), ())), preferred_element_type=F32)


def cut_in_three(values):
    high = values.astype(BF16)
    rest = values - high.astype(F32)
    middle = rest.astype(BF16)
    low = (rest - middle.astype(F32)).astype(BF16)
    return high, middle, low


def exact_rows(rows, product):
    place = iota((8, rows[0].shape[1]), 0)
    stacked = jnp.zeros(place.shape, F32)
    for index, row in enumerate(rows):
        for step, piece in enumerate(cut_in_three(row)):
            stacked = jnp.where(place == 3 * index + step, piece.astype(F32), stacked)
    result = product(jnp.concatenate([stacked, jnp.zeros_like(stacked)], axis=0).astype(BF16))
    return [
        result[3 * i : 3 * i + 1] + result[3 * i + 1 : 3 * i + 2] + result[3 * i + 2 : 3 * i + 3]
        for i in range(len(rows))
    ]


def silu_slope(values):
    sigmoid = 0.5 + 0.5 * jnp.tanh(0.5 * values)
    return sigmoid * (1.0 + values * (1.0 - sigmoid))


def token_rows_of(height):
    return -(-(height // PATCH) // 16) * 16


def to_tokens(pixels):
    channels, columns, height = pixels.shape
    rows = channels * columns
    token_rows = token_rows_of(height)
    flat = pixels.reshape(rows, height)
    width = channels * PATCH * columns
    lane = iota((1, width), 1)
    place = iota((rows, 1), 0)
    mine = place == div(lane, PATCH * columns) * columns + mod(lane, columns)
    in_patch = mod(div(lane, columns), PATCH)
    pixel_row = iota((height, 1), 0)
    token = iota((token_rows, 1), 0)
    tokens = jnp.zeros((token_rows, width), F32)
    for t in range(height // PATCH):
        tiled = matmul(flat, ones_where(pixel_row == in_patch + t * PATCH))
        row = jnp.sum(jnp.where(mine, tiled, 0.0), axis=0, keepdims=True)
        tokens = jnp.where(token == t, row, tokens)
    return tokens.astype(BF16)


def forward_part(tokens, count, bias, gain, load_patch):
    embedded = jnp.zeros((tokens.shape[0], bias.shape[1]), F32)
    for low, high, weight in load_patch():
        embedded = embedded + matmul(tokens[:, low:high], weight)
    rows = -(-count // 8) * 8
    embedded = embedded[:rows] + bias[...]
    centred = embedded - jnp.mean(embedded, axis=1, keepdims=True)
    inv_spread = lax.rsqrt(jnp.mean(centred * centred, axis=1, keepdims=True) + eps_norm)
    normed = centred * inv_spread
    weighted = normed * gain[...]
    inside = iota((rows, 1), 0) < count
    pooled = jnp.sum(jnp.where(inside, weighted, 0.0), axis=0, keepdims=True)
    return normed, inv_spread, pooled


def led_by(leader, devices):
    return [leader] + [d for d in reversed(range(devices)) if d != leader]


def first_order(devices):
    return led_by(devices * 13 // 16, devices)


def message_shape(devices):
    return jax.ShapeDtypeStruct((devices, 4, LANES), F32)


def write_windows(patch_grad, sums, own_rows, height, send):
    span = PATCH * PATCH
    line = jnp.concatenate(
        [
            jnp.concatenate([patch_grad[t : t + 1, k * span : (k + 1) * span] for t in range(height // PATCH)], axis=1)
            for k in range(3)
        ]
        + [jnp.zeros((1, height * PATCH), F32)],
        axis=0,
    )
    line = jnp.concatenate([jnp.zeros((4, LANES), F32), line, jnp.zeros((4, LANES), F32)], axis=1)
    used = iota((4, LANES), 1) < (own_rows + 4) * PATCH
    colour = iota((4, LANES), 0)
    for index, d in enumerate(first_order(send.shape[0])):
        start = LANES + (d * own_rows - 2) * PATCH
        window = jnp.where(used, line[:, start : start + LANES], 0.0)
        send[index] = jnp.where(colour < 3, window, sums[:4])


def channel_sums(hidden):
    values = hidden.reshape(-1, hidden.shape[-1]).astype(F32)
    return jnp.sum(values, axis=0, keepdims=True), jnp.sum(values * values, axis=0, keepdims=True)


def over_group(values, size):
    lane = iota(values.shape, 1)
    lanes = values.shape[1]
    step = 1
    while step < size:
        later = pltpu.roll(values, lanes - step, 1)
        earlier = pltpu.roll(values, step, 1)
        values = values + jnp.where((lane & step) == 0, later, earlier)
        step *= 2
    return values


def group_sums(hidden):
    channels = hidden.shape[-1]
    size = channels // GROUPS
    first, second = [
        over_group(jnp.broadcast_to(x, (8, channels)), size) for x in channel_sums(hidden)
    ]
    lane = mod(iota((8, channels), 1), size)
    return jnp.where(lane == 0, first, jnp.where(lane == 1, second, 0.0))


def pull_back(row, weight):
    parts = []
    for low in range(0, weight.shape[0], LANES):
        product = weight[low : low + LANES, :].astype(F32) * row
        folded = product[:, :LANES]
        for start in range(LANES, weight.shape[1], LANES):
            folded = folded + product[:, start : start + LANES]
        parts.append(jnp.sum(folded.T, axis=0, keepdims=True))
    return jnp.concatenate(parts, axis=1)


def backward_part(
    owner, picks, gain, head_bias, head_out, normed, inv_spread, pooled, weight, head, through_head, slot, own_rows, height, sums, send
):
    (before,) = exact_rows([pooled], through_head)
    slope = head_out[...] * silu_slope(before + head_bias[...])
    pulled = pull_back(slope, head)
    wanted = owner[slot]
    picked = jnp.int32(0)
    for k in range(picks.shape[0]):
        picked = picked + jnp.where(picks[k] == wanted, 1, 0)
    scaled = gain[...] * (picked.astype(F32) * pulled)
    token_grad = inv_spread * (
        scaled
        - jnp.mean(scaled, axis=1, keepdims=True)
        - normed * jnp.mean(scaled * normed, axis=1, keepdims=True)
    )
    filler = jnp.zeros((-token_grad.shape[0] % 16, token_grad.shape[1]), F32)
    token_grad = jnp.concatenate([token_grad, filler], axis=0).astype(BF16)
    patch_grad = matmul_t(token_grad, weight[...]).astype(BF16).astype(F32)
    write_windows(patch_grad, sums, own_rows, height, send)


def write_edges(position, hidden, across, along):
    last = hidden.shape[0] - 1
    even = position % 2 == 0
    across[0] = hidden[jnp.where(even, last, 0)]
    along[0] = hidden[jnp.where(even, 0, last)]


def reward_kernel(*refs):
    position = lax.axis_index("row")
    count, kept = 7, 4
    far, refs = refs[: count + kept + 2], refs[count + kept + 2 :]
    send, across, along = refs[:3]
    near = refs[3 + kept : 3 + kept + count] + refs[3 : 3 + kept] + refs[3 + kept + count : -1]
    sems = refs[-1]
    frames, bias, gain, owner, picks, head_bias, head_out, hidden, _, _, _, patch, head = near
    count += kept
    depths = (256, 256)
    small = [pltpu.make_async_copy(far[i], near[i], sems.at[i]) for i in range(count)]
    pieces = []
    used = count
    for index, rows in enumerate(depths):
        source, target = far[count + index], near[count + index]
        parts = []
        for low in range(0, target.shape[0], rows):
            part = pl.ds(low, rows)
            parts.append(pltpu.make_async_copy(source.at[part], target.at[part], sems.at[used]))
            used += 1
        pieces.append(parts)
    for copy in [small[0], small[7]] + pieces[0] + small[1:7] + pieces[1] + small[8:]:
        copy.start()

    def load_patch():
        for copy in pieces[0] + small[1:3]:
            copy.wait()
        yield 0, patch.shape[0], patch[...]

    height = frames.shape[2]
    patches = height // PATCH
    small[0].wait()
    small[7].wait()
    tokens = to_tokens(frames[...])
    sums = group_sums(hidden[...])
    write_edges(position, hidden, across, along)
    normed, inv_spread, pooled = forward_part(tokens, patches, bias, gain, load_patch)
    for copy in small[3:7]:
        copy.wait()

    def through_head(rows):
        total = jnp.zeros((rows.shape[0], head.shape[1]), F32)
        for index, low in enumerate(range(0, head.shape[0], depths[1])):
            pieces[1][index].wait()
            total = total + matmul(rows[:, low : low + depths[1]], head[low : low + depths[1], :])
        return total

    backward_part(
        owner,
        picks,
        gain,
        head_bias,
        head_out,
        normed,
        inv_spread,
        pooled / patches,
        patch,
        head,
        through_head,
        position,
        hidden.shape[0],
        height,
        sums,
        send,
    )
    for copy in small[8:]:
        copy.wait()


def forward_kernel(frames, bias, gain, patch, normed, inv_spread, pooled):
    width = patch.shape[0]
    tokens = to_tokens(frames[...])
    normed[...], spread, pooled[...] = forward_part(
        tokens, frames.shape[2] // PATCH, bias, gain, lambda: [(0, width, patch[...])]
    )
    inv_spread[...] = jnp.broadcast_to(spread, inv_spread.shape)


def backward_kernel(
    owner,
    picks,
    hidden,
    gain,
    head_bias,
    head_out,
    normed,
    inv_spread,
    pooled,
    patch,
    head,
    send,
    across,
    along,
    *,
    height,
    per_frame,
):
    position = lax.axis_index("row")
    write_edges(position, hidden, across, along)
    backward_part(
        owner,
        picks,
        gain,
        head_bias,
        head_out,
        normed[...],
        inv_spread[...][:, :1],
        pooled[...],
        patch,
        head,
        lambda rows: matmul(rows, head[...]),
        position // per_frame,
        hidden.shape[0],
        height,
        group_sums(hidden[...]),
        send,
    )


def params(cells):
    return pltpu.CompilerParams(vmem_limit_bytes=min(16 + cells // 64, 48) * 1024 * 1024)


def near(array):
    return pltpu.with_memory_space_constraint(array, pltpu.VMEM)


def far(array):
    return pltpu.with_memory_space_constraint(array, pltpu.HBM)


def tap_lane(j, k, e):
    return (j + 1) * PATCH + 4 * k + e


def prepare_kernel(out_weight, wide, scratch):
    amount = scratch.shape[1] // LANES
    scratch[...] = jnp.zeros_like(scratch)
    for a in range(3):
        for e in range(3):
            for b in range(3):
                piece = out_weight[a, b, e].astype(F32)
                for i in range(amount):
                    for k in range(3):
                        at = a * LANES + tap_lane(i - b + 2, k, e)
                        scratch[at : at + 1, i * LANES : (i + 1) * LANES] = piece[k : k + 1]
    wide[...] = scratch[...].astype(BF16)


def norm_constants(totals, cell_total):
    channels = totals.shape[1]
    size = channels // GROUPS
    totals = jnp.broadcast_to(totals, (8, channels))
    lane = mod(iota((8, channels), 1), size)
    first, second = [over_group(jnp.where(lane == i, totals, 0.0), size)[:1] for i in range(2)]
    mean = first / cell_total
    return mean, lax.rsqrt(second / cell_total - mean * mean + eps_norm)


def norm_slopes(state, mean, inverse, gain, shift):
    normed = (state - mean) * inverse
    return normed, silu_slope(normed * gain + shift) * gain


def slope_kernel(
    arrived,
    hidden,
    gain,
    shift,
    wide,
    far_owner,
    direct,
    edge_slopes,
    stats,
    sums,
    slopes_own,
    received,
    taps,
    owner,
    sem,
):
    copy = pltpu.make_async_copy(far_owner, owner, sem.at[0])
    copy.start()
    devices, message_rows, _ = arrived.shape
    own_rows, frame_count, width, channels = hidden.shape
    cells = frame_count * width
    per_frame = devices // frame_count
    got = arrived[...].reshape(received.shape)
    kind = mod(iota((got.shape[0], 1), 0), message_rows)
    totals = jnp.sum(jnp.where(kind == 3, got, 0.0), axis=0, keepdims=True)
    mean, inverse = norm_constants(totals, own_rows * devices * cells * (channels // GROUPS))
    for i in range(own_rows):
        state = hidden[i].reshape(cells, channels).astype(F32)
        slopes_own[i] = norm_slopes(state, mean, inverse, gain[...], shift[...])[1] * inverse

    if per_frame == 1:
        lane = iota((1, LANES), 1)
        entry = iota((LANES, 1), 0)
        turned = ones_where(entry - mod(entry, PATCH) + PATCH - 1 - mod(entry, PATCH) == lane)
        received[...] = matmul(jnp.where(kind < 3, got, 0.0).astype(BF16), turned)
        lane = mod(iota((PATCH, LANES), 1), PATCH)
        column = iota((PATCH, LANES), 0)
        marks = []
        for k in range(3):
            e = lane - 4 * k
            wanted = column - e + 1
            marks.append((e >= 0) & (e < 3) & (wanted >= 0) & (wanted < PATCH))
        copy.wait()
        for d in range(devices):
            row = first_order(devices)[d]
            block = jnp.zeros((PATCH, LANES), F32)
            for k in range(3):
                line = jnp.broadcast_to(received[d * message_rows + k : d * message_rows + k + 1, :], (PATCH, LANES))
                line = pltpu.roll(line, 4 * k + 2, 1, stride=1, stride_axis=0)
                block = jnp.where(marks[k], line, block)
            start = pl.multiple_of(owner[row] * PATCH, PATCH)
            taps[pl.ds(start, PATCH), :] = block.astype(BF16)
    else:
        copy.wait()
        received[...] = got
        lines = [received[pl.ds(k, devices, stride=message_rows), :] for k in range(3)]
        lines = jnp.concatenate(lines, axis=1).astype(BF16)
        place = iota((1, devices), 1)
        source = jnp.zeros_like(place)
        for index, d in enumerate(first_order(devices)):
            source = jnp.where(place == index, d, source)
        home = jnp.zeros((1, devices), jnp.int32)
        for b in range(frame_count):
            home = jnp.where(div(source, per_frame) == b, owner[b] * per_frame, home)
        home = home + mod(source, per_frame)
        cell = iota((cells, 1), 0)
        column = mod(cell, width)
        lane = mod(iota((1, 3 * LANES), 1), PATCH)
        entry = iota((3 * LANES, 1), 0)
        window_row = div(mod(entry, LANES), PATCH)
        found = jnp.zeros((cells, LANES), F32)
        for e in range(3):
            wanted = column - e + 1
            strip = div(cell, width) * per_frame + div(wanted, PATCH)
            placed = matmul(ones_where(home == strip), lines)
            inside = jnp.where((wanted >= 0) & (wanted < width), mod(wanted, PATCH), -1)
            kept = jnp.where(lane == inside, placed, 0.0).astype(BF16)
            target = jnp.where(
                window_row < own_rows + 4, tap_lane(window_row, div(entry, LANES), e), -1
            )
            found = found + matmul(kept, ones_where(target == iota((1, LANES), 1)))
        taps[:cells, :] = found.astype(BF16)
    taps[cells:, :] = jnp.zeros((2 * width, LANES), BF16)
    steps = [taps[(2 - a) * width : (2 - a) * width + cells, :] for a in range(3)]
    result = matmul(jnp.concatenate(steps, axis=1), wide[...])

    first = jnp.zeros((1, channels), F32)
    second = jnp.zeros((1, channels), F32)
    for i in range(own_rows):
        state = hidden[i].reshape(cells, channels).astype(F32)
        part = result[:, (i + 1) * channels : (i + 2) * channels] * slopes_own[i]
        direct[i] = part
        first = first + jnp.sum(part, axis=0, keepdims=True)
        second = second + jnp.sum(part * (state - mean), axis=0, keepdims=True)
    first = first / inverse
    edge_slopes[0] = result[:, :channels]
    edge_slopes[1] = result[:, (own_rows + 1) * channels :]
    stats[0:1, :] = mean
    stats[1:2, :] = inverse
    both = jnp.where(iota((2, channels), 0) == 0, first, second)
    sums[...] = jnp.broadcast_to(both[None], sums.shape)


def late_kernel(
    across, along, slopes, stats, gain, shift, far_weight, direct, states, turned, inner_weight, sem
):
    copy = pltpu.make_async_copy(far_weight, inner_weight, sem.at[0])
    copy.start()
    cells, channels = slopes.shape[1:]
    odd = lax.axis_index("row") % 2 == 1
    mean = stats[0:1, :]
    inverse = stats[1:2, :]
    for i in range(2):
        state = jnp.where(odd == (i == 0), across[0], along[0])
        states[i] = state
        values = state.reshape(cells, channels).astype(F32)
        direct[i] = slopes[i] * norm_slopes(values, mean, inverse, gain[...], shift[...])[1] * inverse
    copy.wait()
    size = inner_weight.shape[3]
    for b in range(3):
        for a in range(3):
            for e in range(3):
                at = (a * 3 + e) * size
                turned[at : at + size, b * size : (b + 1) * size] = inner_weight[a, b, e].T


def inner_kernel(
    arrived, stats, direct, hidden, edge_direct, edge_states, turned, far_out, out, sems, *, devices
):
    own_rows, frame_count, width, channels = out.shape
    cells = frame_count * width
    totals = jnp.sum(arrived[...], axis=0)
    cell_total = own_rows * devices * cells * (channels // GROUPS)
    place_row = iota((8, channels), 0)
    both = jnp.where(place_row == 0, totals[0:1], totals[1:2])
    both = over_group(both, channels // GROUPS)
    first, second = both[0:1], both[1:2]
    mean = stats[0:1, :]
    inverse = stats[1:2, :]
    constant = first / cell_total * inverse
    factor = second / cell_total * inverse * inverse
    position = lax.axis_index("row")
    in_frame = mod(iota((cells, 1), 0), width)
    results = [jnp.zeros((cells, channels), F32) for _ in range(own_rows)]
    copies = []
    for i in range(own_rows + 2):
        if 0 < i < own_rows + 1:
            state, part = hidden[i - 1], direct[i - 1]
        else:
            state, part = edge_states[min(i, 1)], edge_direct[min(i, 1)]
        grad = part - constant - (state.reshape(cells, channels).astype(F32) - mean) * factor
        if i == 0:
            grad = jnp.where(position > 0, grad, 0.0)
        if i == own_rows + 1:
            grad = jnp.where(position < devices - 1, grad, 0.0)
        after = jnp.where(in_frame < width - 1, pltpu.roll(grad, cells - 1, 0), 0.0)
        prior = jnp.where(in_frame > 0, pltpu.roll(grad, 1, 0), 0.0)
        taps = jnp.concatenate([after.astype(BF16), grad.astype(BF16), prior.astype(BF16)], axis=1)
        later = []
        for a in range(3):
            skip = (2 - a) * width
            filler = jnp.zeros((skip, taps.shape[1]), BF16)
            later.append(jnp.concatenate([taps[skip:], filler], axis=0) if skip else taps)
        joined = jnp.concatenate(later, axis=1)
        rows = [b for b in range(3) if 0 <= i + b - 2 < own_rows]
        for low in range(0, len(rows), 2):
            some = rows[low : low + 2]
            product = matmul(joined, turned[:, some[0] * channels : (some[-1] + 1) * channels])
            for step, b in enumerate(some):
                results[i + b - 2] = results[i + b - 2] + product[:, step * channels : (step + 1) * channels]
        if i >= 2:
            out[i - 2] = results[i - 2].reshape(frame_count, width, channels).astype(BF16)
            copies.append(pltpu.make_async_copy(out.at[i - 2], far_out.at[i - 2], sems.at[i - 2]))
            copies[-1].start()
    for copy in copies:
        copy.wait()


def per_device(
    frames,
    frame_owner,
    picks,
    patch_weight,
    patch_bias,
    norm_gain,
    head_weight,
    head_bias,
    head_out,
    hidden_state,
    group_gain,
    group_shift,
    out_weight,
    inner_weight,
):
    devices = lax.axis_size("row")
    per_frame = devices // FRAMES
    height = frames.shape[1]
    own_rows, _, frame_width, channels = hidden_state.shape
    cells = FRAMES * frame_width
    width = patch_weight.shape[1]
    turned_frames = jnp.transpose(frames, (0, 2, 1))
    bias = patch_bias.reshape(1, width)
    gain = norm_gain.reshape(1, width)
    head_bias_row = head_bias.reshape(1, width)
    head_out_row = head_out.reshape(1, width)
    state_rows = own_rows + 2
    edge = jax.ShapeDtypeStruct((1,) + hidden_state.shape[1:], BF16)
    message = (message_shape(devices), edge, edge)
    gain_row = group_gain.reshape(1, channels)
    shift_row = group_shift.reshape(1, channels)
    early = [hidden_state, gain_row, shift_row, out_weight]
    slope_outs = (
        pltpu.VMEM((own_rows, cells, channels), F32),
        pltpu.VMEM((2, cells, channels), F32),
        pltpu.VMEM((8, channels), F32),
        jax.ShapeDtypeStruct((devices, 2, channels), F32),
    )
    if per_frame == 1:
        arrays = [turned_frames, bias, gain, frame_owner, picks, head_bias_row, head_out_row]
        weights = [patch_weight, head_weight]

        def scratch(x):
            return (pltpu.SMEM if x.dtype == jnp.int32 else pltpu.VMEM)(x.shape, x.dtype)

        send, across, along, *early = pl.pallas_call(
            reward_kernel,
            out_shape=message + tuple(pltpu.VMEM(x.shape, x.dtype) for x in early),
            in_specs=[FAR] * (len(arrays) + len(early) + len(weights)),
            out_specs=[VMEM] * (3 + len(early)),
            scratch_shapes=[scratch(x) for x in arrays + weights] + [pltpu.SemaphoreType.DMA((32,))],
            compiler_params=params(0),
            name="reward",
        )(*[far(x) for x in arrays + early + weights])
    else:
        count = height // PATCH
        normed, inv_spread, partial = pl.pallas_call(
            forward_kernel,
            out_shape=(
                jax.ShapeDtypeStruct((-(-count // 8) * 8, width), F32),
                jax.ShapeDtypeStruct((-(-count // 8) * 8, LANES), F32),
                jax.ShapeDtypeStruct((1, width), F32),
            ),
            compiler_params=params(cells),
            name="reward_forward",
        )(turned_frames, bias, gain, patch_weight)
        members = [[b * per_frame + i for i in range(per_frame)] for b in range(FRAMES)]
        pooled = lax.psum(partial, "row", axis_index_groups=members) / (count * per_frame)
        send, across, along = pl.pallas_call(
            functools.partial(backward_kernel, height=height, per_frame=per_frame),
            out_shape=message,
            in_specs=[SMEM] * 2 + [VMEM] * 9,
            out_specs=[VMEM] * 3,
            compiler_params=params(cells),
            name="reward_backward",
        )(
            frame_owner,
            picks,
            hidden_state,
            gain,
            head_bias_row,
            head_out_row,
            normed,
            inv_spread,
            pooled,
            patch_weight,
            head_weight,
        )
    early = [near(x) for x in early]
    wide = pl.pallas_call(
        prepare_kernel,
        out_shape=pltpu.VMEM((3 * LANES, state_rows * channels), BF16),
        in_specs=[VMEM],
        scratch_shapes=[pltpu.VMEM((3 * LANES, state_rows * channels), F32)],
        compiler_params=params(cells),
        name="prepare",
    )(early[3])
    arrived = lax.all_to_all(send, "row", 0, 0, axis_index_groups=[first_order(devices)], tiled=True)
    direct, edge_slopes, stats, sums = pl.pallas_call(
        slope_kernel,
        out_shape=slope_outs,
        in_specs=[VMEM] * 5 + [FAR],
        scratch_shapes=[
            pltpu.VMEM((own_rows, cells, channels), F32),
            pltpu.VMEM((4 * devices, LANES), F32),
            pltpu.VMEM((cells + 2 * frame_width, LANES), BF16),
            pltpu.SMEM(frame_owner.shape, jnp.int32),
            pltpu.SemaphoreType.DMA((1,)),
        ],
        compiler_params=params(cells),
        name="slope",
    )(near(arrived), *early[:3], near(wide), far(frame_owner))
    swaps = [(2 * i, 2 * i + 1) for i in range(devices // 2)]
    across = lax.ppermute(across, "row", swaps + [(b, a) for a, b in swaps])
    swaps = [(2 * i - 1, 2 * i) for i in range(1, devices // 2)]
    along = lax.ppermute(along, "row", swaps + [(b, a) for a, b in swaps])
    summed = lax.all_to_all(sums, "row", 0, 0, axis_index_groups=[led_by(devices - 1, devices)], tiled=True)
    edge_direct, edge_states, turned = pl.pallas_call(
        late_kernel,
        out_shape=(
            pltpu.VMEM((2, cells, channels), F32),
            pltpu.VMEM((2,) + hidden_state.shape[1:], BF16),
            pltpu.VMEM((9 * channels, 3 * channels), BF16),
        ),
        in_specs=[VMEM] * 6 + [FAR],
        scratch_shapes=[pltpu.VMEM(inner_weight.shape, BF16), pltpu.SemaphoreType.DMA((1,))],
        input_output_aliases={2: 0},
        compiler_params=params(cells),
        name="late",
    )(near(across), near(along), near(edge_slopes), near(stats), *early[1:3], far(inner_weight))
    return pl.pallas_call(
        functools.partial(inner_kernel, devices=devices),
        out_shape=jax.ShapeDtypeStruct(hidden_state.shape, BF16),
        in_specs=[VMEM] * 7,
        out_specs=FAR,
        scratch_shapes=[
            pltpu.VMEM(hidden_state.shape, BF16),
            pltpu.SemaphoreType.DMA((own_rows,)),
        ],
        compiler_params=params(cells),
        name="inner",
    )(
        near(summed),
        near(stats),
        near(direct),
        early[0],
        near(edge_direct),
        near(edge_states),
        near(turned),
    )


def solution(mesh):
    return jax.shard_map(
        per_device,
        mesh=mesh,
        in_specs=(
            P(None, None, ("clip", "row")),
            P("clip"),
            P("clip"),
            P(),
            P(),
            P(),
            P(),
            P(),
            P(),
            P(("clip", "row"), None, None, None),
            P(),
            P(),
            P(),
            P(),
        ),
        out_specs=P(("clip", "row"), None, None, None),
        check_vma=False,
    )
```

```python
import functools

import jax
import jax.numpy as jnp
from jax import lax
from jax.experimental import pallas as pl
from jax.experimental.pallas import tpu as pltpu
from jax.sharding import PartitionSpec as P

PATCH = 16
GROUPS = 32
FRAMES = 16
LANES = 128
SLOTS = LANES // PATCH
eps_norm = 1e-06
BF16 = jnp.bfloat16
F32 = jnp.float32

SMEM = pl.BlockSpec(memory_space=pltpu.SMEM)
VMEM = pl.BlockSpec(memory_space=pltpu.VMEM)
FAR = pl.BlockSpec(memory_space=pl.ANY)


def iota(shape, dim):
    return lax.broadcasted_iota(jnp.int32, shape, dim)


def div(values, count):
    if count & (count - 1):
        return values // count
    return values >> (count.bit_length() - 1)


def mod(values, count):
    if count & (count - 1):
        return values % count
    return values & (count - 1)


def ones_where(condition):
    return jnp.where(condition, 1.0, 0.0).astype(BF16)


def matmul(left, right):
    return jnp.dot(left, right, preferred_element_type=F32)


def matmul_t(left, right):
    return lax.dot_general(left, right, (((1,), (1,)), ((), ())), preferred_element_type=F32)


def cut_in_three(values):
    high = values.astype(BF16)
    rest = values - high.astype(F32)
    middle = rest.astype(BF16)
    low = (rest - middle.astype(F32)).astype(BF16)
    return high, middle, low


def exact_rows(rows, product):
    place = iota((8, rows[0].shape[1]), 0)
    stacked = jnp.zeros(place.shape, F32)
    for index, row in enumerate(rows):
        for step, piece in enumerate(cut_in_three(row)):
            stacked = jnp.where(place == 3 * index + step, piece.astype(F32), stacked)
    result = product(jnp.concatenate([stacked, jnp.zeros_like(stacked)], axis=0).astype(BF16))
    return [
        result[3 * i : 3 * i + 1] + result[3 * i + 1 : 3 * i + 2] + result[3 * i + 2 : 3 * i + 3]
        for i in range(len(rows))
    ]


def silu_slope(values):
    small = jnp.exp(-jnp.abs(values))
    large_part = pl.reciprocal(1.0 + small)
    small_part = small * large_part
    positive = values >= 0.0
    sigmoid = jnp.where(positive, large_part, small_part)
    return sigmoid * (1.0 + values * jnp.where(positive, small_part, large_part))


def token_rows_of(height):
    return -(-(height // PATCH) // 16) * 16


def to_tokens(pixels):
    channels, columns, height = pixels.shape
    rows = channels * columns
    token_rows = token_rows_of(height)
    flat = pixels.reshape(rows, height)
    width = channels * PATCH * columns
    lane = iota((1, width), 1)
    place = iota((rows, 1), 0)
    mine = place == div(lane, PATCH * columns) * columns + mod(lane, columns)
    in_patch = mod(div(lane, columns), PATCH)
    pixel_row = iota((height, 1), 0)
    token = iota((token_rows, 1), 0)
    tokens = jnp.zeros((token_rows, width), F32)
    for t in range(height // PATCH):
        tiled = matmul(flat, ones_where(pixel_row == in_patch + t * PATCH))
        row = jnp.sum(jnp.where(mine, tiled, 0.0), axis=0, keepdims=True)
        tokens = jnp.where(token == t, row, tokens)
    return tokens.astype(BF16)


def forward_part(tokens, count, bias, gain, load_patch):
    embedded = jnp.zeros((tokens.shape[0], bias.shape[1]), F32)
    for low, high, weight in load_patch():
        embedded = embedded + matmul(tokens[:, low:high], weight)
    rows = -(-count // 8) * 8
    embedded = embedded[:rows] + bias[...]
    centred = embedded - jnp.mean(embedded, axis=1, keepdims=True)
    inv_spread = lax.rsqrt(jnp.mean(centred * centred, axis=1, keepdims=True) + eps_norm)
    normed = centred * inv_spread
    weighted = normed * gain[...]
    inside = iota((rows, 1), 0) < count
    pooled = jnp.sum(jnp.where(inside, weighted, 0.0), axis=0, keepdims=True)
    return normed, inv_spread, pooled


def led_by(leader, devices):
    return [leader] + [d for d in reversed(range(devices)) if d != leader]


def first_order(devices):
    return led_by(devices * 13 // 16, devices)


def message_shape(devices):
    return jax.ShapeDtypeStruct((devices, 4, LANES), F32)


def write_windows(patch_grad, sums, own_rows, height, send):
    span = PATCH * PATCH
    line = jnp.concatenate(
        [
            jnp.concatenate([patch_grad[t : t + 1, k * span : (k + 1) * span] for t in range(height // PATCH)], axis=1)
            for k in range(3)
        ]
        + [jnp.zeros((1, height * PATCH), F32)],
        axis=0,
    )
    line = jnp.concatenate([jnp.zeros((4, LANES), F32), line, jnp.zeros((4, LANES), F32)], axis=1)
    used = iota((4, LANES), 1) < (own_rows + 4) * PATCH
    colour = iota((4, LANES), 0)
    for index, d in enumerate(first_order(send.shape[0])):
        start = LANES + (d * own_rows - 2) * PATCH
        window = jnp.where(used, line[:, start : start + LANES], 0.0)
        send[index] = jnp.where(colour < 3, window, sums[:4])


def channel_sums(hidden):
    values = hidden.reshape(-1, hidden.shape[-1]).astype(F32)
    return jnp.sum(values, axis=0, keepdims=True), jnp.sum(values * values, axis=0, keepdims=True)


def over_group(values, size):
    lane = iota(values.shape, 1)
    lanes = values.shape[1]
    step = 1
    while step < size:
        later = pltpu.roll(values, lanes - step, 1)
        earlier = pltpu.roll(values, step, 1)
        values = values + jnp.where((lane & step) == 0, later, earlier)
        step *= 2
    return values


def group_sums(hidden):
    channels = hidden.shape[-1]
    size = channels // GROUPS
    first, second = [
        over_group(jnp.broadcast_to(x, (8, channels)), size) for x in channel_sums(hidden)
    ]
    lane = mod(iota((8, channels), 1), size)
    return jnp.where(lane == 0, first, jnp.where(lane == 1, second, 0.0))


def pull_back(row, weight):
    parts = []
    for low in range(0, weight.shape[0], LANES):
        product = weight[low : low + LANES, :].astype(F32) * row
        folded = product[:, :LANES]
        for start in range(LANES, weight.shape[1], LANES):
            folded = folded + product[:, start : start + LANES]
        parts.append(jnp.sum(folded.T, axis=0, keepdims=True))
    return jnp.concatenate(parts, axis=1)


def backward_part(
    owner, picks, gain, head_bias, head_out, normed, inv_spread, pooled, weight, head, through_head, slot, own_rows, height, sums, send
):
    (before,) = exact_rows([pooled], through_head)
    slope = head_out[...] * silu_slope(before + head_bias[...])
    pulled = pull_back(slope, head)
    wanted = owner[slot]
    picked = jnp.int32(0)
    for k in range(picks.shape[0]):
        picked = picked + jnp.where(picks[k] == wanted, 1, 0)
    scaled = gain[...] * (picked.astype(F32) * pulled)
    token_grad = inv_spread * (
        scaled
        - jnp.mean(scaled, axis=1, keepdims=True)
        - normed * jnp.mean(scaled * normed, axis=1, keepdims=True)
    )
    filler = jnp.zeros((-token_grad.shape[0] % 16, token_grad.shape[1]), F32)
    token_grad = jnp.concatenate([token_grad, filler], axis=0).astype(BF16)
    patch_grad = matmul_t(token_grad, weight[...]).astype(BF16).astype(F32)
    write_windows(patch_grad, sums, own_rows, height, send)


def write_edges(position, hidden, across, along):
    last = hidden.shape[0] - 1
    even = position % 2 == 0
    across[0] = hidden[jnp.where(even, last, 0)]
    along[0] = hidden[jnp.where(even, 0, last)]


def reward_kernel(*refs):
    position = lax.axis_index("row")
    count, kept = 7, 4
    far, refs = refs[: count + kept + 2], refs[count + kept + 2 :]
    send, across, along = refs[:3]
    near = refs[3 + kept : 3 + kept + count] + refs[3 : 3 + kept] + refs[3 + kept + count : -1]
    sems = refs[-1]
    frames, bias, gain, owner, picks, head_bias, head_out, hidden, _, _, _, patch, head = near
    count += kept
    depths = (256, 256)
    small = [pltpu.make_async_copy(far[i], near[i], sems.at[i]) for i in range(count)]
    pieces = []
    used = count
    for index, rows in enumerate(depths):
        source, target = far[count + index], near[count + index]
        parts = []
        for low in range(0, target.shape[0], rows):
            part = pl.ds(low, rows)
            parts.append(pltpu.make_async_copy(source.at[part], target.at[part], sems.at[used]))
            used += 1
        pieces.append(parts)
    for copy in [small[0], small[7]] + pieces[0] + small[1:7] + pieces[1] + small[8:]:
        copy.start()

    def load_patch():
        for copy in pieces[0] + small[1:3]:
            copy.wait()
        yield 0, patch.shape[0], patch[...]

    height = frames.shape[2]
    patches = height // PATCH
    small[0].wait()
    small[7].wait()
    tokens = to_tokens(frames[...])
    sums = group_sums(hidden[...])
    write_edges(position, hidden, across, along)
    normed, inv_spread, pooled = forward_part(tokens, patches, bias, gain, load_patch)
    for copy in small[3:7]:
        copy.wait()

    def through_head(rows):
        total = jnp.zeros((rows.shape[0], head.shape[1]), F32)
        for index, low in enumerate(range(0, head.shape[0], depths[1])):
            pieces[1][index].wait()
            total = total + matmul(rows[:, low : low + depths[1]], head[low : low + depths[1], :])
        return total

    backward_part(
        owner,
        picks,
        gain,
        head_bias,
        head_out,
        normed,
        inv_spread,
        pooled / patches,
        patch,
        head,
        through_head,
        position,
        hidden.shape[0],
        height,
        sums,
        send,
    )
    for copy in small[8:]:
        copy.wait()


def forward_kernel(frames, bias, gain, patch, normed, inv_spread, pooled):
    width = patch.shape[0]
    tokens = to_tokens(frames[...])
    normed[...], spread, pooled[...] = forward_part(
        tokens, frames.shape[2] // PATCH, bias, gain, lambda: [(0, width, patch[...])]
    )
    inv_spread[...] = jnp.broadcast_to(spread, inv_spread.shape)


def backward_kernel(
    owner,
    picks,
    hidden,
    gain,
    head_bias,
    head_out,
    normed,
    inv_spread,
    pooled,
    patch,
    head,
    send,
    across,
    along,
    *,
    height,
    per_frame,
):
    position = lax.axis_index("row")
    write_edges(position, hidden, across, along)
    backward_part(
        owner,
        picks,
        gain,
        head_bias,
        head_out,
        normed[...],
        inv_spread[...][:, :1],
        pooled[...],
        patch,
        head,
        lambda rows: matmul(rows, head[...]),
        position // per_frame,
        hidden.shape[0],
        height,
        group_sums(hidden[...]),
        send,
    )


def params(cells):
    return pltpu.CompilerParams(vmem_limit_bytes=min(16 + cells // 64, 48) * 1024 * 1024)


def near(array):
    return pltpu.with_memory_space_constraint(array, pltpu.VMEM)


def far(array):
    return pltpu.with_memory_space_constraint(array, pltpu.HBM)


def tap_lane(j, k, e):
    return (j + 1) * PATCH + 4 * k + e


def prepare_kernel(out_weight, wide, scratch):
    amount = scratch.shape[1] // LANES
    scratch[...] = jnp.zeros_like(scratch)
    for a in range(3):
        for e in range(3):
            for b in range(3):
                piece = out_weight[a, b, e].astype(F32)
                for i in range(amount):
                    for k in range(3):
                        at = a * LANES + tap_lane(i - b + 2, k, e)
                        scratch[at : at + 1, i * LANES : (i + 1) * LANES] = piece[k : k + 1]
    wide[...] = scratch[...].astype(BF16)


def norm_constants(totals, cell_total):
    channels = totals.shape[1]
    size = channels // GROUPS
    totals = jnp.broadcast_to(totals, (8, channels))
    lane = mod(iota((8, channels), 1), size)
    first, second = [over_group(jnp.where(lane == i, totals, 0.0), size)[:1] for i in range(2)]
    mean = first / cell_total
    return mean, lax.rsqrt(second / cell_total - mean * mean + eps_norm)


def norm_slopes(state, mean, inverse, gain, shift):
    normed = (state - mean) * inverse
    return normed, silu_slope(normed * gain + shift) * gain


def slope_kernel(
    arrived,
    hidden,
    gain,
    shift,
    wide,
    far_owner,
    direct,
    edge_slopes,
    stats,
    sums,
    slopes_own,
    received,
    taps,
    owner,
    sem,
):
    copy = pltpu.make_async_copy(far_owner, owner, sem.at[0])
    copy.start()
    devices, message_rows, _ = arrived.shape
    own_rows, frame_count, width, channels = hidden.shape
    cells = frame_count * width
    per_frame = devices // frame_count
    got = arrived[...].reshape(received.shape)
    kind = mod(iota((got.shape[0], 1), 0), message_rows)
    totals = jnp.sum(jnp.where(kind == 3, got, 0.0), axis=0, keepdims=True)
    mean, inverse = norm_constants(totals, own_rows * devices * cells * (channels // GROUPS))
    for i in range(own_rows):
        state = hidden[i].reshape(cells, channels).astype(F32)
        slopes_own[i] = norm_slopes(state, mean, inverse, gain[...], shift[...])[1] * inverse

    if per_frame == 1:
        lane = iota((1, LANES), 1)
        entry = iota((LANES, 1), 0)
        turned = ones_where(entry - mod(entry, PATCH) + PATCH - 1 - mod(entry, PATCH) == lane)
        received[...] = matmul(jnp.where(kind < 3, got, 0.0).astype(BF16), turned)
        lane = mod(iota((PATCH, LANES), 1), PATCH)
        column = iota((PATCH, LANES), 0)
        marks = []
        for k in range(3):
            e = lane - 4 * k
            wanted = column - e + 1
            marks.append((e >= 0) & (e < 3) & (wanted >= 0) & (wanted < PATCH))
        copy.wait()
        for d in range(devices):
            row = first_order(devices)[d]
            block = jnp.zeros((PATCH, LANES), F32)
            for k in range(3):
                line = jnp.broadcast_to(received[d * message_rows + k : d * message_rows + k + 1, :], (PATCH, LANES))
                line = pltpu.roll(line, 4 * k + 2, 1, stride=1, stride_axis=0)
                block = jnp.where(marks[k], line, block)
            start = pl.multiple_of(owner[row] * PATCH, PATCH)
            taps[pl.ds(start, PATCH), :] = block.astype(BF16)
    else:
        copy.wait()
        received[...] = got
        lines = [received[pl.ds(k, devices, stride=message_rows), :] for k in range(3)]
        lines = jnp.concatenate(lines, axis=1).astype(BF16)
        place = iota((1, devices), 1)
        source = jnp.zeros_like(place)
        for index, d in enumerate(first_order(devices)):
            source = jnp.where(place == index, d, source)
        home = jnp.zeros((1, devices), jnp.int32)
        for b in range(frame_count):
            home = jnp.where(div(source, per_frame) == b, owner[b] * per_frame, home)
        home = home + mod(source, per_frame)
        cell = iota((cells, 1), 0)
        column = mod(cell, width)
        lane = mod(iota((1, 3 * LANES), 1), PATCH)
        entry = iota((3 * LANES, 1), 0)
        window_row = div(mod(entry, LANES), PATCH)
        found = jnp.zeros((cells, LANES), F32)
        for e in range(3):
            wanted = column - e + 1
            strip = div(cell, width) * per_frame + div(wanted, PATCH)
            placed = matmul(ones_where(home == strip), lines)
            inside = jnp.where((wanted >= 0) & (wanted < width), mod(wanted, PATCH), -1)
            kept = jnp.where(lane == inside, placed, 0.0).astype(BF16)
            target = jnp.where(
                window_row < own_rows + 4, tap_lane(window_row, div(entry, LANES), e), -1
            )
            found = found + matmul(kept, ones_where(target == iota((1, LANES), 1)))
        taps[:cells, :] = found.astype(BF16)
    taps[cells:, :] = jnp.zeros((2 * width, LANES), BF16)
    steps = [taps[(2 - a) * width : (2 - a) * width + cells, :] for a in range(3)]
    result = matmul(jnp.concatenate(steps, axis=1), wide[...])

    first = jnp.zeros((1, channels), F32)
    second = jnp.zeros((1, channels), F32)
    for i in range(own_rows):
        state = hidden[i].reshape(cells, channels).astype(F32)
        part = result[:, (i + 1) * channels : (i + 2) * channels] * slopes_own[i]
        direct[i] = part
        first = first + jnp.sum(part, axis=0, keepdims=True)
        second = second + jnp.sum(part * (state - mean), axis=0, keepdims=True)
    first = first / inverse
    edge_slopes[0] = result[:, :channels]
    edge_slopes[1] = result[:, (own_rows + 1) * channels :]
    stats[0:1, :] = mean
    stats[1:2, :] = inverse
    both = jnp.where(iota((2, channels), 0) == 0, first, second)
    sums[...] = jnp.broadcast_to(both[None], sums.shape)


def late_kernel(
    across, along, slopes, stats, gain, shift, far_weight, direct, states, turned, inner_weight, sem
):
    copy = pltpu.make_async_copy(far_weight, inner_weight, sem.at[0])
    copy.start()
    cells, channels = slopes.shape[1:]
    odd = lax.axis_index("row") % 2 == 1
    mean = stats[0:1, :]
    inverse = stats[1:2, :]
    for i in range(2):
        state = jnp.where(odd == (i == 0), across[0], along[0])
        states[i] = state
        values = state.reshape(cells, channels).astype(F32)
        direct[i] = slopes[i] * norm_slopes(values, mean, inverse, gain[...], shift[...])[1] * inverse
    copy.wait()
    size = inner_weight.shape[3]
    for b in range(3):
        for a in range(3):
            for e in range(3):
                at = (a * 3 + e) * size
                turned[at : at + size, b * size : (b + 1) * size] = inner_weight[a, b, e].T


def inner_kernel(
    arrived, stats, direct, hidden, edge_direct, edge_states, turned, far_out, out, sems, *, devices
):
    own_rows, frame_count, width, channels = out.shape
    cells = frame_count * width
    totals = jnp.sum(arrived[...], axis=0)
    cell_total = own_rows * devices * cells * (channels // GROUPS)
    place_row = iota((8, channels), 0)
    both = jnp.where(place_row == 0, totals[0:1], totals[1:2])
    both = over_group(both, channels // GROUPS)
    first, second = both[0:1], both[1:2]
    mean = stats[0:1, :]
    inverse = stats[1:2, :]
    constant = first / cell_total * inverse
    factor = second / cell_total * inverse * inverse
    position = lax.axis_index("row")
    in_frame = mod(iota((cells, 1), 0), width)
    results = [jnp.zeros((cells, channels), F32) for _ in range(own_rows)]
    copies = []
    for i in range(own_rows + 2):
        if 0 < i < own_rows + 1:
            state, part = hidden[i - 1], direct[i - 1]
        else:
            state, part = edge_states[min(i, 1)], edge_direct[min(i, 1)]
        grad = part - constant - (state.reshape(cells, channels).astype(F32) - mean) * factor
        if i == 0:
            grad = jnp.where(position > 0, grad, 0.0)
        if i == own_rows + 1:
            grad = jnp.where(position < devices - 1, grad, 0.0)
        after = jnp.where(in_frame < width - 1, pltpu.roll(grad, cells - 1, 0), 0.0)
        prior = jnp.where(in_frame > 0, pltpu.roll(grad, 1, 0), 0.0)
        taps = jnp.concatenate([after.astype(BF16), grad.astype(BF16), prior.astype(BF16)], axis=1)
        later = []
        for a in range(3):
            skip = (2 - a) * width
            filler = jnp.zeros((skip, taps.shape[1]), BF16)
            later.append(jnp.concatenate([taps[skip:], filler], axis=0) if skip else taps)
        joined = jnp.concatenate(later, axis=1)
        rows = [b for b in range(3) if 0 <= i + b - 2 < own_rows]
        for low in range(0, len(rows), 2):
            some = rows[low : low + 2]
            product = matmul(joined, turned[:, some[0] * channels : (some[-1] + 1) * channels])
            for step, b in enumerate(some):
                results[i + b - 2] = results[i + b - 2] + product[:, step * channels : (step + 1) * channels]
        if i >= 2:
            out[i - 2] = results[i - 2].reshape(frame_count, width, channels).astype(BF16)
            copies.append(pltpu.make_async_copy(out.at[i - 2], far_out.at[i - 2], sems.at[i - 2]))
            copies[-1].start()
    for copy in copies:
        copy.wait()


def per_device(
    frames,
    frame_owner,
    picks,
    patch_weight,
    patch_bias,
    norm_gain,
    head_weight,
    head_bias,
    head_out,
    hidden_state,
    group_gain,
    group_shift,
    out_weight,
    inner_weight,
):
    devices = lax.axis_size("row")
    per_frame = devices // FRAMES
    height = frames.shape[1]
    own_rows, _, frame_width, channels = hidden_state.shape
    cells = FRAMES * frame_width
    width = patch_weight.shape[1]
    turned_frames = jnp.transpose(frames, (0, 2, 1))
    bias = patch_bias.reshape(1, width)
    gain = norm_gain.reshape(1, width)
    head_bias_row = head_bias.reshape(1, width)
    head_out_row = head_out.reshape(1, width)
    state_rows = own_rows + 2
    edge = jax.ShapeDtypeStruct((1,) + hidden_state.shape[1:], BF16)
    message = (message_shape(devices), edge, edge)
    gain_row = group_gain.reshape(1, channels)
    shift_row = group_shift.reshape(1, channels)
    early = [hidden_state, gain_row, shift_row, out_weight]
    slope_outs = (
        pltpu.VMEM((own_rows, cells, channels), F32),
        pltpu.VMEM((2, cells, channels), F32),
        pltpu.VMEM((8, channels), F32),
        jax.ShapeDtypeStruct((devices, 2, channels), F32),
    )
    if per_frame == 1:
        arrays = [turned_frames, bias, gain, frame_owner, picks, head_bias_row, head_out_row]
        weights = [patch_weight, head_weight]

        def scratch(x):
            return (pltpu.SMEM if x.dtype == jnp.int32 else pltpu.VMEM)(x.shape, x.dtype)

        send, across, along, *early = pl.pallas_call(
            reward_kernel,
            out_shape=message + tuple(pltpu.VMEM(x.shape, x.dtype) for x in early),
            in_specs=[FAR] * (len(arrays) + len(early) + len(weights)),
            out_specs=[VMEM] * (3 + len(early)),
            scratch_shapes=[scratch(x) for x in arrays + weights] + [pltpu.SemaphoreType.DMA((32,))],
            compiler_params=params(0),
            name="reward",
        )(*[far(x) for x in arrays + early + weights])
    else:
        count = height // PATCH
        normed, inv_spread, partial = pl.pallas_call(
            forward_kernel,
            out_shape=(
                jax.ShapeDtypeStruct((-(-count // 8) * 8, width), F32),
                jax.ShapeDtypeStruct((-(-count // 8) * 8, LANES), F32),
                jax.ShapeDtypeStruct((1, width), F32),
            ),
            compiler_params=params(cells),
            name="reward_forward",
        )(turned_frames, bias, gain, patch_weight)
        members = [[b * per_frame + i for i in range(per_frame)] for b in range(FRAMES)]
        pooled = lax.psum(partial, "row", axis_index_groups=members) / (count * per_frame)
        send, across, along = pl.pallas_call(
            functools.partial(backward_kernel, height=height, per_frame=per_frame),
            out_shape=message,
            in_specs=[SMEM] * 2 + [VMEM] * 9,
            out_specs=[VMEM] * 3,
            compiler_params=params(cells),
            name="reward_backward",
        )(
            frame_owner,
            picks,
            hidden_state,
            gain,
            head_bias_row,
            head_out_row,
            normed,
            inv_spread,
            pooled,
            patch_weight,
            head_weight,
        )
    early = [near(x) for x in early]
    wide = pl.pallas_call(
        prepare_kernel,
        out_shape=pltpu.VMEM((3 * LANES, state_rows * channels), BF16),
        in_specs=[VMEM],
        scratch_shapes=[pltpu.VMEM((3 * LANES, state_rows * channels), F32)],
        compiler_params=params(cells),
        name="prepare",
    )(early[3])
    arrived = lax.all_to_all(send, "row", 0, 0, axis_index_groups=[first_order(devices)], tiled=True)
    direct, edge_slopes, stats, sums = pl.pallas_call(
        slope_kernel,
        out_shape=slope_outs,
        in_specs=[VMEM] * 5 + [FAR],
        scratch_shapes=[
            pltpu.VMEM((own_rows, cells, channels), F32),
            pltpu.VMEM((4 * devices, LANES), F32),
            pltpu.VMEM((cells + 2 * frame_width, LANES), BF16),
            pltpu.SMEM(frame_owner.shape, jnp.int32),
            pltpu.SemaphoreType.DMA((1,)),
        ],
        compiler_params=params(cells),
        name="slope",
    )(near(arrived), *early[:3], near(wide), far(frame_owner))
    swaps = [(2 * i, 2 * i + 1) for i in range(devices // 2)]
    across = lax.ppermute(across, "row", swaps + [(b, a) for a, b in swaps])
    swaps = [(2 * i - 1, 2 * i) for i in range(1, devices // 2)]
    along = lax.ppermute(along, "row", swaps + [(b, a) for a, b in swaps])
    summed = lax.all_to_all(sums, "row", 0, 0, axis_index_groups=[led_by(devices - 1, devices)], tiled=True)
    edge_direct, edge_states, turned = pl.pallas_call(
        late_kernel,
        out_shape=(
            pltpu.VMEM((2, cells, channels), F32),
            pltpu.VMEM((2,) + hidden_state.shape[1:], BF16),
            pltpu.VMEM((9 * channels, 3 * channels), BF16),
        ),
        in_specs=[VMEM] * 6 + [FAR],
        scratch_shapes=[pltpu.VMEM(inner_weight.shape, BF16), pltpu.SemaphoreType.DMA((1,))],
        input_output_aliases={2: 0},
        compiler_params=params(cells),
        name="late",
    )(near(across), near(along), near(edge_slopes), near(stats), *early[1:3], far(inner_weight))
    return pl.pallas_call(
        functools.partial(inner_kernel, devices=devices),
        out_shape=jax.ShapeDtypeStruct(hidden_state.shape, BF16),
        in_specs=[VMEM] * 7,
        out_specs=FAR,
        scratch_shapes=[
            pltpu.VMEM(hidden_state.shape, BF16),
            pltpu.SemaphoreType.DMA((own_rows,)),
        ],
        compiler_params=params(cells),
        name="inner",
    )(
        near(summed),
        near(stats),
        near(direct),
        early[0],
        near(edge_direct),
        near(edge_states),
        near(turned),
    )


def solution(mesh):
    return jax.shard_map(
        per_device,
        mesh=mesh,
        in_specs=(
            P(None, None, ("clip", "row")),
            P("clip"),
            P("clip"),
            P(),
            P(),
            P(),
            P(),
            P(),
            P(),
            P(("clip", "row"), None, None, None),
            P(),
            P(),
            P(),
            P(),
        ),
        out_specs=P(("clip", "row"), None, None, None),
        check_vma=False,
    )
```

```python
import functools

import jax
import jax.numpy as jnp
from jax import lax
from jax.experimental import pallas as pl
from jax.experimental.pallas import tpu as pltpu
from jax.sharding import PartitionSpec as P

PATCH = 16
GROUPS = 32
FRAMES = 16
LANES = 128
SLOTS = LANES // PATCH
eps_norm = 1e-06
BF16 = jnp.bfloat16
F32 = jnp.float32

SMEM = pl.BlockSpec(memory_space=pltpu.SMEM)
VMEM = pl.BlockSpec(memory_space=pltpu.VMEM)
FAR = pl.BlockSpec(memory_space=pl.ANY)


def iota(shape, dim):
    return lax.broadcasted_iota(jnp.int32, shape, dim)


def div(values, count):
    if count & (count - 1):
        return values // count
    return values >> (count.bit_length() - 1)


def mod(values, count):
    if count & (count - 1):
        return values % count
    return values & (count - 1)


def ones_where(condition):
    return jnp.where(condition, 1.0, 0.0).astype(BF16)


def matmul(left, right):
    return jnp.dot(left, right, preferred_element_type=F32)


def matmul_t(left, right):
    return lax.dot_general(left, right, (((1,), (1,)), ((), ())), preferred_element_type=F32)


def cut_in_three(values):
    high = values.astype(BF16)
    rest = values - high.astype(F32)
    middle = rest.astype(BF16)
    low = (rest - middle.astype(F32)).astype(BF16)
    return high, middle, low


def exact_rows(rows, product):
    place = iota((8, rows[0].shape[1]), 0)
    stacked = jnp.zeros(place.shape, F32)
    for index, row in enumerate(rows):
        for step, piece in enumerate(cut_in_three(row)):
            stacked = jnp.where(place == 3 * index + step, piece.astype(F32), stacked)
    result = product(jnp.concatenate([stacked, jnp.zeros_like(stacked)], axis=0).astype(BF16))
    return [
        result[3 * i : 3 * i + 1] + result[3 * i + 1 : 3 * i + 2] + result[3 * i + 2 : 3 * i + 3]
        for i in range(len(rows))
    ]


def silu_slope(values):
    sigmoid = jax.nn.sigmoid(values)
    return sigmoid * (1.0 + values * (1.0 - sigmoid))


def token_rows_of(height):
    return -(-(height // PATCH) // 16) * 16


def to_tokens(pixels):
    channels, columns, height = pixels.shape
    rows = channels * columns
    token_rows = token_rows_of(height)
    flat = pixels.reshape(rows, height)
    width = channels * PATCH * columns
    lane = iota((1, width), 1)
    place = iota((rows, 1), 0)
    mine = place == div(lane, PATCH * columns) * columns + mod(lane, columns)
    in_patch = mod(div(lane, columns), PATCH)
    pixel_row = iota((height, 1), 0)
    token = iota((token_rows, 1), 0)
    tokens = jnp.zeros((token_rows, width), F32)
    for t in range(height // PATCH):
        tiled = matmul(flat, ones_where(pixel_row == in_patch + t * PATCH))
        row = jnp.sum(jnp.where(mine, tiled, 0.0), axis=0, keepdims=True)
        tokens = jnp.where(token == t, row, tokens)
    return tokens.astype(BF16)


def forward_part(tokens, count, bias, gain, load_patch):
    embedded = jnp.zeros((tokens.shape[0], bias.shape[1]), F32)
    for low, high, weight in load_patch():
        embedded = embedded + matmul(tokens[:, low:high], weight)
    rows = -(-count // 8) * 8
    embedded = embedded[:rows] + bias[...]
    centred = embedded - jnp.mean(embedded, axis=1, keepdims=True)
    inv_spread = lax.rsqrt(jnp.mean(centred * centred, axis=1, keepdims=True) + eps_norm)
    normed = centred * inv_spread
    weighted = normed * gain[...]
    inside = iota((rows, 1), 0) < count
    pooled = jnp.sum(jnp.where(inside, weighted, 0.0), axis=0, keepdims=True)
    return normed, inv_spread, pooled


def led_by(leader, devices):
    return [leader] + [d for d in reversed(range(devices)) if d != leader]


def first_order(devices):
    return led_by(devices * 13 // 16, devices)


def message_shape(devices):
    return jax.ShapeDtypeStruct((devices, 4, LANES), F32)


def write_windows(patch_grad, sums, own_rows, height, send):
    span = PATCH * PATCH
    line = jnp.concatenate(
        [
            jnp.concatenate([patch_grad[t : t + 1, k * span : (k + 1) * span] for t in range(height // PATCH)], axis=1)
            for k in range(3)
        ]
        + [jnp.zeros((1, height * PATCH), F32)],
        axis=0,
    )
    line = jnp.concatenate([jnp.zeros((4, LANES), F32), line, jnp.zeros((4, LANES), F32)], axis=1)
    used = iota((4, LANES), 1) < (own_rows + 4) * PATCH
    colour = iota((4, LANES), 0)
    for index, d in enumerate(first_order(send.shape[0])):
        start = LANES + (d * own_rows - 2) * PATCH
        window = jnp.where(used, line[:, start : start + LANES], 0.0)
        send[index] = jnp.where(colour < 3, window, sums[:4])


def channel_sums(hidden):
    values = hidden.reshape(-1, hidden.shape[-1]).astype(F32)
    return jnp.sum(values, axis=0, keepdims=True), jnp.sum(values * values, axis=0, keepdims=True)


def over_group(values, size):
    lane = iota(values.shape, 1)
    lanes = values.shape[1]
    step = 1
    while step < size:
        later = pltpu.roll(values, lanes - step, 1)
        earlier = pltpu.roll(values, step, 1)
        values = values + jnp.where((lane & step) == 0, later, earlier)
        step *= 2
    return values


def group_sums(hidden):
    channels = hidden.shape[-1]
    size = channels // GROUPS
    first, second = [
        over_group(jnp.broadcast_to(x, (8, channels)), size) for x in channel_sums(hidden)
    ]
    lane = mod(iota((8, channels), 1), size)
    return jnp.where(lane == 0, first, jnp.where(lane == 1, second, 0.0))


def pull_back(row, weight):
    parts = []
    for low in range(0, weight.shape[0], LANES):
        product = weight[low : low + LANES, :].astype(F32) * row
        folded = product[:, :LANES]
        for start in range(LANES, weight.shape[1], LANES):
            folded = folded + product[:, start : start + LANES]
        parts.append(jnp.sum(folded.T, axis=0, keepdims=True))
    return jnp.concatenate(parts, axis=1)


def backward_part(
    owner, picks, gain, head_bias, head_out, normed, inv_spread, pooled, weight, head, through_head, slot, own_rows, height, sums, send
):
    (before,) = exact_rows([pooled], through_head)
    slope = head_out[...] * silu_slope(before + head_bias[...])
    pulled = pull_back(slope, head)
    wanted = owner[slot]
    picked = jnp.int32(0)
    for k in range(picks.shape[0]):
        picked = picked + jnp.where(picks[k] == wanted, 1, 0)
    scaled = gain[...] * (picked.astype(F32) * pulled)
    token_grad = inv_spread * (
        scaled
        - jnp.mean(scaled, axis=1, keepdims=True)
        - normed * jnp.mean(scaled * normed, axis=1, keepdims=True)
    )
    filler = jnp.zeros((-token_grad.shape[0] % 16, token_grad.shape[1]), F32)
    token_grad = jnp.concatenate([token_grad, filler], axis=0).astype(BF16)
    patch_grad = matmul_t(token_grad, weight[...]).astype(BF16).astype(F32)
    write_windows(patch_grad, sums, own_rows, height, send)


def write_edges(position, hidden, across, along):
    last = hidden.shape[0] - 1
    even = position % 2 == 0
    across[0] = hidden[jnp.where(even, last, 0)]
    along[0] = hidden[jnp.where(even, 0, last)]


def reward_kernel(*refs):
    position = lax.axis_index("row")
    count, kept = 7, 4
    far, refs = refs[: count + kept + 2], refs[count + kept + 2 :]
    send, across, along = refs[:3]
    near = refs[3 + kept : 3 + kept + count] + refs[3 : 3 + kept] + refs[3 + kept + count : -1]
    sems = refs[-1]
    frames, bias, gain, owner, picks, head_bias, head_out, hidden, _, _, _, patch, head = near
    count += kept
    depths = (256, 256)
    small = [pltpu.make_async_copy(far[i], near[i], sems.at[i]) for i in range(count)]
    pieces = []
    used = count
    for index, rows in enumerate(depths):
        source, target = far[count + index], near[count + index]
        parts = []
        for low in range(0, target.shape[0], rows):
            part = pl.ds(low, rows)
            parts.append(pltpu.make_async_copy(source.at[part], target.at[part], sems.at[used]))
            used += 1
        pieces.append(parts)
    for copy in [small[0], small[7]] + pieces[0] + small[1:7] + pieces[1] + small[8:]:
        copy.start()

    def load_patch():
        for copy in pieces[0] + small[1:3]:
            copy.wait()
        yield 0, patch.shape[0], patch[...]

    height = frames.shape[2]
    patches = height // PATCH
    small[0].wait()
    small[7].wait()
    tokens = to_tokens(frames[...])
    sums = group_sums(hidden[...])
    write_edges(position, hidden, across, along)
    normed, inv_spread, pooled = forward_part(tokens, patches, bias, gain, load_patch)
    for copy in small[3:7]:
        copy.wait()

    def through_head(rows):
        total = jnp.zeros((rows.shape[0], head.shape[1]), F32)
        for index, low in enumerate(range(0, head.shape[0], depths[1])):
            pieces[1][index].wait()
            total = total + matmul(rows[:, low : low + depths[1]], head[low : low + depths[1], :])
        return total

    backward_part(
        owner,
        picks,
        gain,
        head_bias,
        head_out,
        normed,
        inv_spread,
        pooled / patches,
        patch,
        head,
        through_head,
        position,
        hidden.shape[0],
        height,
        sums,
        send,
    )
    for copy in small[8:]:
        copy.wait()


def forward_kernel(frames, bias, gain, patch, normed, inv_spread, pooled):
    width = patch.shape[0]
    tokens = to_tokens(frames[...])
    normed[...], spread, pooled[...] = forward_part(
        tokens, frames.shape[2] // PATCH, bias, gain, lambda: [(0, width, patch[...])]
    )
    inv_spread[...] = jnp.broadcast_to(spread, inv_spread.shape)


def backward_kernel(
    owner,
    picks,
    hidden,
    gain,
    head_bias,
    head_out,
    normed,
    inv_spread,
    pooled,
    patch,
    head,
    send,
    across,
    along,
    *,
    height,
    per_frame,
):
    position = lax.axis_index("row")
    write_edges(position, hidden, across, along)
    backward_part(
        owner,
        picks,
        gain,
        head_bias,
        head_out,
        normed[...],
        inv_spread[...][:, :1],
        pooled[...],
        patch,
        head,
        lambda rows: matmul(rows, head[...]),
        position // per_frame,
        hidden.shape[0],
        height,
        group_sums(hidden[...]),
        send,
    )


def params(cells):
    return pltpu.CompilerParams(vmem_limit_bytes=min(16 + cells // 64, 48) * 1024 * 1024)


def near(array):
    return pltpu.with_memory_space_constraint(array, pltpu.VMEM)


def far(array):
    return pltpu.with_memory_space_constraint(array, pltpu.HBM)


def tap_lane(j, k, e):
    return (j + 1) * PATCH + 4 * k + e


def prepare_kernel(out_weight, wide, scratch):
    amount = scratch.shape[1] // LANES
    scratch[...] = jnp.zeros_like(scratch)
    for a in range(3):
        for e in range(3):
            for b in range(3):
                piece = out_weight[a, b, e].astype(F32)
                for i in range(amount):
                    for k in range(3):
                        at = a * LANES + tap_lane(i - b + 2, k, e)
                        scratch[at : at + 1, i * LANES : (i + 1) * LANES] = piece[k : k + 1]
    wide[...] = scratch[...].astype(BF16)


def norm_constants(totals, cell_total):
    channels = totals.shape[1]
    size = channels // GROUPS
    totals = jnp.broadcast_to(totals, (8, channels))
    lane = mod(iota((8, channels), 1), size)
    first, second = [over_group(jnp.where(lane == i, totals, 0.0), size)[:1] for i in range(2)]
    mean = first / cell_total
    return mean, lax.rsqrt(second / cell_total - mean * mean + eps_norm)


def scaled_slopes(state, mean, inverse, gain, shift):
    scale = gain * inverse
    return silu_slope(state * scale + (shift - mean * scale)) * scale


def slope_kernel(
    arrived,
    hidden,
    gain,
    shift,
    wide,
    far_owner,
    direct,
    edge_slopes,
    stats,
    sums,
    slopes_own,
    received,
    taps,
    owner,
    sem,
):
    copy = pltpu.make_async_copy(far_owner, owner, sem.at[0])
    copy.start()
    devices, message_rows, _ = arrived.shape
    own_rows, frame_count, width, channels = hidden.shape
    cells = frame_count * width
    per_frame = devices // frame_count
    got = arrived[...].reshape(received.shape)
    kind = mod(iota((got.shape[0], 1), 0), message_rows)
    totals = jnp.sum(jnp.where(kind == 3, got, 0.0), axis=0, keepdims=True)
    mean, inverse = norm_constants(totals, own_rows * devices * cells * (channels // GROUPS))
    for i in range(own_rows):
        state = hidden[i].reshape(cells, channels).astype(F32)
        slopes_own[i] = scaled_slopes(state, mean, inverse, gain[...], shift[...])

    if per_frame == 1:
        lane = iota((1, LANES), 1)
        entry = iota((LANES, 1), 0)
        turned = ones_where(entry - mod(entry, PATCH) + PATCH - 1 - mod(entry, PATCH) == lane)
        received[...] = matmul(jnp.where(kind < 3, got, 0.0).astype(BF16), turned)
        lane = mod(iota((PATCH, LANES), 1), PATCH)
        column = iota((PATCH, LANES), 0)
        marks = []
        for k in range(3):
            e = lane - 4 * k
            wanted = column - e + 1
            marks.append((e >= 0) & (e < 3) & (wanted >= 0) & (wanted < PATCH))
        copy.wait()
        for d in range(devices):
            row = first_order(devices)[d]
            block = jnp.zeros((PATCH, LANES), F32)
            for k in range(3):
                line = jnp.broadcast_to(received[d * message_rows + k : d * message_rows + k + 1, :], (PATCH, LANES))
                line = pltpu.roll(line, 4 * k + 2, 1, stride=1, stride_axis=0)
                block = jnp.where(marks[k], line, block)
            start = pl.multiple_of(owner[row] * PATCH, PATCH)
            taps[pl.ds(start, PATCH), :] = block.astype(BF16)
    else:
        copy.wait()
        received[...] = got
        lines = [received[pl.ds(k, devices, stride=message_rows), :] for k in range(3)]
        lines = jnp.concatenate(lines, axis=1).astype(BF16)
        place = iota((1, devices), 1)
        source = jnp.zeros_like(place)
        for index, d in enumerate(first_order(devices)):
            source = jnp.where(place == index, d, source)
        home = jnp.zeros((1, devices), jnp.int32)
        for b in range(frame_count):
            home = jnp.where(div(source, per_frame) == b, owner[b] * per_frame, home)
        home = home + mod(source, per_frame)
        cell = iota((cells, 1), 0)
        column = mod(cell, width)
        lane = mod(iota((1, 3 * LANES), 1), PATCH)
        entry = iota((3 * LANES, 1), 0)
        window_row = div(mod(entry, LANES), PATCH)
        found = jnp.zeros((cells, LANES), F32)
        for e in range(3):
            wanted = column - e + 1
            strip = div(cell, width) * per_frame + div(wanted, PATCH)
            placed = matmul(ones_where(home == strip), lines)
            inside = jnp.where((wanted >= 0) & (wanted < width), mod(wanted, PATCH), -1)
            kept = jnp.where(lane == inside, placed, 0.0).astype(BF16)
            target = jnp.where(
                window_row < own_rows + 4, tap_lane(window_row, div(entry, LANES), e), -1
            )
            found = found + matmul(kept, ones_where(target == iota((1, LANES), 1)))
        taps[:cells, :] = found.astype(BF16)
    taps[cells:, :] = jnp.zeros((2 * width, LANES), BF16)
    steps = [taps[(2 - a) * width : (2 - a) * width + cells, :] for a in range(3)]
    result = matmul(jnp.concatenate(steps, axis=1), wide[...])

    first = jnp.zeros((1, channels), F32)
    second = jnp.zeros((1, channels), F32)
    for i in range(own_rows):
        state = hidden[i].reshape(cells, channels).astype(F32)
        part = result[:, (i + 1) * channels : (i + 2) * channels] * slopes_own[i]
        direct[i] = part
        first = first + jnp.sum(part, axis=0, keepdims=True)
        second = second + jnp.sum(part * (state - mean), axis=0, keepdims=True)
    first = first / inverse
    edge_slopes[0] = result[:, :channels]
    edge_slopes[1] = result[:, (own_rows + 1) * channels :]
    stats[0:1, :] = mean
    stats[1:2, :] = inverse
    both = jnp.where(iota((2, channels), 0) == 0, first, second)
    sums[...] = jnp.broadcast_to(both[None], sums.shape)


def late_kernel(
    across, along, slopes, stats, gain, shift, far_weight, direct, states, turned, inner_weight, sem
):
    copy = pltpu.make_async_copy(far_weight, inner_weight, sem.at[0])
    copy.start()
    cells, channels = slopes.shape[1:]
    odd = lax.axis_index("row") % 2 == 1
    mean = stats[0:1, :]
    inverse = stats[1:2, :]
    for i in range(2):
        state = jnp.where(odd == (i == 0), across[0], along[0])
        states[i] = state
        values = state.reshape(cells, channels).astype(F32)
        direct[i] = slopes[i] * scaled_slopes(values, mean, inverse, gain[...], shift[...])
    copy.wait()
    size = inner_weight.shape[3]
    for b in range(3):
        for a in range(3):
            for e in range(3):
                at = (a * 3 + e) * size
                turned[at : at + size, b * size : (b + 1) * size] = inner_weight[a, b, e].T


def inner_kernel(
    arrived, stats, direct, hidden, edge_direct, edge_states, turned, far_out, out, sems, *, devices
):
    own_rows, frame_count, width, channels = out.shape
    cells = frame_count * width
    totals = jnp.sum(arrived[...], axis=0)
    cell_total = own_rows * devices * cells * (channels // GROUPS)
    place_row = iota((8, channels), 0)
    both = jnp.where(place_row == 0, totals[0:1], totals[1:2])
    both = over_group(both, channels // GROUPS)
    first, second = both[0:1], both[1:2]
    mean = stats[0:1, :]
    inverse = stats[1:2, :]
    constant = first / cell_total * inverse
    factor = second / cell_total * inverse * inverse
    position = lax.axis_index("row")
    in_frame = mod(iota((cells, 1), 0), width)
    results = [jnp.zeros((cells, channels), F32) for _ in range(own_rows)]
    copies = []
    for i in range(own_rows + 2):
        if 0 < i < own_rows + 1:
            state, part = hidden[i - 1], direct[i - 1]
        else:
            state, part = edge_states[min(i, 1)], edge_direct[min(i, 1)]
        grad = part - constant - (state.reshape(cells, channels).astype(F32) - mean) * factor
        if i == 0:
            grad = jnp.where(position > 0, grad, 0.0)
        if i == own_rows + 1:
            grad = jnp.where(position < devices - 1, grad, 0.0)
        after = jnp.where(in_frame < width - 1, pltpu.roll(grad, cells - 1, 0), 0.0)
        prior = jnp.where(in_frame > 0, pltpu.roll(grad, 1, 0), 0.0)
        taps = jnp.concatenate([after.astype(BF16), grad.astype(BF16), prior.astype(BF16)], axis=1)
        later = []
        for a in range(3):
            skip = (2 - a) * width
            filler = jnp.zeros((skip, taps.shape[1]), BF16)
            later.append(jnp.concatenate([taps[skip:], filler], axis=0) if skip else taps)
        joined = jnp.concatenate(later, axis=1)
        rows = [b for b in range(3) if 0 <= i + b - 2 < own_rows]
        for low in range(0, len(rows), 2):
            some = rows[low : low + 2]
            product = matmul(joined, turned[:, some[0] * channels : (some[-1] + 1) * channels])
            for step, b in enumerate(some):
                results[i + b - 2] = results[i + b - 2] + product[:, step * channels : (step + 1) * channels]
        if i >= 2:
            out[i - 2] = results[i - 2].reshape(frame_count, width, channels).astype(BF16)
            copies.append(pltpu.make_async_copy(out.at[i - 2], far_out.at[i - 2], sems.at[i - 2]))
            copies[-1].start()
    for copy in copies:
        copy.wait()


def per_device(
    frames,
    frame_owner,
    picks,
    patch_weight,
    patch_bias,
    norm_gain,
    head_weight,
    head_bias,
    head_out,
    hidden_state,
    group_gain,
    group_shift,
    out_weight,
    inner_weight,
):
    devices = lax.axis_size("row")
    per_frame = devices // FRAMES
    height = frames.shape[1]
    own_rows, _, frame_width, channels = hidden_state.shape
    cells = FRAMES * frame_width
    width = patch_weight.shape[1]
    turned_frames = jnp.transpose(frames, (0, 2, 1))
    bias = patch_bias.reshape(1, width)
    gain = norm_gain.reshape(1, width)
    head_bias_row = head_bias.reshape(1, width)
    head_out_row = head_out.reshape(1, width)
    state_rows = own_rows + 2
    edge = jax.ShapeDtypeStruct((1,) + hidden_state.shape[1:], BF16)
    message = (message_shape(devices), edge, edge)
    gain_row = group_gain.reshape(1, channels)
    shift_row = group_shift.reshape(1, channels)
    early = [hidden_state, gain_row, shift_row, out_weight]
    slope_outs = (
        pltpu.VMEM((own_rows, cells, channels), F32),
        pltpu.VMEM((2, cells, channels), F32),
        pltpu.VMEM((8, channels), F32),
        jax.ShapeDtypeStruct((devices, 2, channels), F32),
    )
    if per_frame == 1:
        arrays = [turned_frames, bias, gain, frame_owner, picks, head_bias_row, head_out_row]
        weights = [patch_weight, head_weight]

        def scratch(x):
            return (pltpu.SMEM if x.dtype == jnp.int32 else pltpu.VMEM)(x.shape, x.dtype)

        send, across, along, *early = pl.pallas_call(
            reward_kernel,
            out_shape=message + tuple(pltpu.VMEM(x.shape, x.dtype) for x in early),
            in_specs=[FAR] * (len(arrays) + len(early) + len(weights)),
            out_specs=[VMEM] * (3 + len(early)),
            scratch_shapes=[scratch(x) for x in arrays + weights] + [pltpu.SemaphoreType.DMA((32,))],
            compiler_params=params(0),
            name="reward",
        )(*[far(x) for x in arrays + early + weights])
    else:
        count = height // PATCH
        normed, inv_spread, partial = pl.pallas_call(
            forward_kernel,
            out_shape=(
                jax.ShapeDtypeStruct((-(-count // 8) * 8, width), F32),
                jax.ShapeDtypeStruct((-(-count // 8) * 8, LANES), F32),
                jax.ShapeDtypeStruct((1, width), F32),
            ),
            compiler_params=params(cells),
            name="reward_forward",
        )(turned_frames, bias, gain, patch_weight)
        members = [[b * per_frame + i for i in range(per_frame)] for b in range(FRAMES)]
        pooled = lax.psum(partial, "row", axis_index_groups=members) / (count * per_frame)
        send, across, along = pl.pallas_call(
            functools.partial(backward_kernel, height=height, per_frame=per_frame),
            out_shape=message,
            in_specs=[SMEM] * 2 + [VMEM] * 9,
            out_specs=[VMEM] * 3,
            compiler_params=params(cells),
            name="reward_backward",
        )(
            frame_owner,
            picks,
            hidden_state,
            gain,
            head_bias_row,
            head_out_row,
            normed,
            inv_spread,
            pooled,
            patch_weight,
            head_weight,
        )
    early = [near(x) for x in early]
    wide = pl.pallas_call(
        prepare_kernel,
        out_shape=pltpu.VMEM((3 * LANES, state_rows * channels), BF16),
        in_specs=[VMEM],
        scratch_shapes=[pltpu.VMEM((3 * LANES, state_rows * channels), F32)],
        compiler_params=params(cells),
        name="prepare",
    )(early[3])
    arrived = lax.all_to_all(send, "row", 0, 0, axis_index_groups=[first_order(devices)], tiled=True)
    direct, edge_slopes, stats, sums = pl.pallas_call(
        slope_kernel,
        out_shape=slope_outs,
        in_specs=[VMEM] * 5 + [FAR],
        scratch_shapes=[
            pltpu.VMEM((own_rows, cells, channels), F32),
            pltpu.VMEM((4 * devices, LANES), F32),
            pltpu.VMEM((cells + 2 * frame_width, LANES), BF16),
            pltpu.SMEM(frame_owner.shape, jnp.int32),
            pltpu.SemaphoreType.DMA((1,)),
        ],
        compiler_params=params(cells),
        name="slope",
    )(near(arrived), *early[:3], near(wide), far(frame_owner))
    swaps = [(2 * i, 2 * i + 1) for i in range(devices // 2)]
    across = lax.ppermute(across, "row", swaps + [(b, a) for a, b in swaps])
    swaps = [(2 * i - 1, 2 * i) for i in range(1, devices // 2)]
    along = lax.ppermute(along, "row", swaps + [(b, a) for a, b in swaps])
    summed = lax.all_to_all(sums, "row", 0, 0, axis_index_groups=[led_by(devices - 1, devices)], tiled=True)
    edge_direct, edge_states, turned = pl.pallas_call(
        late_kernel,
        out_shape=(
            pltpu.VMEM((2, cells, channels), F32),
            pltpu.VMEM((2,) + hidden_state.shape[1:], BF16),
            pltpu.VMEM((9 * channels, 3 * channels), BF16),
        ),
        in_specs=[VMEM] * 6 + [FAR],
        scratch_shapes=[pltpu.VMEM(inner_weight.shape, BF16), pltpu.SemaphoreType.DMA((1,))],
        input_output_aliases={2: 0},
        compiler_params=params(cells),
        name="late",
    )(near(across), near(along), near(edge_slopes), near(stats), *early[1:3], far(inner_weight))
    return pl.pallas_call(
        functools.partial(inner_kernel, devices=devices),
        out_shape=jax.ShapeDtypeStruct(hidden_state.shape, BF16),
        in_specs=[VMEM] * 7,
        out_specs=FAR,
        scratch_shapes=[
            pltpu.VMEM(hidden_state.shape, BF16),
            pltpu.SemaphoreType.DMA((own_rows,)),
        ],
        compiler_params=params(cells),
        name="inner",
    )(
        near(summed),
        near(stats),
        near(direct),
        early[0],
        near(edge_direct),
        near(edge_states),
        near(turned),
    )


def solution(mesh):
    return jax.shard_map(
        per_device,
        mesh=mesh,
        in_specs=(
            P(None, None, ("clip", "row")),
            P("clip"),
            P("clip"),
            P(),
            P(),
            P(),
            P(),
            P(),
            P(),
            P(("clip", "row"), None, None, None),
            P(),
            P(),
            P(),
            P(),
        ),
        out_specs=P(("clip", "row"), None, None, None),
        check_vma=False,
    )
```

```python
import functools

import jax
import jax.numpy as jnp
from jax import lax
from jax.experimental import pallas as pl
from jax.experimental.pallas import tpu as pltpu
from jax.sharding import PartitionSpec as P

PATCH = 16
GROUPS = 32
FRAMES = 16
LANES = 128
SLOTS = LANES // PATCH
eps_norm = 1e-06
BF16 = jnp.bfloat16
F32 = jnp.float32

SMEM = pl.BlockSpec(memory_space=pltpu.SMEM)
VMEM = pl.BlockSpec(memory_space=pltpu.VMEM)
FAR = pl.BlockSpec(memory_space=pl.ANY)


def iota(shape, dim):
    return lax.broadcasted_iota(jnp.int32, shape, dim)


def div(values, count):
    if count & (count - 1):
        return values // count
    return values >> (count.bit_length() - 1)


def mod(values, count):
    if count & (count - 1):
        return values % count
    return values & (count - 1)


def ones_where(condition):
    return jnp.where(condition, 1.0, 0.0).astype(BF16)


def matmul(left, right):
    return jnp.dot(left, right, preferred_element_type=F32)


def matmul_t(left, right):
    return lax.dot_general(left, right, (((1,), (1,)), ((), ())), preferred_element_type=F32)


def cut_in_three(values):
    high = values.astype(BF16)
    rest = values - high.astype(F32)
    middle = rest.astype(BF16)
    low = (rest - middle.astype(F32)).astype(BF16)
    return high, middle, low


def exact_rows(rows, product):
    place = iota((8, rows[0].shape[1]), 0)
    stacked = jnp.zeros(place.shape, F32)
    for index, row in enumerate(rows):
        for step, piece in enumerate(cut_in_three(row)):
            stacked = jnp.where(place == 3 * index + step, piece.astype(F32), stacked)
    result = product(jnp.concatenate([stacked, jnp.zeros_like(stacked)], axis=0).astype(BF16))
    return [
        result[3 * i : 3 * i + 1] + result[3 * i + 1 : 3 * i + 2] + result[3 * i + 2 : 3 * i + 3]
        for i in range(len(rows))
    ]


def silu_slope(values):
    sigmoid = jax.nn.sigmoid(values)
    return sigmoid * (1.0 + values * (1.0 - sigmoid))


def token_rows_of(height):
    return -(-(height // PATCH) // 16) * 16


def to_tokens(pixels):
    channels, columns, height = pixels.shape
    rows = channels * columns
    token_rows = token_rows_of(height)
    flat = pixels.reshape(rows, height)
    width = channels * PATCH * columns
    lane = iota((1, width), 1)
    place = iota((rows, 1), 0)
    mine = place == div(lane, PATCH * columns) * columns + mod(lane, columns)
    in_patch = mod(div(lane, columns), PATCH)
    pixel_row = iota((height, 1), 0)
    token = iota((token_rows, 1), 0)
    tokens = jnp.zeros((token_rows, width), F32)
    for t in range(height // PATCH):
        tiled = matmul(flat, ones_where(pixel_row == in_patch + t * PATCH))
        row = jnp.sum(jnp.where(mine, tiled, 0.0), axis=0, keepdims=True)
        tokens = jnp.where(token == t, row, tokens)
    return tokens.astype(BF16)


def forward_part(tokens, count, bias, gain, load_patch):
    embedded = jnp.zeros((tokens.shape[0], bias.shape[1]), F32)
    for low, high, weight in load_patch():
        embedded = embedded + matmul(tokens[:, low:high], weight)
    rows = -(-count // 8) * 8
    embedded = embedded[:rows] + bias[...]
    centred = embedded - jnp.mean(embedded, axis=1, keepdims=True)
    inv_spread = lax.rsqrt(jnp.mean(centred * centred, axis=1, keepdims=True) + eps_norm)
    normed = centred * inv_spread
    weighted = normed * gain[...]
    inside = iota((rows, 1), 0) < count
    pooled = jnp.sum(jnp.where(inside, weighted, 0.0), axis=0, keepdims=True)
    return normed, inv_spread, pooled


def led_by(leader, devices):
    return [leader] + [d for d in reversed(range(devices)) if d != leader]


def first_order(devices):
    return led_by(devices * 11 // 16, devices)


def message_shape(devices):
    return jax.ShapeDtypeStruct((devices, 4, LANES), F32)


def write_windows(patch_grad, sums, own_rows, height, send):
    span = PATCH * PATCH
    line = jnp.concatenate(
        [
            jnp.concatenate([patch_grad[t : t + 1, k * span : (k + 1) * span] for t in range(height // PATCH)], axis=1)
            for k in range(3)
        ]
        + [jnp.zeros((1, height * PATCH), F32)],
        axis=0,
    )
    line = jnp.concatenate([jnp.zeros((4, LANES), F32), line, jnp.zeros((4, LANES), F32)], axis=1)
    used = iota((4, LANES), 1) < (own_rows + 4) * PATCH
    colour = iota((4, LANES), 0)
    for index, d in enumerate(first_order(send.shape[0])):
        start = LANES + (d * own_rows - 2) * PATCH
        window = jnp.where(used, line[:, start : start + LANES], 0.0)
        send[index] = jnp.where(colour < 3, window, sums[:4])


def channel_sums(hidden):
    values = hidden.reshape(-1, hidden.shape[-1]).astype(F32)
    return jnp.sum(values, axis=0, keepdims=True), jnp.sum(values * values, axis=0, keepdims=True)


def over_group(values, size):
    lane = iota(values.shape, 1)
    lanes = values.shape[1]
    step = 1
    while step < size:
        later = pltpu.roll(values, lanes - step, 1)
        earlier = pltpu.roll(values, step, 1)
        values = values + jnp.where((lane & step) == 0, later, earlier)
        step *= 2
    return values


def group_sums(hidden):
    channels = hidden.shape[-1]
    size = channels // GROUPS
    first, second = [
        over_group(jnp.broadcast_to(x, (8, channels)), size) for x in channel_sums(hidden)
    ]
    lane = mod(iota((8, channels), 1), size)
    return jnp.where(lane == 0, first, jnp.where(lane == 1, second, 0.0))


def pull_back(row, weight):
    parts = []
    for low in range(0, weight.shape[0], LANES):
        product = weight[low : low + LANES, :].astype(F32) * row
        folded = product[:, :LANES]
        for start in range(LANES, weight.shape[1], LANES):
            folded = folded + product[:, start : start + LANES]
        parts.append(jnp.sum(folded.T, axis=0, keepdims=True))
    return jnp.concatenate(parts, axis=1)


def backward_part(
    owner, picks, gain, head_bias, head_out, normed, inv_spread, pooled, weight, head, through_head, slot, own_rows, height, sums, send
):
    (before,) = exact_rows([pooled], through_head)
    slope = head_out[...] * silu_slope(before + head_bias[...])
    pulled = pull_back(slope, head)
    wanted = owner[slot]
    picked = jnp.int32(0)
    for k in range(picks.shape[0]):
        picked = picked + jnp.where(picks[k] == wanted, 1, 0)
    scaled = gain[...] * (picked.astype(F32) * pulled)
    token_grad = inv_spread * (
        scaled
        - jnp.mean(scaled, axis=1, keepdims=True)
        - normed * jnp.mean(scaled * normed, axis=1, keepdims=True)
    )
    filler = jnp.zeros((-token_grad.shape[0] % 16, token_grad.shape[1]), F32)
    token_grad = jnp.concatenate([token_grad, filler], axis=0).astype(BF16)
    patch_grad = matmul_t(token_grad, weight[...]).astype(BF16).astype(F32)
    write_windows(patch_grad, sums, own_rows, height, send)


def write_edges(position, hidden, across, along):
    last = hidden.shape[0] - 1
    even = position % 2 == 0
    across[0] = hidden[jnp.where(even, last, 0)]
    along[0] = hidden[jnp.where(even, 0, last)]


def reward_kernel(*refs):
    position = lax.axis_index("row")
    count, kept = 7, 4
    far, refs = refs[: count + kept + 2], refs[count + kept + 2 :]
    send, across, along = refs[:3]
    near = refs[3 + kept : 3 + kept + count] + refs[3 : 3 + kept] + refs[3 + kept + count : -1]
    sems = refs[-1]
    frames, bias, gain, owner, picks, head_bias, head_out, hidden, _, _, _, patch, head = near
    count += kept
    depths = (256, 256)
    small = [pltpu.make_async_copy(far[i], near[i], sems.at[i]) for i in range(count)]
    pieces = []
    used = count
    for index, rows in enumerate(depths):
        source, target = far[count + index], near[count + index]
        parts = []
        for low in range(0, target.shape[0], rows):
            part = pl.ds(low, rows)
            parts.append(pltpu.make_async_copy(source.at[part], target.at[part], sems.at[used]))
            used += 1
        pieces.append(parts)
    for copy in [small[0], small[7]] + pieces[0] + small[1:7] + pieces[1] + small[8:]:
        copy.start()

    def load_patch():
        for copy in pieces[0] + small[1:3]:
            copy.wait()
        yield 0, patch.shape[0], patch[...]

    height = frames.shape[2]
    patches = height // PATCH
    small[0].wait()
    small[7].wait()
    tokens = to_tokens(frames[...])
    sums = group_sums(hidden[...])
    write_edges(position, hidden, across, along)
    normed, inv_spread, pooled = forward_part(tokens, patches, bias, gain, load_patch)
    for copy in small[3:7]:
        copy.wait()

    def through_head(rows):
        total = jnp.zeros((rows.shape[0], head.shape[1]), F32)
        for index, low in enumerate(range(0, head.shape[0], depths[1])):
            pieces[1][index].wait()
            total = total + matmul(rows[:, low : low + depths[1]], head[low : low + depths[1], :])
        return total

    backward_part(
        owner,
        picks,
        gain,
        head_bias,
        head_out,
        normed,
        inv_spread,
        pooled / patches,
        patch,
        head,
        through_head,
        position,
        hidden.shape[0],
        height,
        sums,
        send,
    )
    for copy in small[8:]:
        copy.wait()


def forward_kernel(frames, bias, gain, patch, normed, inv_spread, pooled):
    width = patch.shape[0]
    tokens = to_tokens(frames[...])
    normed[...], spread, pooled[...] = forward_part(
        tokens, frames.shape[2] // PATCH, bias, gain, lambda: [(0, width, patch[...])]
    )
    inv_spread[...] = jnp.broadcast_to(spread, inv_spread.shape)


def backward_kernel(
    owner,
    picks,
    hidden,
    gain,
    head_bias,
    head_out,
    normed,
    inv_spread,
    pooled,
    patch,
    head,
    send,
    across,
    along,
    *,
    height,
    per_frame,
):
    position = lax.axis_index("row")
    write_edges(position, hidden, across, along)
    backward_part(
        owner,
        picks,
        gain,
        head_bias,
        head_out,
        normed[...],
        inv_spread[...][:, :1],
        pooled[...],
        patch,
        head,
        lambda rows: matmul(rows, head[...]),
        position // per_frame,
        hidden.shape[0],
        height,
        group_sums(hidden[...]),
        send,
    )


def params(cells):
    return pltpu.CompilerParams(vmem_limit_bytes=min(16 + cells // 64, 48) * 1024 * 1024)


def near(array):
    return pltpu.with_memory_space_constraint(array, pltpu.VMEM)


def far(array):
    return pltpu.with_memory_space_constraint(array, pltpu.HBM)


def tap_lane(j, k, e):
    return (j + 1) * PATCH + 4 * k + e


def prepare_kernel(out_weight, wide, scratch):
    amount = scratch.shape[1] // LANES
    scratch[...] = jnp.zeros_like(scratch)
    for a in range(3):
        for e in range(3):
            for b in range(3):
                piece = out_weight[a, b, e].astype(F32)
                for i in range(amount):
                    for k in range(3):
                        at = a * LANES + tap_lane(i - b + 2, k, e)
                        scratch[at : at + 1, i * LANES : (i + 1) * LANES] = piece[k : k + 1]
    wide[...] = scratch[...].astype(BF16)


def norm_constants(totals, cell_total):
    channels = totals.shape[1]
    size = channels // GROUPS
    totals = jnp.broadcast_to(totals, (8, channels))
    lane = mod(iota((8, channels), 1), size)
    first, second = [over_group(jnp.where(lane == i, totals, 0.0), size)[:1] for i in range(2)]
    mean = first / cell_total
    return mean, lax.rsqrt(second / cell_total - mean * mean + eps_norm)


def scaled_slopes(state, mean, inverse, gain, shift):
    scale = gain * inverse
    return silu_slope(state * scale + (shift - mean * scale)) * scale


def slope_kernel(
    arrived,
    hidden,
    gain,
    shift,
    wide,
    far_owner,
    direct,
    edge_slopes,
    stats,
    sums,
    slopes_own,
    received,
    taps,
    owner,
    sem,
):
    copy = pltpu.make_async_copy(far_owner, owner, sem.at[0])
    copy.start()
    devices, message_rows, _ = arrived.shape
    own_rows, frame_count, width, channels = hidden.shape
    cells = frame_count * width
    per_frame = devices // frame_count
    got = arrived[...].reshape(received.shape)
    kind = mod(iota((got.shape[0], 1), 0), message_rows)
    totals = jnp.sum(jnp.where(kind == 3, got, 0.0), axis=0, keepdims=True)
    mean, inverse = norm_constants(totals, own_rows * devices * cells * (channels // GROUPS))
    for i in range(own_rows):
        state = hidden[i].reshape(cells, channels).astype(F32)
        slopes_own[i] = scaled_slopes(state, mean, inverse, gain[...], shift[...])

    if per_frame == 1:
        lane = iota((1, LANES), 1)
        entry = iota((LANES, 1), 0)
        turned = ones_where(entry - mod(entry, PATCH) + PATCH - 1 - mod(entry, PATCH) == lane)
        received[...] = matmul(jnp.where(kind < 3, got, 0.0).astype(BF16), turned)
        lane = mod(iota((PATCH, LANES), 1), PATCH)
        column = iota((PATCH, LANES), 0)
        marks = []
        for k in range(3):
            e = lane - 4 * k
            wanted = column - e + 1
            marks.append((e >= 0) & (e < 3) & (wanted >= 0) & (wanted < PATCH))
        copy.wait()
        for d in range(devices):
            row = first_order(devices)[d]
            block = jnp.zeros((PATCH, LANES), F32)
            for k in range(3):
                line = jnp.broadcast_to(received[d * message_rows + k : d * message_rows + k + 1, :], (PATCH, LANES))
                line = pltpu.roll(line, 4 * k + 2, 1, stride=1, stride_axis=0)
                block = jnp.where(marks[k], line, block)
            start = pl.multiple_of(owner[row] * PATCH, PATCH)
            taps[pl.ds(start, PATCH), :] = block.astype(BF16)
    else:
        copy.wait()
        received[...] = got
        lines = [received[pl.ds(k, devices, stride=message_rows), :] for k in range(3)]
        lines = jnp.concatenate(lines, axis=1).astype(BF16)
        place = iota((1, devices), 1)
        source = jnp.zeros_like(place)
        for index, d in enumerate(first_order(devices)):
            source = jnp.where(place == index, d, source)
        home = jnp.zeros((1, devices), jnp.int32)
        for b in range(frame_count):
            home = jnp.where(div(source, per_frame) == b, owner[b] * per_frame, home)
        home = home + mod(source, per_frame)
        cell = iota((cells, 1), 0)
        column = mod(cell, width)
        lane = mod(iota((1, 3 * LANES), 1), PATCH)
        entry = iota((3 * LANES, 1), 0)
        window_row = div(mod(entry, LANES), PATCH)
        found = jnp.zeros((cells, LANES), F32)
        for e in range(3):
            wanted = column - e + 1
            strip = div(cell, width) * per_frame + div(wanted, PATCH)
            placed = matmul(ones_where(home == strip), lines)
            inside = jnp.where((wanted >= 0) & (wanted < width), mod(wanted, PATCH), -1)
            kept = jnp.where(lane == inside, placed, 0.0).astype(BF16)
            target = jnp.where(
                window_row < own_rows + 4, tap_lane(window_row, div(entry, LANES), e), -1
            )
            found = found + matmul(kept, ones_where(target == iota((1, LANES), 1)))
        taps[:cells, :] = found.astype(BF16)
    taps[cells:, :] = jnp.zeros((2 * width, LANES), BF16)
    steps = [taps[(2 - a) * width : (2 - a) * width + cells, :] for a in range(3)]
    result = matmul(jnp.concatenate(steps, axis=1), wide[...])

    first = jnp.zeros((1, channels), F32)
    second = jnp.zeros((1, channels), F32)
    for i in range(own_rows):
        state = hidden[i].reshape(cells, channels).astype(F32)
        part = result[:, (i + 1) * channels : (i + 2) * channels] * slopes_own[i]
        direct[i] = part
        first = first + jnp.sum(part, axis=0, keepdims=True)
        second = second + jnp.sum(part * (state - mean), axis=0, keepdims=True)
    first = first / inverse
    edge_slopes[0] = result[:, :channels]
    edge_slopes[1] = result[:, (own_rows + 1) * channels :]
    stats[0:1, :] = mean
    stats[1:2, :] = inverse
    both = jnp.where(iota((2, channels), 0) == 0, first, second)
    sums[...] = jnp.broadcast_to(both[None], sums.shape)


def late_kernel(
    across, along, slopes, stats, gain, shift, far_weight, direct, states, turned, inner_weight, sem
):
    copy = pltpu.make_async_copy(far_weight, inner_weight, sem.at[0])
    copy.start()
    cells, channels = slopes.shape[1:]
    odd = lax.axis_index("row") % 2 == 1
    mean = stats[0:1, :]
    inverse = stats[1:2, :]
    for i in range(2):
        state = jnp.where(odd == (i == 0), across[0], along[0])
        states[i] = state
        values = state.reshape(cells, channels).astype(F32)
        direct[i] = slopes[i] * scaled_slopes(values, mean, inverse, gain[...], shift[...])
    copy.wait()
    size = inner_weight.shape[3]
    for b in range(3):
        for a in range(3):
            for e in range(3):
                at = (a * 3 + e) * size
                turned[at : at + size, b * size : (b + 1) * size] = inner_weight[a, b, e].T


def inner_kernel(
    arrived, stats, direct, hidden, edge_direct, edge_states, turned, far_out, out, sems, *, devices
):
    own_rows, frame_count, width, channels = out.shape
    cells = frame_count * width
    totals = jnp.sum(arrived[...], axis=0)
    cell_total = own_rows * devices * cells * (channels // GROUPS)
    place_row = iota((8, channels), 0)
    both = jnp.where(place_row == 0, totals[0:1], totals[1:2])
    both = over_group(both, channels // GROUPS)
    first, second = both[0:1], both[1:2]
    mean = stats[0:1, :]
    inverse = stats[1:2, :]
    constant = first / cell_total * inverse
    factor = second / cell_total * inverse * inverse
    position = lax.axis_index("row")
    in_frame = mod(iota((cells, 1), 0), width)
    results = [jnp.zeros((cells, channels), F32) for _ in range(own_rows)]
    copies = []
    for i in range(own_rows + 2):
        if 0 < i < own_rows + 1:
            state, part = hidden[i - 1], direct[i - 1]
        else:
            state, part = edge_states[min(i, 1)], edge_direct[min(i, 1)]
        grad = part - constant - (state.reshape(cells, channels).astype(F32) - mean) * factor
        if i == 0:
            grad = jnp.where(position > 0, grad, 0.0)
        if i == own_rows + 1:
            grad = jnp.where(position < devices - 1, grad, 0.0)
        after = jnp.where(in_frame < width - 1, pltpu.roll(grad, cells - 1, 0), 0.0)
        prior = jnp.where(in_frame > 0, pltpu.roll(grad, 1, 0), 0.0)
        taps = jnp.concatenate([after.astype(BF16), grad.astype(BF16), prior.astype(BF16)], axis=1)
        later = []
        for a in range(3):
            skip = (2 - a) * width
            filler = jnp.zeros((skip, taps.shape[1]), BF16)
            later.append(jnp.concatenate([taps[skip:], filler], axis=0) if skip else taps)
        joined = jnp.concatenate(later, axis=1)
        rows = [b for b in range(3) if 0 <= i + b - 2 < own_rows]
        for low in range(0, len(rows), 2):
            some = rows[low : low + 2]
            product = matmul(joined, turned[:, some[0] * channels : (some[-1] + 1) * channels])
            for step, b in enumerate(some):
                results[i + b - 2] = results[i + b - 2] + product[:, step * channels : (step + 1) * channels]
        if i >= 2:
            out[i - 2] = results[i - 2].reshape(frame_count, width, channels).astype(BF16)
            copies.append(pltpu.make_async_copy(out.at[i - 2], far_out.at[i - 2], sems.at[i - 2]))
            copies[-1].start()
    for copy in copies:
        copy.wait()


def per_device(
    frames,
    frame_owner,
    picks,
    patch_weight,
    patch_bias,
    norm_gain,
    head_weight,
    head_bias,
    head_out,
    hidden_state,
    group_gain,
    group_shift,
    out_weight,
    inner_weight,
):
    devices = lax.axis_size("row")
    per_frame = devices // FRAMES
    height = frames.shape[1]
    own_rows, _, frame_width, channels = hidden_state.shape
    cells = FRAMES * frame_width
    width = patch_weight.shape[1]
    turned_frames = jnp.transpose(frames, (0, 2, 1))
    bias = patch_bias.reshape(1, width)
    gain = norm_gain.reshape(1, width)
    head_bias_row = head_bias.reshape(1, width)
    head_out_row = head_out.reshape(1, width)
    state_rows = own_rows + 2
    edge = jax.ShapeDtypeStruct((1,) + hidden_state.shape[1:], BF16)
    message = (message_shape(devices), edge, edge)
    gain_row = group_gain.reshape(1, channels)
    shift_row = group_shift.reshape(1, channels)
    early = [hidden_state, gain_row, shift_row, out_weight]
    slope_outs = (
        pltpu.VMEM((own_rows, cells, channels), F32),
        pltpu.VMEM((2, cells, channels), F32),
        pltpu.VMEM((8, channels), F32),
        jax.ShapeDtypeStruct((devices, 2, channels), F32),
    )
    if per_frame == 1:
        arrays = [turned_frames, bias, gain, frame_owner, picks, head_bias_row, head_out_row]
        weights = [patch_weight, head_weight]

        def scratch(x):
            return (pltpu.SMEM if x.dtype == jnp.int32 else pltpu.VMEM)(x.shape, x.dtype)

        send, across, along, *early = pl.pallas_call(
            reward_kernel,
            out_shape=message + tuple(pltpu.VMEM(x.shape, x.dtype) for x in early),
            in_specs=[FAR] * (len(arrays) + len(early) + len(weights)),
            out_specs=[VMEM] * (3 + len(early)),
            scratch_shapes=[scratch(x) for x in arrays + weights] + [pltpu.SemaphoreType.DMA((32,))],
            compiler_params=params(0),
            name="reward",
        )(*[far(x) for x in arrays + early + weights])
    else:
        count = height // PATCH
        normed, inv_spread, partial = pl.pallas_call(
            forward_kernel,
            out_shape=(
                jax.ShapeDtypeStruct((-(-count // 8) * 8, width), F32),
                jax.ShapeDtypeStruct((-(-count // 8) * 8, LANES), F32),
                jax.ShapeDtypeStruct((1, width), F32),
            ),
            compiler_params=params(cells),
            name="reward_forward",
        )(turned_frames, bias, gain, patch_weight)
        members = [[b * per_frame + i for i in range(per_frame)] for b in range(FRAMES)]
        pooled = lax.psum(partial, "row", axis_index_groups=members) / (count * per_frame)
        send, across, along = pl.pallas_call(
            functools.partial(backward_kernel, height=height, per_frame=per_frame),
            out_shape=message,
            in_specs=[SMEM] * 2 + [VMEM] * 9,
            out_specs=[VMEM] * 3,
            compiler_params=params(cells),
            name="reward_backward",
        )(
            frame_owner,
            picks,
            hidden_state,
            gain,
            head_bias_row,
            head_out_row,
            normed,
            inv_spread,
            pooled,
            patch_weight,
            head_weight,
        )
    early = [near(x) for x in early]
    wide = pl.pallas_call(
        prepare_kernel,
        out_shape=pltpu.VMEM((3 * LANES, state_rows * channels), BF16),
        in_specs=[VMEM],
        scratch_shapes=[pltpu.VMEM((3 * LANES, state_rows * channels), F32)],
        compiler_params=params(cells),
        name="prepare",
    )(early[3])
    arrived = lax.all_to_all(send, "row", 0, 0, axis_index_groups=[first_order(devices)], tiled=True)
    direct, edge_slopes, stats, sums = pl.pallas_call(
        slope_kernel,
        out_shape=slope_outs,
        in_specs=[VMEM] * 5 + [FAR],
        scratch_shapes=[
            pltpu.VMEM((own_rows, cells, channels), F32),
            pltpu.VMEM((4 * devices, LANES), F32),
            pltpu.VMEM((cells + 2 * frame_width, LANES), BF16),
            pltpu.SMEM(frame_owner.shape, jnp.int32),
            pltpu.SemaphoreType.DMA((1,)),
        ],
        compiler_params=params(cells),
        name="slope",
    )(near(arrived), *early[:3], near(wide), far(frame_owner))
    swaps = [(2 * i, 2 * i + 1) for i in range(devices // 2)]
    across = lax.ppermute(across, "row", swaps + [(b, a) for a, b in swaps])
    swaps = [(2 * i - 1, 2 * i) for i in range(1, devices // 2)]
    along = lax.ppermute(along, "row", swaps + [(b, a) for a, b in swaps])
    summed = lax.all_to_all(sums, "row", 0, 0, axis_index_groups=[led_by(devices - 1, devices)], tiled=True)
    edge_direct, edge_states, turned = pl.pallas_call(
        late_kernel,
        out_shape=(
            pltpu.VMEM((2, cells, channels), F32),
            pltpu.VMEM((2,) + hidden_state.shape[1:], BF16),
            pltpu.VMEM((9 * channels, 3 * channels), BF16),
        ),
        in_specs=[VMEM] * 6 + [FAR],
        scratch_shapes=[pltpu.VMEM(inner_weight.shape, BF16), pltpu.SemaphoreType.DMA((1,))],
        input_output_aliases={2: 0},
        compiler_params=params(cells),
        name="late",
    )(near(across), near(along), near(edge_slopes), near(stats), *early[1:3], far(inner_weight))
    return pl.pallas_call(
        functools.partial(inner_kernel, devices=devices),
        out_shape=jax.ShapeDtypeStruct(hidden_state.shape, BF16),
        in_specs=[VMEM] * 7,
        out_specs=FAR,
        scratch_shapes=[
            pltpu.VMEM(hidden_state.shape, BF16),
            pltpu.SemaphoreType.DMA((own_rows,)),
        ],
        compiler_params=params(cells),
        name="inner",
    )(
        near(summed),
        near(stats),
        near(direct),
        early[0],
        near(edge_direct),
        near(edge_states),
        near(turned),
    )


def solution(mesh):
    return jax.shard_map(
        per_device,
        mesh=mesh,
        in_specs=(
            P(None, None, ("clip", "row")),
            P("clip"),
            P("clip"),
            P(),
            P(),
            P(),
            P(),
            P(),
            P(),
            P(("clip", "row"), None, None, None),
            P(),
            P(),
            P(),
            P(),
        ),
        out_specs=P(("clip", "row"), None, None, None),
        check_vma=False,
    )
```

```python
import functools

import jax
import jax.numpy as jnp
from jax import lax
from jax.experimental import pallas as pl
from jax.experimental.pallas import tpu as pltpu
from jax.sharding import PartitionSpec as P

PATCH = 16
GROUPS = 32
FRAMES = 16
LANES = 128
SLOTS = LANES // PATCH
eps_norm = 1e-06
BF16 = jnp.bfloat16
F32 = jnp.float32

SMEM = pl.BlockSpec(memory_space=pltpu.SMEM)
VMEM = pl.BlockSpec(memory_space=pltpu.VMEM)
FAR = pl.BlockSpec(memory_space=pl.ANY)


def iota(shape, dim):
    return lax.broadcasted_iota(jnp.int32, shape, dim)


def div(values, count):
    if count & (count - 1):
        return values // count
    return values >> (count.bit_length() - 1)


def mod(values, count):
    if count & (count - 1):
        return values % count
    return values & (count - 1)


def ones_where(condition):
    return jnp.where(condition, 1.0, 0.0).astype(BF16)


def matmul(left, right):
    return jnp.dot(left, right, preferred_element_type=F32)


def matmul_t(left, right):
    return lax.dot_general(left, right, (((1,), (1,)), ((), ())), preferred_element_type=F32)


def cut_in_three(values):
    high = values.astype(BF16)
    rest = values - high.astype(F32)
    middle = rest.astype(BF16)
    low = (rest - middle.astype(F32)).astype(BF16)
    return high, middle, low


def exact_rows(rows, product):
    place = iota((8, rows[0].shape[1]), 0)
    stacked = jnp.zeros(place.shape, F32)
    for index, row in enumerate(rows):
        for step, piece in enumerate(cut_in_three(row)):
            stacked = jnp.where(place == 3 * index + step, piece.astype(F32), stacked)
    result = product(jnp.concatenate([stacked, jnp.zeros_like(stacked)], axis=0).astype(BF16))
    return [
        result[3 * i : 3 * i + 1] + result[3 * i + 1 : 3 * i + 2] + result[3 * i + 2 : 3 * i + 3]
        for i in range(len(rows))
    ]


def silu_slope(values):
    sigmoid = jax.nn.sigmoid(values)
    return sigmoid * (1.0 + values * (1.0 - sigmoid))


def token_rows_of(height):
    return -(-(height // PATCH) // 16) * 16


def to_tokens(pixels):
    channels, columns, height = pixels.shape
    rows = channels * columns
    token_rows = token_rows_of(height)
    flat = pixels.reshape(rows, height)
    width = channels * PATCH * columns
    lane = iota((1, width), 1)
    place = iota((rows, 1), 0)
    mine = place == div(lane, PATCH * columns) * columns + mod(lane, columns)
    in_patch = mod(div(lane, columns), PATCH)
    pixel_row = iota((height, 1), 0)
    token = iota((token_rows, 1), 0)
    tokens = jnp.zeros((token_rows, width), F32)
    for t in range(height // PATCH):
        tiled = matmul(flat, ones_where(pixel_row == in_patch + t * PATCH))
        row = jnp.sum(jnp.where(mine, tiled, 0.0), axis=0, keepdims=True)
        tokens = jnp.where(token == t, row, tokens)
    return tokens.astype(BF16)


def forward_part(tokens, count, bias, gain, load_patch):
    embedded = jnp.zeros((tokens.shape[0], bias.shape[1]), F32)
    for low, high, weight in load_patch():
        embedded = embedded + matmul(tokens[:, low:high], weight)
    rows = -(-count // 8) * 8
    embedded = embedded[:rows] + bias[...]
    centred = embedded - jnp.mean(embedded, axis=1, keepdims=True)
    inv_spread = lax.rsqrt(jnp.mean(centred * centred, axis=1, keepdims=True) + eps_norm)
    normed = centred * inv_spread
    weighted = normed * gain[...]
    inside = iota((rows, 1), 0) < count
    pooled = jnp.sum(jnp.where(inside, weighted, 0.0), axis=0, keepdims=True)
    return normed, inv_spread, pooled


def led_by(leader, devices):
    return [leader] + [d for d in reversed(range(devices)) if d != leader]


def first_order(devices):
    return led_by(devices * 11 // 16, devices)


def message_shape(devices):
    return jax.ShapeDtypeStruct((devices, 4, LANES), F32)


def write_windows(patch_grad, sums, own_rows, height, send):
    span = PATCH * PATCH
    line = jnp.concatenate(
        [
            jnp.concatenate([patch_grad[t : t + 1, k * span : (k + 1) * span] for t in range(height // PATCH)], axis=1)
            for k in range(3)
        ]
        + [jnp.zeros((1, height * PATCH), F32)],
        axis=0,
    )
    line = jnp.concatenate([jnp.zeros((4, LANES), F32), line, jnp.zeros((4, LANES), F32)], axis=1)
    used = iota((4, LANES), 1) < (own_rows + 4) * PATCH
    colour = iota((4, LANES), 0)
    for index, d in enumerate(first_order(send.shape[0])):
        start = LANES + (d * own_rows - 2) * PATCH
        window = jnp.where(used, line[:, start : start + LANES], 0.0)
        send[index] = jnp.where(colour < 3, window, sums[:4])


def channel_sums(hidden):
    values = hidden.reshape(-1, hidden.shape[-1]).astype(F32)
    return jnp.sum(values, axis=0, keepdims=True), jnp.sum(values * values, axis=0, keepdims=True)


def over_group(values, size):
    lane = iota(values.shape, 1)
    lanes = values.shape[1]
    step = 1
    while step < size:
        later = pltpu.roll(values, lanes - step, 1)
        earlier = pltpu.roll(values, step, 1)
        values = values + jnp.where((lane & step) == 0, later, earlier)
        step *= 2
    return values


def group_sums(hidden):
    channels = hidden.shape[-1]
    size = channels // GROUPS
    first, second = [
        over_group(jnp.broadcast_to(x, (8, channels)), size) for x in channel_sums(hidden)
    ]
    lane = mod(iota((8, channels), 1), size)
    return jnp.where(lane == 0, first, jnp.where(lane == 1, second, 0.0))


def pull_back(row, weight):
    parts = []
    for low in range(0, weight.shape[0], LANES):
        product = weight[low : low + LANES, :].astype(F32) * row
        folded = product[:, :LANES]
        for start in range(LANES, weight.shape[1], LANES):
            folded = folded + product[:, start : start + LANES]
        parts.append(jnp.sum(folded.T, axis=0, keepdims=True))
    return jnp.concatenate(parts, axis=1)


def backward_part(
    owner, picks, gain, head_bias, head_out, normed, inv_spread, pooled, weight, head, through_head, slot, own_rows, height, sums, send
):
    (before,) = exact_rows([pooled], through_head)
    slope = head_out[...] * silu_slope(before + head_bias[...])
    pulled = pull_back(slope, head)
    wanted = owner[slot]
    picked = jnp.int32(0)
    for k in range(picks.shape[0]):
        picked = picked + jnp.where(picks[k] == wanted, 1, 0)
    scaled = gain[...] * (picked.astype(F32) * pulled)
    token_grad = inv_spread * (
        scaled
        - jnp.mean(scaled, axis=1, keepdims=True)
        - normed * jnp.mean(scaled * normed, axis=1, keepdims=True)
    )
    filler = jnp.zeros((-token_grad.shape[0] % 16, token_grad.shape[1]), F32)
    token_grad = jnp.concatenate([token_grad, filler], axis=0).astype(BF16)
    patch_grad = matmul_t(token_grad, weight[...]).astype(BF16).astype(F32)
    write_windows(patch_grad, sums, own_rows, height, send)


def write_edges(position, hidden, across, along):
    last = hidden.shape[0] - 1
    even = position % 2 == 0
    across[0] = hidden[jnp.where(even, last, 0)]
    along[0] = hidden[jnp.where(even, 0, last)]


def reward_kernel(*refs):
    position = lax.axis_index("row")
    count, kept = 7, 4
    far, refs = refs[: count + kept + 2], refs[count + kept + 2 :]
    send, across, along = refs[:3]
    near = refs[3 + kept : 3 + kept + count] + refs[3 : 3 + kept] + refs[3 + kept + count : -1]
    sems = refs[-1]
    frames, bias, gain, owner, picks, head_bias, head_out, hidden, _, _, _, patch, head = near
    count += kept
    depths = (256, 256)
    small = [pltpu.make_async_copy(far[i], near[i], sems.at[i]) for i in range(count)]
    pieces = []
    used = count
    for index, rows in enumerate(depths):
        source, target = far[count + index], near[count + index]
        parts = []
        for low in range(0, target.shape[0], rows):
            part = pl.ds(low, rows)
            parts.append(pltpu.make_async_copy(source.at[part], target.at[part], sems.at[used]))
            used += 1
        pieces.append(parts)
    for copy in [small[0], small[7]] + pieces[0] + small[1:7] + pieces[1] + small[8:]:
        copy.start()

    def load_patch():
        for copy in pieces[0] + small[1:3]:
            copy.wait()
        yield 0, patch.shape[0], patch[...]

    height = frames.shape[2]
    patches = height // PATCH
    small[0].wait()
    small[7].wait()
    tokens = to_tokens(frames[...])
    sums = group_sums(hidden[...])
    write_edges(position, hidden, across, along)
    normed, inv_spread, pooled = forward_part(tokens, patches, bias, gain, load_patch)
    for copy in small[3:7]:
        copy.wait()

    def through_head(rows):
        total = jnp.zeros((rows.shape[0], head.shape[1]), F32)
        for index, low in enumerate(range(0, head.shape[0], depths[1])):
            pieces[1][index].wait()
            total = total + matmul(rows[:, low : low + depths[1]], head[low : low + depths[1], :])
        return total

    backward_part(
        owner,
        picks,
        gain,
        head_bias,
        head_out,
        normed,
        inv_spread,
        pooled / patches,
        patch,
        head,
        through_head,
        position,
        hidden.shape[0],
        height,
        sums,
        send,
    )
    for copy in small[8:]:
        copy.wait()


def forward_kernel(frames, bias, gain, patch, normed, inv_spread, pooled):
    width = patch.shape[0]
    tokens = to_tokens(frames[...])
    normed[...], spread, pooled[...] = forward_part(
        tokens, frames.shape[2] // PATCH, bias, gain, lambda: [(0, width, patch[...])]
    )
    inv_spread[...] = jnp.broadcast_to(spread, inv_spread.shape)


def backward_kernel(
    owner,
    picks,
    hidden,
    gain,
    head_bias,
    head_out,
    normed,
    inv_spread,
    pooled,
    patch,
    head,
    send,
    across,
    along,
    *,
    height,
    per_frame,
):
    position = lax.axis_index("row")
    write_edges(position, hidden, across, along)
    backward_part(
        owner,
        picks,
        gain,
        head_bias,
        head_out,
        normed[...],
        inv_spread[...][:, :1],
        pooled[...],
        patch,
        head,
        lambda rows: matmul(rows, head[...]),
        position // per_frame,
        hidden.shape[0],
        height,
        group_sums(hidden[...]),
        send,
    )


def params(cells):
    return pltpu.CompilerParams(vmem_limit_bytes=min(16 + cells // 64, 48) * 1024 * 1024)


def near(array):
    return pltpu.with_memory_space_constraint(array, pltpu.VMEM)


def far(array):
    return pltpu.with_memory_space_constraint(array, pltpu.HBM)


def tap_lane(j, k, e):
    return (j + 1) * PATCH + 4 * k + e


def prepare_kernel(out_weight, wide, scratch):
    amount = scratch.shape[1] // LANES
    scratch[...] = jnp.zeros_like(scratch)
    for a in range(3):
        for e in range(3):
            for b in range(3):
                piece = out_weight[a, b, e].astype(F32)
                for i in range(amount):
                    for k in range(3):
                        at = a * LANES + tap_lane(i - b + 2, k, e)
                        scratch[at : at + 1, i * LANES : (i + 1) * LANES] = piece[k : k + 1]
    wide[...] = scratch[...].astype(BF16)


def norm_constants(totals, cell_total):
    channels = totals.shape[1]
    size = channels // GROUPS
    totals = jnp.broadcast_to(totals, (8, channels))
    lane = mod(iota((8, channels), 1), size)
    first, second = [over_group(jnp.where(lane == i, totals, 0.0), size)[:1] for i in range(2)]
    mean = first / cell_total
    return mean, lax.rsqrt(second / cell_total - mean * mean + eps_norm)


def scaled_slopes(state, mean, inverse, gain, shift):
    scale = gain * inverse
    return silu_slope(state * scale + (shift - mean * scale)) * scale


def slope_kernel(
    arrived,
    hidden,
    gain,
    shift,
    wide,
    far_owner,
    direct,
    edge_slopes,
    stats,
    sums,
    slopes_own,
    received,
    taps,
    owner,
    sem,
):
    copy = pltpu.make_async_copy(far_owner, owner, sem.at[0])
    copy.start()
    devices, message_rows, _ = arrived.shape
    own_rows, frame_count, width, channels = hidden.shape
    cells = frame_count * width
    per_frame = devices // frame_count
    got = arrived[...].reshape(received.shape)
    kind = mod(iota((got.shape[0], 1), 0), message_rows)
    totals = jnp.sum(jnp.where(kind == 3, got, 0.0), axis=0, keepdims=True)
    mean, inverse = norm_constants(totals, own_rows * devices * cells * (channels // GROUPS))
    for i in range(own_rows):
        state = hidden[i].reshape(cells, channels).astype(F32)
        slopes_own[i] = scaled_slopes(state, mean, inverse, gain[...], shift[...])

    if per_frame == 1:
        lane = iota((1, LANES), 1)
        entry = iota((LANES, 1), 0)
        turned = ones_where(entry - mod(entry, PATCH) + PATCH - 1 - mod(entry, PATCH) == lane)
        received[...] = matmul(jnp.where(kind < 3, got, 0.0).astype(BF16), turned)
        lane = mod(iota((PATCH, LANES), 1), PATCH)
        column = iota((PATCH, LANES), 0)
        marks = []
        for k in range(3):
            e = lane - 4 * k
            wanted = column - e + 1
            marks.append((e >= 0) & (e < 3) & (wanted >= 0) & (wanted < PATCH))
        copy.wait()
        for d in range(devices):
            row = first_order(devices)[d]
            block = jnp.zeros((PATCH, LANES), F32)
            for k in range(3):
                line = jnp.broadcast_to(received[d * message_rows + k : d * message_rows + k + 1, :], (PATCH, LANES))
                line = pltpu.roll(line, 4 * k + 2, 1, stride=1, stride_axis=0)
                block = jnp.where(marks[k], line, block)
            start = pl.multiple_of(owner[row] * PATCH, PATCH)
            taps[pl.ds(start, PATCH), :] = block.astype(BF16)
    else:
        copy.wait()
        received[...] = got
        lines = [received[pl.ds(k, devices, stride=message_rows), :] for k in range(3)]
        lines = jnp.concatenate(lines, axis=1).astype(BF16)
        place = iota((1, devices), 1)
        source = jnp.zeros_like(place)
        for index, d in enumerate(first_order(devices)):
            source = jnp.where(place == index, d, source)
        home = jnp.zeros((1, devices), jnp.int32)
        for b in range(frame_count):
            home = jnp.where(div(source, per_frame) == b, owner[b] * per_frame, home)
        home = home + mod(source, per_frame)
        cell = iota((cells, 1), 0)
        column = mod(cell, width)
        lane = mod(iota((1, 3 * LANES), 1), PATCH)
        entry = iota((3 * LANES, 1), 0)
        window_row = div(mod(entry, LANES), PATCH)
        found = jnp.zeros((cells, LANES), F32)
        for e in range(3):
            wanted = column - e + 1
            strip = div(cell, width) * per_frame + div(wanted, PATCH)
            placed = matmul(ones_where(home == strip), lines)
            inside = jnp.where((wanted >= 0) & (wanted < width), mod(wanted, PATCH), -1)
            kept = jnp.where(lane == inside, placed, 0.0).astype(BF16)
            target = jnp.where(
                window_row < own_rows + 4, tap_lane(window_row, div(entry, LANES), e), -1
            )
            found = found + matmul(kept, ones_where(target == iota((1, LANES), 1)))
        taps[:cells, :] = found.astype(BF16)
    taps[cells:, :] = jnp.zeros((2 * width, LANES), BF16)
    steps = [taps[(2 - a) * width : (2 - a) * width + cells, :] for a in range(3)]
    result = matmul(jnp.concatenate(steps, axis=1), wide[...])

    first = jnp.zeros((1, channels), F32)
    second = jnp.zeros((1, channels), F32)
    for i in range(own_rows):
        state = hidden[i].reshape(cells, channels).astype(F32)
        part = result[:, (i + 1) * channels : (i + 2) * channels] * slopes_own[i]
        direct[i] = part
        first = first + jnp.sum(part, axis=0, keepdims=True)
        second = second + jnp.sum(part * (state - mean), axis=0, keepdims=True)
    first = first / inverse
    edge_slopes[0] = result[:, :channels]
    edge_slopes[1] = result[:, (own_rows + 1) * channels :]
    stats[0:1, :] = mean
    stats[1:2, :] = inverse
    both = jnp.where(iota((2, channels), 0) == 0, first, second)
    sums[...] = jnp.broadcast_to(both[None], sums.shape)


def late_kernel(
    across, along, slopes, stats, gain, shift, far_weight, direct, states, turned, inner_weight, sem
):
    copy = pltpu.make_async_copy(far_weight, inner_weight, sem.at[0])
    copy.start()
    cells, channels = slopes.shape[1:]
    odd = lax.axis_index("row") % 2 == 1
    mean = stats[0:1, :]
    inverse = stats[1:2, :]
    for i in range(2):
        state = jnp.where(odd == (i == 0), across[0], along[0])
        states[i] = state
        values = state.reshape(cells, channels).astype(F32)
        direct[i] = slopes[i] * scaled_slopes(values, mean, inverse, gain[...], shift[...])
    copy.wait()
    size = inner_weight.shape[3]
    for b in range(3):
        for a in range(3):
            for e in range(3):
                at = (a * 3 + e) * size
                turned[at : at + size, b * size : (b + 1) * size] = inner_weight[a, b, e].T


def inner_kernel(
    arrived, stats, direct, hidden, edge_direct, edge_states, turned, far_out, out, sems, *, devices
):
    own_rows, frame_count, width, channels = out.shape
    cells = frame_count * width
    totals = jnp.sum(arrived[...], axis=0)
    cell_total = own_rows * devices * cells * (channels // GROUPS)
    place_row = iota((8, channels), 0)
    both = jnp.where(place_row == 0, totals[0:1], totals[1:2])
    both = over_group(both, channels // GROUPS)
    first, second = both[0:1], both[1:2]
    mean = stats[0:1, :]
    inverse = stats[1:2, :]
    constant = first / cell_total * inverse
    factor = second / cell_total * inverse * inverse
    position = lax.axis_index("row")
    in_frame = mod(iota((cells, 1), 0), width)
    results = [jnp.zeros((cells, channels), F32) for _ in range(own_rows)]
    copies = []
    for i in range(own_rows + 2):
        if 0 < i < own_rows + 1:
            state, part = hidden[i - 1], direct[i - 1]
        else:
            state, part = edge_states[min(i, 1)], edge_direct[min(i, 1)]
        grad = part - constant - (state.reshape(cells, channels).astype(F32) - mean) * factor
        if i == 0:
            grad = jnp.where(position > 0, grad, 0.0)
        if i == own_rows + 1:
            grad = jnp.where(position < devices - 1, grad, 0.0)
        after = jnp.where(in_frame < width - 1, pltpu.roll(grad, cells - 1, 0), 0.0)
        prior = jnp.where(in_frame > 0, pltpu.roll(grad, 1, 0), 0.0)
        taps = jnp.concatenate([after.astype(BF16), grad.astype(BF16), prior.astype(BF16)], axis=1)
        later = []
        for a in range(3):
            skip = (2 - a) * width
            filler = jnp.zeros((skip, taps.shape[1]), BF16)
            later.append(jnp.concatenate([taps[skip:], filler], axis=0) if skip else taps)
        joined = jnp.concatenate(later, axis=1)
        rows = [b for b in range(3) if 0 <= i + b - 2 < own_rows]
        for low in range(0, len(rows), 2):
            some = rows[low : low + 2]
            product = matmul(joined, turned[:, some[0] * channels : (some[-1] + 1) * channels])
            for step, b in enumerate(some):
                results[i + b - 2] = results[i + b - 2] + product[:, step * channels : (step + 1) * channels]
        if i >= 2:
            out[i - 2] = results[i - 2].reshape(frame_count, width, channels).astype(BF16)
            copies.append(pltpu.make_async_copy(out.at[i - 2], far_out.at[i - 2], sems.at[i - 2]))
            copies[-1].start()
    for copy in copies:
        copy.wait()


def per_device(
    frames,
    frame_owner,
    picks,
    patch_weight,
    patch_bias,
    norm_gain,
    head_weight,
    head_bias,
    head_out,
    hidden_state,
    group_gain,
    group_shift,
    out_weight,
    inner_weight,
):
    devices = lax.axis_size("row")
    per_frame = devices // FRAMES
    height = frames.shape[1]
    own_rows, _, frame_width, channels = hidden_state.shape
    cells = FRAMES * frame_width
    width = patch_weight.shape[1]
    turned_frames = jnp.transpose(frames, (0, 2, 1))
    bias = patch_bias.reshape(1, width)
    gain = norm_gain.reshape(1, width)
    head_bias_row = head_bias.reshape(1, width)
    head_out_row = head_out.reshape(1, width)
    state_rows = own_rows + 2
    edge = jax.ShapeDtypeStruct((1,) + hidden_state.shape[1:], BF16)
    message = (message_shape(devices), edge, edge)
    gain_row = group_gain.reshape(1, channels)
    shift_row = group_shift.reshape(1, channels)
    early = [hidden_state, gain_row, shift_row, out_weight]
    slope_outs = (
        pltpu.VMEM((own_rows, cells, channels), F32),
        pltpu.VMEM((2, cells, channels), F32),
        pltpu.VMEM((8, channels), F32),
        jax.ShapeDtypeStruct((devices, 2, channels), F32),
    )
    if per_frame == 1:
        arrays = [turned_frames, bias, gain, frame_owner, picks, head_bias_row, head_out_row]
        weights = [patch_weight, head_weight]

        def scratch(x):
            return (pltpu.SMEM if x.dtype == jnp.int32 else pltpu.VMEM)(x.shape, x.dtype)

        send, across, along, *early = pl.pallas_call(
            reward_kernel,
            out_shape=message + tuple(pltpu.VMEM(x.shape, x.dtype) for x in early),
            in_specs=[FAR] * (len(arrays) + len(early) + len(weights)),
            out_specs=[VMEM] * (3 + len(early)),
            scratch_shapes=[scratch(x) for x in arrays + weights] + [pltpu.SemaphoreType.DMA((32,))],
            compiler_params=params(0),
            name="reward",
        )(*[far(x) for x in arrays + early + weights])
    else:
        count = height // PATCH
        normed, inv_spread, partial = pl.pallas_call(
            forward_kernel,
            out_shape=(
                jax.ShapeDtypeStruct((-(-count // 8) * 8, width), F32),
                jax.ShapeDtypeStruct((-(-count // 8) * 8, LANES), F32),
                jax.ShapeDtypeStruct((1, width), F32),
            ),
            compiler_params=params(cells),
            name="reward_forward",
        )(turned_frames, bias, gain, patch_weight)
        members = [[b * per_frame + i for i in range(per_frame)] for b in range(FRAMES)]
        pooled = lax.psum(partial, "row", axis_index_groups=members) / (count * per_frame)
        send, across, along = pl.pallas_call(
            functools.partial(backward_kernel, height=height, per_frame=per_frame),
            out_shape=message,
            in_specs=[SMEM] * 2 + [VMEM] * 9,
            out_specs=[VMEM] * 3,
            compiler_params=params(cells),
            name="reward_backward",
        )(
            frame_owner,
            picks,
            hidden_state,
            gain,
            head_bias_row,
            head_out_row,
            normed,
            inv_spread,
            pooled,
            patch_weight,
            head_weight,
        )
    early = [near(x) for x in early]
    wide = pl.pallas_call(
        prepare_kernel,
        out_shape=pltpu.VMEM((3 * LANES, state_rows * channels), BF16),
        in_specs=[VMEM],
        scratch_shapes=[pltpu.VMEM((3 * LANES, state_rows * channels), F32)],
        compiler_params=params(cells),
        name="prepare",
    )(early[3])
    arrived = lax.all_to_all(send, "row", 0, 0, axis_index_groups=[first_order(devices)], tiled=True)
    direct, edge_slopes, stats, sums = pl.pallas_call(
        slope_kernel,
        out_shape=slope_outs,
        in_specs=[VMEM] * 5 + [FAR],
        scratch_shapes=[
            pltpu.VMEM((own_rows, cells, channels), F32),
            pltpu.VMEM((4 * devices, LANES), F32),
            pltpu.VMEM((cells + 2 * frame_width, LANES), BF16),
            pltpu.SMEM(frame_owner.shape, jnp.int32),
            pltpu.SemaphoreType.DMA((1,)),
        ],
        compiler_params=params(cells),
        name="slope",
    )(near(arrived), *early[:3], near(wide), far(frame_owner))
    swaps = [(2 * i, 2 * i + 1) for i in range(devices // 2)]
    across = lax.ppermute(across, "row", swaps + [(b, a) for a, b in swaps])
    swaps = [(2 * i - 1, 2 * i) for i in range(1, devices // 2)]
    along = lax.ppermute(along, "row", swaps + [(b, a) for a, b in swaps])
    summed = lax.all_to_all(sums, "row", 0, 0, axis_index_groups=[first_order(devices)], tiled=True)
    edge_direct, edge_states, turned = pl.pallas_call(
        late_kernel,
        out_shape=(
            pltpu.VMEM((2, cells, channels), F32),
            pltpu.VMEM((2,) + hidden_state.shape[1:], BF16),
            pltpu.VMEM((9 * channels, 3 * channels), BF16),
        ),
        in_specs=[VMEM] * 6 + [FAR],
        scratch_shapes=[pltpu.VMEM(inner_weight.shape, BF16), pltpu.SemaphoreType.DMA((1,))],
        input_output_aliases={2: 0},
        compiler_params=params(cells),
        name="late",
    )(near(across), near(along), near(edge_slopes), near(stats), *early[1:3], far(inner_weight))
    return pl.pallas_call(
        functools.partial(inner_kernel, devices=devices),
        out_shape=jax.ShapeDtypeStruct(hidden_state.shape, BF16),
        in_specs=[VMEM] * 7,
        out_specs=FAR,
        scratch_shapes=[
            pltpu.VMEM(hidden_state.shape, BF16),
            pltpu.SemaphoreType.DMA((own_rows,)),
        ],
        compiler_params=params(cells),
        name="inner",
    )(
        near(summed),
        near(stats),
        near(direct),
        early[0],
        near(edge_direct),
        near(edge_states),
        near(turned),
    )


def solution(mesh):
    return jax.shard_map(
        per_device,
        mesh=mesh,
        in_specs=(
            P(None, None, ("clip", "row")),
            P("clip"),
            P("clip"),
            P(),
            P(),
            P(),
            P(),
            P(),
            P(),
            P(("clip", "row"), None, None, None),
            P(),
            P(),
            P(),
            P(),
        ),
        out_specs=P(("clip", "row"), None, None, None),
        check_vma=False,
    )
```
